32 devices in a mesh: dp: 8 (over y, x, core), mp: 4 (over z).
Axes of the slice: x: 2, y: 2, z: 4, core: 2. Of those that a mesh axis runs over, the one named last changes fastest.
Arguments:
- block_input: bfloat16 [2016, 12544], P('mp', 'dp'), may hold values from -12 to 12
- output_grad: bfloat16 [2016, 12544], P('mp', 'dp'), may hold values from -1.2e-05 to 1.2e-05
- w_reduce: float32 [2016, 2016], P('dp', 'mp')
- w_group: float32 [2016, 504], P('dp')
- w_squeeze: float32 [2016, 504], P(None, 'mp')
- w_excite: float32 [504, 2016], P(None, 'mp')
- w_expand: float32 [2016, 2016], P('dp', 'mp')
- w_project: float32 [2016, 256], P(None, 'mp')
- prototypes: float32 [256, 3000], P(None, 'mp')
- bn_gains: float32 [3, 2016], P(None, 'mp'), may hold values from 0.5 to 1.5
- bn_biases: float32 [3, 2016], P(None, 'mp'), may hold values from -4 to 4
- m_reduce: float32 [2016, 2016], P('dp', 'mp'), may hold values from -0.00030517578 to 0.00030517578
- m_group: float32 [2016, 504], P('dp'), may hold values from -0.00061035156 to 0.00061035156
- m_squeeze: float32 [2016, 504], P(None, 'mp'), may hold values from -0.00030517578 to 0.00030517578
- m_excite: float32 [504, 2016], P(None, 'mp'), may hold values from -0.0029296875 to 0.0029296875
- m_expand: float32 [2016, 2016], P('dp', 'mp'), may hold values from -0.00030517578 to 0.00030517578
- m_project: float32 [2016, 256], P(None, 'mp'), may hold values from -0.00030517578 to 0.00030517578
- m_protos: float32 [256, 3000], P(None, 'mp'), may hold values from -0.0014648438 to 0.0014648438
- m_gains: float32 [3, 2016], P(None, 'mp'), may hold values from -0.015625 to 0.015625
- m_biases: float32 [3, 2016], P(None, 'mp'), may hold values from -0.00390625 to 0.00390625
- queue_store: float32 [1024, 256], P('dp'), may hold values from -0.7 to 0.7
- queue_slots: int32 [8, 128], P('dp'), may hold values from 0 to 127
- crop_perm: int32 [8, 8], P('dp'), may hold values from 0 to 7, each once within a row
Outputs:
- block_output: bfloat16 [2016, 12544], P('mp', 'dp')
- loss: float32 [], replicated
- input_grad: float32 [2016, 12544], P('mp', 'dp')
- mom_reduce: float32 [2016, 2016], P('dp', 'mp')
- mom_group: float32 [2016, 504], P('dp')
- mom_squeeze: float32 [2016, 504], P(None, 'mp')
- mom_excite: float32 [504, 2016], P(None, 'mp')
- mom_expand: float32 [2016, 2016], P('dp', 'mp')
- mom_project: float32 [2016, 256], P(None, 'mp')
- mom_protos: float32 [256, 3000], P(None, 'mp')
- mom_gains: float32 [3, 2016], P(None, 'mp')
- mom_biases: float32 [3, 2016], P(None, 'mp')
- param_norms: float32 [13, 2], replicated
The draws below stay inside these ranges and needn't reach their ends.
Inputs may be any that keep to these rules, and one draw needn't show every extreme that they name: `queue_slots`: each entry picks one of the 128 rows of queue_store that share the entry's index of dp; a row may be picked more than once. `crop_perm`: each row lists 0 to 7 once.
All inputs are finite; a program needn't handle non-finite values.
Results may differ from the reference program's by a relative error of at most 0.018.
Values may be sent and summed in bfloat16 or wider, within the bound.
No kernel may reach another device: no remote copies, remote signals or barrier semaphores. Data moves between devices by JAX's collectives and lax.ppermute only.
A program may use at most 512 MiB of HBM per device.

```python
import math
import jax
import jax.numpy as jnp
from jax import lax

C = 2016
GROUPS = 36
SE = 504
PD = 256
PROTOS = 3000
HW = 14
SINK = 3
CROPS_DEV = 8
QUEUE_DEV = 128
GW = 56
DATA_GROUPS = 8
CROP_TOTAL = 64
PIX = 12544
QUEUE = 1024
N_DP = 8


def ramp(length, factor):
    position = jnp.arange(length, dtype=jnp.float32) / max(length - 1, 1)
    return jnp.exp(math.log(factor) * (position - 0.5))


def shaped(sample, deviation, row_factor, col_factor):
    return sample * deviation * ramp(sample.shape[0], row_factor)[:, None] * ramp(sample.shape[1], col_factor)[None, :]


def draw_block_input(key, part):
    key = jax.random.fold_in(key, 1)
    pixel_key, crop_key, channel_key = jax.random.split(key, 3)
    pixel_noise = jax.random.normal(pixel_key, (CROP_TOTAL, HW * HW, C), jnp.float32)
    factor = 3.0
    crop_offset = 0.7 * jax.random.normal(crop_key, (CROP_TOTAL, 1, C), jnp.float32)
    channel_scale = jnp.exp(jax.random.uniform(channel_key, (1, 1, C), jnp.float32, -0.7, 0.7))
    values = (pixel_noise + crop_offset) * channel_scale * ramp(CROP_TOTAL, factor)[:, None, None]
    return jnp.clip(values, -12.0, 12.0).reshape(PIX, C).T.astype(jnp.bfloat16)


def draw_output_grad(key, part):
    key = jax.random.fold_in(key, 2)
    pixel_key, channel_key = jax.random.split(key, 2)
    pixel_noise = jax.random.normal(pixel_key, (CROP_TOTAL, HW * HW, C), jnp.float32)
    factor = 3.0
    channel_scale = jnp.exp(jax.random.uniform(channel_key, (1, 1, C), jnp.float32, -0.7, 0.7))
    values = pixel_noise * channel_scale * ramp(CROP_TOTAL, factor)[:, None, None]
    values = jnp.clip(values, -12.0, 12.0) * 1e-06
    return values.reshape(PIX, C).T.astype(jnp.bfloat16)


def matrix_sample(key, rows, cols):
    return jnp.clip(jax.random.normal(key, (rows, cols), jnp.float32), -6.0, 6.0)


def draw_w_reduce(key, part):
    key = jax.random.fold_in(key, 3)
    return shaped(matrix_sample(key, C, C), C ** (-0.5), 3.0, 3.0)


def draw_w_group(key, part):
    key = jax.random.fold_in(key, 4)
    return shaped(matrix_sample(key, C, 9 * GW), (9 * GW) ** (-0.5), 3.0, 1.0)


def draw_w_squeeze(key, part):
    key = jax.random.fold_in(key, 5)
    return shaped(matrix_sample(key, C, SE), C ** (-0.5), 1.0, 3.0)


def draw_w_excite(key, part):
    key = jax.random.fold_in(key, 6)
    return shaped(matrix_sample(key, SE, C), 4.0 * SE ** (-0.5), 1.0, 3.0)


def draw_w_expand(key, part):
    key = jax.random.fold_in(key, 7)
    return shaped(matrix_sample(key, C, C), C ** (-0.5), 3.0, 3.0)


def draw_w_project(key, part):
    key = jax.random.fold_in(key, 8)
    return shaped(matrix_sample(key, C, PD), C ** (-0.5), 1.0, 3.0)


def draw_prototypes(key, part):
    key = jax.random.fold_in(key, 9)
    return shaped(matrix_sample(key, PD, PROTOS), 0.12, 1.0, 3.0)


def draw_queue_store(key, part):
    key = jax.random.fold_in(key, 10)
    sample = shaped(matrix_sample(key, QUEUE, PD), PD ** (-0.5), 3.0, 1.0)
    return jnp.clip(sample, -0.7, 0.7)


def place_ends(values, rng, least, high):
    spot = [jax.random.randint(jax.random.fold_in(rng, axis), (), 0, length) for axis, length in enumerate(values.shape)]
    longest = values.shape.index(max(values.shape))
    neighbour = spot[:longest] + [(spot[longest] + 1) % values.shape[longest]] + spot[longest + 1:]
    return values.at[tuple(spot)].set(least).at[tuple(neighbour)].set(high)


def level_of(rng, extent, cuts, least, largest):
    factor_of, own = 1.0, jax.random.fold_in(rng, 6)
    for dim, blocks in cuts:
        steps = jnp.exp(jax.random.uniform(jax.random.fold_in(own, dim), (blocks,), jnp.float32, least / len(cuts), largest / len(cuts)))
        factor_of = factor_of * jnp.repeat(steps, extent[dim] // blocks).reshape([-1 if axis == dim else 1 for axis in range(len(extent))])
    return factor_of


def centred(stream_key, dims, width, bound, pieces=(), held_as=jnp.bfloat16):
    gain = level_of(stream_key, dims, pieces, -0.22, 0.18) if pieces else 1.0
    entries = jax.random.normal(stream_key, dims, jnp.float32) * width * gain
    return jnp.minimum(jnp.maximum(entries, -bound), bound).astype(held_as)


def setup_inputs(seed: int = 0) -> dict:
    keys = jax.random.split(jax.random.key(seed), 24)
    block_input = draw_block_input(jax.random.fold_in(keys[23], 71), 0)
    output_grad = draw_output_grad(jax.random.fold_in(keys[23], 71), 0)
    w_reduce = draw_w_reduce(jax.random.fold_in(keys[23], 71), 0)
    w_group = draw_w_group(jax.random.fold_in(keys[23], 71), 0)
    w_squeeze = draw_w_squeeze(jax.random.fold_in(keys[23], 71), 0)
    w_excite = draw_w_excite(jax.random.fold_in(keys[23], 71), 0)
    w_expand = draw_w_expand(jax.random.fold_in(keys[23], 71), 0)
    w_project = draw_w_project(jax.random.fold_in(keys[23], 71), 0)
    prototypes = draw_prototypes(jax.random.fold_in(keys[23], 71), 0)
    bn_gains = jnp.clip(1.0 + 0.1 * jax.random.normal(keys[9], (3, C), jnp.float32), 0.5, 1.5)
    bn_biases = centred(keys[10], (3, C), 0.3, 4.0, ((1, 4),), jnp.float32)
    m_reduce = centred(keys[11], (C, C), 0.00002, 0.00030517578, ((0, 8), (1, 4)), jnp.float32)
    m_group = centred(keys[12], (C, 9 * GW), 0.00004, 0.00061035156, ((0, 8),), jnp.float32)
    m_squeeze = centred(keys[13], (C, SE), 0.00002, 0.00030517578, ((1, 4),), jnp.float32)
    m_excite = centred(keys[14], (SE, C), 0.0002, 0.0029296875, ((1, 4),), jnp.float32)
    m_expand = centred(keys[15], (C, C), 0.00002, 0.00030517578, ((0, 8), (1, 4)), jnp.float32)
    m_project = centred(keys[16], (C, PD), 0.00002, 0.00030517578, ((1, 4),), jnp.float32)
    m_protos = centred(keys[17], (PD, PROTOS), 0.0001, 0.0014648438, ((1, 4),), jnp.float32)
    m_gains = centred(keys[18], (3, C), 0.001, 0.015625, ((1, 4),), jnp.float32)
    m_biases = centred(keys[19], (3, C), 0.0003, 0.00390625, ((1, 4),), jnp.float32)
    queue_store = draw_queue_store(jax.random.fold_in(keys[23], 71), 0)
    queue_slots = place_ends(jax.random.randint(keys[21], (DATA_GROUPS, QUEUE_DEV), 0, QUEUE_DEV), jax.random.fold_in(keys[21], 1), 0, QUEUE_DEV - 1).astype(jnp.int32)
    crop_perm = jax.vmap(lambda own: jax.random.permutation(own, CROPS_DEV))(jax.random.split(keys[22], DATA_GROUPS)).reshape((DATA_GROUPS, CROPS_DEV)).astype(jnp.int32)
    return dict(block_input=block_input, output_grad=output_grad, w_reduce=w_reduce, w_group=w_group, w_squeeze=w_squeeze, w_excite=w_excite, w_expand=w_expand, w_project=w_project, prototypes=prototypes, bn_gains=bn_gains, bn_biases=bn_biases, m_reduce=m_reduce, m_group=m_group, m_squeeze=m_squeeze, m_excite=m_excite, m_expand=m_expand, m_project=m_project, m_protos=m_protos, m_gains=m_gains, m_biases=m_biases, queue_store=queue_store, queue_slots=queue_slots, crop_perm=crop_perm)


EPS_BN = 1e-05
EPS_NORM = 1e-06
EPS_SINK = 0.05
SOFTMAX_TEMPER = 0.1
TRUST = 0.001
DECAY = 1e-06
MOMENTUM = 0.9
HIGHEST = lax.Precision.HIGHEST

@jax.custom_vjp
def low(v):
    return lax.optimization_barrier(v.astype(jnp.bfloat16)).astype(jnp.float32)

@jax.custom_vjp
def low_back(v):
    return v

def low_keep(v):
    return (low(v), None)

def low_pass(kept, grad):
    return (grad,)

def back_keep(v):
    return (v, None)

def back_low(kept, grad):
    return (low(grad),)
low.defvjp(low_keep, low_pass)
low_back.defvjp(back_keep, back_low)

def product(left, right):
    return jnp.dot(left, right, precision=HIGHEST, preferred_element_type=jnp.float32)

def batch_norm(values, gain_row, shift_row):
    average = lax.optimization_barrier(jnp.mean(values, 0))
    spread = lax.optimization_barrier(jnp.mean(values * values, 0)) - average * average
    return (values - average) * lax.rsqrt(spread + EPS_BN) * gain_row + shift_row

def crop_mean(values):
    return lax.optimization_barrier(jnp.mean(values.reshape(CROP_TOTAL, HW * HW, C), 1))

def forward(inputs, w_reduce, w_group, w_squeeze, w_excite, w_expand, w_project, prototypes, bn_gains, bn_biases):
    reduced = low_back(product(inputs, low(w_reduce)))
    reduced_act = low_back(low(jax.nn.silu(batch_norm(reduced, bn_gains[0], bn_biases[0]))))
    kernel = low(w_group).reshape(C, 3, 3, GW)
    grouped = lax.conv_general_dilated(reduced_act.reshape(CROP_TOTAL, HW, HW, C), kernel, (1, 1), ((1, 1), (1, 1)), dimension_numbers=('NHWC', 'OHWI', 'NHWC'), feature_group_count=GROUPS, precision=HIGHEST)
    grouped_low = low_back(low(grouped.reshape(PIX, C)))
    grouped_act = jax.nn.silu(batch_norm(grouped_low, bn_gains[1], bn_biases[1]))
    pooled = low(crop_mean(grouped_act))
    squeezed = low_back(product(pooled, low(w_squeeze)))
    squeeze_act = low(jax.nn.silu(squeezed))
    excited = low_back(product(squeeze_act, low(w_excite)))
    gating = jax.nn.sigmoid(excited)
    gated_low = low((grouped_act.reshape(CROP_TOTAL, HW * HW, C) * gating[:, None, :]).reshape(PIX, C))
    expanded = low_back(product(gated_low, low(w_expand)))
    block_value = jax.nn.silu(inputs + batch_norm(expanded, bn_gains[2], bn_biases[2]))
    summary = low(crop_mean(block_value))
    embedded = low_back(product(summary, low(w_project)))
    unit_embed = low(embedded * lax.rsqrt(lax.optimization_barrier(jnp.sum(embedded * embedded, 1, keepdims=True)) + EPS_NORM))
    prototype_scores = low_back(product(unit_embed, low(prototypes)))
    return (block_value, prototype_scores)

def reference(block_input, output_grad, w_reduce, w_group, w_squeeze, w_excite, w_expand, w_project, prototypes, bn_gains, bn_biases, m_reduce, m_group, m_squeeze, m_excite, m_expand, m_project, m_protos, m_gains, m_biases, queue_store, queue_slots, crop_perm):
    pixel_input = block_input.astype(jnp.float32).T
    pixel_cotangent = output_grad.astype(jnp.float32).T
    outputs, pullback = jax.vjp(forward, pixel_input, w_reduce, w_group, w_squeeze, w_excite, w_expand, w_project, prototypes, bn_gains, bn_biases)
    block_value, prototype_scores = outputs
    picks = (jnp.arange(N_DP, dtype=jnp.int32)[:, None] * QUEUE_DEV + queue_slots).reshape(-1).astype(jnp.int32)
    queue_rows = jnp.take(queue_store, picks, axis=0)
    queue_scores = product(low(queue_rows), low(prototypes))
    transport = jnp.exp(jnp.concatenate([prototype_scores, queue_scores], 0) / EPS_SINK)
    for sweep_index in range(SINK):
        transport = transport / lax.optimization_barrier(jnp.sum(transport, 0, keepdims=True))
        transport = transport / lax.optimization_barrier(jnp.sum(transport, 1, keepdims=True))
    assigned = transport[:CROP_TOTAL].reshape(N_DP, CROPS_DEV, PROTOS)
    pairing = (crop_perm[:, None, :] == jnp.bitwise_xor(crop_perm, 1)[:, :, None]).astype(jnp.float32)
    target_codes = jnp.einsum('dij,djk->dik', pairing, assigned, precision=HIGHEST).reshape(CROP_TOTAL, PROTOS)

    def swap_loss(values_of_scores):
        return -jnp.sum(target_codes * jax.nn.log_softmax(values_of_scores / SOFTMAX_TEMPER, axis=1)) / CROP_TOTAL
    loss_value, gradient_of_scores = jax.value_and_grad(swap_loss)(prototype_scores)
    gradients = pullback((pixel_cotangent, gradient_of_scores))
    weight_list = [w_reduce, w_group, w_squeeze, w_excite, w_expand, w_project, prototypes] + [bn_gains[row_index] for row_index in range(3)] + [bn_biases[row_index] for row_index in range(3)]
    grad_list = list(gradients[1:8]) + [gradients[8][row_index] for row_index in range(3)] + [gradients[9][row_index] for row_index in range(3)]
    moment_list = [m_reduce, m_group, m_squeeze, m_excite, m_expand, m_project, m_protos] + [m_gains[row_index] for row_index in range(3)] + [m_biases[row_index] for row_index in range(3)]
    mom_list = []
    norm_rows = []
    for weight, gradient, momentum in zip(weight_list, grad_list, moment_list):
        weight_norm = jnp.sqrt(jnp.sum(weight * weight) + EPS_NORM)
        grad_norm = jnp.sqrt(jnp.sum(gradient * gradient) + EPS_NORM)
        local_rate = TRUST * weight_norm / (grad_norm + DECAY * weight_norm)
        moment = MOMENTUM * momentum + local_rate * (gradient + DECAY * weight)
        mom_list.append(moment)
        norm_rows.append(jnp.stack([weight_norm, grad_norm]))
    return (block_value.T.astype(jnp.bfloat16), loss_value, gradients[0].T, mom_list[0], mom_list[1], mom_list[2], mom_list[3], mom_list[4], mom_list[5], mom_list[6], jnp.stack(mom_list[7:10]), jnp.stack(mom_list[10:13]), jnp.stack(norm_rows))
```

```python
import functools

import jax
import jax.numpy as jnp
import numpy as np
from jax import lax
from jax.experimental import pallas as pl
from jax.experimental.pallas import tpu as pltpu
from jax.sharding import PartitionSpec as P

HW = 14
PIXELS = HW * HW
SINK = 3
EPS_BN = 1e-05
EPS_NORM = 1e-06
EPS_SINK = 0.05
SOFTMAX_TEMPER = 0.1
TRUST = 0.001
DECAY = 1e-06
MOMENTUM = 0.9

QUADS = 4
QUAD = 504
HALF = 252
LANES = 512
GAP = LANES - QUAD
GROUP = 56
SE_PART = 63
SE_LANES = 64
PITCH = 16
VMEM_BYTES = 48 * 1024 * 1024
f32 = jnp.float32
bf16 = jnp.bfloat16
NN = (((1,), (0,)), ((), ()))
NT = (((1,), (1,)), ((), ()))
TN = (((0,), (0,)), ((), ()))


def dot(a, b, dims=NN):
    return lax.dot_general(a, b, dims, preferred_element_type=f32)


def widen(v, axis):
    first = lax.slice_in_dim(v, 0, HALF, axis=axis)
    last = lax.slice_in_dim(v, HALF, QUAD, axis=axis)
    shape = list(v.shape)
    shape[axis] = GAP
    return jnp.concatenate([first, jnp.zeros(shape, v.dtype), last], axis)


def narrow(v, axis):
    first = lax.slice_in_dim(v, 0, HALF, axis=axis)
    last = lax.slice_in_dim(v, HALF + GAP, LANES, axis=axis)
    return jnp.concatenate([first, last], axis)


def spread_channels(v):
    lead = v.shape[:-1]
    return widen(v.reshape(lead + (QUADS, QUAD)), len(lead) + 1).reshape(lead + (QUADS * LANES,))


def pack_channels(v):
    lead = v.shape[:-1]
    return narrow(v.reshape(lead + (QUADS, LANES)), len(lead) + 1).reshape(lead + (QUADS * QUAD,))


def half_rows(v, position):
    pad = 256 - HALF
    padded = jnp.pad(v, ((pad, pad),) + ((0, 0),) * (v.ndim - 1))
    return lax.dynamic_slice_in_dim(padded, pad * (1 - position % 2), 256, 0)


def unhalf_rows(v, position):
    return lax.dynamic_slice_in_dim(v, (256 - HALF) * (position % 2), HALF, 0)


def spread_inner(v):
    lead = v.shape[:-1]
    parts = v.shape[-1] // SE_PART
    v = v.reshape(lead + (parts, SE_PART))
    v = jnp.pad(v, ((0, 0),) * (v.ndim - 1) + ((0, SE_LANES - SE_PART),))
    return v.reshape(lead + (parts * SE_LANES,))


def pack_inner(v):
    lead = v.shape[:-1]
    parts = v.shape[-1] // SE_LANES
    return v.reshape(lead + (parts, SE_LANES))[..., :SE_PART].reshape(lead + (parts * SE_PART,))


def sum_axis(v, axis):
    n = lax.axis_size(axis)
    step = 1
    while step < n:
        v = v + lax.ppermute(v, axis, [(i, i ^ step) for i in range(n)])
        step *= 2
    return v


def total(v):
    return sum_axis(sum_axis(v, "mp"), "dp")


def gather_axis(v, axis):
    n = lax.axis_size(axis)
    me = lax.axis_index(axis)
    out = v[None]
    step = 1
    while step < n:
        got = lax.ppermute(out, axis, [(i, i ^ step) for i in range(n)])
        out = jnp.where(
            (me & step) == 0, jnp.concatenate([out, got]), jnp.concatenate([got, out])
        )
        step *= 2
    return out


def gather_all(v):
    out = gather_axis(gather_axis(v, "mp"), "dp")
    return out.reshape((-1,) + v.shape[1:])


def exchange(blocks):
    n = lax.axis_size("mp")
    me = lax.axis_index("mp")
    got = [
        lax.ppermute(
            lax.dynamic_index_in_dim(blocks, me ^ k, 0, keepdims=False),
            "mp",
            [(i, i ^ k) for i in range(n)],
        )
        for k in range(1, n)
    ]
    out = blocks
    for k in range(1, n):
        out = lax.dynamic_update_index_in_dim(out, got[k - 1], me ^ k, 0)
    return out


def to_slab(v):
    n = lax.axis_size("mp")
    quick = v.shape[0] == QUAD
    if quick:
        v = widen(v, 0)
    rows = v.shape[1] // n
    got = exchange(v.T.reshape(n, rows, v.shape[0]))
    out = got.transpose(1, 0, 2).reshape(rows, n * v.shape[0])
    return out if quick else spread_channels(out)


def from_slab(v, channels):
    n = lax.axis_size("mp")
    quick = channels == QUAD
    if not quick:
        v = pack_channels(v)
    rows = v.shape[0]
    got = exchange(v.reshape(rows, n, -1).transpose(1, 0, 2))
    out = got.reshape(n * rows, -1).T
    return narrow(out, 0) if quick else out


def gather_square(w):
    low = w.astype(bf16)
    if low.shape == (HALF, QUAD):
        low = half_rows(widen(low, 1), lax.axis_index("dp"))
        return lax.all_gather(lax.all_gather(low, "mp"), "dp")
    full = lax.all_gather(lax.all_gather(low, "mp", axis=1, tiled=True), "dp", axis=0, tiled=True)
    full = spread_channels(spread_channels(full).T).T
    return full.reshape(2 * QUADS, 256, QUADS, LANES).transpose(0, 2, 1, 3)


def scatter_square(g, shape):
    if shape == (HALF, QUAD):
        part = lax.psum_scatter(g, "dp", scatter_dimension=0, tiled=False)
        part = lax.psum_scatter(part, "mp", scatter_dimension=0, tiled=False)
        return narrow(unhalf_rows(part, lax.axis_index("dp")).astype(f32), 1)
    full = g.transpose(0, 2, 1, 3).reshape(2 * QUADS * 256, QUADS * LANES)
    full = pack_channels(pack_channels(full).T).T
    part = lax.psum_scatter(full, "dp", scatter_dimension=0, tiled=True)
    return lax.psum_scatter(part, "mp", scatter_dimension=1, tiled=True).astype(f32)


def gather_kernel(w):
    low = w.astype(bf16)
    if low.shape[0] == HALF:
        return lax.all_gather(half_rows(low, lax.axis_index("dp")).T, "dp")
    full = lax.all_gather(low, "dp", axis=0, tiled=True)
    return spread_channels(full.T).reshape(-1, 2 * QUADS, 256).transpose(1, 0, 2)


def scatter_kernel(g, rows):
    if rows == HALF:
        part = lax.psum_scatter(g, "dp", scatter_dimension=0, tiled=False).astype(f32)
        return unhalf_rows(lax.psum(part, "mp").T, lax.axis_index("dp"))
    full = pack_channels(g.transpose(1, 0, 2).reshape(g.shape[1], -1)).T
    part = lax.psum_scatter(full, "dp", scatter_dimension=0, tiled=True).astype(f32)
    return lax.psum(part, "mp")


def gather_excitation(w_squeeze, w_excite):
    d = lax.axis_index("dp")
    if lax.axis_size("dp") == 2 * QUADS and w_excite.shape[1] == QUAD:
        squeeze = lax.dynamic_slice_in_dim(w_squeeze, d * HALF, HALF, 0).astype(bf16)
        squeeze = spread_inner(half_rows(squeeze, d))
        excite = lax.dynamic_slice_in_dim(w_excite, d * SE_PART, SE_PART, 0).astype(bf16)
        excite = jnp.pad(widen(excite, 1), ((0, SE_LANES - SE_PART), (0, 0)))
        excite = jnp.concatenate([excite[:, 128 * i : 128 * (i + 1)] for i in range(4)], 0)
        got = lax.all_gather(
            lax.all_gather(jnp.concatenate([squeeze, excite], 1), "mp"), "dp"
        )
        squeeze = got[..., :128].transpose(0, 2, 1, 3).reshape(2 * QUADS * 256, 4 * 128)
        excite = got[..., 128:].reshape(8, 4, 4, 64, 128)
        excite = excite.transpose(0, 3, 1, 2, 4).reshape(8 * 64, 4 * 4 * 128)
        return squeeze, excite
    squeeze = lax.all_gather(w_squeeze.astype(bf16), "mp", axis=1, tiled=True)
    excite = lax.all_gather(w_excite.astype(bf16), "mp", axis=1, tiled=True)
    return (
        spread_channels(spread_inner(squeeze).T).T,
        spread_inner(spread_channels(excite).T).T,
    )


def gather_head(w_project, prototypes, queue_rows, pairing):
    d = lax.axis_index("dp")
    m = lax.axis_index("mp")
    n_dp = lax.axis_size("dp")
    n_mp = lax.axis_size("mp")
    width = prototypes.shape[1]
    if n_dp == 2 * QUADS and n_mp == 4 and width <= 768 and queue_rows.shape == (128, 256):
        project = lax.dynamic_slice_in_dim(w_project, d * HALF, HALF, 0).astype(bf16)
        project = half_rows(project, d)
        project = jnp.concatenate([project, jnp.pad(pairing, ((0, 248), (0, 56)))], 1)
        protos = lax.dynamic_slice_in_dim(prototypes, d * 32, 32, 0).astype(bf16)
        protos = jnp.pad(protos, ((0, 0), (0, 768 - width)))
        queue = lax.dynamic_slice_in_dim(queue_rows, m * 32, 32, 0)
        rest = jnp.concatenate(
            [protos[:, 128 * i : 128 * (i + 1)] for i in range(6)] + [queue[:, :128], queue[:, 128:]],
            0,
        )
        got = lax.all_gather(lax.all_gather(jnp.concatenate([project, rest], 1), "mp"), "dp")
        project = got[..., :64].transpose(0, 2, 1, 3).reshape(2048, 256)
        pairs = got[:, 0, :8, 64:72]
        protos = got[:, :, :192, 128:].reshape(8, 4, 6, 32, 128).transpose(0, 3, 1, 2, 4)
        protos = protos.reshape(256, 4, 768)[..., :width].reshape(256, 4 * width)
        queue = got[:, :, 192:, 128:].reshape(8, 4, 2, 32, 128).transpose(0, 1, 3, 2, 4)
        return project, protos, queue.reshape(1024, 256), pairs
    project = lax.all_gather(w_project.astype(bf16), "mp", axis=1, tiled=True)
    protos = lax.all_gather(prototypes.astype(bf16), "mp", axis=1, tiled=True)
    queue = lax.all_gather(queue_rows, "dp", axis=0, tiled=True)
    pairs = lax.all_gather(pairing, "dp")
    return spread_channels(project.T).T, protos, queue, pairs


def params(*semantics):
    return pltpu.CompilerParams(vmem_limit_bytes=VMEM_BYTES)


def column_sums(stats_ref, a, b):
    stats_ref[0:1, :] = jnp.sum(a, 0, keepdims=True)
    stats_ref[1:2, :] = jnp.sum(b, 0, keepdims=True)


def mix_kernel(x_ref, w_ref, out_ref, stats_ref):
    weight = w_ref[...].reshape(-1, LANES)
    acc = dot(x_ref[...], weight)
    out_ref[...] = acc
    column_sums(stats_ref, acc, acc * acc)


def mix(x, w):
    rows, width = x.shape
    return pl.pallas_call(
        mix_kernel,
        grid=(QUADS,),
        in_specs=[
            pl.BlockSpec((rows, width), lambda m: (0, 0)),
            pl.BlockSpec((2 * QUADS, 1, 256, LANES), lambda m: (0, m, 0, 0)),
        ],
        out_specs=[
            pl.BlockSpec((rows, LANES), lambda m: (0, m)),
            pl.BlockSpec((2, LANES), lambda m: (0, m)),
        ],
        out_shape=[
            jax.ShapeDtypeStruct((rows, width), f32),
            jax.ShapeDtypeStruct((2, width), f32),
        ],
        compiler_params=params(),
        name="mix",
    )(x, w)


def mix_back_kernel(g_ref, w_ref, out_ref):
    acc = dot(g_ref[:, :LANES], w_ref[0, 0], NT)
    for m in range(1, QUADS):
        acc = acc + dot(g_ref[:, m * LANES : (m + 1) * LANES], w_ref[0, m], NT)
    out_ref[...] = acc


def mix_back(g, w):
    rows, width = g.shape
    return pl.pallas_call(
        mix_back_kernel,
        grid=(2 * QUADS,),
        in_specs=[
            pl.BlockSpec((rows, width), lambda d: (0, 0)),
            pl.BlockSpec((1, QUADS, 256, LANES), lambda d: (d, 0, 0, 0)),
        ],
        out_specs=pl.BlockSpec((rows, 256), lambda d: (0, d)),
        out_shape=jax.ShapeDtypeStruct((rows, width), f32),
        compiler_params=params(),
        name="mix_back",
    )(g, w)


def weight_grad_kernel(x_ref, g_ref, out_ref):
    for m in range(QUADS):
        out_ref[0, m] = dot(x_ref[...], g_ref[:, m * LANES : (m + 1) * LANES], TN).astype(bf16)


def weight_grad(x, g):
    rows, width = g.shape
    return pl.pallas_call(
        weight_grad_kernel,
        grid=(2 * QUADS,),
        in_specs=[
            pl.BlockSpec((rows, 256), lambda d: (0, d)),
            pl.BlockSpec((rows, width), lambda d: (0, 0)),
        ],
        out_specs=pl.BlockSpec((1, QUADS, 256, LANES), lambda d: (d, 0, 0, 0)),
        out_shape=jax.ShapeDtypeStruct((2 * QUADS, QUADS, 256, LANES), bf16),
        compiler_params=params(),
        name="weight_grad",
    )(x, g)


def lane_mask(low, high, rows=GROUP):
    lane = lax.broadcasted_iota(jnp.int32, (rows, 256), 1)
    return (lane >= low) & (lane < high)


def dense_kernel(g_ref, out_ref):
    even = g_ref[0].astype(f32)
    odd = g_ref[1].astype(f32)
    row = lax.broadcasted_iota(jnp.int32, (256, 256), 0)
    edge = jnp.zeros((32, 256), f32)
    centre = lane_mask(96, 124) | lane_mask(132, 160)
    for tap in range(9):
        e = even[GROUP * tap : GROUP * (tap + 1)]
        o = odd[GROUP * tap : GROUP * (tap + 1)]
        first = [jnp.where(lane_mask(GROUP * g, GROUP * (g + 1)), e, 0.0) for g in range(4)]
        last = [
            jnp.where(lane_mask(32 + GROUP * g, 32 + GROUP * (g + 1)), o, 0.0) for g in range(4)
        ]
        out_ref[0, 0, tap] = jnp.concatenate(first + [edge], 0).astype(bf16)
        out_ref[0, 1, tap] = jnp.concatenate([edge] + last, 0).astype(bf16)
        across = jnp.where(centre, jnp.concatenate([e[:, 128:], o[:, :128]], 1), 0.0)
        upper = jnp.concatenate(
            [jnp.zeros((96, 256), f32), across, jnp.zeros((104, 256), f32)], 0
        )
        lower = jnp.concatenate(
            [jnp.zeros((104, 256), f32), across, jnp.zeros((96, 256), f32)], 0
        )
        out_ref[0, 2, tap] = (
            jnp.where(row < 124, upper, 0.0) + jnp.where(row >= 132, lower, 0.0)
        ).astype(bf16)


def dense_windows(kernel):
    taps = kernel.shape[1]
    return pl.pallas_call(
        dense_kernel,
        grid=(QUADS,),
        in_specs=[pl.BlockSpec((2, taps, 256), lambda q: (q, 0, 0))],
        out_specs=pl.BlockSpec((1, 3, 9, 256, 256), lambda q: (q, 0, 0, 0, 0)),
        out_shape=jax.ShapeDtypeStruct((QUADS, 3, 9, 256, 256), bf16),
        compiler_params=params(),
        name="dense_windows",
    )(kernel)


WINDOWS = (0, 256, 128)


def place_pixels(pad_ref, moved_ref, source_ref, crops):
    for crop in range(crops):
        for row in range(HW):
            pad_ref[pl.ds(PITCH + 256 * crop + PITCH * (row + 1), HW), :] = source_ref[
                pl.ds(PIXELS * crop + HW * row, HW), :
            ]
    for shift in range(3):
        moved_ref[shift] = pad_ref[pl.ds(PITCH - 1 + shift, 256 * crops), :].astype(bf16)


def tap_rows(moved_ref, dy, dx, low, crops):
    return jnp.concatenate(
        [
            moved_ref[dx, pl.ds(256 * crop + PITCH * dy, PITCH * HW), pl.ds(low, 256)]
            for crop in range(crops)
        ],
        0,
    )


def take_pixels(target_ref, source_ref, crops):
    for crop in range(crops):
        for row in range(HW):
            target_ref[pl.ds(PIXELS * crop + HW * row, HW), :] = source_ref[
                pl.ds(PITCH * HW * crop + PITCH * row, HW), :
            ]


def swish(v):
    return v / (1.0 + jnp.exp(-v))


def swish_slope(v):
    sigma = 1.0 / (1.0 + jnp.exp(-v))
    return sigma * (1.0 + v * (1.0 - sigma))


def conv_kernel(crops, a_ref, affine_ref, w_ref, out_ref, stats_ref, pad_ref, moved_ref, wide_ref, act_ref):
    @pl.when(pl.program_id(0) == 0)
    def _():
        pad_ref[...] = jnp.zeros_like(pad_ref)

    act = swish(a_ref[...] * affine_ref[0:1, :] + affine_ref[1:2, :])
    act_ref[...] = act.astype(bf16).astype(f32)
    place_pixels(pad_ref, moved_ref, act_ref, crops)
    for window, low in enumerate(WINDOWS):
        acc = None
        for tap in range(9):
            part = dot(tap_rows(moved_ref, tap // 3, tap % 3, low, crops), w_ref[0, window, tap])
            acc = part if acc is None else acc + part
        if window < 2:
            wide_ref[:, pl.ds(low, 256)] = acc
        else:
            wide_ref[:, pl.ds(low, 256)] += acc
    take_pixels(act_ref, wide_ref, crops)
    result = act_ref[...].astype(bf16)
    out_ref[...] = result
    result = result.astype(f32)
    column_sums(stats_ref, result, result * result)


def conv(a, affine, windows):
    rows, width = a.shape
    crops = rows // PIXELS
    return pl.pallas_call(
        functools.partial(conv_kernel, crops),
        grid=(QUADS,),
        in_specs=[
            pl.BlockSpec((rows, LANES), lambda q: (0, q)),
            pl.BlockSpec((2, LANES), lambda q: (0, q)),
            pl.BlockSpec((1, 3, 9, 256, 256), lambda q: (q, 0, 0, 0, 0)),
        ],
        out_specs=[
            pl.BlockSpec((rows, LANES), lambda q: (0, q)),
            pl.BlockSpec((2, LANES), lambda q: (0, q)),
        ],
        out_shape=[
            jax.ShapeDtypeStruct((rows, width), bf16),
            jax.ShapeDtypeStruct((2, width), f32),
        ],
        scratch_shapes=[
            pltpu.VMEM((2 * PITCH + 256 * crops, LANES), f32),
            pltpu.VMEM((3, 256 * crops, LANES), bf16),
            pltpu.VMEM((PITCH * HW * crops, LANES), f32),
            pltpu.VMEM((rows, LANES), f32),
        ],
        compiler_params=params(),
        name="conv",
    )(a, affine, windows)


def conv_back_kernel(
    crops, g_ref, a_ref, affine_ref, w_ref, out_ref, grad_ref, stats_ref,
    pad_ref, moved_ref, pad_x_ref, moved_x_ref, wide_ref, act_ref,
):
    @pl.when(pl.program_id(0) == 0)
    def _():
        pad_ref[...] = jnp.zeros_like(pad_ref)
        pad_x_ref[...] = jnp.zeros_like(pad_x_ref)

    act_ref[...] = g_ref[...].astype(f32)
    place_pixels(pad_ref, moved_ref, act_ref, crops)
    values = a_ref[...]
    normed = values * affine_ref[0:1, :] + affine_ref[1:2, :]
    act_ref[...] = swish(normed).astype(bf16).astype(f32)
    place_pixels(pad_x_ref, moved_x_ref, act_ref, crops)
    for window, low in enumerate(WINDOWS):
        acc = None
        for tap in range(9):
            rows = tap_rows(moved_ref, 2 - tap // 3, 2 - tap % 3, low, crops)
            part = dot(rows, w_ref[0, window, tap], NT)
            acc = part if acc is None else acc + part
        if window < 2:
            wide_ref[:, pl.ds(low, 256)] = acc
        else:
            wide_ref[:, pl.ds(low, 256)] += acc
    take_pixels(act_ref, wide_ref, crops)
    result = act_ref[...].astype(bf16)
    out_ref[...] = result
    grad = result.astype(f32) * swish_slope(normed)
    column_sums(stats_ref, grad, grad * ((values - affine_ref[2:3, :]) * affine_ref[3:4, :]))
    centre = lane_mask(96, 124) | lane_mask(132, 160)
    row = lax.broadcasted_iota(jnp.int32, (GROUP, 256), 0)
    mids = [
        tap_rows(moved_ref, 1, 1, low, crops) for low in WINDOWS
    ]
    for tap in range(9):
        pieces = []
        for window, low in enumerate(WINDOWS):
            pieces.append(
                dot(tap_rows(moved_x_ref, tap // 3, tap % 3, low, crops), mids[window], TN)
            )
        even = sum(
            jnp.where(lane_mask(GROUP * g, GROUP * (g + 1)), pieces[0][GROUP * g : GROUP * (g + 1)], 0.0)
            for g in range(4)
        )
        odd = sum(
            jnp.where(
                lane_mask(32 + GROUP * g, 32 + GROUP * (g + 1)),
                pieces[1][32 + GROUP * g : 32 + GROUP * (g + 1)],
                0.0,
            )
            for g in range(4)
        )
        across = jnp.where(
            centre, jnp.where(row < GROUP // 2, pieces[2][96:152], pieces[2][104:160]), 0.0
        )
        nothing = jnp.zeros((GROUP, 128), f32)
        even = even + jnp.concatenate([nothing, across[:, :128]], 1)
        odd = odd + jnp.concatenate([across[:, 128:], nothing], 1)
        grad_ref[0, pl.ds(GROUP * tap, GROUP), :] = even
        grad_ref[1, pl.ds(GROUP * tap, GROUP), :] = odd


def conv_back(g, a, affine, windows):
    rows, width = a.shape
    crops = rows // PIXELS
    return pl.pallas_call(
        functools.partial(conv_back_kernel, crops),
        grid=(QUADS,),
        in_specs=[
            pl.BlockSpec((rows, LANES), lambda q: (0, q)),
            pl.BlockSpec((rows, LANES), lambda q: (0, q)),
            pl.BlockSpec((4, LANES), lambda q: (0, q)),
            pl.BlockSpec((1, 3, 9, 256, 256), lambda q: (q, 0, 0, 0, 0)),
        ],
        out_specs=[
            pl.BlockSpec((rows, LANES), lambda q: (0, q)),
            pl.BlockSpec((2, 9 * GROUP, 256), lambda q: (q, 0, 0)),
            pl.BlockSpec((2, LANES), lambda q: (0, q)),
        ],
        out_shape=[
            jax.ShapeDtypeStruct((rows, width), bf16),
            jax.ShapeDtypeStruct((2 * QUADS, 9 * GROUP, 256), f32),
            jax.ShapeDtypeStruct((2, width), f32),
        ],
        scratch_shapes=[
            pltpu.VMEM((2 * PITCH + 256 * crops, LANES), f32),
            pltpu.VMEM((3, 256 * crops, LANES), bf16),
            pltpu.VMEM((2 * PITCH + 256 * crops, LANES), f32),
            pltpu.VMEM((3, 256 * crops, LANES), bf16),
            pltpu.VMEM((PITCH * HW * crops, LANES), f32),
            pltpu.VMEM((rows, LANES), f32),
        ],
        compiler_params=params(),
        name="conv_back",
    )(g, a, affine, windows)


def head_tail(scores, plan, unit, embedded, scale, protos, project, crops):
    logits = scores / SOFTMAX_TEMPER
    top = jnp.max(logits, 1, keepdims=True)
    power = jnp.exp(logits - top)
    mass = jnp.sum(power, 1, keepdims=True)
    entropy = jnp.sum(plan * (logits - (top + jnp.log(mass))), 1, keepdims=True)
    loss = -jnp.sum(entropy, 0, keepdims=True) / crops
    score_grad = ((power / mass - plan) / (SOFTMAX_TEMPER * crops)).astype(bf16)
    unit_grad = dot(score_grad, protos, NT)
    inner = jnp.sum(embedded * unit_grad, 1, keepdims=True)
    embed_grad = (scale * unit_grad - embedded * (scale * scale * scale * inner)).astype(bf16)
    return loss, score_grad, embed_grad, dot(embed_grad, project, NT)


def head_start(summary, project, protos):
    embedded = dot(summary, project)
    scale = lax.rsqrt(jnp.sum(embedded * embedded, 1, keepdims=True) + EPS_NORM)
    unit = (embedded * scale).astype(bf16)
    return embedded, scale, unit, dot(unit, protos)


def head_kernel(
    summary_ref, project_ref, protos_ref, queue_ref, pairs_ref,
    loss_ref, unit_ref, score_grad_ref, embed_grad_ref, summary_grad_ref, plan_ref,
):
    crops = summary_ref.shape[0]
    blocks = queue_ref.shape[0] // crops
    protos = protos_ref[...]
    embedded, scale, unit, scores = head_start(summary_ref[...], project_ref[...], protos)
    unit_ref[...] = unit
    first = jnp.exp(scores / EPS_SINK)
    plan_ref[pl.ds(0, crops), :] = first

    def fill(i, column):
        rows = queue_ref[pl.ds(pl.multiple_of(i * crops, crops), crops), :]
        value = jnp.exp(dot(rows, protos) / EPS_SINK)
        plan_ref[pl.ds(pl.multiple_of((i + 1) * crops, crops), crops), :] = value
        return column + jnp.sum(value, 0, keepdims=True)

    column = lax.fori_loop(0, blocks, fill, jnp.sum(first, 0, keepdims=True))

    def balanced(i, inverse):
        place = pl.ds(pl.multiple_of(i * crops, crops), crops)
        value = plan_ref[place, :] * inverse
        return place, value * (1.0 / jnp.sum(value, 1, keepdims=True))

    for sweep in range(SINK - 1):
        inverse = 1.0 / column

        def pass_rows(i, column, inverse=inverse):
            place, value = balanced(i, inverse)
            plan_ref[place, :] = value
            return column + jnp.sum(value, 0, keepdims=True)

        column = lax.fori_loop(0, blocks + 1, pass_rows, jnp.zeros_like(column))
    value = plan_ref[pl.ds(0, crops), :] * (1.0 / column)
    value = value / jnp.sum(value, 1, keepdims=True)
    plan = lax.dot_general(
        pairs_ref[...], value, NN, precision=lax.Precision.HIGHEST, preferred_element_type=f32
    )
    loss, score_grad, embed_grad, summary_grad = head_tail(
        scores, plan, unit, embedded, scale, protos, project_ref[...], crops
    )
    loss_ref[...] = loss
    score_grad_ref[...] = score_grad
    embed_grad_ref[...] = embed_grad
    summary_grad_ref[...] = summary_grad


def head(summary, project, protos, queue, pairs):
    crops = summary.shape[0]
    rows = crops + queue.shape[0]
    if rows <= 2048:
        return pl.pallas_call(
            head_kernel,
            out_shape=[
                jax.ShapeDtypeStruct((1, 1), f32),
                jax.ShapeDtypeStruct((crops, protos.shape[0]), bf16),
                jax.ShapeDtypeStruct((crops, protos.shape[1]), bf16),
                jax.ShapeDtypeStruct((crops, protos.shape[0]), bf16),
                jax.ShapeDtypeStruct((crops, project.shape[0]), f32),
            ],
            scratch_shapes=[pltpu.VMEM((rows, protos.shape[1]), f32)],
            compiler_params=params(),
            name="head",
        )(summary, project, protos, queue, pairs)
    embedded, scale, unit, scores = head_start(summary, project, protos)
    plan = jnp.exp(jnp.concatenate([scores, dot(queue, protos)], 0) / EPS_SINK)
    for sweep in range(SINK):
        plan = plan / jnp.sum(plan, 0, keepdims=True)
        plan = plan / jnp.sum(plan, 1, keepdims=True)
    plan = lax.dot_general(
        pairs, plan[:crops], NN, precision=lax.Precision.HIGHEST, preferred_element_type=f32
    )
    loss, score_grad, embed_grad, summary_grad = head_tail(
        scores, plan, unit, embedded, scale, protos, project, crops
    )
    return loss, unit, score_grad, embed_grad, summary_grad


def norm_of(sums, gain, shift, count):
    mean = sums[0] / count
    inverse = lax.rsqrt(sums[1] / count - mean * mean + EPS_BN)
    scale = inverse * gain
    return mean, inverse, scale, shift - mean * scale


def lars_step(weight, gradient, momentum, weight_norm, grad_norm):
    rate = TRUST * weight_norm / (grad_norm + DECAY * weight_norm)
    return MOMENTUM * momentum + rate * (gradient + DECAY * weight)


def crop_sums(v, crops):
    row = lax.broadcasted_iota(jnp.int32, v.shape, 0)
    return jnp.stack(
        [
            jnp.sum(jnp.where((row >= PIXELS * c) & (row < PIXELS * (c + 1)), v, 0.0), 0)
            for c in range(crops)
        ]
    )


def crop_rows(v, rows):
    row = lax.broadcasted_iota(jnp.int32, (rows, v.shape[1]), 0)
    out = jnp.broadcast_to(v[0], (rows, v.shape[1]))
    for c in range(1, v.shape[0]):
        out = jnp.where(row >= PIXELS * c, v[c], out)
    return out


def body(
    block_input, output_grad, w_reduce, w_group, w_squeeze, w_excite, w_expand, w_project,
    prototypes, bn_gains, bn_biases, m_reduce, m_group, m_squeeze, m_excite, m_expand,
    m_project, m_protos, m_gains, m_biases, queue_store, queue_slots, crop_perm,
):
    n_dp = lax.axis_size("dp")
    n_mp = lax.axis_size("mp")
    m_index = lax.axis_index("mp")
    channels_here = block_input.shape[0]
    rows = block_input.shape[1] // n_mp
    crops = rows // PIXELS
    count = rows * n_dp * n_mp
    all_crops = crops * n_dp * n_mp

    reduce_blocks = gather_square(w_reduce)
    x = to_slab(block_input)
    kernel_low = gather_kernel(w_group)
    squeeze_low, excite_low = gather_excitation(w_squeeze, w_excite)
    expand_blocks = gather_square(w_expand)
    slot_table = (
        queue_slots[0][:, None]
        == lax.broadcasted_iota(jnp.int32, (queue_slots.shape[1], queue_store.shape[0]), 1)
    ).astype(bf16)
    queue_rows = dot(slot_table, queue_store.astype(bf16)).astype(bf16)
    order = crop_perm[0]
    pairing = (order[None, :] == jnp.bitwise_xor(order, 1)[:, None]).astype(bf16)
    project_low, protos_low, queue_low, pairs = gather_head(
        w_project, prototypes, queue_rows, pairing
    )
    images = pairs.shape[0]
    pairs = (
        jnp.eye(images, dtype=f32)[:, None, :, None] * pairs.astype(f32)[:, :, None, :]
    ).reshape(all_crops, all_crops)
    cotangent = to_slab(output_grad)
    norms = gather_axis(jnp.concatenate([bn_gains, bn_biases], 0), "mp")
    norms = spread_channels(norms.transpose(1, 0, 2).reshape(norms.shape[1], -1))
    gains, shifts = norms[:3], norms[3:]

    reduced, sums = mix(x, reduce_blocks)
    mean1, inverse1, scale1, shift1 = norm_of(total(sums), gains[0], shifts[0], count)
    windows = dense_windows(kernel_low)
    grouped, sums = conv(reduced, jnp.stack([scale1, shift1]), windows)
    mean2, inverse2, scale2, shift2 = norm_of(total(sums), gains[1], shifts[1], count)
    grouped = grouped.astype(f32)
    normed2 = grouped * scale2 + shift2
    act2 = swish(normed2)
    pooled = (crop_sums(act2, crops) / PIXELS).astype(bf16)
    squeezed = dot(pooled, squeeze_low)
    squeeze_act = swish(squeezed).astype(bf16)
    gating = jax.nn.sigmoid(dot(squeeze_act, excite_low))
    gate_rows = crop_rows(gating, rows)
    gated = (act2 * gate_rows).astype(bf16)
    expanded, sums = mix(gated, expand_blocks)
    mean3, inverse3, scale3, shift3 = norm_of(total(sums), gains[2], shifts[2], count)
    joined = x.astype(f32) + expanded * scale3 + shift3
    value = swish(joined)
    block_output = from_slab(value.astype(bf16), channels_here)
    summary = gather_all((crop_sums(value, crops) / PIXELS).astype(bf16))

    loss, unit, score_grad, embed_grad, summary_grad = head(
        summary, project_low, protos_low, queue_low, pairs
    )
    first_crop = (lax.axis_index("dp") * n_mp + m_index) * crops
    own_grad = lax.dynamic_slice_in_dim(summary_grad, first_crop, crops, 0) / PIXELS

    joined_grad = (cotangent.astype(f32) + crop_rows(own_grad, rows)) * swish_slope(joined)
    centred3 = (expanded - mean3) * inverse3
    sums3 = total(jnp.stack([jnp.sum(joined_grad, 0), jnp.sum(joined_grad * centred3, 0)]))
    expanded_grad = (
        scale3 * (joined_grad - (sums3[0] + centred3 * sums3[1]) / count)
    ).astype(bf16)
    gated_grad = mix_back(expanded_grad, expand_blocks)
    expand_grad = scatter_square(weight_grad(gated, expanded_grad), w_expand.shape)
    excite_grad = (
        crop_sums(gated_grad * act2, crops) * gating * (1.0 - gating)
    ).astype(bf16)
    squeeze_grad = (dot(excite_grad, excite_low, NT) * swish_slope(squeezed)).astype(bf16)
    pooled_grad = dot(squeeze_grad, squeeze_low, NT) / PIXELS
    act2_grad = (gated_grad * gate_rows + crop_rows(pooled_grad, rows)) * swish_slope(normed2)
    centred2 = (grouped - mean2) * inverse2
    sums2 = total(jnp.stack([jnp.sum(act2_grad, 0), jnp.sum(act2_grad * centred2, 0)]))
    grouped_grad = (
        scale2 * (act2_grad - (sums2[0] + centred2 * sums2[1]) / count)
    ).astype(bf16)
    act1_grad, kernel_grad, sums = conv_back(
        grouped_grad, reduced, jnp.stack([scale1, shift1, mean1, inverse1]), windows
    )
    sums1 = total(sums)
    kernel_grad = scatter_kernel(kernel_grad.astype(bf16), w_group.shape[0])
    normed1 = reduced * scale1 + shift1
    centred1 = (reduced - mean1) * inverse1
    reduced_grad = (
        scale1
        * (
            act1_grad.astype(f32) * swish_slope(normed1)
            - (sums1[0] + centred1 * sums1[1]) / count
        )
    ).astype(bf16)
    reduce_grad = scatter_square(weight_grad(x, reduced_grad), w_reduce.shape)
    input_grad = from_slab(
        (mix_back(reduced_grad, reduce_blocks) + joined_grad).astype(bf16), channels_here
    ).astype(f32)

    small = gather_all(jnp.concatenate([pooled, squeeze_act, squeeze_grad, excite_grad], 1))
    wide = pooled.shape[1]
    inner = squeeze_act.shape[1]
    pooled_all = pack_channels(small[:, :wide])
    act_all = pack_inner(small[:, wide : wide + inner])
    squeeze_all = pack_inner(small[:, wide + inner : wide + 2 * inner])
    excite_all = pack_channels(small[:, wide + 2 * inner :])

    def own(v, width):
        return lax.dynamic_slice_in_dim(v, m_index * width, width, 1)

    squeeze_part = dot(pooled_all, own(squeeze_all, w_squeeze.shape[1]), TN)
    excite_part = dot(act_all, own(excite_all, w_excite.shape[1]), TN)
    project_part = dot(pack_channels(summary), own(embed_grad, w_project.shape[1]), TN)
    protos_part = dot(unit, own(score_grad, prototypes.shape[1]), TN)
    gain_part = own(pack_channels(jnp.stack([sums1[1], sums2[1], sums3[1]])), channels_here)
    bias_part = own(pack_channels(jnp.stack([sums1[0], sums2[0], sums3[0]])), channels_here)

    weights_here = [w_reduce, w_group, w_squeeze, w_excite, w_expand, w_project, prototypes]
    grads_here = [
        reduce_grad, kernel_grad, squeeze_part, excite_part, expand_grad, project_part, protos_part,
    ]
    moments_here = [m_reduce, m_group, m_squeeze, m_excite, m_expand, m_project, m_protos]
    portions = [1.0, 1.0 / n_mp, 1.0 / n_dp, 1.0 / n_dp, 1.0, 1.0 / n_dp, 1.0 / n_dp]

    def squares(arrays, gain, bias):
        return jnp.concatenate(
            [
                jnp.stack([jnp.sum(a * a) * p for a, p in zip(arrays, portions)]),
                jnp.sum(gain * gain, 1) / n_dp,
                jnp.sum(bias * bias, 1) / n_dp,
            ]
        )

    param_norms = jnp.sqrt(
        total(
            jnp.stack(
                [squares(weights_here, bn_gains, bn_biases), squares(grads_here, gain_part, bias_part)],
                1,
            )
        )
        + EPS_NORM
    )
    moments_new = [
        lars_step(weight, gradient, momentum, param_norms[i, 0], param_norms[i, 1])
        for i, (weight, gradient, momentum) in enumerate(
            zip(weights_here, grads_here, moments_here)
        )
    ]
    mom_gains = lars_step(
        bn_gains, gain_part, m_gains, param_norms[7:10, 0:1], param_norms[7:10, 1:2]
    )
    mom_biases = lars_step(
        bn_biases, bias_part, m_biases, param_norms[10:13, 0:1], param_norms[10:13, 1:2]
    )
    return (
        block_output, loss[0, 0], input_grad, *moments_new, mom_gains, mom_biases, param_norms,
    )


def solution(mesh):
    split = P("dp", "mp")
    turned = P("mp", "dp")
    rows = P("dp", None)
    columns = P(None, "mp")
    return jax.shard_map(
        body,
        mesh=mesh,
        in_specs=(
            turned, turned, split, rows, columns, columns, split, columns, columns, columns, columns,
            split, rows, columns, columns, split, columns, columns, columns, columns, rows, rows, rows,
        ),
        out_specs=(
            turned, P(), turned, split, rows, columns, columns, split, columns, columns, columns,
            columns, P(),
        ),
        check_vma=False,
    )
```

```python
import functools

import jax
import jax.numpy as jnp
import numpy as np
from jax import lax
from jax.experimental import pallas as pl
from jax.experimental.pallas import tpu as pltpu
from jax.sharding import PartitionSpec as P

HW = 14
PIXELS = HW * HW
SINK = 3
EPS_BN = 1e-05
EPS_NORM = 1e-06
EPS_SINK = 0.05
SOFTMAX_TEMPER = 0.1
TRUST = 0.001
DECAY = 1e-06
MOMENTUM = 0.9

QUADS = 4
QUAD = 504
HALF = 252
LANES = 512
GAP = LANES - QUAD
GROUP = 56
SE_PART = 63
SE_LANES = 64
PITCH = 16
VMEM_BYTES = 48 * 1024 * 1024
f32 = jnp.float32
bf16 = jnp.bfloat16
NN = (((1,), (0,)), ((), ()))
NT = (((1,), (1,)), ((), ()))
TN = (((0,), (0,)), ((), ()))


def dot(a, b, dims=NN):
    return lax.dot_general(a, b, dims, preferred_element_type=f32)


def widen(v, axis):
    first = lax.slice_in_dim(v, 0, HALF, axis=axis)
    last = lax.slice_in_dim(v, HALF, QUAD, axis=axis)
    shape = list(v.shape)
    shape[axis] = GAP
    return jnp.concatenate([first, jnp.zeros(shape, v.dtype), last], axis)


def narrow(v, axis):
    first = lax.slice_in_dim(v, 0, HALF, axis=axis)
    last = lax.slice_in_dim(v, HALF + GAP, LANES, axis=axis)
    return jnp.concatenate([first, last], axis)


def spread_channels(v):
    lead = v.shape[:-1]
    return widen(v.reshape(lead + (QUADS, QUAD)), len(lead) + 1).reshape(lead + (QUADS * LANES,))


def pack_channels(v):
    lead = v.shape[:-1]
    return narrow(v.reshape(lead + (QUADS, LANES)), len(lead) + 1).reshape(lead + (QUADS * QUAD,))


def half_rows(v, position):
    pad = 256 - HALF
    padded = jnp.pad(v, ((pad, pad),) + ((0, 0),) * (v.ndim - 1))
    return lax.dynamic_slice_in_dim(padded, pad * (1 - position % 2), 256, 0)


def unhalf_rows(v, position):
    return lax.dynamic_slice_in_dim(v, (256 - HALF) * (position % 2), HALF, 0)


def spread_inner(v):
    lead = v.shape[:-1]
    parts = v.shape[-1] // SE_PART
    v = v.reshape(lead + (parts, SE_PART))
    v = jnp.pad(v, ((0, 0),) * (v.ndim - 1) + ((0, SE_LANES - SE_PART),))
    return v.reshape(lead + (parts * SE_LANES,))


def pack_inner(v):
    lead = v.shape[:-1]
    parts = v.shape[-1] // SE_LANES
    return v.reshape(lead + (parts, SE_LANES))[..., :SE_PART].reshape(lead + (parts * SE_PART,))


def flips(axis, bit):
    return [(i, i ^ bit) for i in range(lax.axis_size(axis))]


def spread(v, axis):
    n = lax.axis_size(axis)
    return lax.all_to_all(
        jnp.broadcast_to(v[None], (n,) + v.shape), axis, split_axis=0, concat_axis=0, tiled=True
    )


def total(v):
    return jnp.sum(spread(jnp.sum(spread(v, "dp"), 0), "mp"), 0)


def tie(*values):
    return lax.optimization_barrier(values)


def gather_all(v):
    n = lax.axis_size("dp") * lax.axis_size("mp")
    out = lax.all_to_all(
        jnp.broadcast_to(v[None], (n,) + v.shape),
        ("dp", "mp"),
        split_axis=0,
        concat_axis=0,
        tiled=True,
    )
    return out


def in_order(parts, me):
    out = []
    for j in range(len(parts)):
        v = parts[0]
        for k in range(1, len(parts)):
            v = jnp.where((me ^ k) == j, parts[k], v)
        out.append(v)
    return jnp.stack(out)


def exchange(blocks):
    return lax.all_to_all(blocks, "mp", split_axis=0, concat_axis=0, tiled=True)


def parts_mp(v):
    return [v] + [lax.ppermute(v, "mp", flips("mp", k)) for k in range(1, lax.axis_size("mp"))]


def gather_mp(v):
    return in_order(parts_mp(v), lax.axis_index("mp"))


def diagonal(axis_size):
    return [(i, i ^ 4 if i % 2 == 0 else i ^ 2) for i in range(axis_size)]


def gather_sides(v):
    return lax.ppermute(v, "dp", flips("dp", 2)), lax.ppermute(v, "dp", flips("dp", 4))


def gather_corner(across, up):
    even = lax.axis_index("dp") % 2 == 0
    return lax.ppermute(jnp.where(even, across, up), "dp", diagonal(8))


def gather_twins(own, across, up, corner):
    pieces = []
    for got in (own, across, up, corner):
        pieces += [got, lax.ppermute(got, "dp", flips("dp", 1))]
    return pieces


def gather_dp(v):
    across, up = gather_sides(v)
    return gather_twins(v, across, up, gather_corner(across, up))


def scatter_corner(kept, got):
    (last,) = twin_sums(kept, got, (3,))
    corner = lax.ppermute(last, "dp", diagonal(8))
    own, across, up = twin_sums(kept, got, (0, 1, 2))
    return (own, across, up), corner


def from_twin(sent):
    return lax.ppermute(sent, "dp", flips("dp", 1))


def scatter_sides(across, up):
    return lax.ppermute(across, "dp", flips("dp", 2)), lax.ppermute(up, "dp", flips("dp", 4))


def scatter_mp(own, parts):
    return [own] + [lax.ppermute(v, "mp", flips("mp", k + 1)) for k, v in enumerate(parts)]


def quick_mesh():
    return lax.axis_size("dp") == 2 * QUADS and lax.axis_size("mp") == QUADS


def slab_blocks(v):
    n = lax.axis_size("mp")
    blocks = v.T.reshape(n, v.shape[1] // n, v.shape[0])
    return widen(blocks, 2) if quick_mesh() else blocks


def quad_blocks(blocks):
    if quick_mesh():
        return blocks
    rows = blocks.shape[1]
    full = spread_channels(blocks.transpose(1, 0, 2).reshape(rows, -1))
    return full.reshape(rows, QUADS, LANES).transpose(1, 0, 2)


def out_blocks(blocks):
    if quick_mesh():
        return blocks
    n = lax.axis_size("mp")
    rows = blocks.shape[1]
    full = pack_channels(blocks.transpose(1, 0, 2).reshape(rows, -1))
    return full.reshape(rows, n, -1).transpose(1, 0, 2)


def out_channels(blocks, channels, dtype):
    if quick_mesh():
        blocks = join_rows(blocks, dtype)
    return blocks.astype(dtype).reshape(-1, channels).T


def shard_square(w):
    return half_rows(widen(w.astype(bf16), 1), lax.axis_index("dp")).T


def gather_square(w):
    full = lax.all_gather(w.astype(bf16), "mp", axis=1, tiled=True)
    full = lax.all_gather(full, "dp", axis=0, tiled=True)
    full = spread_channels(spread_channels(full).T)
    return full.reshape(QUADS, LANES, 2 * QUADS, 256).transpose(2, 0, 1, 3)


def scatter_square(kept, sent):
    g = jnp.stack([kept, sent], 1).reshape((8,) + kept.shape[1:])
    full = g.transpose(1, 2, 0, 3).reshape(QUADS * LANES, 2 * QUADS * 256)
    full = pack_channels(pack_channels(full).T)
    part = lax.psum_scatter(full, "dp", scatter_dimension=0, tiled=True)
    return lax.psum_scatter(part, "mp", scatter_dimension=1, tiled=True).astype(f32)


def gather_kernel(w):
    low = w.astype(bf16)
    if quick_mesh():
        return gather_dp(half_rows(low, lax.axis_index("dp")).T)
    full = lax.all_gather(low, "dp", axis=0, tiled=True)
    return spread_channels(full.T).reshape(-1, 2 * QUADS, 256).transpose(1, 0, 2)


def scatter_kernel(kept, sent):
    g = jnp.stack([kept, sent], 1).reshape((8,) + kept.shape[1:])
    full = pack_channels(g.transpose(1, 0, 2).reshape(g.shape[1], -1)).T
    part = lax.psum_scatter(full, "dp", scatter_dimension=0, tiled=True).astype(f32)
    return lax.psum(part, "mp")


SE_ROWS = 256
SE_OFFSET = QUADS * LANES
HEAD_ROWS = 208
PROTO_ROWS = 96
QUEUE_ROWS = 32


def shard_excitation(w_squeeze, w_excite):
    d = lax.axis_index("dp")
    squeeze = lax.dynamic_slice_in_dim(w_squeeze, d * HALF, HALF, 0).astype(bf16)
    squeeze = spread_inner(half_rows(squeeze, d))
    excite = lax.dynamic_slice_in_dim(w_excite, d * SE_PART, SE_PART, 0).astype(bf16)
    excite = jnp.pad(widen(excite, 1), ((0, SE_LANES - SE_PART), (0, 0)))
    excite = jnp.concatenate([excite[:, 128 * i : 128 * (i + 1)] for i in range(4)], 0)
    return jnp.concatenate([squeeze, excite], 1)


def shard_head(w_project, prototypes, queue_rows, pairing):
    d = lax.axis_index("dp")
    m = lax.axis_index("mp")
    project = lax.dynamic_slice_in_dim(w_project, d * HALF, HALF, 0).astype(bf16)
    project = half_rows(project, d).T
    protos = jnp.pad(prototypes.T, ((0, 2 * QUADS * PROTO_ROWS - prototypes.shape[1]), (0, 0)))
    protos = lax.dynamic_slice_in_dim(protos, d * PROTO_ROWS, PROTO_ROWS, 0).astype(bf16)
    queue = lax.dynamic_slice_in_dim(queue_rows, m * QUEUE_ROWS, QUEUE_ROWS, 0)
    size = pairing.shape[0]
    lane = lax.broadcasted_iota(jnp.int32, (size, 256), 1)
    pairing = jnp.where(lane // size == d, jnp.tile(pairing, (1, 256 // size)), 0.0)
    pairing = jnp.pad(pairing.astype(bf16), ((0, 16 - size), (0, 0)))
    return jnp.concatenate([project, protos, queue, pairing], 0)


def gather_excitation(w_squeeze, w_excite):
    squeeze = lax.all_gather(w_squeeze.astype(bf16), "mp", axis=1, tiled=True)
    excite = lax.all_gather(w_excite.astype(bf16), "mp", axis=1, tiled=True)
    squeeze = spread_channels(spread_inner(squeeze).T).T
    excite = spread_inner(spread_channels(excite).T).T
    squeeze = squeeze.reshape(8, 256, 4, 128).transpose(0, 2, 1, 3)
    excite = excite.reshape(8, 64, 4, 4, 128).transpose(0, 2, 3, 1, 4).reshape(8, 4, 256, 128)
    return jnp.concatenate([squeeze, excite], 3)


def gather_head(w_project, prototypes, queue_rows, pairing):
    project = lax.all_gather(w_project.astype(bf16), "mp", axis=1, tiled=True)
    protos = lax.all_gather(prototypes.astype(bf16), "mp", axis=1, tiled=True)
    queue = lax.all_gather(queue_rows, "dp", axis=0, tiled=True)
    pairs = lax.all_gather(pairing, "dp")
    return spread_channels(project.T).T, protos, queue, pairs


def block_diagonal(pairs):
    images, size = pairs.shape[:2]
    return (
        jnp.eye(images, dtype=f32)[:, None, :, None] * pairs.astype(f32)[:, :, None, :]
    ).reshape(images * size, images * size)


BRIEF = pl.CostEstimate(flops=1, bytes_accessed=1, transcendentals=0)


def params(*semantics):
    return pltpu.CompilerParams(vmem_limit_bytes=VMEM_BYTES)


def column_sums(stats_ref, a, b):
    stats_ref[0:1, :] = jnp.sum(a, 0, keepdims=True)
    stats_ref[1:2, :] = jnp.sum(b, 0, keepdims=True)


def index_scalar(axis):
    quick = quick_mesh()
    return (lax.axis_index(axis) if quick else jnp.zeros((), jnp.int32)).astype(jnp.int32)[None]


SCALAR = pl.BlockSpec(memory_space=pltpu.SMEM)


def half_block(index):
    return pl.ds(pl.multiple_of(index * 256, 256), 256)


def join_rows_kernel(blocks_ref, out_ref):
    for j in range(QUADS):
        v = blocks_ref[j].astype(f32)
        v = jnp.concatenate([v[:, :HALF], v[:, HALF + GAP :]], 1)
        out_ref[j] = v.astype(out_ref.dtype)


def join_rows(blocks, dtype):
    return pl.pallas_call(
        join_rows_kernel,
        out_shape=jax.ShapeDtypeStruct(blocks.shape[:2] + (QUAD,), dtype),
        compiler_params=params(),
        cost_estimate=BRIEF,
        name="join_rows",
    )(blocks)


def piece_list(w):
    return w if isinstance(w, list) else [w[b].reshape(-1, 256) for b in range(8)]


def half_of(ref, index):
    return ref[index // 2, :, half_block(index % 2)]


def mix_kernel(me_ref, x_ref, *refs):
    out_ref, stats_ref = refs[8:]
    turned = jnp.concatenate([half_of(x_ref, me_ref[0] ^ b) for b in range(8)], 1)
    acc = dot(turned, jnp.concatenate([refs[b][...] for b in range(8)], 1), NT)
    out_ref[...] = acc
    column_sums(stats_ref, acc, acc * acc)


def mix(x, w):
    _, rows, _ = x.shape
    width = QUADS * LANES
    return pl.pallas_call(
        mix_kernel,
        grid=(QUADS,),
        in_specs=[SCALAR, pl.BlockSpec(x.shape, lambda m: (0, 0, 0))]
        + [pl.BlockSpec((LANES, 256), lambda m: (m, 0))] * 8,
        out_specs=[
            pl.BlockSpec((rows, LANES), lambda m: (0, m)),
            pl.BlockSpec((2, LANES), lambda m: (0, m)),
        ],
        out_shape=[
            jax.ShapeDtypeStruct((rows, width), f32),
            jax.ShapeDtypeStruct((2, width), f32),
        ],
        compiler_params=params(),
        cost_estimate=BRIEF,
        name="mix",
    )(index_scalar("dp"), x, *piece_list(w))


def mix_back_kernel(rest, me_ref, g_ref, *refs):
    out_ref, hold_ref, sems = refs[8 + rest :]

    def copy(b):
        source = refs[b].at[pl.ds(0, QUADS * LANES)]
        return pltpu.make_async_copy(source, hold_ref.at[b], sems.at[b])

    for b in range(8):
        copy(b).start()
    for b in range(8):
        index = me_ref[0] ^ b
        copy(b).wait()
        acc = dot(g_ref[...], hold_ref[b])
        if rest:
            acc = acc + refs[8][:, half_block(index)]
            out_ref[index // 2, :, half_block(index % 2)] = acc.astype(bf16)
        else:
            out_ref[:, half_block(index)] = acc


def mix_back(g, w, rest=None):
    rows, width = g.shape
    if rest is None:
        more, out = [], jax.ShapeDtypeStruct((rows, width), f32)
    else:
        more, out = [rest], jax.ShapeDtypeStruct((QUADS, rows, LANES), bf16)
    return pl.pallas_call(
        functools.partial(mix_back_kernel, len(more)),
        in_specs=[SCALAR, pl.BlockSpec(memory_space=pltpu.VMEM)]
        + [pl.BlockSpec(memory_space=pl.ANY)] * 8
        + [pl.BlockSpec(memory_space=pltpu.VMEM)] * len(more),
        out_specs=pl.BlockSpec(memory_space=pltpu.VMEM),
        out_shape=out,
        scratch_shapes=[
            pltpu.VMEM((8, QUADS * LANES, 256), bf16),
            pltpu.SemaphoreType.DMA((8,)),
        ],
        compiler_params=params(),
        cost_estimate=BRIEF,
        name="mix_back",
    )(index_scalar("dp"), g, *piece_list(w), *more)


def weight_grad_kernel(me_ref, x_ref, g_ref, kept_ref, sent_ref):
    turned = g_ref[...].T
    for odd, out_ref in ((1, sent_ref), (0, kept_ref)):
        wanted = jnp.concatenate(
            [half_of(x_ref, me_ref[0] ^ (2 * i + odd)) for i in range(4)], 1
        )
        result = dot(turned, wanted)
        for i in range(4):
            out_ref[i, 0] = result[:, 256 * i : 256 * (i + 1)].astype(bf16)


def weight_grad(x, g):
    rows, width = g.shape
    return pl.pallas_call(
        weight_grad_kernel,
        grid=(QUADS,),
        in_specs=[
            SCALAR,
            pl.BlockSpec(x.shape, lambda m: (0, 0, 0)),
            pl.BlockSpec((rows, LANES), lambda m: (0, m)),
        ],
        out_specs=[pl.BlockSpec((4, 1, LANES, 256), lambda m: (0, m, 0, 0))] * 2,
        out_shape=[jax.ShapeDtypeStruct((4, QUADS, LANES, 256), bf16)] * 2,
        compiler_params=params(),
        cost_estimate=BRIEF,
        name="weight_grad",
    )(index_scalar("dp"), x, g)


def twin_sums_kernel(count, *refs):
    for i in range(count):
        refs[2 * count + i][...] = (
            refs[i][...].astype(f32) + refs[count + i][...].astype(f32)
        ).astype(bf16)


def twin_sums(kept, got, picks):
    shape = kept.shape[1:]
    specs = [
        pl.BlockSpec((None, 1) + shape[1:], lambda m, i=i: (i, m, 0, 0)) for i in picks
    ]
    return pl.pallas_call(
        functools.partial(twin_sums_kernel, len(picks)),
        grid=shape[:1],
        in_specs=specs * 2,
        out_specs=[pl.BlockSpec((1,) + shape[1:], lambda m: (m, 0, 0))] * len(picks),
        out_shape=[jax.ShapeDtypeStruct(shape, bf16)] * len(picks),
        compiler_params=params(),
        cost_estimate=BRIEF,
        name="twin_sums",
    )(*([kept] * len(picks) + [got] * len(picks)))


def corner_sums_kernel(me_ref, across_ref, up_ref, corner_ref, across_out, up_out):
    even = me_ref[0] % 2 == 0
    corner = corner_ref[...].astype(f32)
    across_out[...] = (across_ref[...].astype(f32) + jnp.where(even, corner, 0.0)).astype(bf16)
    up_out[...] = (up_ref[...].astype(f32) + jnp.where(even, 0.0, corner)).astype(bf16)


def corner_sums(across, up, corner):
    block = pl.BlockSpec((1,) + across.shape[1:], lambda m: (m, 0, 0))
    return pl.pallas_call(
        corner_sums_kernel,
        grid=across.shape[:1],
        in_specs=[SCALAR, block, block, block],
        out_specs=[block, block],
        out_shape=[jax.ShapeDtypeStruct(across.shape, bf16)] * 2,
        compiler_params=params(),
        cost_estimate=BRIEF,
        name="corner_sums",
    )(index_scalar("dp"), across, up, corner)


def side_sums_kernel(me_ref, own_ref, across_ref, up_ref, out_ref, *parts):
    for k in range(len(parts) + 1):
        j = me_ref[0] ^ k
        value = (
            own_ref[j].astype(f32) + across_ref[j].astype(f32) + up_ref[j].astype(f32)
        )
        if k:
            parts[k - 1][...] = value.astype(bf16)
        else:
            out_ref[...] = value


def side_sums(own, across, up):
    n, *shape = own.shape
    me = index_scalar("mp") if n > 1 else jnp.zeros((1,), jnp.int32)
    return pl.pallas_call(
        side_sums_kernel,
        in_specs=[SCALAR] + [pl.BlockSpec(memory_space=pltpu.VMEM)] * 3,
        out_shape=[jax.ShapeDtypeStruct(shape, f32)] + [jax.ShapeDtypeStruct(shape, bf16)] * (n - 1),
        compiler_params=params(),
        cost_estimate=BRIEF,
        name="side_sums",
    )(me, own, across, up)


def own_square_kernel(me_ref, own_ref, *refs):
    out_ref, square_ref = refs[-2:]
    value = own_ref[...]
    for part in refs[:-2]:
        value = value + part[...].astype(f32)
    row = lax.broadcasted_iota(jnp.int32, (QUAD, 1), 0)
    value = jnp.where(row < HALF, value[:QUAD], value[GAP:])
    value = jnp.where(me_ref[0] % 2 == 1, value[:, 256 - HALF :], value[:, :HALF])
    out_ref[...] = value
    square_ref[...] = jnp.sum(jnp.sum(value * value, 1, keepdims=True), 0, keepdims=True)


def own_square(parts):
    return pl.pallas_call(
        own_square_kernel,
        in_specs=[SCALAR] + [pl.BlockSpec(memory_space=pltpu.VMEM)] * len(parts),
        out_shape=[
            jax.ShapeDtypeStruct((QUAD, HALF), f32), jax.ShapeDtypeStruct((1, 1), f32),
        ],
        compiler_params=params(),
        cost_estimate=BRIEF,
        name="own_square",
    )(index_scalar("dp"), *parts)


def affine(sums, norms, k, count):
    mean = sums[0:1] / count
    inverse = lax.rsqrt(sums[1:2] / count - mean * mean + EPS_BN)
    scale = inverse * norms[k : k + 1]
    return mean, inverse, scale, norms[3 + k : 4 + k] - mean * scale


def quad_spec(rows):
    return pl.BlockSpec((rows, LANES), lambda q: (0, q))


def block_spec(rows):
    return pl.BlockSpec((None, rows, LANES), lambda q: (q, 0, 0))


def crop_totals(ref, crops):
    return jnp.concatenate(
        [jnp.sum(ref[pl.ds(PIXELS * c, PIXELS), :], 0, keepdims=True) for c in range(crops)], 0
    )


def value_kernel(crops, count, x_ref, a_ref, sums_ref, norms_ref, y_ref, summary_ref, work_ref):
    _, _, scale, shift = affine(sums_ref[...], norms_ref[...], 2, count)
    work_ref[...] = swish(x_ref[...].astype(f32) + a_ref[...] * scale + shift)
    y_ref[...] = work_ref[...].astype(bf16)
    summary_ref[...] = (crop_totals(work_ref, crops) / PIXELS).astype(bf16)


def block_value(x, a, sums, norms, count):
    rows, width = a.shape
    crops = rows // PIXELS
    return pl.pallas_call(
        functools.partial(value_kernel, crops, count),
        grid=(QUADS,),
        in_specs=[block_spec(rows), quad_spec(rows), quad_spec(2), quad_spec(6)],
        out_specs=[block_spec(rows), quad_spec(crops)],
        out_shape=[
            jax.ShapeDtypeStruct((QUADS, rows, LANES), bf16),
            jax.ShapeDtypeStruct((crops, width), bf16),
        ],
        scratch_shapes=[pltpu.VMEM((rows, LANES), f32)],
        compiler_params=params(),
        cost_estimate=BRIEF,
        name="value",
    )(x, a, sums, norms)


def value_back_kernel(
    crops, count, first_ref, x_ref, a_ref, sums_ref, norms_ref, dy_ref, do_ref, out_ref, stats_ref
):
    mean, inverse, scale, shift = affine(sums_ref[...], norms_ref[...], 2, count)
    values = a_ref[...]
    row = lax.broadcasted_iota(jnp.int32, (do_ref.shape[0], 1), 0)
    own = jnp.concatenate(
        [
            jnp.sum(jnp.where(row == first_ref[0] + c, do_ref[...], 0.0), 0, keepdims=True)
            for c in range(crops)
        ],
        0,
    )
    slope = swish_slope(x_ref[...].astype(f32) + values * scale + shift)
    grad = (dy_ref[...].astype(f32) + rows_of_crops(own / PIXELS, values.shape[0])) * slope
    out_ref[...] = grad
    column_sums(stats_ref, grad, grad * ((values - mean) * inverse))


def value_back(first, x, a, sums, norms, dy, do, count):
    rows, width = a.shape
    return pl.pallas_call(
        functools.partial(value_back_kernel, rows // PIXELS, count),
        grid=(QUADS,),
        in_specs=[
            SCALAR, block_spec(rows), quad_spec(rows), quad_spec(2), quad_spec(6),
            block_spec(rows), quad_spec(do.shape[0]),
        ],
        out_specs=[quad_spec(rows), quad_spec(2)],
        out_shape=[
            jax.ShapeDtypeStruct((rows, width), f32), jax.ShapeDtypeStruct((2, width), f32),
        ],
        compiler_params=params(),
        cost_estimate=BRIEF,
        name="value_back",
    )(first, x, a, sums, norms, dy, do)


def norm_back(grad, values, sums, norms, k, grad_sums, count):
    mean, inverse, scale, _ = affine(sums, norms, k, count)
    centred = (values - mean) * inverse
    return scale * (grad - (grad_sums[0:1] + centred * grad_sums[1:2]) / count)


def norm_back_kernel(k, sloped, count, g_ref, a_ref, sums_ref, norms_ref, grad_sums_ref, out_ref):
    grad, values = g_ref[...].astype(f32), a_ref[...]
    if sloped:
        _, _, scale, shift = affine(sums_ref[...], norms_ref[...], k, count)
        grad = grad * swish_slope(values * scale + shift)
    out_ref[...] = norm_back(
        grad, values, sums_ref[...], norms_ref[...], k, grad_sums_ref[...], count
    ).astype(bf16)


def norm_backward(g, a, sums, norms, k, grad_sums, count, sloped):
    rows, width = a.shape
    return pl.pallas_call(
        functools.partial(norm_back_kernel, k, sloped, count),
        grid=(QUADS,),
        in_specs=[quad_spec(rows), quad_spec(rows), quad_spec(2), quad_spec(6), quad_spec(2)],
        out_specs=quad_spec(rows),
        out_shape=jax.ShapeDtypeStruct((rows, width), bf16),
        compiler_params=params(),
        cost_estimate=BRIEF,
        name="norm_backward",
    )(g, a, sums, norms, grad_sums)


def lane_mask(low, high, rows=GROUP):
    lane = lax.broadcasted_iota(jnp.int32, (rows, 256), 1)
    return (lane >= low) & (lane < high)


def dense_kernel(me_ref, *refs):
    out_ref, hold_ref = refs[8:]

    @pl.when(pl.program_id(0) == 0)
    def _():
        for b in range(8):
            hold_ref[me_ref[0] ^ b] = refs[b][...]

    even = hold_ref[2 * pl.program_id(0)].astype(f32)
    odd = hold_ref[2 * pl.program_id(0) + 1].astype(f32)
    row = lax.broadcasted_iota(jnp.int32, (256, 256), 0)
    edge = jnp.zeros((32, 256), f32)
    centre = lane_mask(96, 124) | lane_mask(132, 160)
    for tap in range(9):
        e = even[GROUP * tap : GROUP * (tap + 1)]
        o = odd[GROUP * tap : GROUP * (tap + 1)]
        first = [jnp.where(lane_mask(GROUP * g, GROUP * (g + 1)), e, 0.0) for g in range(4)]
        last = [
            jnp.where(lane_mask(32 + GROUP * g, 32 + GROUP * (g + 1)), o, 0.0) for g in range(4)
        ]
        out_ref[0, 0, tap] = jnp.concatenate(first + [edge], 0).astype(bf16)
        out_ref[0, 1, tap] = jnp.concatenate([edge] + last, 0).astype(bf16)
        across = jnp.where(centre, jnp.concatenate([e[:, 128:], o[:, :128]], 1), 0.0)
        upper = jnp.concatenate(
            [jnp.zeros((96, 256), f32), across, jnp.zeros((104, 256), f32)], 0
        )
        lower = jnp.concatenate(
            [jnp.zeros((104, 256), f32), across, jnp.zeros((96, 256), f32)], 0
        )
        out_ref[0, 2, tap] = (
            jnp.where(row < 124, upper, 0.0) + jnp.where(row >= 132, lower, 0.0)
        ).astype(bf16)


def dense_windows(kernel):
    pieces = [kernel[b] for b in range(8)]
    return pl.pallas_call(
        dense_kernel,
        grid=(QUADS,),
        in_specs=[SCALAR] + [pl.BlockSpec(memory_space=pltpu.VMEM)] * 8,
        out_specs=pl.BlockSpec((1, 3, 9, 256, 256), lambda q: (q, 0, 0, 0, 0)),
        out_shape=jax.ShapeDtypeStruct((QUADS, 3, 9, 256, 256), bf16),
        scratch_shapes=[pltpu.VMEM((8,) + pieces[0].shape, bf16)],
        compiler_params=params(),
        cost_estimate=BRIEF,
        name="dense_windows",
    )(index_scalar("dp"), *pieces)


WINDOWS = (0, 256, 128)


def place_pixels(pad_ref, moved_ref, source_ref, crops):
    for crop in range(crops):
        for row in range(HW):
            pad_ref[pl.ds(PITCH + 256 * crop + PITCH * (row + 1), HW), :] = source_ref[
                pl.ds(PIXELS * crop + HW * row, HW), :
            ]
    for shift in range(3):
        moved_ref[shift] = pad_ref[pl.ds(PITCH - 1 + shift, 256 * crops), :].astype(bf16)


def tap_rows(moved_ref, dy, dx, low, crops):
    return jnp.concatenate(
        [
            moved_ref[dx, pl.ds(256 * crop + PITCH * dy, PITCH * HW), pl.ds(low, 256)]
            for crop in range(crops)
        ],
        0,
    )


def take_pixels(target_ref, source_ref, crops):
    for crop in range(crops):
        for row in range(HW):
            target_ref[pl.ds(PIXELS * crop + HW * row, HW), :] = source_ref[
                pl.ds(PITCH * HW * crop + PITCH * row, HW), :
            ]


def swish(v):
    return v / (1.0 + jnp.exp(-v))


def swish_slope(v):
    sigma = 1.0 / (1.0 + jnp.exp(-v))
    return sigma * (1.0 + v * (1.0 - sigma))


def conv_kernel(crops, count, a_ref, sums_ref, norms_ref, w_ref, out_ref, stats_ref, pad_ref, moved_ref, wide_ref, act_ref):
    @pl.when(pl.program_id(0) == 0)
    def _():
        pad_ref[...] = jnp.zeros_like(pad_ref)

    _, _, scale, shift = affine(sums_ref[...], norms_ref[...], 0, count)
    act = swish(a_ref[...] * scale + shift)
    act_ref[...] = act.astype(bf16).astype(f32)
    place_pixels(pad_ref, moved_ref, act_ref, crops)
    for window, low in enumerate(WINDOWS):
        taps = [tap_rows(moved_ref, tap // 3, tap % 3, low, crops) for tap in range(9)]
        acc = dot(jnp.concatenate(taps, 1), w_ref[0, window].reshape(9 * 256, 256))
        if window < 2:
            wide_ref[:, pl.ds(low, 256)] = acc
        else:
            wide_ref[:, pl.ds(low, 256)] += acc
    take_pixels(act_ref, wide_ref, crops)
    result = act_ref[...].astype(bf16)
    out_ref[...] = result
    result = result.astype(f32)
    column_sums(stats_ref, result, result * result)


def conv(a, sums, norms, windows, count):
    rows, width = a.shape
    crops = rows // PIXELS
    return pl.pallas_call(
        functools.partial(conv_kernel, crops, count),
        grid=(QUADS,),
        in_specs=[
            quad_spec(rows), quad_spec(2), quad_spec(6),
            pl.BlockSpec((1, 3, 9, 256, 256), lambda q: (q, 0, 0, 0, 0)),
        ],
        out_specs=[
            pl.BlockSpec((rows, LANES), lambda q: (0, q)),
            pl.BlockSpec((2, LANES), lambda q: (0, q)),
        ],
        out_shape=[
            jax.ShapeDtypeStruct((rows, width), bf16),
            jax.ShapeDtypeStruct((2, width), f32),
        ],
        scratch_shapes=[
            pltpu.VMEM((2 * PITCH + 256 * crops, LANES), f32),
            pltpu.VMEM((3, 256 * crops, LANES), bf16),
            pltpu.VMEM((PITCH * HW * crops, LANES), f32),
            pltpu.VMEM((rows, LANES), f32),
        ],
        compiler_params=params(),
        cost_estimate=BRIEF,
        name="conv",
    )(a, sums, norms, windows)


def conv_back_kernel(
    crops, count, me_ref, g_ref, a2_ref, sums2_ref, grad_sums_ref, a_ref, sums_ref, norms_ref, w_ref,
    out_ref, kept_ref, sent_ref, stats_ref,
    pad_ref, moved_ref, pad_x_ref, moved_x_ref, wide_ref, act_ref, hold_ref,
):
    @pl.when(pl.program_id(0) == 0)
    def _():
        pad_ref[...] = jnp.zeros_like(pad_ref)
        pad_x_ref[...] = jnp.zeros_like(pad_x_ref)

    norms = norms_ref[...]
    grad = norm_back(
        g_ref[...], a2_ref[...].astype(f32), sums2_ref[...], norms, 1, grad_sums_ref[...], count
    )
    act_ref[...] = grad.astype(bf16).astype(f32)
    place_pixels(pad_ref, moved_ref, act_ref, crops)
    values = a_ref[...]
    mean, inverse, scale, shift = affine(sums_ref[...], norms, 0, count)
    normed = values * scale + shift
    act_ref[...] = swish(normed).astype(bf16).astype(f32)
    place_pixels(pad_x_ref, moved_x_ref, act_ref, crops)
    for window, low in enumerate(WINDOWS):
        taps = [tap_rows(moved_ref, 2 - tap // 3, 2 - tap % 3, low, crops) for tap in range(9)]
        weight = jnp.concatenate([w_ref[0, window, tap] for tap in range(9)], 1)
        acc = dot(jnp.concatenate(taps, 1), weight, NT)
        if window < 2:
            wide_ref[:, pl.ds(low, 256)] = acc
        else:
            wide_ref[:, pl.ds(low, 256)] += acc
    take_pixels(act_ref, wide_ref, crops)
    result = act_ref[...].astype(bf16)
    out_ref[...] = result
    grad = result.astype(f32) * swish_slope(normed)
    column_sums(stats_ref, grad, grad * ((values - mean) * inverse))
    centre = lane_mask(96, 124) | lane_mask(132, 160)
    row = lax.broadcasted_iota(jnp.int32, (GROUP, 256), 0)
    mids = [
        tap_rows(moved_ref, 1, 1, low, crops) for low in WINDOWS
    ]
    for tap in range(9):
        pieces = []
        for window, low in enumerate(WINDOWS):
            pieces.append(
                dot(tap_rows(moved_x_ref, tap // 3, tap % 3, low, crops), mids[window], TN)
            )
        even = sum(
            jnp.where(lane_mask(GROUP * g, GROUP * (g + 1)), pieces[0][GROUP * g : GROUP * (g + 1)], 0.0)
            for g in range(4)
        )
        odd = sum(
            jnp.where(
                lane_mask(32 + GROUP * g, 32 + GROUP * (g + 1)),
                pieces[1][32 + GROUP * g : 32 + GROUP * (g + 1)],
                0.0,
            )
            for g in range(4)
        )
        across = jnp.where(
            centre, jnp.where(row < GROUP // 2, pieces[2][96:152], pieces[2][104:160]), 0.0
        )
        nothing = jnp.zeros((GROUP, 128), f32)
        even = even + jnp.concatenate([nothing, across[:, :128]], 1)
        odd = odd + jnp.concatenate([across[:, 128:], nothing], 1)
        twin = me_ref[0] % 2 == 1
        hold_ref[0, pl.ds(GROUP * tap, GROUP), :] = jnp.where(twin, odd, even)
        hold_ref[1, pl.ds(GROUP * tap, GROUP), :] = jnp.where(twin, even, odd)
    kept_ref[0, 0] = hold_ref[0].astype(bf16)
    sent_ref[0, 0] = hold_ref[1].astype(bf16)


def conv_back(g, a2, sums2, grad_sums, a, sums, norms, windows, count):
    rows, width = a.shape
    crops = rows // PIXELS
    piece = pl.BlockSpec((1, 1, 9 * GROUP, 256), lambda q, me: (q ^ (me[0] // 2), 0, 0, 0))

    def quad(n):
        return pl.BlockSpec((n, LANES), lambda q, me: (0, q))

    spec = pltpu.PrefetchScalarGridSpec(
        num_scalar_prefetch=1,
        grid=(QUADS,),
        in_specs=[
            quad(rows), quad(rows), quad(2), quad(2), quad(rows), quad(2), quad(6),
            pl.BlockSpec((1, 3, 9, 256, 256), lambda q, me: (q, 0, 0, 0, 0)),
        ],
        out_specs=[quad(rows), piece, piece, quad(2)],
        scratch_shapes=[
            pltpu.VMEM((2 * PITCH + 256 * crops, LANES), f32),
            pltpu.VMEM((3, 256 * crops, LANES), bf16),
            pltpu.VMEM((2 * PITCH + 256 * crops, LANES), f32),
            pltpu.VMEM((3, 256 * crops, LANES), bf16),
            pltpu.VMEM((PITCH * HW * crops, LANES), f32),
            pltpu.VMEM((rows, LANES), f32),
            pltpu.VMEM((2, 9 * GROUP, 256), f32),
        ],
    )
    return pl.pallas_call(
        functools.partial(conv_back_kernel, crops, count),
        grid_spec=spec,
        out_shape=[
            jax.ShapeDtypeStruct((rows, width), bf16),
            jax.ShapeDtypeStruct((QUADS, 1, 9 * GROUP, 256), bf16),
            jax.ShapeDtypeStruct((QUADS, 1, 9 * GROUP, 256), bf16),
            jax.ShapeDtypeStruct((2, width), f32),
        ],
        compiler_params=params(),
        cost_estimate=BRIEF,
        name="conv_back",
    )(index_scalar("dp"), g, a2, sums2, grad_sums, a, sums, norms, windows)


def squeeze_weight(se_ref, d):
    return jnp.concatenate([se_ref[d, m, :, :128] for m in range(QUADS)], 1)


def excite_weight(se_ref, m):
    return jnp.concatenate(
        [
            jnp.concatenate(
                [se_ref[d, m, 64 * i : 64 * (i + 1), 128:] for i in range(4)], 1
            )
            for d in range(2 * QUADS)
        ],
        0,
    )


def rows_of_crops(values, rows):
    row = lax.broadcasted_iota(jnp.int32, (rows, 1), 0)
    out = values[0:1]
    for c in range(1, values.shape[0]):
        out = jnp.where(row >= PIXELS * c, values[c : c + 1], out)
    return out


def fetch_pieces(me_ref, pieces, hold_ref, sems, offset):
    size = hold_ref.shape[2]
    copies = [
        pltpu.make_async_copy(
            piece.at[pl.ds(offset + m * size, size)],
            hold_ref.at[me_ref[0] ^ b, m],
            sems.at[b * QUADS + m],
        )
        for b, piece in enumerate(pieces)
        for m in range(QUADS)
    ]
    for copy in copies:
        copy.start()
    return copies


def fetch_scratch(size):
    return [
        pltpu.VMEM((2 * QUADS, QUADS, size, 256), bf16),
        pltpu.SemaphoreType.DMA((8 * QUADS,)),
    ]


def gate_kernel(crops, count, me_ref, a_ref, sums_ref, norms_ref, *refs):
    h_ref, pooled_ref, squeezed_ref, act_ref, gate_ref, f2_ref, se_ref, sems = refs[8:]
    copies = fetch_pieces(me_ref, refs[:8], se_ref, sems, SE_OFFSET)
    rows = a_ref.shape[0]
    _, _, scale, shift = affine(sums_ref[...], norms_ref[...], 1, count)
    f2_ref[...] = swish(a_ref[...].astype(f32) * scale + shift)
    pooled = jnp.concatenate(
        [
            jnp.sum(f2_ref[pl.ds(PIXELS * c, PIXELS), :], 0, keepdims=True) / PIXELS
            for c in range(crops)
        ],
        0,
    ).astype(bf16)
    pooled_ref[...] = pooled
    for copy in copies:
        copy.wait()
    squeezed = sum(
        dot(pooled[:, 256 * d : 256 * (d + 1)], squeeze_weight(se_ref, d)) for d in range(8)
    )
    squeezed_ref[...] = squeezed
    act = swish(squeezed).astype(bf16)
    act_ref[...] = act
    for m in range(QUADS):
        lanes = pl.ds(m * LANES, LANES)
        gate = 1.0 / (1.0 + jnp.exp(-dot(act, excite_weight(se_ref, m))))
        gate_ref[:, lanes] = gate
        h_ref[m] = (f2_ref[:, lanes] * rows_of_crops(gate, rows)).astype(bf16)


def gate(a, sums, norms, se, count):
    rows, width = a.shape
    crops = rows // PIXELS
    return pl.pallas_call(
        functools.partial(gate_kernel, crops, count),
        in_specs=[SCALAR] + [pl.BlockSpec(memory_space=pltpu.VMEM)] * 3
        + [pl.BlockSpec(memory_space=pl.ANY)] * 8,
        out_shape=[
            jax.ShapeDtypeStruct((QUADS, rows, LANES), bf16),
            jax.ShapeDtypeStruct((crops, width), bf16),
            jax.ShapeDtypeStruct((crops, 512), f32),
            jax.ShapeDtypeStruct((crops, 512), bf16),
            jax.ShapeDtypeStruct((crops, width), f32),
        ],
        scratch_shapes=[pltpu.VMEM((rows, width), f32)] + fetch_scratch(SE_ROWS),
        compiler_params=params(),
        cost_estimate=BRIEF,
        name="gate",
    )(index_scalar("dp"), a, sums, norms, *se)


def gate_back_kernel(
    crops, count, me_ref, dh_ref, a_ref, sums_ref, norms_ref, gate_ref, squeezed_ref, *refs
):
    q_ref, stats_ref, excite_grad_ref, squeeze_grad_ref, work_ref, se_ref, sems = refs[8:]
    copies = fetch_pieces(me_ref, refs[:8], se_ref, sems, SE_OFFSET)
    rows = a_ref.shape[0]
    for m in range(QUADS):
        lanes = pl.ds(m * LANES, LANES)
        _, _, scale, shift = affine(sums_ref[:, lanes], norms_ref[:, lanes], 1, count)
        normed = a_ref[:, lanes].astype(f32) * scale + shift
        work_ref[:, lanes] = dh_ref[:, lanes] * swish(normed)
    sums = jnp.concatenate(
        [
            jnp.sum(work_ref[pl.ds(PIXELS * c, PIXELS), :], 0, keepdims=True)
            for c in range(crops)
        ],
        0,
    )
    gates = gate_ref[...]
    excite_grad = (sums * gates * (1.0 - gates)).astype(bf16)
    excite_grad_ref[...] = excite_grad
    for copy in copies:
        copy.wait()
    act_grad = sum(
        dot(excite_grad[:, m * LANES : (m + 1) * LANES], excite_weight(se_ref, m), NT)
        for m in range(QUADS)
    )
    squeeze_grad = (act_grad * swish_slope(squeezed_ref[...])).astype(bf16)
    squeeze_grad_ref[...] = squeeze_grad
    for d in range(8):
        lanes = pl.ds(d * 256, 256)
        pooled_grad = dot(squeeze_grad, squeeze_weight(se_ref, d), NT) / PIXELS
        values = a_ref[:, lanes].astype(f32)
        mean, inverse, scale, shift = affine(sums_ref[:, lanes], norms_ref[:, lanes], 1, count)
        normed = values * scale + shift
        q = (
            dh_ref[:, lanes] * rows_of_crops(gate_ref[:, lanes], rows)
            + rows_of_crops(pooled_grad, rows)
        ) * swish_slope(normed)
        q_ref[:, lanes] = q
        centred = (values - mean) * inverse
        stats_ref[0:1, lanes] = jnp.sum(q, 0, keepdims=True)
        stats_ref[1:2, lanes] = jnp.sum(q * centred, 0, keepdims=True)


def gate_back(dh, a, sums, norms, gates, squeezed, se, count):
    rows, width = a.shape
    crops = rows // PIXELS
    return pl.pallas_call(
        functools.partial(gate_back_kernel, crops, count),
        in_specs=[SCALAR] + [pl.BlockSpec(memory_space=pltpu.VMEM)] * 6
        + [pl.BlockSpec(memory_space=pl.ANY)] * 8,
        out_shape=[
            jax.ShapeDtypeStruct((rows, width), f32),
            jax.ShapeDtypeStruct((2, width), f32),
            jax.ShapeDtypeStruct((crops, width), bf16),
            jax.ShapeDtypeStruct((crops, 512), bf16),
        ],
        scratch_shapes=[pltpu.VMEM((rows, width), f32)] + fetch_scratch(SE_ROWS),
        compiler_params=params(),
        cost_estimate=BRIEF,
        name="gate_back",
    )(index_scalar("dp"), dh, a, sums, norms, gates, squeezed, *se)


def head_kernel(
    width, me_ref, summary_ref, *refs
):
    (
        loss_ref, unit_ref, score_grad_ref, embed_grad_ref, summary_grad_ref, all_ref,
        hold_ref, plan_ref, protos_ref, queue_ref, project_ref, bundle_ref, sems,
    ) = refs[8:]
    copies = fetch_pieces(me_ref, refs[:8], bundle_ref, sems, 0)
    crops = all_ref.shape[0]
    each = summary_ref.shape[1]
    for i in range(summary_ref.shape[0]):
        hold_ref[pl.ds(each * i, each), :] = summary_ref[i].astype(f32)
    all_ref[...] = hold_ref[...].astype(bf16)
    for copy in copies:
        copy.wait()
    parts = 2 * QUADS * QUADS
    blocks = parts * QUEUE_ROWS // crops
    for i in range(parts):
        d, m = i // QUADS, i % QUADS
        low = 64
        project_ref[d, pl.ds(64 * m, 64), :] = bundle_ref[d, m, 0:low, :]
        protos_ref[pl.ds(PROTO_ROWS * i, PROTO_ROWS), :] = bundle_ref[d, m, low : low + PROTO_ROWS, :]
        low = low + PROTO_ROWS
        queue_ref[pl.ds(QUEUE_ROWS * i, QUEUE_ROWS), :] = bundle_ref[d, m, low : low + QUEUE_ROWS, :]
    protos = protos_ref[...]
    embedded = sum(
        dot(all_ref[:, 256 * d : 256 * (d + 1)], project_ref[d], NT) for d in range(8)
    )
    scale = lax.rsqrt(jnp.sum(embedded * embedded, 1, keepdims=True) + EPS_NORM)
    unit = (embedded * scale).astype(bf16)
    unit_ref[...] = unit
    scores = dot(unit, protos, NT)
    lane = lax.broadcasted_iota(jnp.int32, (1, parts * PROTO_ROWS), 1)
    block = lane // PROTO_ROWS
    there = (block // QUADS) * PROTO_ROWS + (lane - block * PROTO_ROWS) < width
    first = jnp.where(there, jnp.exp(scores / EPS_SINK), 0.0)
    plan_ref[pl.ds(0, crops), :] = first

    def fill(i, column):
        rows = queue_ref[pl.ds(pl.multiple_of(i * crops, crops), crops), :]
        value = jnp.exp(dot(rows, protos, NT) / EPS_SINK)
        plan_ref[pl.ds(pl.multiple_of((i + 1) * crops, crops), crops), :] = value
        return column + jnp.sum(value, 0, keepdims=True)

    column = lax.fori_loop(0, blocks, fill, jnp.sum(first, 0, keepdims=True))
    inverse = jnp.where(there, 1.0 / column, 0.0)
    for sweep in range(SINK - 1):

        def pass_rows(i, column, inverse=inverse):
            place = pl.ds(pl.multiple_of(i * crops, crops), crops)
            value = plan_ref[place, :] * inverse
            value = value * (1.0 / jnp.sum(value, 1, keepdims=True))
            plan_ref[place, :] = value
            return column + jnp.sum(value, 0, keepdims=True)

        column = lax.fori_loop(0, blocks + 1, pass_rows, jnp.zeros_like(column))
        inverse = jnp.where(there, 1.0 / column, 0.0)
    value = plan_ref[pl.ds(0, crops), :] * inverse
    value = value / jnp.sum(value, 1, keepdims=True)
    pairs = jnp.concatenate(
        [bundle_ref[d, 0, HEAD_ROWS - 16 : HEAD_ROWS, :].astype(f32)[:8, :crops] for d in range(8)], 0
    )
    plan = lax.dot_general(
        pairs, value, NN, precision=lax.Precision.HIGHEST, preferred_element_type=f32
    )
    logits = scores / SOFTMAX_TEMPER
    top = jnp.max(jnp.where(there, logits, -jnp.inf), 1, keepdims=True)
    power = jnp.where(there, jnp.exp(logits - top), 0.0)
    mass = jnp.sum(power, 1, keepdims=True)
    entropy = jnp.sum(plan * (logits - (top + jnp.log(mass))), 1, keepdims=True)
    loss_ref[...] = -jnp.sum(entropy, 0, keepdims=True) / crops
    score_grad = ((power / mass - plan) / (SOFTMAX_TEMPER * crops)).astype(bf16)
    score_grad_ref[...] = score_grad.T
    unit_grad = dot(score_grad, protos)
    inner = jnp.sum(embedded * unit_grad, 1, keepdims=True)
    embed_grad = (scale * unit_grad - embedded * (scale * scale * scale * inner)).astype(bf16)
    embed_grad_ref[...] = embed_grad
    for d in range(8):
        summary_grad_ref[:, 256 * d : 256 * (d + 1)] = dot(embed_grad, project_ref[d])


def head(summary, bundle, width):
    devices, each, channels = summary.shape
    crops = devices * each
    parts = 2 * QUADS * QUADS
    return pl.pallas_call(
        functools.partial(head_kernel, width),
        in_specs=[SCALAR, pl.BlockSpec(memory_space=pltpu.VMEM)]
        + [pl.BlockSpec(memory_space=pl.ANY)] * 8,
        out_shape=[
            jax.ShapeDtypeStruct((1, 1), f32),
            jax.ShapeDtypeStruct((crops, 256), bf16),
            jax.ShapeDtypeStruct((parts * PROTO_ROWS, crops), bf16),
            jax.ShapeDtypeStruct((crops, 256), bf16),
            jax.ShapeDtypeStruct((crops, channels), f32),
            jax.ShapeDtypeStruct((crops, channels), bf16),
        ],
        scratch_shapes=[
            pltpu.VMEM((crops, channels), f32),
            pltpu.VMEM((crops + parts * QUEUE_ROWS, parts * PROTO_ROWS), f32),
            pltpu.VMEM((parts * PROTO_ROWS, 256), bf16),
            pltpu.VMEM((parts * QUEUE_ROWS, 256), bf16),
            pltpu.VMEM((8, 256, 256), bf16),
        ]
        + fetch_scratch(HEAD_ROWS),
        compiler_params=params(),
        cost_estimate=BRIEF,
        name="head",
    )(index_scalar("dp"), summary, *bundle)


def plain_head(summary, project, protos, queue, pairs):
    crops = summary.shape[0]
    embedded = dot(summary, project)
    scale = lax.rsqrt(jnp.sum(embedded * embedded, 1, keepdims=True) + EPS_NORM)
    unit = (embedded * scale).astype(bf16)
    scores = dot(unit, protos)
    plan = jnp.exp(jnp.concatenate([scores, dot(queue, protos)], 0) / EPS_SINK)
    for sweep in range(SINK):
        plan = plan / jnp.sum(plan, 0, keepdims=True)
        plan = plan / jnp.sum(plan, 1, keepdims=True)
    plan = lax.dot_general(
        pairs, plan[:crops], NN, precision=lax.Precision.HIGHEST, preferred_element_type=f32
    )
    logits = scores / SOFTMAX_TEMPER
    loss = -jnp.sum(plan * jax.nn.log_softmax(logits, axis=1)) / crops
    score_grad = ((jax.nn.softmax(logits, axis=1) - plan) / (SOFTMAX_TEMPER * crops)).astype(bf16)
    unit_grad = dot(score_grad, protos, NT)
    inner = jnp.sum(embedded * unit_grad, 1, keepdims=True)
    embed_grad = (scale * unit_grad - embedded * (scale * scale * scale * inner)).astype(bf16)
    return loss.reshape(1, 1), unit, score_grad, embed_grad, dot(embed_grad, project, NT)


def picks(rows, columns, source):
    row = lax.broadcasted_iota(jnp.int32, (rows, columns), 0)
    column = lax.broadcasted_iota(jnp.int32, (rows, columns), 1)
    return jnp.where(row == source(column), 1.0, 0.0).astype(bf16)


def narrow_lanes(v):
    return jnp.concatenate([v[:, :HALF], v[:, HALF + GAP :]], 1)


def square_sum(v):
    return jnp.sum(jnp.sum(v * v, 1, keepdims=True), 0, keepdims=True)


def small_grads_kernel(
    m_ref, small_ref, summary_ref, embed_grad_ref, score_grad_ref, unit_ref,
    squeeze_ref, excite_ref, project_ref, protos_ref, squares_ref, hold_ref,
):
    m = m_ref[0]
    devices, each, _ = small_ref.shape
    for i in range(devices):
        hold_ref[pl.ds(each * i, each), :] = small_ref[i].astype(f32)
    wide, inner = QUADS * LANES, 8 * SE_LANES

    def rows_of(base, size):
        return hold_ref[:, pl.ds(pl.multiple_of(base, 128), size)]

    squeeze_grad = rows_of(wide + inner + 128 * m, 128).astype(bf16)
    squeeze_grad = dot(
        squeeze_grad, picks(128, 2 * SE_PART, lambda c: (c // SE_PART) * SE_LANES + c % SE_PART)
    ).astype(bf16)
    squares = []
    total_square = jnp.zeros((1, 1), f32)
    for q in range(QUADS):
        pooled = narrow_lanes(rows_of(q * LANES, LANES)).astype(bf16)
        part = dot(pooled, squeeze_grad, TN)
        squeeze_ref[pl.ds(QUAD * q, QUAD), :] = part
        total_square = total_square + square_sum(part)
    squares.append(total_square)
    act = rows_of(wide, inner).astype(bf16)
    act = dot(act, picks(inner, QUAD, lambda c: (c // SE_PART) * SE_LANES + c % SE_PART)).astype(bf16)
    excite_grad = narrow_lanes(rows_of(wide + 2 * inner + LANES * m, LANES)).astype(bf16)
    part = dot(act, excite_grad, TN)
    excite_ref[...] = part
    squares.append(square_sum(part))
    embed_grad = dot(embed_grad_ref[...], picks(256, 64, lambda c: 64 * m + c)).astype(bf16)
    summary = jnp.concatenate(
        [
            narrow_lanes(summary_ref[:, q * LANES : (q + 1) * LANES].astype(f32))
            for q in range(QUADS)
        ],
        1,
    ).astype(bf16)
    part = dot(embed_grad, summary, TN)
    project_ref[...] = part
    squares.append(square_sum(part))
    total_square = jnp.zeros((1, 1), f32)
    last = protos_ref.shape[0]
    for d in range(8):
        place = pl.ds(pl.multiple_of((QUADS * d + m) * PROTO_ROWS, PROTO_ROWS), PROTO_ROWS)
        part = dot(score_grad_ref[place, :], unit_ref[...])
        size = min(PROTO_ROWS, last - PROTO_ROWS * d)
        protos_ref[pl.ds(PROTO_ROWS * d, size), :] = part[:size]
        total_square = total_square + square_sum(part)
    squares.append(total_square)
    lane = lax.broadcasted_iota(jnp.int32, (1, 128), 1)
    squares_ref[...] = sum(jnp.where(lane == i, v, 0.0) for i, v in enumerate(squares))


def small_grads(small, summary, embed_grad, score_grad, unit, width):
    crops = summary.shape[0]
    return pl.pallas_call(
        small_grads_kernel,
        in_specs=[SCALAR] + [pl.BlockSpec(memory_space=pltpu.VMEM)] * 5,
        out_shape=[
            jax.ShapeDtypeStruct((QUADS * QUAD, 2 * SE_PART), f32),
            jax.ShapeDtypeStruct((QUAD, QUAD), f32),
            jax.ShapeDtypeStruct((64, QUADS * QUAD), f32),
            jax.ShapeDtypeStruct((width, 256), f32),
            jax.ShapeDtypeStruct((1, 128), f32),
        ],
        scratch_shapes=[pltpu.VMEM((crops, small.shape[2]), f32)],
        compiler_params=params(),
        cost_estimate=BRIEF,
        name="small_grads",
    )(index_scalar("mp"), small, summary, embed_grad, score_grad, unit)


def own_kernel_kernel(me_ref, v_ref, out_ref, square_ref):
    value = v_ref[: 9 * GROUP].astype(f32)
    value = jnp.where(me_ref[0] % 2 == 1, value[:, 256 - HALF :], value[:, :HALF])
    out_ref[...] = value
    square_ref[...] = square_sum(value)


def own_kernel(v):
    return pl.pallas_call(
        own_kernel_kernel,
        in_specs=[SCALAR, pl.BlockSpec(memory_space=pltpu.VMEM)],
        out_shape=[
            jax.ShapeDtypeStruct((9 * GROUP, HALF), f32), jax.ShapeDtypeStruct((1, 1), f32),
        ],
        compiler_params=params(),
        cost_estimate=BRIEF,
        name="own_kernel",
    )(index_scalar("dp"), v)


def weight_sums_kernel(*refs):
    lane = lax.broadcasted_iota(jnp.int32, (1, 128), 1)
    refs[-1][...] = sum(
        jnp.where(lane == i, square_sum(ref[...]), 0.0) for i, ref in enumerate(refs[:-1])
    )


def weight_sums(weights):
    values = [w if w.shape[1] == 2 * SE_PART or w.shape[0] == w.shape[1] else w.T for w in weights]
    return pl.pallas_call(
        weight_sums_kernel,
        out_shape=jax.ShapeDtypeStruct((1, 128), f32),
        compiler_params=params(),
        cost_estimate=BRIEF,
        name="weight_sums",
    )(*values)


def squares_kernel(
    n_dp, n_mp, weights_ref, norms_ref, small_ref, reduce_ref, expand_ref, kernel_ref,
    g1_ref, g2_ref, g3_ref, out_ref,
):
    lane = lax.broadcasted_iota(jnp.int32, (1, 128), 1)

    def at(i, v):
        return jnp.where(lane == i, v, 0.0)

    portions = at(0, 1.0) + at(1, 1.0 / n_mp) + at(4, 1.0)
    for i in (2, 3, 5, 6):
        portions = portions + at(i, 1.0 / n_dp)
    weights = weights_ref[...] * portions
    small = small_ref[...]
    grads = at(0, reduce_ref[...]) + at(1, kernel_ref[...] / n_mp) + at(4, expand_ref[...])
    for i, k in enumerate((2, 3, 5, 6)):
        grads = grads + at(k, small[:, i : i + 1] / n_dp)
    everywhere = 1.0 / (n_dp * n_mp)
    for k, ref in enumerate((g1_ref, g2_ref, g3_ref)):
        for row, first in ((1, 7), (0, 10)):
            grads = grads + at(first + k, square_sum(ref[row : row + 1, :]) * everywhere)
        weights = weights + at(7 + k, square_sum(norms_ref[k : k + 1, :]) * everywhere)
        weights = weights + at(10 + k, square_sum(norms_ref[3 + k : 4 + k, :]) * everywhere)
    out_ref[0:1, :] = weights
    out_ref[1:2, :] = grads


def squares(n_dp, n_mp, *values):
    return pl.pallas_call(
        functools.partial(squares_kernel, n_dp, n_mp),
        out_shape=jax.ShapeDtypeStruct((2, 128), f32),
        compiler_params=params(),
        cost_estimate=BRIEF,
        name="squares",
    )(*values)


def rate_of(norm_squares, i):
    norms = jnp.sqrt(norm_squares[:, i : i + 1] + EPS_NORM)
    return TRUST * norms[0:1] / (norms[1:2] + DECAY * norms[0:1])


def step(weight, gradient, momentum, norm_squares, i):
    return MOMENTUM * momentum + rate_of(norm_squares, i) * (gradient + DECAY * weight)


def lars_prepare_kernel(*refs):
    n = len(refs) // 5
    for i in range(n):
        weight, gradient, momentum = (refs[3 * i + j] for j in range(3))
        refs[3 * n + 2 * i][...] = gradient[...] + DECAY * weight[...]
        refs[3 * n + 2 * i + 1][...] = MOMENTUM * momentum[...]


def lars_prepare(items):
    return pl.pallas_call(
        lars_prepare_kernel,
        out_shape=[jax.ShapeDtypeStruct(w.shape, f32) for w, _, _ in items for _ in range(2)],
        compiler_params=params(),
        cost_estimate=BRIEF,
        name="lars_prepare",
    )(*[v for item in items for v in item])


def lars_kernel(squares_ref, weight_ref, gradient_ref, momentum_ref, *refs):
    norm_squares = squares_ref[...]
    n = len(refs) // 3
    refs[2 * n][...] = step(
        weight_ref[...], gradient_ref[...], momentum_ref[...], norm_squares, 0
    )
    for i in range(n):
        refs[2 * n + 1 + i][...] = (
            refs[2 * i + 1][...] + rate_of(norm_squares, i + 1) * refs[2 * i][...]
        )


def lars(norm_squares, weight, gradient, momentum, prepared):
    shapes = [weight.shape] + [v.shape for v in prepared[::2]]
    return pl.pallas_call(
        lars_kernel,
        out_shape=[jax.ShapeDtypeStruct(shape, f32) for shape in shapes],
        compiler_params=params(),
        cost_estimate=BRIEF,
        name="lars",
    )(norm_squares, weight, gradient, momentum, *prepared)


def lars_norms_kernel(
    m_ref, squares_ref, gains_ref, biases_ref, m_gains_ref, m_biases_ref, g1_ref, g2_ref, g3_ref,
    gains_out, biases_out,
):
    norm_squares = squares_ref[...]
    lanes = pl.ds(pl.multiple_of(m_ref[0] * LANES, LANES), LANES)
    for k, ref in enumerate((g1_ref, g2_ref, g3_ref)):
        own = narrow_lanes(ref[:, lanes])
        row = slice(k, k + 1)
        gains_out[row, :] = step(gains_ref[row, :], own[1:2], m_gains_ref[row, :], norm_squares, 7 + k)
        biases_out[row, :] = step(
            biases_ref[row, :], own[0:1], m_biases_ref[row, :], norm_squares, 10 + k
        )


def lars_norms(norm_squares, *values):
    return pl.pallas_call(
        lars_norms_kernel,
        in_specs=[SCALAR] + [pl.BlockSpec(memory_space=pltpu.VMEM)] * 8,
        out_shape=[jax.ShapeDtypeStruct(values[0].shape, f32)] * 2,
        compiler_params=params(),
        cost_estimate=BRIEF,
        name="lars_norms",
    )(index_scalar("mp"), norm_squares, *values)


def plain_finish(
    small, summary, unit, score_grad, embed_grad, grad_sums, channels_here, big_grads, weights, moments
):
    n_dp, n_mp, m_index = lax.axis_size("dp"), lax.axis_size("mp"), lax.axis_index("mp")
    w_reduce, w_group, w_squeeze, w_excite, w_expand, w_project, prototypes, bn_gains, bn_biases = weights
    small = small.reshape(-1, small.shape[-1])
    wide, inner = QUADS * LANES, 8 * SE_LANES
    pooled_all = pack_channels(small[:, :wide])
    act_all = pack_inner(small[:, wide : wide + inner])
    squeeze_all = pack_inner(small[:, wide + inner : wide + 2 * inner])
    excite_all = pack_channels(small[:, wide + 2 * inner :])

    def own(v, width):
        return lax.dynamic_slice_in_dim(v, m_index * width, width, 1)

    reduce_grad, kernel_grad, expand_grad = big_grads
    gain_part = own(pack_channels(jnp.stack([v[1] for v in grad_sums])), channels_here)
    bias_part = own(pack_channels(jnp.stack([v[0] for v in grad_sums])), channels_here)
    grads = [
        reduce_grad,
        kernel_grad,
        dot(pooled_all, own(squeeze_all, w_squeeze.shape[1]), TN),
        dot(act_all, own(excite_all, w_excite.shape[1]), TN),
        expand_grad,
        dot(pack_channels(summary), own(embed_grad, w_project.shape[1]), TN),
        dot(unit, own(score_grad, prototypes.shape[1]), TN),
    ]
    portions = [1.0, 1.0 / n_mp, 1.0 / n_dp, 1.0 / n_dp, 1.0, 1.0 / n_dp, 1.0 / n_dp]

    def shares(arrays, gain, bias):
        return jnp.concatenate(
            [
                jnp.stack([jnp.sum(a * a) * p for a, p in zip(arrays, portions)]),
                jnp.sum(gain * gain, 1) / n_dp,
                jnp.sum(bias * bias, 1) / n_dp,
            ]
        )

    norms = total(
        jnp.stack([shares(weights[:7], bn_gains, bn_biases), shares(grads, gain_part, bias_part)])
    )
    stepped = [
        step(w, g, m, norms, i) for i, (w, g, m) in enumerate(zip(weights[:7], grads, moments[:7]))
    ]
    for values, part, momentum, first in (
        (bn_gains, gain_part, moments[7], 7), (bn_biases, bias_part, moments[8], 10),
    ):
        stepped.append(
            jnp.concatenate(
                [
                    step(values[k : k + 1], part[k : k + 1], momentum[k : k + 1], norms, first + k)
                    for k in range(3)
                ]
            )
        )
    return stepped, norms


def body(
    block_input, output_grad, w_reduce, w_group, w_squeeze, w_excite, w_expand, w_project,
    prototypes, bn_gains, bn_biases, m_reduce, m_group, m_squeeze, m_excite, m_expand,
    m_project, m_protos, m_gains, m_biases, queue_store, queue_slots, crop_perm,
):
    n_dp = lax.axis_size("dp")
    n_mp = lax.axis_size("mp")
    m_index = lax.axis_index("mp")
    channels_here = block_input.shape[0]
    rows = block_input.shape[1] // n_mp
    crops = rows // PIXELS
    count = rows * n_dp * n_mp
    all_crops = crops * n_dp * n_mp
    quick = quick_mesh()
    weights = [
        w_reduce, w_group, w_squeeze, w_excite, w_expand, w_project, prototypes, bn_gains, bn_biases,
    ]
    moments = [
        m_reduce, m_group, m_squeeze, m_excite, m_expand, m_project, m_protos, m_gains, m_biases,
    ]

    slot_table = (
        queue_slots[0][:, None]
        == lax.broadcasted_iota(jnp.int32, (queue_slots.shape[1], queue_store.shape[0]), 1)
    ).astype(bf16)
    queue_rows = dot(slot_table, queue_store.astype(bf16)).astype(bf16)
    order = crop_perm[0]
    pairing = (order[None, :] == jnp.bitwise_xor(order, 1)[:, None]).astype(f32)
    kernel_low = gather_kernel(w_group)
    x_blocks = slab_blocks(block_input)
    y_grad_blocks = slab_blocks(output_grad)
    norms = spread(jnp.concatenate([bn_gains, bn_biases], 0), "mp")
    norms = spread_channels(norms.transpose(1, 0, 2).reshape(norms.shape[1], -1))
    if quick:
        reduce_quads = gather_mp(shard_square(w_reduce)).reshape(-1, 256)
        rest = jnp.concatenate([shard_square(w_expand), shard_excitation(w_squeeze, w_excite)], 0)
        reduce_quads, rest, norms, *kernel_low = tie(reduce_quads, rest, norms, *kernel_low)
        across, up = gather_sides(reduce_quads)
        rest_parts = parts_mp(rest)
        windows = dense_windows(kernel_low)
        across, up, windows, x_blocks = tie(across, up, windows, x_blocks)
        corner = gather_corner(across, up)
        x_blocks, corner, *rest_parts = tie(x_blocks, corner, *rest_parts)
        x_blocks = exchange(x_blocks)
        rest = in_order(rest_parts, m_index)
        rest = jnp.concatenate(
            [rest[:, :LANES].reshape(-1, 256), rest[:, LANES:].reshape(-1, 256)], 0
        )
        rest_across, rest_up = gather_sides(rest)
        reduce_pieces = gather_twins(reduce_quads, across, up, corner)
        head_values = tie(w_project, prototypes, queue_rows, pairing, corner)
        bundle = shard_head(*head_values[:4])
    else:
        x_blocks = exchange(x_blocks)
        y_grad_blocks = exchange(y_grad_blocks)
        reduce_pieces = gather_square(w_reduce)
        rest_pieces = gather_excitation(w_squeeze, w_excite)
        expand_pieces = gather_square(w_expand)
        rest_pieces = jnp.concatenate(
            [expand_pieces.reshape(8, -1, 256), rest_pieces.reshape(8, -1, 256)], 1
        )
        rest_pieces = [rest_pieces[b] for b in range(8)]
        project_low, protos_low, queue_low, pairs = gather_head(
            w_project, prototypes, queue_rows, pairing
        )
        pairs = block_diagonal(pairs)
        windows = dense_windows(kernel_low)
    x = quad_blocks(x_blocks)

    reduced, sums1 = mix(x, reduce_pieces)
    if quick:
        sums1, rest_across, rest_up = tie(sums1, rest_across, rest_up)
        rest_corner = gather_corner(rest_across, rest_up)
    sums1 = total(sums1)
    if quick:
        sums1, bundle, rest_corner = tie(sums1, bundle, rest_corner)
        bundle = gather_mp(bundle).reshape(-1, 256)
    grouped, sums2 = conv(reduced, sums1, norms, windows, count)
    if quick:
        sums2, bundle = tie(sums2, bundle)
    sums2 = total(sums2)
    if quick:
        weight_squares = weight_sums(weights[:7])
        sums2, weight_squares = tie(sums2, weight_squares)
        rest_pieces = expand_pieces = gather_twins(rest, rest_across, rest_up, rest_corner)
    gated, pooled, squeezed, squeeze_act, gates = gate(grouped, sums2, norms, rest_pieces, count)
    if quick:
        gated, bundle = tie(gated, bundle)
        across, up = gather_sides(bundle)
    expanded, sums3 = mix(gated, expand_pieces)
    if quick:
        sums3, across, up = tie(sums3, across, up)
        corner = gather_corner(across, up)
    sums3 = total(sums3)
    if quick:
        sums3, corner = tie(sums3, corner)
        bundle = gather_twins(bundle, across, up, corner)
    y_blocks, summary = block_value(x, expanded, sums3, norms, count)
    summary = gather_all(summary)

    first_crop = ((lax.axis_index("dp") * n_mp + m_index) * crops).astype(jnp.int32)[None]
    if quick:
        summary, y_grad_blocks = tie(summary, y_grad_blocks)
        y_grad_blocks = exchange(y_grad_blocks)
        loss, unit, score_grad, embed_grad, summary_grad, summary = head(
            summary, bundle, prototypes.shape[1]
        )
    else:
        summary = summary.reshape(all_crops, -1)
        loss, unit, score_grad, embed_grad, summary_grad = plain_head(
            summary, project_low, protos_low, queue_low, pairs
        )

    joined_grad, grad_sums3 = value_back(
        first_crop, x, expanded, sums3, norms, quad_blocks(y_grad_blocks), summary_grad, count
    )
    grad_sums3 = total(grad_sums3)
    expanded_grad = norm_backward(joined_grad, expanded, sums3, norms, 2, grad_sums3, count, False)
    expand_kept, expand_sent = weight_grad(gated, expanded_grad)
    if quick:
        expand_got = from_twin(expand_sent)
    gated_grad = mix_back(expanded_grad, expand_pieces)
    if quick:
        gated_grad, expand_got = tie(gated_grad, expand_got)
        expand_sums, expand_corner = scatter_corner(expand_kept, expand_got)
    act2_grad, grad_sums2, excite_grad, squeeze_grad = gate_back(
        gated_grad, grouped, sums2, norms, gates, squeezed, rest_pieces, count
    )
    small = jnp.concatenate([pooled, squeeze_act, squeeze_grad, excite_grad], 1)
    if quick:
        grad_sums2, expand_corner = tie(grad_sums2, expand_corner)
    grad_sums2 = total(grad_sums2)
    grad_sums2, y_blocks = tie(grad_sums2, y_blocks)
    y_blocks = exchange(out_blocks(y_blocks))
    if quick:
        expand_own, across, up = expand_sums
        across, up = corner_sums(across, up, expand_corner)
        across, up = scatter_sides(across, up)
    act1_grad, kernel_kept, kernel_sent, grad_sums1 = conv_back(
        act2_grad, grouped, sums2, grad_sums2, reduced, sums1, norms, windows, count
    )
    if quick:
        grad_sums1, across, up, kernel_kept, kernel_sent, y_blocks = tie(
            grad_sums1, across, up, kernel_kept, kernel_sent, y_blocks
        )
        expand_own, *expand_parts = side_sums(expand_own, across, up)
        expand_parts = scatter_mp(expand_own, expand_parts)
        kernel_sums, kernel_corner = scatter_corner(kernel_kept, from_twin(kernel_sent))
        kernel_own, across, up = kernel_sums
        kernel_across, kernel_up = corner_sums(across, up, kernel_corner)
        grad_sums1 = jnp.sum(spread(grad_sums1, "dp"), 0)
        grad_sums1, expand_parts, kernel_across, kernel_up = tie(
            grad_sums1, expand_parts, kernel_across, kernel_up
        )
        kernel_across, kernel_up = scatter_sides(kernel_across, kernel_up)
        grad_sums1 = jnp.sum(spread(grad_sums1, "mp"), 0)
    else:
        grad_sums1 = total(grad_sums1)
    reduced_grad = norm_backward(act1_grad, reduced, sums1, norms, 0, grad_sums1, count, True)
    if quick:
        reduced_grad, kernel_across, kernel_up, small = tie(
            reduced_grad, kernel_across, kernel_up, small
        )
        kernel_sum = side_sums(kernel_own, kernel_across, kernel_up)[0].astype(bf16)
        kernel_sum = kernel_sum + lax.ppermute(kernel_sum, "mp", flips("mp", 1))
    small = gather_all(small)
    reduce_kept, reduce_sent = weight_grad(x, reduced_grad)
    if quick:
        reduce_got = from_twin(reduce_sent)
        reduce_got, kernel_sum = tie(reduce_got, kernel_sum)
        kernel_sum = kernel_sum + lax.ppermute(kernel_sum, "mp", flips("mp", 2))
    x_grad = out_blocks(mix_back(reduced_grad, reduce_pieces, joined_grad))
    if quick:
        x_grad, reduce_got, kernel_sum, small = tie(x_grad, reduce_got, kernel_sum, small)
        (own, across, up), corner = scatter_corner(reduce_kept, reduce_got)
        x_grad = exchange(x_grad)
        across, up = corner_sums(across, up, corner)
        across, up, small, kernel_sum = tie(across, up, small, kernel_sum)
        across, up = scatter_sides(across, up)
        squeeze_part, excite_part, project_part, protos_part, small_squares = small_grads(
            small, summary, embed_grad, score_grad, unit, prototypes.shape[1]
        )
        expand_grad, expand_square = own_square(expand_parts)
        kernel_grad, kernel_square = own_kernel(kernel_sum)
        across, up, x_grad, small_squares, expand_square, kernel_square = tie(
            across, up, x_grad, small_squares, expand_square, kernel_square
        )
        own, *parts = side_sums(own, across, up)
        parts = scatter_mp(own, parts)
        input_grad = out_channels(x_grad, channels_here, f32)
        block_output = out_channels(y_blocks, channels_here, bf16)
        prepared = lars_prepare(
            [
                (w_group.T, kernel_grad, m_group.T),
                (w_squeeze, squeeze_part, m_squeeze),
                (w_excite, excite_part, m_excite),
                (w_expand.T, expand_grad, m_expand.T),
                (w_project.T, project_part, m_project.T),
                (prototypes.T, protos_part, m_protos.T),
            ]
        )
        parts, input_grad, block_output, *prepared = tie(
            parts, input_grad, block_output, *prepared
        )
        reduce_grad, reduce_square = own_square(parts)
        norm_squares = total(
            squares(
                n_dp, n_mp, weight_squares, norms, small_squares, reduce_square, expand_square,
                kernel_square, grad_sums1, grad_sums2, grad_sums3,
            )
        )
        mom_reduce, mom_group, mom_squeeze, mom_excite, mom_expand, mom_project, mom_protos = lars(
            norm_squares, w_reduce.T, reduce_grad, m_reduce.T, prepared
        )
        mom_gains, mom_biases = lars_norms(
            norm_squares, bn_gains, bn_biases, m_gains, m_biases, grad_sums1, grad_sums2, grad_sums3
        )
        stepped = [
            mom_reduce.T, mom_group.T, mom_squeeze, mom_excite, mom_expand.T, mom_project.T,
            mom_protos.T, mom_gains, mom_biases,
        ]
    else:
        input_grad = out_channels(exchange(x_grad), channels_here, f32)
        block_output = out_channels(y_blocks, channels_here, bf16)
        big_grads = (
            scatter_square(reduce_kept, reduce_sent),
            scatter_kernel(kernel_kept[:, 0], kernel_sent[:, 0]),
            scatter_square(expand_kept, expand_sent),
        )
        stepped, norm_squares = plain_finish(
            small, summary, unit, score_grad, embed_grad, (grad_sums1, grad_sums2, grad_sums3),
            channels_here, big_grads, weights, moments,
        )
    param_norms = jnp.sqrt(norm_squares[:, :13].T + EPS_NORM)
    return (block_output, loss[0, 0], input_grad, *stepped, param_norms)


def solution(mesh):
    split = P("dp", "mp")
    turned = P("mp", "dp")
    rows = P("dp", None)
    columns = P(None, "mp")
    return jax.shard_map(
        body,
        mesh=mesh,
        in_specs=(
            turned, turned, split, rows, columns, columns, split, columns, columns, columns, columns,
            split, rows, columns, columns, split, columns, columns, columns, columns, rows, rows, rows,
        ),
        out_specs=(
            turned, P(), turned, split, rows, columns, columns, split, columns, columns, columns,
            columns, P(),
        ),
        check_vma=False,
    )
```

```python
import functools

import jax
import jax.numpy as jnp
import numpy as np
from jax import lax
from jax.experimental import pallas as pl
from jax.experimental.pallas import tpu as pltpu
from jax.sharding import PartitionSpec as P

HW = 14
PIXELS = HW * HW
SINK = 3
EPS_BN = 1e-05
EPS_NORM = 1e-06
EPS_SINK = 0.05
SOFTMAX_TEMPER = 0.1
TRUST = 0.001
DECAY = 1e-06
MOMENTUM = 0.9

QUADS = 4
QUAD = 504
HALF = 252
LANES = 512
GAP = LANES - QUAD
GROUP = 56
SE_PART = 63
SE_LANES = 64
PITCH = 16
VMEM_BYTES = 60 * 1024 * 1024
f32 = jnp.float32
bf16 = jnp.bfloat16
NN = (((1,), (0,)), ((), ()))
NT = (((1,), (1,)), ((), ()))
TN = (((0,), (0,)), ((), ()))


def dot(a, b, dims=NN):
    return lax.dot_general(a, b, dims, preferred_element_type=f32)


def widen(v, axis):
    first = lax.slice_in_dim(v, 0, HALF, axis=axis)
    last = lax.slice_in_dim(v, HALF, QUAD, axis=axis)
    shape = list(v.shape)
    shape[axis] = GAP
    return jnp.concatenate([first, jnp.zeros(shape, v.dtype), last], axis)


def narrow(v, axis):
    first = lax.slice_in_dim(v, 0, HALF, axis=axis)
    last = lax.slice_in_dim(v, HALF + GAP, LANES, axis=axis)
    return jnp.concatenate([first, last], axis)


def spread_channels(v):
    lead = v.shape[:-1]
    return widen(v.reshape(lead + (QUADS, QUAD)), len(lead) + 1).reshape(lead + (QUADS * LANES,))


def pack_channels(v):
    lead = v.shape[:-1]
    return narrow(v.reshape(lead + (QUADS, LANES)), len(lead) + 1).reshape(lead + (QUADS * QUAD,))


def half_rows(v, position):
    pad = 256 - HALF
    padded = jnp.pad(v, ((pad, pad),) + ((0, 0),) * (v.ndim - 1))
    return lax.dynamic_slice_in_dim(padded, pad * (1 - position % 2), 256, 0)


def unhalf_rows(v, position):
    return lax.dynamic_slice_in_dim(v, (256 - HALF) * (position % 2), HALF, 0)


def spread_inner(v):
    lead = v.shape[:-1]
    parts = v.shape[-1] // SE_PART
    v = v.reshape(lead + (parts, SE_PART))
    v = jnp.pad(v, ((0, 0),) * (v.ndim - 1) + ((0, SE_LANES - SE_PART),))
    return v.reshape(lead + (parts * SE_LANES,))


def pack_inner(v):
    lead = v.shape[:-1]
    parts = v.shape[-1] // SE_LANES
    return v.reshape(lead + (parts, SE_LANES))[..., :SE_PART].reshape(lead + (parts * SE_PART,))


def flips(axis, bit):
    return [(i, i ^ bit) for i in range(lax.axis_size(axis))]


def spread(v, axis):
    n = lax.axis_size(axis)
    return lax.all_to_all(
        jnp.broadcast_to(v[None], (n,) + v.shape), axis, split_axis=0, concat_axis=0, tiled=True
    )


def sum_axis(v, axis):
    n = lax.axis_size(axis)
    bit = 1
    while bit < n:
        v = v + lax.ppermute(v, axis, flips(axis, bit))
        bit *= 2
    return v


def total(v):
    return jnp.sum(spread(jnp.sum(spread(v, "dp"), 0), "mp"), 0)


def tie(*values):
    return lax.optimization_barrier(values)


def gather_all(v):
    n = lax.axis_size("dp") * lax.axis_size("mp")
    out = lax.all_to_all(
        jnp.broadcast_to(v[None], (n,) + v.shape),
        ("dp", "mp"),
        split_axis=0,
        concat_axis=0,
        tiled=True,
    )
    return out


def in_order(parts, me):
    out = []
    for j in range(len(parts)):
        v = parts[0]
        for k in range(1, len(parts)):
            v = jnp.where((me ^ k) == j, parts[k], v)
        out.append(v)
    return jnp.stack(out)


def exchange(blocks):
    return lax.all_to_all(blocks, "mp", split_axis=0, concat_axis=0, tiled=True)


def parts_mp(v):
    return [v] + [lax.ppermute(v, "mp", flips("mp", k)) for k in range(1, lax.axis_size("mp"))]


def gather_mp(v):
    return in_order(parts_mp(v), lax.axis_index("mp"))


def diagonal(axis_size):
    return [(i, i ^ 4 if i % 2 == 0 else i ^ 2) for i in range(axis_size)]


def gather_sides(v):
    return lax.ppermute(v, "dp", flips("dp", 2)), lax.ppermute(v, "dp", flips("dp", 4))


def gather_corner(across, up):
    even = lax.axis_index("dp") % 2 == 0
    return lax.ppermute(jnp.where(even, across, up), "dp", diagonal(8))


def gather_twins(own, across, up, corner):
    pieces = []
    for got in (own, across, up, corner):
        pieces += [got, lax.ppermute(got, "dp", flips("dp", 1))]
    return pieces


def gather_dp(v):
    across, up = gather_sides(v)
    return gather_twins(v, across, up, gather_corner(across, up))


def scatter_corner(kept, got):
    return lax.ppermute(twin_sum(kept, got), "dp", diagonal(8))


def from_twin(sent):
    return lax.ppermute(sent, "dp", flips("dp", 1))


def scatter_sides(across, up):
    return lax.ppermute(across, "dp", flips("dp", 2)), lax.ppermute(up, "dp", flips("dp", 4))


def scatter_mp(own, parts):
    return [own] + [lax.ppermute(v, "mp", flips("mp", k + 1)) for k, v in enumerate(parts)]


def quick_mesh():
    return lax.axis_size("dp") == 2 * QUADS and lax.axis_size("mp") == QUADS


def slab_blocks(v):
    n = lax.axis_size("mp")
    blocks = v.T.reshape(n, v.shape[1] // n, v.shape[0])
    return widen(blocks, 2) if quick_mesh() else blocks


def quad_blocks(blocks):
    if quick_mesh():
        return blocks
    rows = blocks.shape[1]
    full = spread_channels(blocks.transpose(1, 0, 2).reshape(rows, -1))
    return full.reshape(rows, QUADS, LANES).transpose(1, 0, 2)


def out_blocks(blocks):
    if quick_mesh():
        return blocks
    n = lax.axis_size("mp")
    rows = blocks.shape[1]
    full = pack_channels(blocks.transpose(1, 0, 2).reshape(rows, -1))
    return full.reshape(rows, n, -1).transpose(1, 0, 2)


def natural_channels(blocks, channels, dtype):
    return blocks.astype(dtype).reshape(-1, channels).T


def out_channels(parts, channels, dtype, me):
    return natural_channels(join_rows(parts, dtype, me), channels, dtype)


def shard_square(w):
    return half_rows(widen(w.astype(bf16), 1), lax.axis_index("dp")).T


def gather_square(w):
    full = lax.all_gather(w.astype(bf16), "mp", axis=1, tiled=True)
    full = lax.all_gather(full, "dp", axis=0, tiled=True)
    full = spread_channels(spread_channels(full).T)
    return full.reshape(QUADS, LANES, 2 * QUADS, 256).transpose(2, 0, 1, 3)


def scatter_square(kept, sent):
    g = jnp.stack([kept, sent], 1).reshape((8,) + kept.shape[1:])
    full = g.transpose(1, 2, 0, 3).reshape(QUADS * LANES, 2 * QUADS * 256)
    full = pack_channels(pack_channels(full).T)
    part = lax.psum_scatter(full, "dp", scatter_dimension=0, tiled=True)
    return lax.psum_scatter(part, "mp", scatter_dimension=1, tiled=True).astype(f32)


def gather_kernel(w):
    low = w.astype(bf16)
    if quick_mesh():
        return gather_dp(half_rows(low, lax.axis_index("dp")).T)
    full = lax.all_gather(low, "dp", axis=0, tiled=True)
    return spread_channels(full.T).reshape(-1, 2 * QUADS, 256).transpose(1, 0, 2)


def scatter_kernel(kept, sent):
    g = jnp.stack([kept, sent], 1).reshape((8,) + kept.shape[1:])
    full = pack_channels(g.transpose(1, 0, 2).reshape(g.shape[1], -1)).T
    part = lax.psum_scatter(full, "dp", scatter_dimension=0, tiled=True).astype(f32)
    return lax.psum(part, "mp")


SE_ROWS = 256
HEAD_ROWS = 208
PROTO_ROWS = 96
QUEUE_ROWS = 32


def shard_excitation(w_squeeze, w_excite):
    d = lax.axis_index("dp")
    squeeze = lax.dynamic_slice_in_dim(w_squeeze, d * HALF, HALF, 0).astype(bf16)
    squeeze = spread_inner(half_rows(squeeze, d))
    excite = lax.dynamic_slice_in_dim(w_excite, d * SE_PART, SE_PART, 0).astype(bf16)
    excite = jnp.pad(widen(excite, 1), ((0, SE_LANES - SE_PART), (0, 0)))
    excite = jnp.concatenate([excite[:, 128 * i : 128 * (i + 1)] for i in range(4)], 0)
    return jnp.concatenate([squeeze, excite], 1)


def shard_head(w_project, prototypes, queue_rows, pairing):
    d = lax.axis_index("dp")
    m = lax.axis_index("mp")
    project = lax.dynamic_slice_in_dim(w_project, d * HALF, HALF, 0).astype(bf16)
    project = half_rows(project, d).T
    protos = jnp.pad(prototypes.T, ((0, 2 * QUADS * PROTO_ROWS - prototypes.shape[1]), (0, 0)))
    protos = lax.dynamic_slice_in_dim(protos, d * PROTO_ROWS, PROTO_ROWS, 0).astype(bf16)
    queue = lax.dynamic_slice_in_dim(queue_rows, m * QUEUE_ROWS, QUEUE_ROWS, 0)
    size = pairing.shape[0]
    lane = lax.broadcasted_iota(jnp.int32, (size, 256), 1)
    pairing = jnp.where(lane // size == d, jnp.tile(pairing, (1, 256 // size)), 0.0)
    pairing = jnp.pad(pairing.astype(bf16), ((0, 16 - size), (0, 0)))
    return jnp.concatenate([project, protos, queue, pairing], 0)


def gather_excitation(w_squeeze, w_excite):
    squeeze = lax.all_gather(w_squeeze.astype(bf16), "mp", axis=1, tiled=True)
    excite = lax.all_gather(w_excite.astype(bf16), "mp", axis=1, tiled=True)
    squeeze = spread_channels(spread_inner(squeeze).T).T
    excite = spread_inner(spread_channels(excite).T).T
    squeeze = squeeze.reshape(8, 256, 4, 128).transpose(0, 2, 1, 3)
    excite = excite.reshape(8, 64, 4, 4, 128).transpose(0, 2, 3, 1, 4).reshape(8, 4, 256, 128)
    return jnp.concatenate([squeeze, excite], 3)


def gather_head(w_project, prototypes, queue_rows, pairing):
    project = lax.all_gather(w_project.astype(bf16), "mp", axis=1, tiled=True)
    protos = lax.all_gather(prototypes.astype(bf16), "mp", axis=1, tiled=True)
    queue = lax.all_gather(queue_rows, "dp", axis=0, tiled=True)
    pairs = lax.all_gather(pairing, "dp")
    return spread_channels(project.T).T, protos, queue, pairs


def block_diagonal(pairs):
    images, size = pairs.shape[:2]
    return (
        jnp.eye(images, dtype=f32)[:, None, :, None] * pairs.astype(f32)[:, :, None, :]
    ).reshape(images * size, images * size)


BRIEF = pl.CostEstimate(flops=1, bytes_accessed=1, transcendentals=0)


def params(*semantics):
    return pltpu.CompilerParams(vmem_limit_bytes=VMEM_BYTES)


def column_sums(stats_ref, a, b):
    stats_ref[0:1, :] = jnp.sum(a, 0, keepdims=True)
    stats_ref[1:2, :] = jnp.sum(b, 0, keepdims=True)


def index_scalar(axis):
    quick = quick_mesh()
    return (lax.axis_index(axis) if quick else jnp.zeros((), jnp.int32)).astype(jnp.int32)[None]


SCALAR = pl.BlockSpec(memory_space=pltpu.SMEM)


def half_block(index):
    return pl.ds(pl.multiple_of(index * 256, 256), 256)


def join_rows_kernel(me_ref, *refs):
    out_ref = refs[-1]
    for k, part in enumerate(refs[:-1]):
        v = part[...].astype(f32)
        v = jnp.concatenate([v[:, :HALF], v[:, HALF + GAP :]], 1)
        out_ref[me_ref[0] ^ k] = v.astype(out_ref.dtype)


def join_rows(parts, dtype, me):
    rows = parts[0].shape[0]
    return pl.pallas_call(
        join_rows_kernel,
        in_specs=[SCALAR] + [pl.BlockSpec(memory_space=pltpu.VMEM)] * len(parts),
        out_shape=jax.ShapeDtypeStruct((len(parts), rows, QUAD), dtype),
        compiler_params=params(),
        cost_estimate=BRIEF,
        name="join_rows",
    )(me, *parts)


def piece_list(w):
    return w if isinstance(w, list) else [w[b].reshape(-1, 256) for b in range(8)]


def half_of(ref, index):
    return ref[index // 2, :, half_block(index % 2)]


def mix_kernel(me_ref, x_ref, *refs):
    out_ref, stats_ref = refs[8:]
    turned = jnp.concatenate([half_of(x_ref, me_ref[0] ^ b) for b in range(8)], 1)
    acc = dot(turned, jnp.concatenate([refs[b][...] for b in range(8)], 1), NT)
    out_ref[...] = acc
    column_sums(stats_ref, acc, acc * acc)


def mix(x, w):
    _, rows, _ = x.shape
    width = QUADS * LANES
    return pl.pallas_call(
        mix_kernel,
        grid=(QUADS,),
        in_specs=[SCALAR, pl.BlockSpec(x.shape, lambda m: (0, 0, 0))]
        + [pl.BlockSpec((LANES, 256), lambda m: (m, 0))] * 8,
        out_specs=[
            pl.BlockSpec((rows, LANES), lambda m: (0, m)),
            pl.BlockSpec((2, LANES), lambda m: (0, m)),
        ],
        out_shape=[
            jax.ShapeDtypeStruct((rows, width), f32),
            jax.ShapeDtypeStruct((2, width), f32),
        ],
        compiler_params=params(),
        cost_estimate=BRIEF,
        name="mix",
    )(index_scalar("dp"), x, *piece_list(w))


def mix_back_kernel(rest, me_ref, g_ref, *refs):
    out_ref, hold_ref, sems = refs[8 + rest :]

    def copy(b):
        source = refs[b].at[pl.ds(0, QUADS * LANES)]
        return pltpu.make_async_copy(source, hold_ref.at[b], sems.at[b])

    for b in range(8):
        copy(b).start()
    for b in range(0, 8, 2):
        copy(b).wait()
        copy(b + 1).wait()
        pair = dot(g_ref[...], jnp.concatenate([hold_ref[b], hold_ref[b + 1]], 1))
        for i in range(2):
            index = me_ref[0] ^ (b + i)
            acc = pair[:, 256 * i : 256 * (i + 1)]
            if rest:
                acc = acc + refs[8][:, half_block(index)]
                out_ref[index // 2, :, half_block(index % 2)] = acc.astype(bf16)
            else:
                out_ref[:, half_block(index)] = acc


def mix_back(g, w, rest=None):
    rows, width = g.shape
    if rest is None:
        more, out = [], jax.ShapeDtypeStruct((rows, width), f32)
    else:
        more, out = [rest], jax.ShapeDtypeStruct((QUADS, rows, LANES), bf16)
    return pl.pallas_call(
        functools.partial(mix_back_kernel, len(more)),
        in_specs=[SCALAR, pl.BlockSpec(memory_space=pltpu.VMEM)]
        + [pl.BlockSpec(memory_space=pl.ANY)] * 8
        + [pl.BlockSpec(memory_space=pltpu.VMEM)] * len(more),
        out_specs=pl.BlockSpec(memory_space=pltpu.VMEM),
        out_shape=out,
        scratch_shapes=[
            pltpu.VMEM((8, QUADS * LANES, 256), bf16),
            pltpu.SemaphoreType.DMA((8,)),
        ],
        compiler_params=params(),
        cost_estimate=BRIEF,
        name="mix_back",
    )(index_scalar("dp"), g, *piece_list(w), *more)


def piece_grads(me_ref, x_ref, g, odd, out_ref):
    wanted = jnp.concatenate([half_of(x_ref, me_ref[0] ^ (2 * i + odd)) for i in range(4)], 1)
    result = dot(g.T, wanted)
    for i in range(4):
        out_ref[i, 0] = result[:, 256 * i : 256 * (i + 1)].astype(bf16)


def sent_grads_kernel(
    k, sloped, count, me_ref, x_ref, g_ref, a_ref, sums_ref, norms_ref, grad_sums_ref, grad_ref, out_ref
):
    grad, values = g_ref[...].astype(f32), a_ref[...]
    if sloped:
        _, _, scale, shift = affine(sums_ref[...], norms_ref[...], k, count)
        grad = grad * swish_slope(values * scale + shift)
    grad = norm_back(
        grad, values, sums_ref[...], norms_ref[...], k, grad_sums_ref[...], count
    ).astype(bf16)
    grad_ref[...] = grad
    piece_grads(me_ref, x_ref, grad, 1, out_ref)


PIECES = jax.ShapeDtypeStruct((4, QUADS, LANES, 256), bf16)


def pieces_spec():
    return pl.BlockSpec((4, 1, LANES, 256), lambda m: (0, m, 0, 0))


def sent_grads(x, g, a, sums, norms, k, grad_sums, count, sloped):
    rows, width = a.shape
    return pl.pallas_call(
        functools.partial(sent_grads_kernel, k, sloped, count),
        grid=(QUADS,),
        in_specs=[
            SCALAR, pl.BlockSpec(x.shape, lambda m: (0, 0, 0)), quad_spec(rows), quad_spec(rows),
            quad_spec(2), quad_spec(6), quad_spec(2),
        ],
        out_specs=[quad_spec(rows), pieces_spec()],
        out_shape=[jax.ShapeDtypeStruct((rows, width), bf16), PIECES],
        compiler_params=params(),
        cost_estimate=BRIEF,
        name="sent_grads",
    )(index_scalar("dp"), x, g, a, sums, norms, grad_sums)


def kept_grads_kernel(me_ref, x_ref, g_ref, out_ref):
    piece_grads(me_ref, x_ref, g_ref[...], 0, out_ref)


def kept_grads(x, g):
    rows, width = g.shape
    return pl.pallas_call(
        kept_grads_kernel,
        grid=(QUADS,),
        in_specs=[SCALAR, pl.BlockSpec(x.shape, lambda m: (0, 0, 0)), quad_spec(rows)],
        out_specs=pieces_spec(),
        out_shape=PIECES,
        compiler_params=params(),
        cost_estimate=BRIEF,
        name="kept_grads",
    )(index_scalar("dp"), x, g)


def entry_spec(shape, i, steps):
    return pl.BlockSpec((None, shape[1] // steps) + shape[2:], lambda m, i=i: (i, m, 0, 0))


def twin_sum_kernel(a_ref, b_ref, out_ref):
    out_ref[...] = (a_ref[...].astype(f32) + b_ref[...].astype(f32)).astype(bf16)


def twin_sum(kept, got):
    shape = kept.shape
    steps = min(2, shape[1])
    return pl.pallas_call(
        twin_sum_kernel,
        grid=(steps,),
        in_specs=[entry_spec(shape, 3, steps)] * 2,
        out_specs=pl.BlockSpec((shape[1] // steps,) + shape[2:], lambda m: (m, 0, 0)),
        out_shape=jax.ShapeDtypeStruct(shape[1:], bf16),
        compiler_params=params(),
        cost_estimate=BRIEF,
        name="twin_sum",
    )(kept, got)


def corner_sums_kernel(me_ref, a1_ref, b1_ref, a2_ref, b2_ref, corner_ref, across_ref, up_ref):
    even = me_ref[0] % 2 == 0
    corner = corner_ref[...].astype(f32)
    across = a1_ref[...].astype(f32) + b1_ref[...].astype(f32)
    across_ref[...] = (across + jnp.where(even, corner, 0.0)).astype(bf16)
    up = a2_ref[...].astype(f32) + b2_ref[...].astype(f32)
    up_ref[...] = (up + jnp.where(even, 0.0, corner)).astype(bf16)


def corner_sums(kept, got, corner):
    shape = kept.shape
    steps = min(2, shape[1])
    block = pl.BlockSpec((shape[1] // steps,) + shape[2:], lambda m: (m, 0, 0))
    return pl.pallas_call(
        corner_sums_kernel,
        grid=(steps,),
        in_specs=[SCALAR] + [entry_spec(shape, i, steps) for i in (1, 1, 2, 2)] + [block],
        out_specs=[block, block],
        out_shape=[jax.ShapeDtypeStruct(shape[1:], bf16)] * 2,
        compiler_params=params(),
        cost_estimate=BRIEF,
        name="corner_sums",
    )(index_scalar("dp"), kept, got, kept, got, corner)


def side_sums_kernel(me_ref, a_ref, b_ref, across_ref, up_ref, out_ref, *parts):
    value = (
        a_ref[...].astype(f32)
        + b_ref[...].astype(f32)
        + across_ref[...].astype(f32)
        + up_ref[...].astype(f32)
    )

    @pl.when(pl.program_id(0) == 0)
    def _():
        out_ref[...] = value

    for k, part in enumerate(parts):

        @pl.when(pl.program_id(0) == k + 1)
        def _(part=part):
            part[...] = value.astype(bf16)


def side_sums(kept, got, across, up):
    _, n, *shape = kept.shape
    me = index_scalar("mp") if n > 1 else jnp.zeros((1,), jnp.int32)
    entry = pl.BlockSpec((None, None, *shape), lambda k, me: (0, me[0] ^ k, 0, 0))
    block = pl.BlockSpec((None, *shape), lambda k, me: (me[0] ^ k, 0, 0))
    spec = pltpu.PrefetchScalarGridSpec(
        num_scalar_prefetch=1,
        grid=(n,),
        in_specs=[entry, entry, block, block],
        out_specs=[pl.BlockSpec(tuple(shape), lambda k, me: (0, 0))] * n,
    )
    return pl.pallas_call(
        side_sums_kernel,
        grid_spec=spec,
        out_shape=[jax.ShapeDtypeStruct(shape, f32)] + [jax.ShapeDtypeStruct(shape, bf16)] * (n - 1),
        compiler_params=params(),
        cost_estimate=BRIEF,
        name="side_sums",
    )(me, kept, got, across, up)


def own_square_kernel(me_ref, own_ref, *refs):
    out_ref, square_ref = refs[-2:]
    value = own_ref[...]
    for part in refs[:-2]:
        value = value + part[...].astype(f32)
    row = lax.broadcasted_iota(jnp.int32, (QUAD, 1), 0)
    value = jnp.where(row < HALF, value[:QUAD], value[GAP:])
    value = jnp.where(me_ref[0] % 2 == 1, value[:, 256 - HALF :], value[:, :HALF])
    out_ref[...] = value
    square_ref[...] = jnp.sum(jnp.sum(value * value, 1, keepdims=True), 0, keepdims=True)


def own_square(parts):
    return pl.pallas_call(
        own_square_kernel,
        in_specs=[SCALAR] + [pl.BlockSpec(memory_space=pltpu.VMEM)] * len(parts),
        out_shape=[
            jax.ShapeDtypeStruct((QUAD, HALF), f32), jax.ShapeDtypeStruct((1, 1), f32),
        ],
        compiler_params=params(),
        cost_estimate=BRIEF,
        name="own_square",
    )(index_scalar("dp"), *parts)


def affine(sums, norms, k, count):
    mean = sums[0:1] / count
    inverse = lax.rsqrt(sums[1:2] / count - mean * mean + EPS_BN)
    scale = inverse * norms[k : k + 1]
    return mean, inverse, scale, norms[3 + k : 4 + k] - mean * scale


def quad_spec(rows):
    return pl.BlockSpec((rows, LANES), lambda q: (0, q))


def block_spec(rows):
    return pl.BlockSpec((None, rows, LANES), lambda q: (q, 0, 0))


def crop_totals(ref, crops):
    return jnp.concatenate(
        [jnp.sum(ref[pl.ds(PIXELS * c, PIXELS), :], 0, keepdims=True) for c in range(crops)], 0
    )


def turned_quad(rows):
    return pl.BlockSpec((rows, LANES), lambda k, me, *_: (0, me[0] ^ k))


def turned_block(rows):
    return pl.BlockSpec((None, rows, LANES), lambda k, me, *_: (me[0] ^ k, 0, 0))


def whole_part(rows):
    return pl.BlockSpec((rows, LANES), lambda k, *_: (0, 0))


def value_kernel(crops, count, me_ref, x_ref, a_ref, sums_ref, norms_ref, *refs):
    parts, summary_ref, work_ref = refs[:-2], refs[-2], refs[-1]
    _, _, scale, shift = affine(sums_ref[...], norms_ref[...], 2, count)
    work_ref[...] = swish(x_ref[...].astype(f32) + a_ref[...] * scale + shift)
    for k, part in enumerate(parts):

        @pl.when(pl.program_id(0) == k)
        def _(part=part):
            part[...] = work_ref[...].astype(bf16)

    summary_ref[...] = (crop_totals(work_ref, crops) / PIXELS).astype(bf16)


def block_value(x, a, sums, norms, count):
    rows, width = a.shape
    crops = rows // PIXELS
    spec = pltpu.PrefetchScalarGridSpec(
        num_scalar_prefetch=1,
        grid=(QUADS,),
        in_specs=[turned_block(rows), turned_quad(rows), turned_quad(2), turned_quad(6)],
        out_specs=[whole_part(rows)] * QUADS + [turned_quad(crops)],
        scratch_shapes=[pltpu.VMEM((rows, LANES), f32)],
    )
    return pl.pallas_call(
        functools.partial(value_kernel, crops, count),
        grid_spec=spec,
        out_shape=[jax.ShapeDtypeStruct((rows, LANES), bf16)] * QUADS
        + [jax.ShapeDtypeStruct((crops, width), bf16)],
        compiler_params=params(),
        cost_estimate=BRIEF,
        name="value",
    )(index_scalar("mp"), x, a, sums, norms)


def value_back_kernel(
    crops, count, me_ref, first_ref, x_ref, a_ref, sums_ref, norms_ref, do_ref, *refs
):
    parts, (out_ref, stats_ref, work_ref) = refs[:-3], refs[-3:]
    for k, part in enumerate(parts):

        @pl.when(pl.program_id(0) == k)
        def _(part=part):
            work_ref[...] = part[...].astype(f32)

    mean, inverse, scale, shift = affine(sums_ref[...], norms_ref[...], 2, count)
    values = a_ref[...]
    row = lax.broadcasted_iota(jnp.int32, (do_ref.shape[0], 1), 0)
    own = jnp.concatenate(
        [
            jnp.sum(jnp.where(row == first_ref[0] + c, do_ref[...], 0.0), 0, keepdims=True)
            for c in range(crops)
        ],
        0,
    )
    slope = swish_slope(x_ref[...].astype(f32) + values * scale + shift)
    grad = (work_ref[...] + rows_of_crops(own / PIXELS, values.shape[0])) * slope
    out_ref[...] = grad
    column_sums(stats_ref, grad, grad * ((values - mean) * inverse))


def value_back(first, x, a, sums, norms, dy_parts, do, count):
    rows, width = a.shape
    spec = pltpu.PrefetchScalarGridSpec(
        num_scalar_prefetch=2,
        grid=(QUADS,),
        in_specs=[
            turned_block(rows), turned_quad(rows), turned_quad(2), turned_quad(6),
            turned_quad(do.shape[0]),
        ]
        + [whole_part(rows)] * QUADS,
        out_specs=[turned_quad(rows), turned_quad(2)],
        scratch_shapes=[pltpu.VMEM((rows, LANES), f32)],
    )
    return pl.pallas_call(
        functools.partial(value_back_kernel, rows // PIXELS, count),
        grid_spec=spec,
        out_shape=[
            jax.ShapeDtypeStruct((rows, width), f32), jax.ShapeDtypeStruct((2, width), f32),
        ],
        compiler_params=params(),
        cost_estimate=BRIEF,
        name="value_back",
    )(index_scalar("mp"), first, x, a, sums, norms, do, *dy_parts)


def norm_back(grad, values, sums, norms, k, grad_sums, count):
    mean, inverse, scale, _ = affine(sums, norms, k, count)
    centred = (values - mean) * inverse
    return scale * (grad - (grad_sums[0:1] + centred * grad_sums[1:2]) / count)


def lane_mask(low, high, rows=GROUP):
    lane = lax.broadcasted_iota(jnp.int32, (rows, 256), 1)
    return (lane >= low) & (lane < high)


def dense_kernel(me_ref, *refs):
    out_ref, hold_ref = refs[8:]

    @pl.when(pl.program_id(0) == 0)
    def _():
        for b in range(8):
            hold_ref[me_ref[0] ^ b] = refs[b][...]

    even = hold_ref[2 * pl.program_id(0)].astype(f32)
    odd = hold_ref[2 * pl.program_id(0) + 1].astype(f32)
    row = lax.broadcasted_iota(jnp.int32, (256, 256), 0)
    edge = jnp.zeros((32, 256), f32)
    centre = lane_mask(96, 124) | lane_mask(132, 160)
    for tap in range(9):
        e = even[GROUP * tap : GROUP * (tap + 1)]
        o = odd[GROUP * tap : GROUP * (tap + 1)]
        first = [jnp.where(lane_mask(GROUP * g, GROUP * (g + 1)), e, 0.0) for g in range(4)]
        last = [
            jnp.where(lane_mask(32 + GROUP * g, 32 + GROUP * (g + 1)), o, 0.0) for g in range(4)
        ]
        out_ref[0, 0, tap] = jnp.concatenate(first + [edge], 0).astype(bf16)
        out_ref[0, 1, tap] = jnp.concatenate([edge] + last, 0).astype(bf16)
        across = jnp.where(centre, jnp.concatenate([e[:, 128:], o[:, :128]], 1), 0.0)
        upper = jnp.concatenate(
            [jnp.zeros((96, 256), f32), across, jnp.zeros((104, 256), f32)], 0
        )
        lower = jnp.concatenate(
            [jnp.zeros((104, 256), f32), across, jnp.zeros((96, 256), f32)], 0
        )
        out_ref[0, 2, tap] = (
            jnp.where(row < 124, upper, 0.0) + jnp.where(row >= 132, lower, 0.0)
        ).astype(bf16)


def dense_windows(kernel):
    pieces = [kernel[b] for b in range(8)]
    return pl.pallas_call(
        dense_kernel,
        grid=(QUADS,),
        in_specs=[SCALAR] + [pl.BlockSpec(memory_space=pltpu.VMEM)] * 8,
        out_specs=pl.BlockSpec((1, 3, 9, 256, 256), lambda q: (q, 0, 0, 0, 0)),
        out_shape=jax.ShapeDtypeStruct((QUADS, 3, 9, 256, 256), bf16),
        scratch_shapes=[pltpu.VMEM((8,) + pieces[0].shape, bf16)],
        compiler_params=params(),
        cost_estimate=BRIEF,
        name="dense_windows",
    )(index_scalar("dp"), *pieces)


WINDOWS = (0, 256, 128)


def place_pixels(pad_ref, moved_ref, source_ref, crops):
    for crop in range(crops):
        for row in range(HW):
            pad_ref[pl.ds(PITCH + 256 * crop + PITCH * (row + 1), HW), :] = source_ref[
                pl.ds(PIXELS * crop + HW * row, HW), :
            ]
    for shift in range(3):
        moved_ref[shift] = pad_ref[pl.ds(PITCH - 1 + shift, 256 * crops), :].astype(bf16)


def tap_rows(moved_ref, dy, dx, low, crops):
    return jnp.concatenate(
        [
            moved_ref[dx, pl.ds(256 * crop + PITCH * dy, PITCH * HW), pl.ds(low, 256)]
            for crop in range(crops)
        ],
        0,
    )


def take_pixels(target_ref, source_ref, crops):
    for crop in range(crops):
        for row in range(HW):
            target_ref[pl.ds(PIXELS * crop + HW * row, HW), :] = source_ref[
                pl.ds(PITCH * HW * crop + PITCH * row, HW), :
            ]


def swish(v):
    return v / (1.0 + jnp.exp(-v))


def swish_slope(v):
    sigma = 1.0 / (1.0 + jnp.exp(-v))
    return sigma * (1.0 + v * (1.0 - sigma))


def conv_kernel(crops, count, a_ref, sums_ref, norms_ref, w_ref, out_ref, stats_ref, pad_ref, moved_ref, wide_ref, act_ref):
    @pl.when(pl.program_id(0) == 0)
    def _():
        pad_ref[...] = jnp.zeros_like(pad_ref)

    _, _, scale, shift = affine(sums_ref[...], norms_ref[...], 0, count)
    act = swish(a_ref[...] * scale + shift)
    act_ref[...] = act.astype(bf16).astype(f32)
    place_pixels(pad_ref, moved_ref, act_ref, crops)
    for window, low in enumerate(WINDOWS):
        taps = [tap_rows(moved_ref, tap // 3, tap % 3, low, crops) for tap in range(9)]
        acc = dot(jnp.concatenate(taps, 1), w_ref[0, window].reshape(9 * 256, 256))
        if window < 2:
            wide_ref[:, pl.ds(low, 256)] = acc
        else:
            wide_ref[:, pl.ds(low, 256)] += acc
    take_pixels(act_ref, wide_ref, crops)
    result = act_ref[...].astype(bf16)
    out_ref[...] = result
    result = result.astype(f32)
    column_sums(stats_ref, result, result * result)


def conv(a, sums, norms, windows, count):
    rows, width = a.shape
    crops = rows // PIXELS
    return pl.pallas_call(
        functools.partial(conv_kernel, crops, count),
        grid=(QUADS,),
        in_specs=[
            quad_spec(rows), quad_spec(2), quad_spec(6),
            pl.BlockSpec((1, 3, 9, 256, 256), lambda q: (q, 0, 0, 0, 0)),
        ],
        out_specs=[
            pl.BlockSpec((rows, LANES), lambda q: (0, q)),
            pl.BlockSpec((2, LANES), lambda q: (0, q)),
        ],
        out_shape=[
            jax.ShapeDtypeStruct((rows, width), bf16),
            jax.ShapeDtypeStruct((2, width), f32),
        ],
        scratch_shapes=[
            pltpu.VMEM((2 * PITCH + 256 * crops, LANES), f32),
            pltpu.VMEM((3, 256 * crops, LANES), bf16),
            pltpu.VMEM((PITCH * HW * crops, LANES), f32),
            pltpu.VMEM((rows, LANES), f32),
        ],
        compiler_params=params(),
        cost_estimate=BRIEF,
        name="conv",
    )(a, sums, norms, windows)


def conv_back_kernel(
    crops, count, me_ref, g_ref, a2_ref, sums2_ref, grad_sums_ref, a_ref, sums_ref, norms_ref, w_ref,
    out_ref, kept_ref, sent_ref, stats_ref,
    pad_ref, moved_ref, pad_x_ref, moved_x_ref, wide_ref, act_ref, hold_ref,
):
    @pl.when(pl.program_id(0) == 0)
    def _():
        pad_ref[...] = jnp.zeros_like(pad_ref)
        pad_x_ref[...] = jnp.zeros_like(pad_x_ref)

    norms = norms_ref[...]
    grad = norm_back(
        g_ref[...], a2_ref[...].astype(f32), sums2_ref[...], norms, 1, grad_sums_ref[...], count
    )
    act_ref[...] = grad.astype(bf16).astype(f32)
    place_pixels(pad_ref, moved_ref, act_ref, crops)
    values = a_ref[...]
    mean, inverse, scale, shift = affine(sums_ref[...], norms, 0, count)
    normed = values * scale + shift
    act_ref[...] = swish(normed).astype(bf16).astype(f32)
    place_pixels(pad_x_ref, moved_x_ref, act_ref, crops)
    for window, low in enumerate(WINDOWS):
        taps = [tap_rows(moved_ref, 2 - tap // 3, 2 - tap % 3, low, crops) for tap in range(9)]
        weight = jnp.concatenate([w_ref[0, window, tap] for tap in range(9)], 1)
        acc = dot(jnp.concatenate(taps, 1), weight, NT)
        if window < 2:
            wide_ref[:, pl.ds(low, 256)] = acc
        else:
            wide_ref[:, pl.ds(low, 256)] += acc
    take_pixels(act_ref, wide_ref, crops)
    result = act_ref[...].astype(bf16)
    out_ref[...] = result
    grad = result.astype(f32) * swish_slope(normed)
    column_sums(stats_ref, grad, grad * ((values - mean) * inverse))
    centre = lane_mask(96, 124) | lane_mask(132, 160)
    row = lax.broadcasted_iota(jnp.int32, (GROUP, 256), 0)
    mids = [
        tap_rows(moved_ref, 1, 1, low, crops) for low in WINDOWS
    ]
    for tap in range(9):
        pieces = []
        for window, low in enumerate(WINDOWS):
            pieces.append(
                dot(tap_rows(moved_x_ref, tap // 3, tap % 3, low, crops), mids[window], TN)
            )
        even = sum(
            jnp.where(lane_mask(GROUP * g, GROUP * (g + 1)), pieces[0][GROUP * g : GROUP * (g + 1)], 0.0)
            for g in range(4)
        )
        odd = sum(
            jnp.where(
                lane_mask(32 + GROUP * g, 32 + GROUP * (g + 1)),
                pieces[1][32 + GROUP * g : 32 + GROUP * (g + 1)],
                0.0,
            )
            for g in range(4)
        )
        across = jnp.where(
            centre, jnp.where(row < GROUP // 2, pieces[2][96:152], pieces[2][104:160]), 0.0
        )
        nothing = jnp.zeros((GROUP, 128), f32)
        even = even + jnp.concatenate([nothing, across[:, :128]], 1)
        odd = odd + jnp.concatenate([across[:, 128:], nothing], 1)
        twin = me_ref[0] % 2 == 1
        hold_ref[0, pl.ds(GROUP * tap, GROUP), :] = jnp.where(twin, odd, even)
        hold_ref[1, pl.ds(GROUP * tap, GROUP), :] = jnp.where(twin, even, odd)
    kept_ref[0, 0] = hold_ref[0].astype(bf16)
    sent_ref[0, 0] = hold_ref[1].astype(bf16)


def conv_back(g, a2, sums2, grad_sums, a, sums, norms, windows, count):
    rows, width = a.shape
    crops = rows // PIXELS
    piece = pl.BlockSpec((1, 1, 9 * GROUP, 256), lambda q, me: (q ^ (me[0] // 2), 0, 0, 0))

    def quad(n):
        return pl.BlockSpec((n, LANES), lambda q, me: (0, q))

    spec = pltpu.PrefetchScalarGridSpec(
        num_scalar_prefetch=1,
        grid=(QUADS,),
        in_specs=[
            quad(rows), quad(rows), quad(2), quad(2), quad(rows), quad(2), quad(6),
            pl.BlockSpec((1, 3, 9, 256, 256), lambda q, me: (q, 0, 0, 0, 0)),
        ],
        out_specs=[quad(rows), piece, piece, quad(2)],
        scratch_shapes=[
            pltpu.VMEM((2 * PITCH + 256 * crops, LANES), f32),
            pltpu.VMEM((3, 256 * crops, LANES), bf16),
            pltpu.VMEM((2 * PITCH + 256 * crops, LANES), f32),
            pltpu.VMEM((3, 256 * crops, LANES), bf16),
            pltpu.VMEM((PITCH * HW * crops, LANES), f32),
            pltpu.VMEM((rows, LANES), f32),
            pltpu.VMEM((2, 9 * GROUP, 256), f32),
        ],
    )
    return pl.pallas_call(
        functools.partial(conv_back_kernel, crops, count),
        grid_spec=spec,
        out_shape=[
            jax.ShapeDtypeStruct((rows, width), bf16),
            jax.ShapeDtypeStruct((QUADS, 1, 9 * GROUP, 256), bf16),
            jax.ShapeDtypeStruct((QUADS, 1, 9 * GROUP, 256), bf16),
            jax.ShapeDtypeStruct((2, width), f32),
        ],
        compiler_params=params(),
        cost_estimate=BRIEF,
        name="conv_back",
    )(index_scalar("dp"), g, a2, sums2, grad_sums, a, sums, norms, windows)


def squeeze_weight(se_ref, d):
    return jnp.concatenate([se_ref[d, m, :, :128] for m in range(QUADS)], 1)


def excite_weight(se_ref, m):
    return jnp.concatenate(
        [
            jnp.concatenate(
                [se_ref[d, m, 64 * i : 64 * (i + 1), 128:] for i in range(4)], 1
            )
            for d in range(2 * QUADS)
        ],
        0,
    )


def rows_of_crops(values, rows):
    row = lax.broadcasted_iota(jnp.int32, (rows, 1), 0)
    out = values[0:1]
    for c in range(1, values.shape[0]):
        out = jnp.where(row >= PIXELS * c, values[c : c + 1], out)
    return out


def fetch_pieces(me_ref, pieces, hold_ref, sems, offset):
    size = hold_ref.shape[2]
    copies = [
        pltpu.make_async_copy(
            piece.at[pl.ds(offset + m * size, size)],
            hold_ref.at[me_ref[0] ^ b, m],
            sems.at[b * QUADS + m],
        )
        for b, piece in enumerate(pieces)
        for m in range(QUADS)
    ]
    for copy in copies:
        copy.start()
    return copies


def fetch_scratch(size):
    return [
        pltpu.VMEM((2 * QUADS, QUADS, size, 256), bf16),
        pltpu.SemaphoreType.DMA((8 * QUADS,)),
    ]


def gate_kernel(crops, count, me_ref, a_ref, sums_ref, norms_ref, *refs):
    h_ref, pooled_ref, squeezed_ref, act_ref, gate_ref, f2_ref, se_ref, sems = refs[8:]
    copies = fetch_pieces(me_ref, refs[:8], se_ref, sems, 0)
    rows = a_ref.shape[0]
    _, _, scale, shift = affine(sums_ref[...], norms_ref[...], 1, count)
    f2_ref[...] = swish(a_ref[...].astype(f32) * scale + shift)
    pooled = jnp.concatenate(
        [
            jnp.sum(f2_ref[pl.ds(PIXELS * c, PIXELS), :], 0, keepdims=True) / PIXELS
            for c in range(crops)
        ],
        0,
    ).astype(bf16)
    pooled_ref[...] = pooled
    for copy in copies:
        copy.wait()
    squeezed = sum(
        dot(pooled[:, 256 * d : 256 * (d + 1)], squeeze_weight(se_ref, d)) for d in range(8)
    )
    squeezed_ref[...] = squeezed
    act = swish(squeezed).astype(bf16)
    act_ref[...] = act
    for m in range(QUADS):
        lanes = pl.ds(m * LANES, LANES)
        gate = 1.0 / (1.0 + jnp.exp(-dot(act, excite_weight(se_ref, m))))
        gate_ref[:, lanes] = gate
        h_ref[m] = (f2_ref[:, lanes] * rows_of_crops(gate, rows)).astype(bf16)


def gate(a, sums, norms, se, count):
    rows, width = a.shape
    crops = rows // PIXELS
    return pl.pallas_call(
        functools.partial(gate_kernel, crops, count),
        in_specs=[SCALAR] + [pl.BlockSpec(memory_space=pltpu.VMEM)] * 3
        + [pl.BlockSpec(memory_space=pl.ANY)] * 8,
        out_shape=[
            jax.ShapeDtypeStruct((QUADS, rows, LANES), bf16),
            jax.ShapeDtypeStruct((crops, width), bf16),
            jax.ShapeDtypeStruct((crops, 512), f32),
            jax.ShapeDtypeStruct((crops, 512), bf16),
            jax.ShapeDtypeStruct((crops, width), f32),
        ],
        scratch_shapes=[pltpu.VMEM((rows, width), f32)] + fetch_scratch(SE_ROWS),
        compiler_params=params(),
        cost_estimate=BRIEF,
        name="gate",
    )(index_scalar("dp"), a, sums, norms, *se)


def gate_back_kernel(
    crops, count, me_ref, dh_ref, a_ref, sums_ref, norms_ref, gate_ref, squeezed_ref, *refs
):
    q_ref, stats_ref, excite_grad_ref, squeeze_grad_ref, work_ref, se_ref, sems = refs[8:]
    copies = fetch_pieces(me_ref, refs[:8], se_ref, sems, 0)
    rows = a_ref.shape[0]
    for m in range(QUADS):
        lanes = pl.ds(m * LANES, LANES)
        _, _, scale, shift = affine(sums_ref[:, lanes], norms_ref[:, lanes], 1, count)
        normed = a_ref[:, lanes].astype(f32) * scale + shift
        work_ref[:, lanes] = dh_ref[:, lanes] * swish(normed)
    sums = jnp.concatenate(
        [
            jnp.sum(work_ref[pl.ds(PIXELS * c, PIXELS), :], 0, keepdims=True)
            for c in range(crops)
        ],
        0,
    )
    gates = gate_ref[...]
    excite_grad = (sums * gates * (1.0 - gates)).astype(bf16)
    excite_grad_ref[...] = excite_grad
    for copy in copies:
        copy.wait()
    act_grad = sum(
        dot(excite_grad[:, m * LANES : (m + 1) * LANES], excite_weight(se_ref, m), NT)
        for m in range(QUADS)
    )
    squeeze_grad = (act_grad * swish_slope(squeezed_ref[...])).astype(bf16)
    squeeze_grad_ref[...] = squeeze_grad
    for d in range(8):
        lanes = pl.ds(d * 256, 256)
        pooled_grad = dot(squeeze_grad, squeeze_weight(se_ref, d), NT) / PIXELS
        values = a_ref[:, lanes].astype(f32)
        mean, inverse, scale, shift = affine(sums_ref[:, lanes], norms_ref[:, lanes], 1, count)
        normed = values * scale + shift
        q = (
            dh_ref[:, lanes] * rows_of_crops(gate_ref[:, lanes], rows)
            + rows_of_crops(pooled_grad, rows)
        ) * swish_slope(normed)
        q_ref[:, lanes] = q
        centred = (values - mean) * inverse
        stats_ref[0:1, lanes] = jnp.sum(q, 0, keepdims=True)
        stats_ref[1:2, lanes] = jnp.sum(q * centred, 0, keepdims=True)


def gate_back(dh, a, sums, norms, gates, squeezed, se, count):
    rows, width = a.shape
    crops = rows // PIXELS
    return pl.pallas_call(
        functools.partial(gate_back_kernel, crops, count),
        in_specs=[SCALAR] + [pl.BlockSpec(memory_space=pltpu.VMEM)] * 6
        + [pl.BlockSpec(memory_space=pl.ANY)] * 8,
        out_shape=[
            jax.ShapeDtypeStruct((rows, width), f32),
            jax.ShapeDtypeStruct((2, width), f32),
            jax.ShapeDtypeStruct((crops, width), bf16),
            jax.ShapeDtypeStruct((crops, 512), bf16),
        ],
        scratch_shapes=[pltpu.VMEM((rows, width), f32)] + fetch_scratch(SE_ROWS),
        compiler_params=params(),
        cost_estimate=BRIEF,
        name="gate_back",
    )(index_scalar("dp"), dh, a, sums, norms, gates, squeezed, *se)


def head_kernel(
    width, me_ref, summary_ref, *refs
):
    (
        loss_ref, unit_ref, score_grad_ref, embed_grad_ref, summary_grad_ref, all_ref,
        hold_ref, plan_ref, protos_ref, queue_ref, project_ref, bundle_ref, sems,
    ) = refs[8:]
    copies = fetch_pieces(me_ref, refs[:8], bundle_ref, sems, 0)
    crops = all_ref.shape[0]
    each = summary_ref.shape[1]
    for i in range(summary_ref.shape[0]):
        hold_ref[pl.ds(each * i, each), :] = summary_ref[i].astype(f32)
    all_ref[...] = hold_ref[...].astype(bf16)
    for copy in copies:
        copy.wait()
    parts = 2 * QUADS * QUADS
    for i in range(parts):
        d, m = i // QUADS, i % QUADS
        low = 64
        project_ref[d, pl.ds(64 * m, 64), :] = bundle_ref[d, m, 0:low, :]
        protos_ref[pl.ds(PROTO_ROWS * i, PROTO_ROWS), :] = bundle_ref[d, m, low : low + PROTO_ROWS, :]
        low = low + PROTO_ROWS
        queue_ref[pl.ds(QUEUE_ROWS * i, QUEUE_ROWS), :] = bundle_ref[d, m, low : low + QUEUE_ROWS, :]
    protos = protos_ref[...]
    embedded = sum(
        dot(all_ref[:, 256 * d : 256 * (d + 1)], project_ref[d], NT) for d in range(8)
    )
    scale = lax.rsqrt(jnp.sum(embedded * embedded, 1, keepdims=True) + EPS_NORM)
    unit = (embedded * scale).astype(bf16)
    unit_ref[...] = unit
    scores = dot(unit, protos, NT)
    lane = lax.broadcasted_iota(jnp.int32, (1, parts * PROTO_ROWS), 1)
    block = lane // PROTO_ROWS
    there = (block // QUADS) * PROTO_ROWS + (lane - block * PROTO_ROWS) < width
    first = jnp.where(there, jnp.exp(scores / EPS_SINK), 0.0)
    plan_ref[pl.ds(0, crops), :] = first

    size = 2 * crops

    def partial_sums(value):
        return jnp.sum(value.reshape(-1, 8, value.shape[1]), 0)

    def rows_at(i):
        return pl.ds(pl.multiple_of(crops + i * size, crops), size)

    def fill(i, column):
        rows = queue_ref[pl.ds(pl.multiple_of(i * size, size), size), :]
        value = jnp.exp(dot(rows, protos, NT) / EPS_SINK)
        plan_ref[rows_at(i), :] = value
        return column + partial_sums(value)

    steps = parts * QUEUE_ROWS // size
    column = lax.fori_loop(0, steps, fill, partial_sums(first))
    column = jnp.sum(column, 0, keepdims=True)
    large = jnp.where(column > 1e37, 2.0**-8, 1.0)
    inverse = jnp.where(there, 1.0 / (column * large), 0.0)
    for sweep in range(SINK - 1):

        def balanced(place, inverse=inverse, sweep=sweep):
            value = plan_ref[place, :]
            if sweep == 0:
                value = value * large
            value = value * inverse
            value = value * (1.0 / jnp.sum(value, 1, keepdims=True))
            plan_ref[place, :] = value
            return partial_sums(value)

        column = lax.fori_loop(
            0, steps, lambda i, column: column + balanced(rows_at(i)), balanced(pl.ds(0, crops))
        )
        inverse = jnp.where(there, 1.0 / jnp.sum(column, 0, keepdims=True), 0.0)
    value = plan_ref[pl.ds(0, crops), :] * inverse
    value = value / jnp.sum(value, 1, keepdims=True)
    pairs = jnp.concatenate(
        [bundle_ref[d, 0, HEAD_ROWS - 16 : HEAD_ROWS, :].astype(f32)[:8, :crops] for d in range(8)], 0
    )
    plan = lax.dot_general(
        pairs, value, NN, precision=lax.Precision.HIGHEST, preferred_element_type=f32
    )
    logits = scores / SOFTMAX_TEMPER
    top = jnp.max(jnp.where(there, logits, -jnp.inf), 1, keepdims=True)
    power = jnp.where(there, jnp.exp(logits - top), 0.0)
    mass = jnp.sum(power, 1, keepdims=True)
    entropy = jnp.sum(plan * (logits - (top + jnp.log(mass))), 1, keepdims=True)
    loss_ref[...] = -jnp.sum(entropy, 0, keepdims=True) / crops
    score_grad = ((power / mass - plan) / (SOFTMAX_TEMPER * crops)).astype(bf16)
    score_grad_ref[...] = score_grad.T
    unit_grad = dot(score_grad, protos)
    inner = jnp.sum(embedded * unit_grad, 1, keepdims=True)
    embed_grad = (scale * unit_grad - embedded * (scale * scale * scale * inner)).astype(bf16)
    embed_grad_ref[...] = embed_grad
    for d in range(8):
        summary_grad_ref[:, 256 * d : 256 * (d + 1)] = dot(embed_grad, project_ref[d])


def head(summary, bundle, width):
    devices, each, channels = summary.shape
    crops = devices * each
    parts = 2 * QUADS * QUADS
    return pl.pallas_call(
        functools.partial(head_kernel, width),
        in_specs=[SCALAR, pl.BlockSpec(memory_space=pltpu.VMEM)]
        + [pl.BlockSpec(memory_space=pl.ANY)] * 8,
        out_shape=[
            jax.ShapeDtypeStruct((1, 1), f32),
            jax.ShapeDtypeStruct((crops, 256), bf16),
            jax.ShapeDtypeStruct((parts * PROTO_ROWS, crops), bf16),
            jax.ShapeDtypeStruct((crops, 256), bf16),
            jax.ShapeDtypeStruct((crops, channels), f32),
            jax.ShapeDtypeStruct((crops, channels), bf16),
        ],
        scratch_shapes=[
            pltpu.VMEM((crops, channels), f32),
            pltpu.VMEM((crops + parts * QUEUE_ROWS, parts * PROTO_ROWS), f32),
            pltpu.VMEM((parts * PROTO_ROWS, 256), bf16),
            pltpu.VMEM((parts * QUEUE_ROWS, 256), bf16),
            pltpu.VMEM((8, 256, 256), bf16),
        ]
        + fetch_scratch(HEAD_ROWS),
        compiler_params=params(),
        cost_estimate=BRIEF,
        name="head",
    )(index_scalar("dp"), summary, *bundle)


def plain_head(summary, project, protos, queue, pairs):
    crops = summary.shape[0]
    embedded = dot(summary, project)
    scale = lax.rsqrt(jnp.sum(embedded * embedded, 1, keepdims=True) + EPS_NORM)
    unit = (embedded * scale).astype(bf16)
    scores = dot(unit, protos)
    plan = jnp.exp(jnp.concatenate([scores, dot(queue, protos)], 0) / EPS_SINK)
    for sweep in range(SINK):
        plan = plan / jnp.sum(plan, 0, keepdims=True)
        plan = plan / jnp.sum(plan, 1, keepdims=True)
    plan = lax.dot_general(
        pairs, plan[:crops], NN, precision=lax.Precision.HIGHEST, preferred_element_type=f32
    )
    logits = scores / SOFTMAX_TEMPER
    loss = -jnp.sum(plan * jax.nn.log_softmax(logits, axis=1)) / crops
    score_grad = ((jax.nn.softmax(logits, axis=1) - plan) / (SOFTMAX_TEMPER * crops)).astype(bf16)
    unit_grad = dot(score_grad, protos, NT)
    inner = jnp.sum(embedded * unit_grad, 1, keepdims=True)
    embed_grad = (scale * unit_grad - embedded * (scale * scale * scale * inner)).astype(bf16)
    return loss.reshape(1, 1), unit, score_grad, embed_grad, dot(embed_grad, project, NT)


def picks(rows, columns, source):
    row = lax.broadcasted_iota(jnp.int32, (rows, columns), 0)
    column = lax.broadcasted_iota(jnp.int32, (rows, columns), 1)
    return jnp.where(row == source(column), 1.0, 0.0).astype(bf16)


def narrow_lanes(v):
    return jnp.concatenate([v[:, :HALF], v[:, HALF + GAP :]], 1)


def square_sum(v):
    return jnp.sum(jnp.sum(v * v, 1, keepdims=True), 0, keepdims=True)


def small_grads_kernel(
    m_ref, small_ref, summary_ref, embed_grad_ref, score_grad_ref, unit_ref,
    squeeze_ref, excite_ref, project_ref, protos_ref, squares_ref, hold_ref,
):
    m = m_ref[0]
    devices, each, _ = small_ref.shape
    for i in range(devices):
        hold_ref[pl.ds(each * i, each), :] = small_ref[i].astype(f32)
    wide, inner = QUADS * LANES, 8 * SE_LANES

    def rows_of(base, size):
        return hold_ref[:, pl.ds(pl.multiple_of(base, 128), size)]

    squeeze_grad = rows_of(wide + inner + 128 * m, 128).astype(bf16)
    squeeze_grad = dot(
        squeeze_grad, picks(128, 2 * SE_PART, lambda c: (c // SE_PART) * SE_LANES + c % SE_PART)
    ).astype(bf16)
    squares = []
    total_square = jnp.zeros((1, 1), f32)
    for q in range(QUADS):
        pooled = narrow_lanes(rows_of(q * LANES, LANES)).astype(bf16)
        part = dot(pooled, squeeze_grad, TN)
        squeeze_ref[pl.ds(QUAD * q, QUAD), :] = part
        total_square = total_square + square_sum(part)
    squares.append(total_square)
    act = rows_of(wide, inner).astype(bf16)
    act = dot(act, picks(inner, QUAD, lambda c: (c // SE_PART) * SE_LANES + c % SE_PART)).astype(bf16)
    excite_grad = narrow_lanes(rows_of(wide + 2 * inner + LANES * m, LANES)).astype(bf16)
    part = dot(act, excite_grad, TN)
    excite_ref[...] = part
    squares.append(square_sum(part))
    embed_grad = dot(embed_grad_ref[...], picks(256, 64, lambda c: 64 * m + c)).astype(bf16)
    summary = jnp.concatenate(
        [
            narrow_lanes(summary_ref[:, q * LANES : (q + 1) * LANES].astype(f32))
            for q in range(QUADS)
        ],
        1,
    ).astype(bf16)
    part = dot(embed_grad, summary, TN)
    project_ref[...] = part
    squares.append(square_sum(part))
    total_square = jnp.zeros((1, 1), f32)
    last = protos_ref.shape[0]
    for d in range(8):
        place = pl.ds(pl.multiple_of((QUADS * d + m) * PROTO_ROWS, PROTO_ROWS), PROTO_ROWS)
        part = dot(score_grad_ref[place, :], unit_ref[...])
        size = min(PROTO_ROWS, last - PROTO_ROWS * d)
        protos_ref[pl.ds(PROTO_ROWS * d, size), :] = part[:size]
        total_square = total_square + square_sum(part)
    squares.append(total_square)
    lane = lax.broadcasted_iota(jnp.int32, (1, 128), 1)
    squares_ref[...] = sum(jnp.where(lane == i, v, 0.0) for i, v in enumerate(squares))


def small_grads(small, summary, embed_grad, score_grad, unit, width):
    crops = summary.shape[0]
    return pl.pallas_call(
        small_grads_kernel,
        in_specs=[SCALAR] + [pl.BlockSpec(memory_space=pltpu.VMEM)] * 5,
        out_shape=[
            jax.ShapeDtypeStruct((QUADS * QUAD, 2 * SE_PART), f32),
            jax.ShapeDtypeStruct((QUAD, QUAD), f32),
            jax.ShapeDtypeStruct((64, QUADS * QUAD), f32),
            jax.ShapeDtypeStruct((width, 256), f32),
            jax.ShapeDtypeStruct((1, 128), f32),
        ],
        scratch_shapes=[pltpu.VMEM((crops, small.shape[2]), f32)],
        compiler_params=params(),
        cost_estimate=BRIEF,
        name="small_grads",
    )(index_scalar("mp"), small, summary, embed_grad, score_grad, unit)


def own_kernel_kernel(me_ref, v_ref, out_ref, square_ref):
    value = v_ref[: 9 * GROUP].astype(f32)
    value = jnp.where(me_ref[0] % 2 == 1, value[:, 256 - HALF :], value[:, :HALF])
    out_ref[...] = value
    square_ref[...] = square_sum(value)


def own_kernel(v):
    return pl.pallas_call(
        own_kernel_kernel,
        in_specs=[SCALAR, pl.BlockSpec(memory_space=pltpu.VMEM)],
        out_shape=[
            jax.ShapeDtypeStruct((9 * GROUP, HALF), f32), jax.ShapeDtypeStruct((1, 1), f32),
        ],
        compiler_params=params(),
        cost_estimate=BRIEF,
        name="own_kernel",
    )(index_scalar("dp"), v)


def weight_sums_kernel(*refs):
    lane = lax.broadcasted_iota(jnp.int32, (1, 128), 1)
    refs[-1][...] = sum(
        jnp.where(lane == i, square_sum(ref[...]), 0.0) for i, ref in enumerate(refs[:-1])
    )


def weight_sums(weights):
    values = [w if w.shape[1] == 2 * SE_PART or w.shape[0] == w.shape[1] else w.T for w in weights]
    return pl.pallas_call(
        weight_sums_kernel,
        out_shape=jax.ShapeDtypeStruct((1, 128), f32),
        compiler_params=params(),
        cost_estimate=BRIEF,
        name="weight_sums",
    )(*values)


def squares_kernel(
    n_dp, n_mp, weights_ref, norms_ref, small_ref, expand_ref, kernel_ref,
    g1_ref, g2_ref, g3_ref, out_ref,
):
    lane = lax.broadcasted_iota(jnp.int32, (1, 128), 1)

    def at(i, v):
        return jnp.where(lane == i, v, 0.0)

    portions = at(0, 1.0) + at(1, 1.0 / n_mp) + at(4, 1.0)
    for i in (2, 3, 5, 6):
        portions = portions + at(i, 1.0 / n_dp)
    weights = weights_ref[...] * portions
    small = small_ref[...]
    grads = at(1, kernel_ref[...] / n_mp) + at(4, expand_ref[...])
    for i, k in enumerate((2, 3, 5, 6)):
        grads = grads + at(k, small[:, i : i + 1] / n_dp)
    everywhere = 1.0 / (n_dp * n_mp)
    for k, ref in enumerate((g1_ref, g2_ref, g3_ref)):
        for row, first in ((1, 7), (0, 10)):
            grads = grads + at(first + k, square_sum(ref[row : row + 1, :]) * everywhere)
        weights = weights + at(7 + k, square_sum(norms_ref[k : k + 1, :]) * everywhere)
        weights = weights + at(10 + k, square_sum(norms_ref[3 + k : 4 + k, :]) * everywhere)
    out_ref[0:1, :] = weights
    out_ref[1:2, :] = grads


def first_gradient():
    lane = lax.broadcasted_iota(jnp.int32, (2, 128), 1)
    row = lax.broadcasted_iota(jnp.int32, (2, 128), 0)
    return (lane == 0) & (row == 1)


def squares(n_dp, n_mp, *values):
    return pl.pallas_call(
        functools.partial(squares_kernel, n_dp, n_mp),
        out_shape=jax.ShapeDtypeStruct((2, 128), f32),
        compiler_params=params(),
        cost_estimate=BRIEF,
        name="squares",
    )(*values)


def rate_of(norm_squares, i):
    norms = jnp.sqrt(norm_squares[:, i : i + 1] + EPS_NORM)
    return TRUST * norms[0:1] / (norms[1:2] + DECAY * norms[0:1])


def step(weight, gradient, momentum, norm_squares, i):
    return MOMENTUM * momentum + rate_of(norm_squares, i) * (gradient + DECAY * weight)


def lars_prepare_kernel(*refs):
    n = len(refs) // 5
    for i in range(n):
        weight, gradient, momentum = (refs[3 * i + j] for j in range(3))
        refs[3 * n + 2 * i][...] = gradient[...] + DECAY * weight[...]
        refs[3 * n + 2 * i + 1][...] = MOMENTUM * momentum[...]


def lars_prepare(items):
    return pl.pallas_call(
        lars_prepare_kernel,
        out_shape=[jax.ShapeDtypeStruct(w.shape, f32) for w, _, _ in items for _ in range(2)],
        compiler_params=params(),
        cost_estimate=BRIEF,
        name="lars_prepare",
    )(*[v for item in items for v in item])


def lars_kernel(
    m_ref, squares_ref, weight_ref, gradient_ref, momentum_ref,
    gains_ref, biases_ref, m_gains_ref, m_biases_ref, g1_ref, g2_ref, g3_ref, *refs
):
    norm_squares = squares_ref[...]
    n = (len(refs) - 3) // 3
    out = refs[2 * n :]
    out[0][...] = step(weight_ref[...], gradient_ref[...], momentum_ref[...], norm_squares, 0)
    for i in range(n):
        out[1 + i][...] = refs[2 * i + 1][...] + rate_of(norm_squares, i + 1) * refs[2 * i][...]
    lanes = pl.ds(pl.multiple_of(m_ref[0] * LANES, LANES), LANES)
    for k, ref in enumerate((g1_ref, g2_ref, g3_ref)):
        own = narrow_lanes(ref[:, lanes])
        row = slice(k, k + 1)
        out[n + 1][row, :] = step(
            gains_ref[row, :], own[1:2], m_gains_ref[row, :], norm_squares, 7 + k
        )
        out[n + 2][row, :] = step(
            biases_ref[row, :], own[0:1], m_biases_ref[row, :], norm_squares, 10 + k
        )


def lars(norm_squares, weight, gradient, momentum, norm_values, prepared):
    shapes = [weight.shape] + [v.shape for v in prepared[::2]] + [norm_values[0].shape] * 2
    values = [norm_squares, weight, gradient, momentum, *norm_values, *prepared]
    return pl.pallas_call(
        lars_kernel,
        in_specs=[SCALAR] + [pl.BlockSpec(memory_space=pltpu.VMEM)] * len(values),
        out_shape=[jax.ShapeDtypeStruct(shape, f32) for shape in shapes],
        compiler_params=params(),
        cost_estimate=BRIEF,
        name="lars",
    )(index_scalar("mp"), *values)


def plain_finish(
    small, summary, unit, score_grad, embed_grad, grad_sums, channels_here, big_grads, weights, moments
):
    n_dp, n_mp, m_index = lax.axis_size("dp"), lax.axis_size("mp"), lax.axis_index("mp")
    w_reduce, w_group, w_squeeze, w_excite, w_expand, w_project, prototypes, bn_gains, bn_biases = weights
    small = small.reshape(-1, small.shape[-1])
    wide, inner = QUADS * LANES, 8 * SE_LANES
    pooled_all = pack_channels(small[:, :wide])
    act_all = pack_inner(small[:, wide : wide + inner])
    squeeze_all = pack_inner(small[:, wide + inner : wide + 2 * inner])
    excite_all = pack_channels(small[:, wide + 2 * inner :])

    def own(v, width):
        return lax.dynamic_slice_in_dim(v, m_index * width, width, 1)

    reduce_grad, kernel_grad, expand_grad = big_grads
    gain_part = own(pack_channels(jnp.stack([v[1] for v in grad_sums])), channels_here)
    bias_part = own(pack_channels(jnp.stack([v[0] for v in grad_sums])), channels_here)
    grads = [
        reduce_grad,
        kernel_grad,
        dot(pooled_all, own(squeeze_all, w_squeeze.shape[1]), TN),
        dot(act_all, own(excite_all, w_excite.shape[1]), TN),
        expand_grad,
        dot(pack_channels(summary), own(embed_grad, w_project.shape[1]), TN),
        dot(unit, own(score_grad, prototypes.shape[1]), TN),
    ]
    portions = [1.0, 1.0 / n_mp, 1.0 / n_dp, 1.0 / n_dp, 1.0, 1.0 / n_dp, 1.0 / n_dp]

    def shares(arrays, gain, bias):
        return jnp.concatenate(
            [
                jnp.stack([jnp.sum(a * a) * p for a, p in zip(arrays, portions)]),
                jnp.sum(gain * gain, 1) / n_dp,
                jnp.sum(bias * bias, 1) / n_dp,
            ]
        )

    norms = total(
        jnp.stack([shares(weights[:7], bn_gains, bn_biases), shares(grads, gain_part, bias_part)])
    )
    stepped = [
        step(w, g, m, norms, i) for i, (w, g, m) in enumerate(zip(weights[:7], grads, moments[:7]))
    ]
    for values, part, momentum, first in (
        (bn_gains, gain_part, moments[7], 7), (bn_biases, bias_part, moments[8], 10),
    ):
        stepped.append(
            jnp.concatenate(
                [
                    step(values[k : k + 1], part[k : k + 1], momentum[k : k + 1], norms, first + k)
                    for k in range(3)
                ]
            )
        )
    return stepped, norms


def body(
    block_input, output_grad, w_reduce, w_group, w_squeeze, w_excite, w_expand, w_project,
    prototypes, bn_gains, bn_biases, m_reduce, m_group, m_squeeze, m_excite, m_expand,
    m_project, m_protos, m_gains, m_biases, queue_store, queue_slots, crop_perm,
):
    n_dp = lax.axis_size("dp")
    n_mp = lax.axis_size("mp")
    m_index = lax.axis_index("mp")
    channels_here = block_input.shape[0]
    rows = block_input.shape[1] // n_mp
    crops = rows // PIXELS
    count = rows * n_dp * n_mp
    all_crops = crops * n_dp * n_mp
    quick = quick_mesh()
    weights = [
        w_reduce, w_group, w_squeeze, w_excite, w_expand, w_project, prototypes, bn_gains, bn_biases,
    ]
    moments = [
        m_reduce, m_group, m_squeeze, m_excite, m_expand, m_project, m_protos, m_gains, m_biases,
    ]

    slot_table = (
        queue_slots[0][:, None]
        == lax.broadcasted_iota(jnp.int32, (queue_slots.shape[1], queue_store.shape[0]), 1)
    ).astype(bf16)
    queue_rows = dot(slot_table, queue_store.astype(bf16)).astype(bf16)
    order = crop_perm[0]
    pairing = (order[None, :] == jnp.bitwise_xor(order, 1)[:, None]).astype(f32)
    kernel_low = gather_kernel(w_group)
    x_blocks = slab_blocks(block_input)
    y_grad_blocks = slab_blocks(output_grad)
    norms = spread(jnp.concatenate([bn_gains, bn_biases], 0), "mp")
    norms = spread_channels(norms.transpose(1, 0, 2).reshape(norms.shape[1], -1))
    if quick:
        low = gather_mp(shard_square(w_reduce)).reshape(-1, 256)
        expand_low = shard_square(w_expand)
        se_low = shard_excitation(w_squeeze, w_excite)
        low, x_blocks, norms, expand_low, se_low, *kernel_low = tie(
            low, x_blocks, norms, expand_low, se_low, *kernel_low
        )
        across, up = gather_sides(low)
        x_blocks = exchange(x_blocks)
        windows = dense_windows(kernel_low)
        across, up, windows = tie(across, up, windows)
        corner = gather_corner(across, up)
        x_blocks, se_low = tie(x_blocks, se_low)
        se_low = spread(se_low, "mp").reshape(-1, 256)
        reduce_pieces = gather_twins(low, across, up, corner)
        head_values = tie(w_project, prototypes, queue_rows, pairing, corner)
        bundle = shard_head(*head_values[:4])
    else:
        x_blocks = exchange(x_blocks)
        y_grad_parts = list(quad_blocks(exchange(y_grad_blocks)))
        reduce_pieces = gather_square(w_reduce)
        se_pieces = list(gather_excitation(w_squeeze, w_excite).reshape(8, -1, 256))
        expand_pieces = gather_square(w_expand)
        project_low, protos_low, queue_low, pairs = gather_head(
            w_project, prototypes, queue_rows, pairing
        )
        pairs = block_diagonal(pairs)
        windows = dense_windows(kernel_low)
    x = quad_blocks(x_blocks)

    reduced, sums1 = mix(x, reduce_pieces)
    if quick:
        sums1 = sum_axis(sums1, "dp")
        sums1, expand_low, se_low = tie(sums1, expand_low, se_low)
        expand_low = spread(expand_low, "mp").reshape(-1, 256)
        se_across, se_up = gather_sides(se_low)
        sums1 = sum_axis(sums1, "mp")
        sums1, expand_low, se_across, se_up = tie(sums1, expand_low, se_across, se_up)
        se_corner = gather_corner(se_across, se_up)
        across, up = gather_sides(expand_low)
        y_grad_parts = [
            lax.dynamic_index_in_dim(y_grad_blocks, m_index ^ k, 0, keepdims=False) for k in range(QUADS)
        ]
        sums1, bundle, y_grad_parts[1] = tie(sums1, bundle, y_grad_parts[1])
        y_grad_parts[1] = lax.ppermute(y_grad_parts[1], "mp", flips("mp", 1))
        bundle = spread(bundle, "mp").reshape(-1, 256)
    else:
        sums1 = total(sums1)
    grouped, sums2 = conv(reduced, sums1, norms, windows, count)
    if quick:
        sums2, bundle, across, up, se_corner, y_grad_parts[1] = tie(
            sums2, bundle, across, up, se_corner, y_grad_parts[1]
        )
        se_pieces = gather_twins(se_low, se_across, se_up, se_corner)
        corner = gather_corner(across, up)
        sums2 = jnp.sum(spread(sums2, "dp"), 0)
        sums2, corner = tie(sums2, corner)
        expand_pieces = gather_twins(expand_low, across, up, corner)
        sums2 = jnp.sum(spread(sums2, "mp"), 0)
    else:
        sums2 = total(sums2)
    if quick:
        sums2, y_grad_parts[2] = tie(sums2, y_grad_parts[2])
        y_grad_parts[2] = lax.ppermute(y_grad_parts[2], "mp", flips("mp", 2))
    gated, pooled, squeezed, squeeze_act, gates = gate(grouped, sums2, norms, se_pieces, count)
    expanded, sums3 = mix(gated, expand_pieces)
    if quick:
        sums3, bundle = tie(sums3, bundle)
        sums3 = jnp.sum(spread(sums3, "dp"), 0)
        sums3, bundle, y_grad_parts[2] = tie(sums3, bundle, y_grad_parts[2])
        across, up = gather_sides(bundle)
        sums3 = jnp.sum(spread(sums3, "mp"), 0)
        sums3, across, up = tie(sums3, across, up)
        corner = gather_corner(across, up)
    else:
        sums3 = total(sums3)
    *y_parts, summary = block_value(x, expanded, sums3, norms, count)
    if quick:
        summary, corner = tie(summary, corner)
        bundle = gather_twins(bundle, across, up, corner)
    summary = gather_all(summary)
    if quick:
        summary, y_grad_parts[3], y_parts[1] = tie(summary, y_grad_parts[3], y_parts[1])
        y_grad_parts[3] = lax.ppermute(y_grad_parts[3], "mp", flips("mp", 3))
        y_parts[1] = lax.ppermute(y_parts[1], "mp", flips("mp", 1))

    first_crop = ((lax.axis_index("dp") * n_mp + m_index) * crops).astype(jnp.int32)[None]
    if quick:
        loss, unit, score_grad, embed_grad, summary_grad, summary = head(
            summary, bundle, prototypes.shape[1]
        )
    else:
        summary = summary.reshape(all_crops, -1)
        loss, unit, score_grad, embed_grad, summary_grad = plain_head(
            summary, project_low, protos_low, queue_low, pairs
        )

    joined_grad, grad_sums3 = value_back(
        first_crop, x, expanded, sums3, norms, y_grad_parts, summary_grad, count
    )
    if quick:
        grad_sums3, y_parts[1] = tie(grad_sums3, y_parts[1])
    grad_sums3 = total(grad_sums3)
    if quick:
        grad_sums3, y_parts[2], y_parts[3] = tie(grad_sums3, y_parts[2], y_parts[3])
        y_parts[2] = lax.ppermute(y_parts[2], "mp", flips("mp", 2))
    expanded_grad, expand_sent = sent_grads(
        gated, joined_grad, expanded, sums3, norms, 2, grad_sums3, count, False
    )
    if quick:
        expand_got = from_twin(expand_sent)
    expand_kept = kept_grads(gated, expanded_grad)
    gated_grad = mix_back(expanded_grad, expand_pieces)
    if quick:
        gated_grad, expand_got = tie(gated_grad, expand_got)
        last = twin_sum(expand_kept, expand_got)
        last, gated_grad, y_parts[2] = tie(last, gated_grad, y_parts[2])
        expand_corner = lax.ppermute(last, "dp", diagonal(8))
    act2_grad, grad_sums2, excite_grad, squeeze_grad = gate_back(
        gated_grad, grouped, sums2, norms, gates, squeezed, se_pieces, count
    )
    small = jnp.concatenate([pooled, squeeze_act, squeeze_grad, excite_grad], 1)
    if quick:
        grad_sums2, expand_corner = tie(grad_sums2, expand_corner)
    grad_sums2 = total(grad_sums2)
    grad_sums2, small = tie(grad_sums2, small)
    small = gather_all(small)
    if quick:
        grad_sums2, y_parts[3] = tie(grad_sums2, y_parts[3])
        y_parts[3] = lax.ppermute(y_parts[3], "mp", flips("mp", 3))
        across, up = corner_sums(expand_kept, expand_got, expand_corner)
        across, up = scatter_sides(across, up)
    act1_grad, kernel_kept, kernel_sent, grad_sums1 = conv_back(
        act2_grad, grouped, sums2, grad_sums2, reduced, sums1, norms, windows, count
    )
    if quick:
        grad_sums1, across, up, kernel_kept, kernel_sent, small, y_parts[3] = tie(
            grad_sums1, across, up, kernel_kept, kernel_sent, small, y_parts[3]
        )
        expand_own, *expand_parts = side_sums(expand_kept, expand_got, across, up)
        expand_parts = scatter_mp(expand_own, expand_parts)
        kernel_got = from_twin(kernel_sent)
        kernel_across, kernel_up = corner_sums(
            kernel_kept, kernel_got, scatter_corner(kernel_kept, kernel_got)
        )
        grad_sums1 = jnp.sum(spread(grad_sums1, "dp"), 0)
        grad_sums1, expand_parts, kernel_across, kernel_up = tie(
            grad_sums1, expand_parts, kernel_across, kernel_up
        )
        kernel_across, kernel_up = scatter_sides(kernel_across, kernel_up)
        grad_sums1 = jnp.sum(spread(grad_sums1, "mp"), 0)
        grad_sums1, kernel_across, kernel_up = tie(grad_sums1, kernel_across, kernel_up)
        kernel_sum = side_sums(kernel_kept, kernel_got, kernel_across, kernel_up)[0].astype(bf16)
        kernel_got = lax.ppermute(kernel_sum, "mp", flips("mp", 2))
    else:
        grad_sums1 = total(grad_sums1)
    reduced_grad, reduce_sent = sent_grads(
        x, act1_grad, reduced, sums1, norms, 0, grad_sums1, count, True
    )
    if quick:
        reduced_grad, reduce_sent, kernel_got = tie(reduced_grad, reduce_sent, kernel_got)
        reduce_got = from_twin(reduce_sent)
        kernel_sum = kernel_sum + kernel_got
        kernel_got = lax.ppermute(kernel_sum, "mp", flips("mp", 1))
    reduce_kept = kept_grads(x, reduced_grad)
    if quick:
        reduced_grad, reduce_got, reduce_kept, kernel_got = tie(
            reduced_grad, reduce_got, reduce_kept, kernel_got
        )
        kernel_sum = kernel_sum + kernel_got
        corner = scatter_corner(reduce_kept, reduce_got)
    x_grad = out_blocks(mix_back(reduced_grad, reduce_pieces, joined_grad))
    if quick:
        x_grad, corner = tie(x_grad, corner)
        x_grad = exchange(x_grad)
        across, up = corner_sums(reduce_kept, reduce_got, corner)
        across, up, small, kernel_sum = tie(across, up, small, kernel_sum)
        across, up = scatter_sides(across, up)
        squeeze_part, excite_part, project_part, protos_part, small_squares = small_grads(
            small, summary, embed_grad, score_grad, unit, prototypes.shape[1]
        )
        expand_grad, expand_square = own_square(expand_parts)
        kernel_grad, kernel_square = own_kernel(kernel_sum)
        across, up, small_squares, expand_square, kernel_square = tie(
            across, up, small_squares, expand_square, kernel_square
        )
        own, *parts = side_sums(reduce_kept, reduce_got, across, up)
        parts = scatter_mp(own, parts)
        input_grad = out_channels(list(x_grad), channels_here, f32, jnp.zeros((1,), jnp.int32))
        block_output = out_channels(y_parts, channels_here, bf16, index_scalar("mp"))
        prepared = lars_prepare(
            [
                (w_group.T, kernel_grad, m_group.T),
                (w_squeeze, squeeze_part, m_squeeze),
                (w_excite, excite_part, m_excite),
                (w_expand.T, expand_grad, m_expand.T),
                (w_project.T, project_part, m_project.T),
                (prototypes.T, protos_part, m_protos.T),
            ]
        )
        weight_squares = weight_sums(weights[:7])
        shares = squares(
            n_dp, n_mp, weight_squares, norms, small_squares, expand_square, kernel_square,
            grad_sums1, grad_sums2, grad_sums3,
        )
        parts, input_grad, block_output, shares, *prepared = tie(
            parts, input_grad, block_output, shares, *prepared
        )
        reduce_grad, reduce_square = own_square(parts)
        norm_squares = total(jnp.where(first_gradient(), reduce_square, shares))
        (
            mom_reduce, mom_group, mom_squeeze, mom_excite, mom_expand, mom_project, mom_protos,
            mom_gains, mom_biases,
        ) = lars(
            norm_squares, w_reduce.T, reduce_grad, m_reduce.T,
            [bn_gains, bn_biases, m_gains, m_biases, grad_sums1, grad_sums2, grad_sums3], prepared,
        )
        stepped = [
            mom_reduce.T, mom_group.T, mom_squeeze, mom_excite, mom_expand.T, mom_project.T,
            mom_protos.T, mom_gains, mom_biases,
        ]
    else:
        input_grad = natural_channels(exchange(x_grad), channels_here, f32)
        block_output = natural_channels(
            exchange(out_blocks(jnp.stack(y_parts))), channels_here, bf16
        )
        big_grads = (
            scatter_square(reduce_kept, reduce_sent),
            scatter_kernel(kernel_kept[:, 0], kernel_sent[:, 0]),
            scatter_square(expand_kept, expand_sent),
        )
        stepped, norm_squares = plain_finish(
            small, summary, unit, score_grad, embed_grad, (grad_sums1, grad_sums2, grad_sums3),
            channels_here, big_grads, weights, moments,
        )
    param_norms = jnp.sqrt(norm_squares[:, :13].T + EPS_NORM)
    return (block_output, loss[0, 0], input_grad, *stepped, param_norms)


def solution(mesh):
    split = P("dp", "mp")
    turned = P("mp", "dp")
    rows = P("dp", None)
    columns = P(None, "mp")
    return jax.shard_map(
        body,
        mesh=mesh,
        in_specs=(
            turned, turned, split, rows, columns, columns, split, columns, columns, columns, columns,
            split, rows, columns, columns, split, columns, columns, columns, columns, rows, rows, rows,
        ),
        out_specs=(
            turned, P(), turned, split, rows, columns, columns, split, columns, columns, columns,
            columns, P(),
        ),
        check_vma=False,
    )
```

```python
import functools

import jax
import jax.numpy as jnp
import numpy as np
from jax import lax
from jax.experimental import pallas as pl
from jax.experimental.pallas import tpu as pltpu
from jax.sharding import PartitionSpec as P

HW = 14
PIXELS = HW * HW
SINK = 3
EPS_BN = 1e-05
EPS_NORM = 1e-06
EPS_SINK = 0.05
SOFTMAX_TEMPER = 0.1
TRUST = 0.001
DECAY = 1e-06
MOMENTUM = 0.9

QUADS = 4
QUAD = 504
HALF = 252
LANES = 512
GAP = LANES - QUAD
GROUP = 56
SE_PART = 63
SE_LANES = 64
PITCH = 16
VMEM_BYTES = 60 * 1024 * 1024
f32 = jnp.float32
bf16 = jnp.bfloat16
NN = (((1,), (0,)), ((), ()))
NT = (((1,), (1,)), ((), ()))
TN = (((0,), (0,)), ((), ()))


def dot(a, b, dims=NN):
    return lax.dot_general(a, b, dims, preferred_element_type=f32)


def widen(v, axis):
    first = lax.slice_in_dim(v, 0, HALF, axis=axis)
    last = lax.slice_in_dim(v, HALF, QUAD, axis=axis)
    shape = list(v.shape)
    shape[axis] = GAP
    return jnp.concatenate([first, jnp.zeros(shape, v.dtype), last], axis)


def narrow(v, axis):
    first = lax.slice_in_dim(v, 0, HALF, axis=axis)
    last = lax.slice_in_dim(v, HALF + GAP, LANES, axis=axis)
    return jnp.concatenate([first, last], axis)


def spread_channels(v):
    lead = v.shape[:-1]
    return widen(v.reshape(lead + (QUADS, QUAD)), len(lead) + 1).reshape(lead + (QUADS * LANES,))


def pack_channels(v):
    lead = v.shape[:-1]
    return narrow(v.reshape(lead + (QUADS, LANES)), len(lead) + 1).reshape(lead + (QUADS * QUAD,))


def half_rows(v, position):
    pad = 256 - HALF
    padded = jnp.pad(v, ((pad, pad),) + ((0, 0),) * (v.ndim - 1))
    return lax.dynamic_slice_in_dim(padded, pad * (1 - position % 2), 256, 0)


def unhalf_rows(v, position):
    return lax.dynamic_slice_in_dim(v, (256 - HALF) * (position % 2), HALF, 0)


def spread_inner(v):
    lead = v.shape[:-1]
    parts = v.shape[-1] // SE_PART
    v = v.reshape(lead + (parts, SE_PART))
    v = jnp.pad(v, ((0, 0),) * (v.ndim - 1) + ((0, SE_LANES - SE_PART),))
    return v.reshape(lead + (parts * SE_LANES,))


def pack_inner(v):
    lead = v.shape[:-1]
    parts = v.shape[-1] // SE_LANES
    return v.reshape(lead + (parts, SE_LANES))[..., :SE_PART].reshape(lead + (parts * SE_PART,))


def flips(axis, bit):
    return [(i, i ^ bit) for i in range(lax.axis_size(axis))]


def spread(v, axis):
    n = lax.axis_size(axis)
    return lax.all_to_all(
        jnp.broadcast_to(v[None], (n,) + v.shape), axis, split_axis=0, concat_axis=0, tiled=True
    )


def sum_axis(v, axis):
    n = lax.axis_size(axis)
    bit = 1
    while bit < n:
        v = v + lax.ppermute(v, axis, flips(axis, bit))
        bit *= 2
    return v


def total(v):
    return jnp.sum(spread(jnp.sum(spread(v, "dp"), 0), "mp"), 0)


def tie(*values):
    return lax.optimization_barrier(values)


def gather_all(v):
    n = lax.axis_size("dp") * lax.axis_size("mp")
    out = lax.all_to_all(
        jnp.broadcast_to(v[None], (n,) + v.shape),
        ("dp", "mp"),
        split_axis=0,
        concat_axis=0,
        tiled=True,
    )
    return out


def in_order(parts, me):
    out = []
    for j in range(len(parts)):
        v = parts[0]
        for k in range(1, len(parts)):
            v = jnp.where((me ^ k) == j, parts[k], v)
        out.append(v)
    return jnp.stack(out)


def exchange(blocks):
    return lax.all_to_all(blocks, "mp", split_axis=0, concat_axis=0, tiled=True)


def parts_mp(v):
    return [v] + [lax.ppermute(v, "mp", flips("mp", k)) for k in range(1, lax.axis_size("mp"))]


def gather_mp(v):
    return in_order(parts_mp(v), lax.axis_index("mp"))


def diagonal(axis_size):
    return [(i, i ^ 4 if i % 2 == 0 else i ^ 2) for i in range(axis_size)]


def gather_sides(v):
    return lax.ppermute(v, "dp", flips("dp", 2)), lax.ppermute(v, "dp", flips("dp", 4))


def gather_corner(across, up):
    even = lax.axis_index("dp") % 2 == 0
    return lax.ppermute(jnp.where(even, across, up), "dp", diagonal(8))


def gather_twins(own, across, up, corner):
    pieces = []
    for got in (own, across, up, corner):
        pieces += [got, lax.ppermute(got, "dp", flips("dp", 1))]
    return pieces


def gather_dp(v):
    across, up = gather_sides(v)
    return gather_twins(v, across, up, gather_corner(across, up))


def scatter_corner(kept, got):
    return lax.ppermute(twin_sum(kept, got), "dp", diagonal(8))


def from_twin(sent):
    return lax.ppermute(sent, "dp", flips("dp", 1))


def scatter_sides(across, up):
    return lax.ppermute(across, "dp", flips("dp", 2)), lax.ppermute(up, "dp", flips("dp", 4))


def scatter_mp(own, parts):
    return [own] + [lax.ppermute(v, "mp", flips("mp", k + 1)) for k, v in enumerate(parts)]


def quick_mesh():
    return lax.axis_size("dp") == 2 * QUADS and lax.axis_size("mp") == QUADS


def slab_blocks(v):
    n = lax.axis_size("mp")
    blocks = v.T.reshape(n, v.shape[1] // n, v.shape[0])
    return widen(blocks, 2) if quick_mesh() else blocks


def quad_blocks(blocks):
    if quick_mesh():
        return blocks
    rows = blocks.shape[1]
    full = spread_channels(blocks.transpose(1, 0, 2).reshape(rows, -1))
    return full.reshape(rows, QUADS, LANES).transpose(1, 0, 2)


def out_blocks(blocks):
    if quick_mesh():
        return blocks
    n = lax.axis_size("mp")
    rows = blocks.shape[1]
    full = pack_channels(blocks.transpose(1, 0, 2).reshape(rows, -1))
    return full.reshape(rows, n, -1).transpose(1, 0, 2)


def natural_channels(blocks, channels, dtype):
    return blocks.astype(dtype).reshape(-1, channels).T


def out_channels(parts, channels, dtype, me):
    return natural_channels(join_rows(parts, dtype, me), channels, dtype)


def shard_square(w):
    return half_rows(widen(w.astype(bf16), 1), lax.axis_index("dp")).T


def gather_square(w):
    full = lax.all_gather(w.astype(bf16), "mp", axis=1, tiled=True)
    full = lax.all_gather(full, "dp", axis=0, tiled=True)
    full = spread_channels(spread_channels(full).T)
    return full.reshape(QUADS, LANES, 2 * QUADS, 256).transpose(2, 0, 1, 3)


def scatter_square(g):
    full = g.transpose(1, 2, 0, 3).reshape(QUADS * LANES, 2 * QUADS * 256)
    full = pack_channels(pack_channels(full).T)
    part = lax.psum_scatter(full, "dp", scatter_dimension=0, tiled=True)
    return lax.psum_scatter(part, "mp", scatter_dimension=1, tiled=True).astype(f32)


def gather_kernel(w):
    low = w.astype(bf16)
    if quick_mesh():
        return gather_dp(half_rows(low, lax.axis_index("dp")).T)
    full = lax.all_gather(low, "dp", axis=0, tiled=True)
    return spread_channels(full.T).reshape(-1, 2 * QUADS, 256).transpose(1, 0, 2)


def scatter_kernel(g):
    full = pack_channels(g.transpose(1, 0, 2).reshape(g.shape[1], -1)).T
    part = lax.psum_scatter(full, "dp", scatter_dimension=0, tiled=True).astype(f32)
    return lax.psum(part, "mp")


SE_ROWS = 256
HEAD_ROWS = 208
PROTO_ROWS = 96
QUEUE_ROWS = 32


def shard_excitation(w_squeeze, w_excite):
    d = lax.axis_index("dp")
    squeeze = lax.dynamic_slice_in_dim(w_squeeze, d * HALF, HALF, 0).astype(bf16)
    squeeze = spread_inner(half_rows(squeeze, d))
    excite = lax.dynamic_slice_in_dim(w_excite, d * SE_PART, SE_PART, 0).astype(bf16)
    excite = jnp.pad(widen(excite, 1), ((0, SE_LANES - SE_PART), (0, 0)))
    excite = jnp.concatenate([excite[:, 128 * i : 128 * (i + 1)] for i in range(4)], 0)
    return jnp.concatenate([squeeze, excite], 1)


def shard_head(w_project, prototypes, queue_rows, pairing):
    d = lax.axis_index("dp")
    m = lax.axis_index("mp")
    project = lax.dynamic_slice_in_dim(w_project, d * HALF, HALF, 0).astype(bf16)
    project = half_rows(project, d).T
    protos = jnp.pad(prototypes.T, ((0, 2 * QUADS * PROTO_ROWS - prototypes.shape[1]), (0, 0)))
    protos = lax.dynamic_slice_in_dim(protos, d * PROTO_ROWS, PROTO_ROWS, 0).astype(bf16)
    queue = lax.dynamic_slice_in_dim(queue_rows, m * QUEUE_ROWS, QUEUE_ROWS, 0)
    size = pairing.shape[0]
    lane = lax.broadcasted_iota(jnp.int32, (size, 256), 1)
    pairing = jnp.where(lane // size == d, jnp.tile(pairing, (1, 256 // size)), 0.0)
    pairing = jnp.pad(pairing.astype(bf16), ((0, 16 - size), (0, 0)))
    return jnp.concatenate([project, protos, queue, pairing], 0)


def gather_excitation(w_squeeze, w_excite):
    squeeze = lax.all_gather(w_squeeze.astype(bf16), "mp", axis=1, tiled=True)
    excite = lax.all_gather(w_excite.astype(bf16), "mp", axis=1, tiled=True)
    squeeze = spread_channels(spread_inner(squeeze).T).T
    excite = spread_inner(spread_channels(excite).T).T
    squeeze = squeeze.reshape(8, 256, 4, 128).transpose(0, 2, 1, 3)
    excite = excite.reshape(8, 64, 4, 4, 128).transpose(0, 2, 3, 1, 4).reshape(8, 4, 256, 128)
    return jnp.concatenate([squeeze, excite], 3)


def gather_head(w_project, prototypes, queue_rows, pairing):
    project = lax.all_gather(w_project.astype(bf16), "mp", axis=1, tiled=True)
    protos = lax.all_gather(prototypes.astype(bf16), "mp", axis=1, tiled=True)
    queue = lax.all_gather(queue_rows, "dp", axis=0, tiled=True)
    pairs = lax.all_gather(pairing, "dp")
    return spread_channels(project.T).T, protos, queue, pairs


def block_diagonal(pairs):
    images, size = pairs.shape[:2]
    return (
        jnp.eye(images, dtype=f32)[:, None, :, None] * pairs.astype(f32)[:, :, None, :]
    ).reshape(images * size, images * size)


BRIEF = pl.CostEstimate(flops=1, bytes_accessed=1, transcendentals=0)


def params(*semantics):
    return pltpu.CompilerParams(vmem_limit_bytes=VMEM_BYTES)


def column_sums(stats_ref, a, b):
    stats_ref[0:1, :] = jnp.sum(a, 0, keepdims=True)
    stats_ref[1:2, :] = jnp.sum(b, 0, keepdims=True)


def index_scalar(axis):
    quick = quick_mesh()
    return (lax.axis_index(axis) if quick else jnp.zeros((), jnp.int32)).astype(jnp.int32)[None]


SCALAR = pl.BlockSpec(memory_space=pltpu.SMEM)


def half_block(index):
    return pl.ds(pl.multiple_of(index * 256, 256), 256)


def join_rows_kernel(me_ref, *refs):
    out_ref = refs[-1]
    for k, part in enumerate(refs[:-1]):
        v = part[...].astype(f32)
        v = jnp.concatenate([v[:, :HALF], v[:, HALF + GAP :]], 1)
        out_ref[me_ref[0] ^ k] = v.astype(out_ref.dtype)


def join_rows(parts, dtype, me):
    rows = parts[0].shape[0]
    return pl.pallas_call(
        join_rows_kernel,
        in_specs=[SCALAR] + [pl.BlockSpec(memory_space=pltpu.VMEM)] * len(parts),
        out_shape=jax.ShapeDtypeStruct((len(parts), rows, QUAD), dtype),
        compiler_params=params(),
        cost_estimate=BRIEF,
        name="join_rows",
    )(me, *parts)


def piece_list(w):
    return w if isinstance(w, list) else [w[b].reshape(-1, 256) for b in range(8)]


def half_of(ref, index):
    return ref[index // 2, :, half_block(index % 2)]


def mix_kernel(me_ref, x_ref, *refs):
    out_ref, stats_ref = refs[8:]
    turned = jnp.concatenate([half_of(x_ref, me_ref[0] ^ b) for b in range(8)], 1)
    acc = dot(turned, jnp.concatenate([refs[b][...] for b in range(8)], 1), NT)
    out_ref[...] = acc
    column_sums(stats_ref, acc, acc * acc)


def mix(x, w):
    _, rows, _ = x.shape
    width = QUADS * LANES
    return pl.pallas_call(
        mix_kernel,
        grid=(QUADS,),
        in_specs=[SCALAR, pl.BlockSpec(x.shape, lambda m: (0, 0, 0))]
        + [pl.BlockSpec((LANES, 256), lambda m: (m, 0))] * 8,
        out_specs=[
            pl.BlockSpec((rows, LANES), lambda m: (0, m)),
            pl.BlockSpec((2, LANES), lambda m: (0, m)),
        ],
        out_shape=[
            jax.ShapeDtypeStruct((rows, width), f32),
            jax.ShapeDtypeStruct((2, width), f32),
        ],
        compiler_params=params(),
        cost_estimate=BRIEF,
        name="mix",
    )(index_scalar("dp"), x, *piece_list(w))


def mix_back_kernel(rest, me_ref, g_ref, *refs):
    out_ref, hold_ref, sems = refs[8 + rest :]

    def copy(b):
        source = refs[b].at[pl.ds(0, QUADS * LANES)]
        return pltpu.make_async_copy(source, hold_ref.at[b], sems.at[b])

    for b in range(8):
        copy(b).start()
    for b in range(0, 8, 2):
        copy(b).wait()
        copy(b + 1).wait()
        pair = dot(g_ref[...], jnp.concatenate([hold_ref[b], hold_ref[b + 1]], 1))
        for i in range(2):
            index = me_ref[0] ^ (b + i)
            acc = pair[:, 256 * i : 256 * (i + 1)]
            if rest:
                acc = acc + refs[8][:, half_block(index)]
                out_ref[index // 2, :, half_block(index % 2)] = acc.astype(bf16)
            else:
                out_ref[:, half_block(index)] = acc


def mix_back(g, w, rest=None):
    rows, width = g.shape
    if rest is None:
        more, out = [], jax.ShapeDtypeStruct((rows, width), f32)
    else:
        more, out = [rest], jax.ShapeDtypeStruct((QUADS, rows, LANES), bf16)
    return pl.pallas_call(
        functools.partial(mix_back_kernel, len(more)),
        in_specs=[SCALAR, pl.BlockSpec(memory_space=pltpu.VMEM)]
        + [pl.BlockSpec(memory_space=pl.ANY)] * 8
        + [pl.BlockSpec(memory_space=pltpu.VMEM)] * len(more),
        out_specs=pl.BlockSpec(memory_space=pltpu.VMEM),
        out_shape=out,
        scratch_shapes=[
            pltpu.VMEM((8, QUADS * LANES, 256), bf16),
            pltpu.SemaphoreType.DMA((8,)),
        ],
        compiler_params=params(),
        cost_estimate=BRIEF,
        name="mix_back",
    )(index_scalar("dp"), g, *piece_list(w), *more)


def piece_grads(me_ref, x_ref, g, odd, out_ref):
    wanted = jnp.concatenate([half_of(x_ref, me_ref[0] ^ (2 * i + odd)) for i in range(4)], 1)
    result = dot(g.T, wanted)
    for i in range(4):
        out_ref[i, 0] = result[:, 256 * i : 256 * (i + 1)].astype(bf16)


def sent_grads_kernel(
    k, sloped, count, me_ref, x_ref, g_ref, a_ref, sums_ref, norms_ref, grad_sums_ref, grad_ref, out_ref
):
    grad, values = g_ref[...].astype(f32), a_ref[...]
    if sloped:
        _, _, scale, shift = affine(sums_ref[...], norms_ref[...], k, count)
        grad = grad * swish_slope(values * scale + shift)
    grad = norm_back(
        grad, values, sums_ref[...], norms_ref[...], k, grad_sums_ref[...], count
    ).astype(bf16)
    grad_ref[...] = grad
    piece_grads(me_ref, x_ref, grad, 1, out_ref)


PIECES = jax.ShapeDtypeStruct((4, QUADS, LANES, 256), bf16)


def pieces_spec():
    return pl.BlockSpec((4, 1, LANES, 256), lambda m: (0, m, 0, 0))


def sent_grads(x, g, a, sums, norms, k, grad_sums, count, sloped):
    rows, width = a.shape
    return pl.pallas_call(
        functools.partial(sent_grads_kernel, k, sloped, count),
        grid=(QUADS,),
        in_specs=[
            SCALAR, pl.BlockSpec(x.shape, lambda m: (0, 0, 0)), quad_spec(rows), quad_spec(rows),
            quad_spec(2), quad_spec(6), quad_spec(2),
        ],
        out_specs=[quad_spec(rows), pieces_spec()],
        out_shape=[jax.ShapeDtypeStruct((rows, width), bf16), PIECES],
        compiler_params=params(),
        cost_estimate=BRIEF,
        name="sent_grads",
    )(index_scalar("dp"), x, g, a, sums, norms, grad_sums)


def all_grads_kernel(
    k, count, x_ref, g_ref, a_ref, sums_ref, norms_ref, grad_sums_ref, grad_ref, out_ref
):
    grad = norm_back(
        g_ref[...], a_ref[...], sums_ref[...], norms_ref[...], k, grad_sums_ref[...], count
    ).astype(bf16)
    grad_ref[...] = grad
    turned = grad.T
    for q in range(QUADS):
        result = dot(turned, x_ref[q])
        for i in range(2):
            out_ref[2 * q + i, 0] = result[:, 256 * i : 256 * (i + 1)].astype(bf16)


def all_grads(x, g, a, sums, norms, k, grad_sums, count):
    rows, width = a.shape
    return pl.pallas_call(
        functools.partial(all_grads_kernel, k, count),
        grid=(QUADS,),
        in_specs=[
            pl.BlockSpec(x.shape, lambda m: (0, 0, 0)), quad_spec(rows), quad_spec(rows),
            quad_spec(2), quad_spec(6), quad_spec(2),
        ],
        out_specs=[
            quad_spec(rows), pl.BlockSpec((8, 1, LANES, 256), lambda m: (0, m, 0, 0)),
        ],
        out_shape=[
            jax.ShapeDtypeStruct((rows, width), bf16),
            jax.ShapeDtypeStruct((8, QUADS, LANES, 256), bf16),
        ],
        compiler_params=params(),
        cost_estimate=BRIEF,
        name="all_grads",
    )(x, g, a, sums, norms, grad_sums)


def kept_grads_kernel(me_ref, x_ref, g_ref, out_ref):
    piece_grads(me_ref, x_ref, g_ref[...], 0, out_ref)


def kept_grads(x, g):
    rows, width = g.shape
    return pl.pallas_call(
        kept_grads_kernel,
        grid=(QUADS,),
        in_specs=[SCALAR, pl.BlockSpec(x.shape, lambda m: (0, 0, 0)), quad_spec(rows)],
        out_specs=pieces_spec(),
        out_shape=PIECES,
        compiler_params=params(),
        cost_estimate=BRIEF,
        name="kept_grads",
    )(index_scalar("dp"), x, g)


def entry_spec(shape, i, steps):
    return pl.BlockSpec((None, shape[1] // steps) + shape[2:], lambda m, i=i: (i, m, 0, 0))


def twin_sum_kernel(a_ref, b_ref, out_ref):
    out_ref[...] = (a_ref[...].astype(f32) + b_ref[...].astype(f32)).astype(bf16)


def twin_sum(kept, got):
    shape = kept.shape
    steps = min(2, shape[1])
    return pl.pallas_call(
        twin_sum_kernel,
        grid=(steps,),
        in_specs=[entry_spec(shape, 3, steps)] * 2,
        out_specs=pl.BlockSpec((shape[1] // steps,) + shape[2:], lambda m: (m, 0, 0)),
        out_shape=jax.ShapeDtypeStruct(shape[1:], bf16),
        compiler_params=params(),
        cost_estimate=BRIEF,
        name="twin_sum",
    )(kept, got)


def corner_sums_kernel(me_ref, a1_ref, b1_ref, a2_ref, b2_ref, corner_ref, across_ref, up_ref):
    even = me_ref[0] % 2 == 0
    corner = corner_ref[...].astype(f32)
    across = a1_ref[...].astype(f32) + b1_ref[...].astype(f32)
    across_ref[...] = (across + jnp.where(even, corner, 0.0)).astype(bf16)
    up = a2_ref[...].astype(f32) + b2_ref[...].astype(f32)
    up_ref[...] = (up + jnp.where(even, 0.0, corner)).astype(bf16)


def corner_sums(kept, got, corner):
    shape = kept.shape
    steps = min(2, shape[1])
    block = pl.BlockSpec((shape[1] // steps,) + shape[2:], lambda m: (m, 0, 0))
    return pl.pallas_call(
        corner_sums_kernel,
        grid=(steps,),
        in_specs=[SCALAR] + [entry_spec(shape, i, steps) for i in (1, 1, 2, 2)] + [block],
        out_specs=[block, block],
        out_shape=[jax.ShapeDtypeStruct(shape[1:], bf16)] * 2,
        compiler_params=params(),
        cost_estimate=BRIEF,
        name="corner_sums",
    )(index_scalar("dp"), kept, got, kept, got, corner)


def side_sums_kernel(me_ref, a_ref, b_ref, across_ref, up_ref, more_ref, out_ref, *parts):
    value = (
        a_ref[...].astype(f32)
        + b_ref[...].astype(f32)
        + across_ref[...].astype(f32)
        + up_ref[...].astype(f32)
    )
    rows = value.shape[0]

    @pl.when(pl.program_id(0) == 0)
    def _():
        out_ref[:rows, :] = value
        out_ref[rows:, :] = more_ref[...].astype(f32)

    for k, part in enumerate(parts):

        @pl.when(pl.program_id(0) == k + 1)
        def _(part=part):
            part[:rows, :] = value.astype(bf16)
            part[rows:, :] = more_ref[...]


def side_sums(kept, got, across, up, more):
    _, n, *shape = kept.shape
    rows = shape[0] + more.shape[1]
    entry = pl.BlockSpec((None, None, *shape), lambda k, me: (0, me[0] ^ k, 0, 0))
    block = pl.BlockSpec((None, *shape), lambda k, me: (me[0] ^ k, 0, 0))
    spec = pltpu.PrefetchScalarGridSpec(
        num_scalar_prefetch=1,
        grid=(n,),
        in_specs=[
            entry, entry, block, block,
            pl.BlockSpec((None,) + more.shape[1:], lambda k, me: (me[0] ^ k, 0, 0)),
        ],
        out_specs=[pl.BlockSpec((rows, 256), lambda k, me: (0, 0))] * n,
    )
    return pl.pallas_call(
        side_sums_kernel,
        grid_spec=spec,
        out_shape=[jax.ShapeDtypeStruct((rows, 256), f32)]
        + [jax.ShapeDtypeStruct((rows, 256), bf16)] * (n - 1),
        compiler_params=params(),
        cost_estimate=BRIEF,
        name="side_sums",
    )(index_scalar("mp"), kept, got, across, up, more)


def without_padding(value, odd):
    row = lax.broadcasted_iota(jnp.int32, (QUAD, 1), 0)
    value = jnp.where(row < HALF, value[:QUAD], value[GAP:])
    return jnp.where(odd, value[:, 256 - HALF :], value[:, :HALF])


def own_plain_kernel(me_ref, own_ref, out_ref, square_ref):
    value = without_padding(own_ref[...].astype(f32), me_ref[0] % 2 == 1)
    out_ref[...] = value
    square_ref[...] = square_sum(value)


def own_plain(v):
    return pl.pallas_call(
        own_plain_kernel,
        in_specs=[SCALAR, pl.BlockSpec(memory_space=pltpu.VMEM)],
        out_shape=[
            jax.ShapeDtypeStruct((QUAD, HALF), f32), jax.ShapeDtypeStruct((1, 1), f32),
        ],
        compiler_params=params(),
        cost_estimate=BRIEF,
        name="own_plain",
    )(index_scalar("dp"), v)


def gradient_lane(i):
    lane = lax.broadcasted_iota(jnp.int32, (2, 128), 1)
    row = lax.broadcasted_iota(jnp.int32, (2, 128), 0)
    return (lane == i) & (row == 1)


def own_square_kernel(me_ref, own_ref, *refs):
    out_ref, more_ref, squares_ref = refs[-3:]
    value = own_ref[...]
    for part in refs[:-3]:
        value = value + part[...].astype(f32)
    more = value[LANES:]
    value = without_padding(value[:LANES], me_ref[0] % 2 == 1)
    out_ref[...] = value
    more_ref[...] = more.astype(bf16)
    squares_ref[...] = jnp.where(gradient_lane(0), square_sum(value), 0.0) + jnp.where(
        gradient_lane(1), square_sum(more), 0.0
    )


def own_square(parts):
    return pl.pallas_call(
        own_square_kernel,
        in_specs=[SCALAR] + [pl.BlockSpec(memory_space=pltpu.VMEM)] * len(parts),
        out_shape=[
            jax.ShapeDtypeStruct((QUAD, HALF), f32),
            jax.ShapeDtypeStruct((parts[0].shape[0] - LANES, 256), bf16),
            jax.ShapeDtypeStruct((2, 128), f32),
        ],
        compiler_params=params(),
        cost_estimate=BRIEF,
        name="own_square",
    )(index_scalar("dp"), *parts)


def affine(sums, norms, k, count):
    mean = sums[0:1] / count
    inverse = lax.rsqrt(sums[1:2] / count - mean * mean + EPS_BN)
    scale = inverse * norms[k : k + 1]
    return mean, inverse, scale, norms[3 + k : 4 + k] - mean * scale


def quad_spec(rows):
    return pl.BlockSpec((rows, LANES), lambda q: (0, q))


def block_spec(rows):
    return pl.BlockSpec((None, rows, LANES), lambda q: (q, 0, 0))


def crop_totals(ref, crops):
    return jnp.concatenate(
        [jnp.sum(ref[pl.ds(PIXELS * c, PIXELS), :], 0, keepdims=True) for c in range(crops)], 0
    )


def turned_quad(rows):
    return pl.BlockSpec((rows, LANES), lambda k, me, *_: (0, me[0] ^ k))


def turned_block(rows):
    return pl.BlockSpec((None, rows, LANES), lambda k, me, *_: (me[0] ^ k, 0, 0))


def whole_part(rows):
    return pl.BlockSpec((rows, LANES), lambda k, *_: (0, 0))


def value_kernel(crops, count, me_ref, x_ref, a_ref, sums_ref, norms_ref, *refs):
    parts, summary_ref, work_ref = refs[:-2], refs[-2], refs[-1]
    _, _, scale, shift = affine(sums_ref[...], norms_ref[...], 2, count)
    work_ref[...] = swish(x_ref[...].astype(f32) + a_ref[...] * scale + shift)
    for k, part in enumerate(parts):

        @pl.when(pl.program_id(0) == k)
        def _(part=part):
            part[...] = work_ref[...].astype(bf16)

    summary_ref[...] = (crop_totals(work_ref, crops) / PIXELS).astype(bf16)


def block_value(x, a, sums, norms, count):
    rows, width = a.shape
    crops = rows // PIXELS
    spec = pltpu.PrefetchScalarGridSpec(
        num_scalar_prefetch=1,
        grid=(QUADS,),
        in_specs=[turned_block(rows), turned_quad(rows), turned_quad(2), turned_quad(6)],
        out_specs=[whole_part(rows)] * QUADS + [turned_quad(crops)],
        scratch_shapes=[pltpu.VMEM((rows, LANES), f32)],
    )
    return pl.pallas_call(
        functools.partial(value_kernel, crops, count),
        grid_spec=spec,
        out_shape=[jax.ShapeDtypeStruct((rows, LANES), bf16)] * QUADS
        + [jax.ShapeDtypeStruct((crops, width), bf16)],
        compiler_params=params(),
        cost_estimate=BRIEF,
        name="value",
    )(index_scalar("mp"), x, a, sums, norms)


def value_back_kernel(
    crops, count, me_ref, first_ref, x_ref, a_ref, sums_ref, norms_ref, do_ref, *refs
):
    parts, (out_ref, stats_ref, work_ref) = refs[:-3], refs[-3:]
    for k, part in enumerate(parts):

        @pl.when(pl.program_id(0) == k)
        def _(part=part):
            work_ref[...] = part[...].astype(f32)

    mean, inverse, scale, shift = affine(sums_ref[...], norms_ref[...], 2, count)
    values = a_ref[...]
    row = lax.broadcasted_iota(jnp.int32, (do_ref.shape[0], 1), 0)
    own = jnp.concatenate(
        [
            jnp.sum(jnp.where(row == first_ref[0] + c, do_ref[...], 0.0), 0, keepdims=True)
            for c in range(crops)
        ],
        0,
    )
    slope = swish_slope(x_ref[...].astype(f32) + values * scale + shift)
    grad = (work_ref[...] + rows_of_crops(own / PIXELS, values.shape[0])) * slope
    out_ref[...] = grad
    column_sums(stats_ref, grad, grad * ((values - mean) * inverse))


def value_back(first, x, a, sums, norms, dy_parts, do, count):
    rows, width = a.shape
    spec = pltpu.PrefetchScalarGridSpec(
        num_scalar_prefetch=2,
        grid=(QUADS,),
        in_specs=[
            turned_block(rows), turned_quad(rows), turned_quad(2), turned_quad(6),
            turned_quad(do.shape[0]),
        ]
        + [whole_part(rows)] * QUADS,
        out_specs=[turned_quad(rows), turned_quad(2)],
        scratch_shapes=[pltpu.VMEM((rows, LANES), f32)],
    )
    return pl.pallas_call(
        functools.partial(value_back_kernel, rows // PIXELS, count),
        grid_spec=spec,
        out_shape=[
            jax.ShapeDtypeStruct((rows, width), f32), jax.ShapeDtypeStruct((2, width), f32),
        ],
        compiler_params=params(),
        cost_estimate=BRIEF,
        name="value_back",
    )(index_scalar("mp"), first, x, a, sums, norms, do, *dy_parts)


def norm_back(grad, values, sums, norms, k, grad_sums, count):
    mean, inverse, scale, _ = affine(sums, norms, k, count)
    centred = (values - mean) * inverse
    return scale * (grad - (grad_sums[0:1] + centred * grad_sums[1:2]) / count)


def lane_mask(low, high, rows=GROUP):
    lane = lax.broadcasted_iota(jnp.int32, (rows, 256), 1)
    return (lane >= low) & (lane < high)


def dense_kernel(me_ref, *refs):
    out_ref, hold_ref = refs[8:]

    @pl.when(pl.program_id(0) == 0)
    def _():
        for b in range(8):
            hold_ref[me_ref[0] ^ b] = refs[b][...]

    even = hold_ref[2 * pl.program_id(0)].astype(f32)
    odd = hold_ref[2 * pl.program_id(0) + 1].astype(f32)
    row = lax.broadcasted_iota(jnp.int32, (256, 256), 0)
    edge = jnp.zeros((32, 256), f32)
    centre = lane_mask(96, 124) | lane_mask(132, 160)
    for tap in range(9):
        e = even[GROUP * tap : GROUP * (tap + 1)]
        o = odd[GROUP * tap : GROUP * (tap + 1)]
        first = [jnp.where(lane_mask(GROUP * g, GROUP * (g + 1)), e, 0.0) for g in range(4)]
        last = [
            jnp.where(lane_mask(32 + GROUP * g, 32 + GROUP * (g + 1)), o, 0.0) for g in range(4)
        ]
        out_ref[0, 0, tap] = jnp.concatenate(first + [edge], 0).astype(bf16)
        out_ref[0, 1, tap] = jnp.concatenate([edge] + last, 0).astype(bf16)
        across = jnp.where(centre, jnp.concatenate([e[:, 128:], o[:, :128]], 1), 0.0)
        upper = jnp.concatenate(
            [jnp.zeros((96, 256), f32), across, jnp.zeros((104, 256), f32)], 0
        )
        lower = jnp.concatenate(
            [jnp.zeros((104, 256), f32), across, jnp.zeros((96, 256), f32)], 0
        )
        out_ref[0, 2, tap] = (
            jnp.where(row < 124, upper, 0.0) + jnp.where(row >= 132, lower, 0.0)
        ).astype(bf16)


def dense_windows(kernel):
    pieces = [kernel[b] for b in range(8)]
    return pl.pallas_call(
        dense_kernel,
        grid=(QUADS,),
        in_specs=[SCALAR] + [pl.BlockSpec(memory_space=pltpu.VMEM)] * 8,
        out_specs=pl.BlockSpec((1, 3, 9, 256, 256), lambda q: (q, 0, 0, 0, 0)),
        out_shape=jax.ShapeDtypeStruct((QUADS, 3, 9, 256, 256), bf16),
        scratch_shapes=[pltpu.VMEM((8,) + pieces[0].shape, bf16)],
        compiler_params=params(),
        cost_estimate=BRIEF,
        name="dense_windows",
    )(index_scalar("dp"), *pieces)


WINDOWS = (0, 256, 128)


def place_pixels(pad_ref, moved_ref, source_ref, crops):
    for crop in range(crops):
        for row in range(HW):
            pad_ref[pl.ds(PITCH + 256 * crop + PITCH * (row + 1), HW), :] = source_ref[
                pl.ds(PIXELS * crop + HW * row, HW), :
            ]
    for shift in range(3):
        moved_ref[shift] = pad_ref[pl.ds(PITCH - 1 + shift, 256 * crops), :].astype(bf16)


def tap_rows(moved_ref, dy, dx, low, crops):
    return jnp.concatenate(
        [
            moved_ref[dx, pl.ds(256 * crop + PITCH * dy, PITCH * HW), pl.ds(low, 256)]
            for crop in range(crops)
        ],
        0,
    )


def take_pixels(target_ref, source_ref, crops):
    for crop in range(crops):
        for row in range(HW):
            target_ref[pl.ds(PIXELS * crop + HW * row, HW), :] = source_ref[
                pl.ds(PITCH * HW * crop + PITCH * row, HW), :
            ]


def swish(v):
    return v / (1.0 + jnp.exp(-v))


def swish_slope(v):
    sigma = 1.0 / (1.0 + jnp.exp(-v))
    return sigma * (1.0 + v * (1.0 - sigma))


def conv_kernel(crops, count, a_ref, sums_ref, norms_ref, w_ref, out_ref, stats_ref, pad_ref, moved_ref, wide_ref, act_ref):
    @pl.when(pl.program_id(0) == 0)
    def _():
        pad_ref[...] = jnp.zeros_like(pad_ref)

    _, _, scale, shift = affine(sums_ref[...], norms_ref[...], 0, count)
    act = swish(a_ref[...] * scale + shift)
    act_ref[...] = act.astype(bf16).astype(f32)
    place_pixels(pad_ref, moved_ref, act_ref, crops)
    for window, low in enumerate(WINDOWS):
        taps = [tap_rows(moved_ref, tap // 3, tap % 3, low, crops) for tap in range(9)]
        acc = dot(jnp.concatenate(taps, 1), w_ref[0, window].reshape(9 * 256, 256))
        if window < 2:
            wide_ref[:, pl.ds(low, 256)] = acc
        else:
            wide_ref[:, pl.ds(low, 256)] += acc
    take_pixels(act_ref, wide_ref, crops)
    result = act_ref[...].astype(bf16)
    out_ref[...] = result
    result = result.astype(f32)
    column_sums(stats_ref, result, result * result)


def conv(a, sums, norms, windows, count):
    rows, width = a.shape
    crops = rows // PIXELS
    return pl.pallas_call(
        functools.partial(conv_kernel, crops, count),
        grid=(QUADS,),
        in_specs=[
            quad_spec(rows), quad_spec(2), quad_spec(6),
            pl.BlockSpec((1, 3, 9, 256, 256), lambda q: (q, 0, 0, 0, 0)),
        ],
        out_specs=[
            pl.BlockSpec((rows, LANES), lambda q: (0, q)),
            pl.BlockSpec((2, LANES), lambda q: (0, q)),
        ],
        out_shape=[
            jax.ShapeDtypeStruct((rows, width), bf16),
            jax.ShapeDtypeStruct((2, width), f32),
        ],
        scratch_shapes=[
            pltpu.VMEM((2 * PITCH + 256 * crops, LANES), f32),
            pltpu.VMEM((3, 256 * crops, LANES), bf16),
            pltpu.VMEM((PITCH * HW * crops, LANES), f32),
            pltpu.VMEM((rows, LANES), f32),
        ],
        compiler_params=params(),
        cost_estimate=BRIEF,
        name="conv",
    )(a, sums, norms, windows)


def conv_back_kernel(
    crops, count, g_ref, a2_ref, sums2_ref, grad_sums_ref, a_ref, sums_ref, norms_ref, w_ref,
    out_ref, grads_ref, stats_ref,
    pad_ref, moved_ref, pad_x_ref, moved_x_ref, wide_ref, act_ref, hold_ref,
):
    @pl.when(pl.program_id(0) == 0)
    def _():
        pad_ref[...] = jnp.zeros_like(pad_ref)
        pad_x_ref[...] = jnp.zeros_like(pad_x_ref)

    norms = norms_ref[...]
    grad = norm_back(
        g_ref[...], a2_ref[...].astype(f32), sums2_ref[...], norms, 1, grad_sums_ref[...], count
    )
    act_ref[...] = grad.astype(bf16).astype(f32)
    place_pixels(pad_ref, moved_ref, act_ref, crops)
    values = a_ref[...]
    mean, inverse, scale, shift = affine(sums_ref[...], norms, 0, count)
    normed = values * scale + shift
    act_ref[...] = swish(normed).astype(bf16).astype(f32)
    place_pixels(pad_x_ref, moved_x_ref, act_ref, crops)
    for window, low in enumerate(WINDOWS):
        taps = [tap_rows(moved_ref, 2 - tap // 3, 2 - tap % 3, low, crops) for tap in range(9)]
        weight = jnp.concatenate([w_ref[0, window, tap] for tap in range(9)], 1)
        acc = dot(jnp.concatenate(taps, 1), weight, NT)
        if window < 2:
            wide_ref[:, pl.ds(low, 256)] = acc
        else:
            wide_ref[:, pl.ds(low, 256)] += acc
    take_pixels(act_ref, wide_ref, crops)
    result = act_ref[...].astype(bf16)
    out_ref[...] = result
    grad = result.astype(f32) * swish_slope(normed)
    column_sums(stats_ref, grad, grad * ((values - mean) * inverse))
    centre = lane_mask(96, 124) | lane_mask(132, 160)
    row = lax.broadcasted_iota(jnp.int32, (GROUP, 256), 0)
    mids = [
        tap_rows(moved_ref, 1, 1, low, crops) for low in WINDOWS
    ]
    for tap in range(9):
        pieces = []
        for window, low in enumerate(WINDOWS):
            pieces.append(
                dot(tap_rows(moved_x_ref, tap // 3, tap % 3, low, crops), mids[window], TN)
            )
        even = sum(
            jnp.where(lane_mask(GROUP * g, GROUP * (g + 1)), pieces[0][GROUP * g : GROUP * (g + 1)], 0.0)
            for g in range(4)
        )
        odd = sum(
            jnp.where(
                lane_mask(32 + GROUP * g, 32 + GROUP * (g + 1)),
                pieces[1][32 + GROUP * g : 32 + GROUP * (g + 1)],
                0.0,
            )
            for g in range(4)
        )
        across = jnp.where(
            centre, jnp.where(row < GROUP // 2, pieces[2][96:152], pieces[2][104:160]), 0.0
        )
        nothing = jnp.zeros((GROUP, 128), f32)
        even = even + jnp.concatenate([nothing, across[:, :128]], 1)
        odd = odd + jnp.concatenate([across[:, 128:], nothing], 1)
        hold_ref[0, pl.ds(GROUP * tap, GROUP), :] = even
        hold_ref[1, pl.ds(GROUP * tap, GROUP), :] = odd
    grads_ref[:, : 9 * GROUP, :] = hold_ref[...].astype(bf16)
    grads_ref[:, 9 * GROUP :, :] = jnp.zeros((2, LANES - 9 * GROUP, 256), bf16)


def conv_back(g, a2, sums2, grad_sums, a, sums, norms, windows, count):
    rows, width = a.shape
    crops = rows // PIXELS
    return pl.pallas_call(
        functools.partial(conv_back_kernel, crops, count),
        grid=(QUADS,),
        in_specs=[
            quad_spec(rows), quad_spec(rows), quad_spec(2), quad_spec(2), quad_spec(rows),
            quad_spec(2), quad_spec(6),
            pl.BlockSpec((1, 3, 9, 256, 256), lambda q: (q, 0, 0, 0, 0)),
        ],
        out_specs=[
            quad_spec(rows), pl.BlockSpec((2, LANES, 256), lambda q: (q, 0, 0)), quad_spec(2),
        ],
        scratch_shapes=[
            pltpu.VMEM((2 * PITCH + 256 * crops, LANES), f32),
            pltpu.VMEM((3, 256 * crops, LANES), bf16),
            pltpu.VMEM((2 * PITCH + 256 * crops, LANES), f32),
            pltpu.VMEM((3, 256 * crops, LANES), bf16),
            pltpu.VMEM((PITCH * HW * crops, LANES), f32),
            pltpu.VMEM((rows, LANES), f32),
            pltpu.VMEM((2, 9 * GROUP, 256), f32),
        ],
        out_shape=[
            jax.ShapeDtypeStruct((rows, width), bf16),
            jax.ShapeDtypeStruct((8, LANES, 256), bf16),
            jax.ShapeDtypeStruct((2, width), f32),
        ],
        compiler_params=params(),
        cost_estimate=BRIEF,
        name="conv_back",
    )(g, a2, sums2, grad_sums, a, sums, norms, windows)


def squeeze_weight(se_ref, d):
    return jnp.concatenate([se_ref[d, m, :, :128] for m in range(QUADS)], 1)


def excite_weight(se_ref, m):
    return jnp.concatenate(
        [
            jnp.concatenate(
                [se_ref[d, m, 64 * i : 64 * (i + 1), 128:] for i in range(4)], 1
            )
            for d in range(2 * QUADS)
        ],
        0,
    )


def rows_of_crops(values, rows):
    row = lax.broadcasted_iota(jnp.int32, (rows, 1), 0)
    out = values[0:1]
    for c in range(1, values.shape[0]):
        out = jnp.where(row >= PIXELS * c, values[c : c + 1], out)
    return out


def fetch_pieces(me_ref, pieces, hold_ref, sems, offset):
    size = hold_ref.shape[2]
    copies = [
        pltpu.make_async_copy(
            piece.at[pl.ds(offset + m * size, size)],
            hold_ref.at[me_ref[0] ^ b, m],
            sems.at[b * QUADS + m],
        )
        for b, piece in enumerate(pieces)
        for m in range(QUADS)
    ]
    for copy in copies:
        copy.start()
    return copies


def fetch_scratch(size):
    return [
        pltpu.VMEM((2 * QUADS, QUADS, size, 256), bf16),
        pltpu.SemaphoreType.DMA((8 * QUADS,)),
    ]


def gate_kernel(crops, count, me_ref, a_ref, sums_ref, norms_ref, *refs):
    h_ref, pooled_ref, squeezed_ref, act_ref, gate_ref, f2_ref, se_ref, sems = refs[8:]
    copies = fetch_pieces(me_ref, refs[:8], se_ref, sems, 0)
    rows = a_ref.shape[0]
    _, _, scale, shift = affine(sums_ref[...], norms_ref[...], 1, count)
    f2_ref[...] = swish(a_ref[...].astype(f32) * scale + shift)
    pooled = jnp.concatenate(
        [
            jnp.sum(f2_ref[pl.ds(PIXELS * c, PIXELS), :], 0, keepdims=True) / PIXELS
            for c in range(crops)
        ],
        0,
    ).astype(bf16)
    pooled_ref[...] = pooled
    for copy in copies:
        copy.wait()
    squeezed = sum(
        dot(pooled[:, 256 * d : 256 * (d + 1)], squeeze_weight(se_ref, d)) for d in range(8)
    )
    squeezed_ref[...] = squeezed
    act = swish(squeezed).astype(bf16)
    act_ref[...] = act
    for m in range(QUADS):
        lanes = pl.ds(m * LANES, LANES)
        gate = 1.0 / (1.0 + jnp.exp(-dot(act, excite_weight(se_ref, m))))
        gate_ref[:, lanes] = gate
        h_ref[m] = (f2_ref[:, lanes] * rows_of_crops(gate, rows)).astype(bf16)


def gate(a, sums, norms, se, count):
    rows, width = a.shape
    crops = rows // PIXELS
    return pl.pallas_call(
        functools.partial(gate_kernel, crops, count),
        in_specs=[SCALAR] + [pl.BlockSpec(memory_space=pltpu.VMEM)] * 3
        + [pl.BlockSpec(memory_space=pl.ANY)] * 8,
        out_shape=[
            jax.ShapeDtypeStruct((QUADS, rows, LANES), bf16),
            jax.ShapeDtypeStruct((crops, width), bf16),
            jax.ShapeDtypeStruct((crops, 512), f32),
            jax.ShapeDtypeStruct((crops, 512), bf16),
            jax.ShapeDtypeStruct((crops, width), f32),
        ],
        scratch_shapes=[pltpu.VMEM((rows, width), f32)] + fetch_scratch(SE_ROWS),
        compiler_params=params(),
        cost_estimate=BRIEF,
        name="gate",
    )(index_scalar("dp"), a, sums, norms, *se)


def gate_back_kernel(
    crops, count, me_ref, dh_ref, a_ref, sums_ref, norms_ref, gate_ref, squeezed_ref, *refs
):
    q_ref, stats_ref, excite_grad_ref, squeeze_grad_ref, work_ref, se_ref, sems = refs[8:]
    copies = fetch_pieces(me_ref, refs[:8], se_ref, sems, 0)
    rows = a_ref.shape[0]
    for m in range(QUADS):
        lanes = pl.ds(m * LANES, LANES)
        _, _, scale, shift = affine(sums_ref[:, lanes], norms_ref[:, lanes], 1, count)
        normed = a_ref[:, lanes].astype(f32) * scale + shift
        work_ref[:, lanes] = dh_ref[:, lanes] * swish(normed)
    sums = jnp.concatenate(
        [
            jnp.sum(work_ref[pl.ds(PIXELS * c, PIXELS), :], 0, keepdims=True)
            for c in range(crops)
        ],
        0,
    )
    gates = gate_ref[...]
    excite_grad = (sums * gates * (1.0 - gates)).astype(bf16)
    excite_grad_ref[...] = excite_grad
    for copy in copies:
        copy.wait()
    act_grad = sum(
        dot(excite_grad[:, m * LANES : (m + 1) * LANES], excite_weight(se_ref, m), NT)
        for m in range(QUADS)
    )
    squeeze_grad = (act_grad * swish_slope(squeezed_ref[...])).astype(bf16)
    squeeze_grad_ref[...] = squeeze_grad
    for d in range(8):
        lanes = pl.ds(d * 256, 256)
        pooled_grad = dot(squeeze_grad, squeeze_weight(se_ref, d), NT) / PIXELS
        values = a_ref[:, lanes].astype(f32)
        mean, inverse, scale, shift = affine(sums_ref[:, lanes], norms_ref[:, lanes], 1, count)
        normed = values * scale + shift
        q = (
            dh_ref[:, lanes] * rows_of_crops(gate_ref[:, lanes], rows)
            + rows_of_crops(pooled_grad, rows)
        ) * swish_slope(normed)
        q_ref[:, lanes] = q
        centred = (values - mean) * inverse
        stats_ref[0:1, lanes] = jnp.sum(q, 0, keepdims=True)
        stats_ref[1:2, lanes] = jnp.sum(q * centred, 0, keepdims=True)


def gate_back(dh, a, sums, norms, gates, squeezed, se, count):
    rows, width = a.shape
    crops = rows // PIXELS
    return pl.pallas_call(
        functools.partial(gate_back_kernel, crops, count),
        in_specs=[SCALAR] + [pl.BlockSpec(memory_space=pltpu.VMEM)] * 6
        + [pl.BlockSpec(memory_space=pl.ANY)] * 8,
        out_shape=[
            jax.ShapeDtypeStruct((rows, width), f32),
            jax.ShapeDtypeStruct((2, width), f32),
            jax.ShapeDtypeStruct((crops, width), bf16),
            jax.ShapeDtypeStruct((crops, 512), bf16),
        ],
        scratch_shapes=[pltpu.VMEM((rows, width), f32)] + fetch_scratch(SE_ROWS),
        compiler_params=params(),
        cost_estimate=BRIEF,
        name="gate_back",
    )(index_scalar("dp"), dh, a, sums, norms, gates, squeezed, *se)


def head_kernel(
    width, me_ref, summary_ref, *refs
):
    (
        loss_ref, unit_ref, score_grad_ref, embed_grad_ref, summary_grad_ref, all_ref,
        hold_ref, plan_ref, protos_ref, queue_ref, project_ref, bundle_ref, sems,
    ) = refs[8:]
    copies = fetch_pieces(me_ref, refs[:8], bundle_ref, sems, 0)
    crops = all_ref.shape[0]
    each = summary_ref.shape[1]
    for i in range(summary_ref.shape[0]):
        hold_ref[pl.ds(each * i, each), :] = summary_ref[i].astype(f32)
    all_ref[...] = hold_ref[...].astype(bf16)
    for copy in copies:
        copy.wait()
    parts = 2 * QUADS * QUADS
    for i in range(parts):
        d, m = i // QUADS, i % QUADS
        low = 64
        project_ref[d, pl.ds(64 * m, 64), :] = bundle_ref[d, m, 0:low, :]
        protos_ref[pl.ds(PROTO_ROWS * i, PROTO_ROWS), :] = bundle_ref[d, m, low : low + PROTO_ROWS, :]
        low = low + PROTO_ROWS
        queue_ref[pl.ds(QUEUE_ROWS * i, QUEUE_ROWS), :] = bundle_ref[d, m, low : low + QUEUE_ROWS, :]
    protos = protos_ref[...]
    embedded = sum(
        dot(all_ref[:, 256 * d : 256 * (d + 1)], project_ref[d], NT) for d in range(8)
    )
    scale = lax.rsqrt(jnp.sum(embedded * embedded, 1, keepdims=True) + EPS_NORM)
    unit = (embedded * scale).astype(bf16)
    unit_ref[...] = unit
    scores = dot(unit, protos, NT)
    lane = lax.broadcasted_iota(jnp.int32, (1, parts * PROTO_ROWS), 1)
    block = lane // PROTO_ROWS
    there = (block // QUADS) * PROTO_ROWS + (lane - block * PROTO_ROWS) < width
    first = jnp.where(there, jnp.exp(scores / EPS_SINK), 0.0)
    plan_ref[pl.ds(0, crops), :] = first

    size = 2 * crops

    def partial_sums(value):
        return jnp.sum(value.reshape(-1, 8, value.shape[1]), 0)

    def rows_at(i):
        return pl.ds(pl.multiple_of(crops + i * size, crops), size)

    def fill(i, column):
        rows = queue_ref[pl.ds(pl.multiple_of(i * size, size), size), :]
        value = jnp.exp(dot(rows, protos, NT) / EPS_SINK)
        plan_ref[rows_at(i), :] = value
        return column + partial_sums(value)

    steps = parts * QUEUE_ROWS // size
    column = lax.fori_loop(0, steps, fill, partial_sums(first))
    column = jnp.sum(column, 0, keepdims=True)
    large = jnp.where(column > 1e37, 2.0**-8, 1.0)
    inverse = jnp.where(there, 1.0 / (column * large), 0.0)
    for sweep in range(SINK - 1):

        def balanced(place, inverse=inverse, sweep=sweep):
            value = plan_ref[place, :]
            if sweep == 0:
                value = value * large
            value = value * inverse
            value = value * (1.0 / jnp.sum(value, 1, keepdims=True))
            plan_ref[place, :] = value
            return partial_sums(value)

        column = lax.fori_loop(
            0, steps, lambda i, column: column + balanced(rows_at(i)), balanced(pl.ds(0, crops))
        )
        inverse = jnp.where(there, 1.0 / jnp.sum(column, 0, keepdims=True), 0.0)
    value = plan_ref[pl.ds(0, crops), :] * inverse
    value = value / jnp.sum(value, 1, keepdims=True)
    pairs = jnp.concatenate(
        [bundle_ref[d, 0, HEAD_ROWS - 16 : HEAD_ROWS, :].astype(f32)[:8, :crops] for d in range(8)], 0
    )
    plan = lax.dot_general(
        pairs, value, NN, precision=lax.Precision.HIGHEST, preferred_element_type=f32
    )
    logits = scores / SOFTMAX_TEMPER
    top = jnp.max(jnp.where(there, logits, -jnp.inf), 1, keepdims=True)
    power = jnp.where(there, jnp.exp(logits - top), 0.0)
    mass = jnp.sum(power, 1, keepdims=True)
    entropy = jnp.sum(plan * (logits - (top + jnp.log(mass))), 1, keepdims=True)
    loss_ref[...] = -jnp.sum(entropy, 0, keepdims=True) / crops
    score_grad = ((power / mass - plan) / (SOFTMAX_TEMPER * crops)).astype(bf16)
    score_grad_ref[...] = score_grad.T
    unit_grad = dot(score_grad, protos)
    inner = jnp.sum(embedded * unit_grad, 1, keepdims=True)
    embed_grad = (scale * unit_grad - embedded * (scale * scale * scale * inner)).astype(bf16)
    embed_grad_ref[...] = embed_grad
    for d in range(8):
        summary_grad_ref[:, 256 * d : 256 * (d + 1)] = dot(embed_grad, project_ref[d])


def head(summary, bundle, width):
    devices, each, channels = summary.shape
    crops = devices * each
    parts = 2 * QUADS * QUADS
    return pl.pallas_call(
        functools.partial(head_kernel, width),
        in_specs=[SCALAR, pl.BlockSpec(memory_space=pltpu.VMEM)]
        + [pl.BlockSpec(memory_space=pl.ANY)] * 8,
        out_shape=[
            jax.ShapeDtypeStruct((1, 1), f32),
            jax.ShapeDtypeStruct((crops, 256), bf16),
            jax.ShapeDtypeStruct((parts * PROTO_ROWS, crops), bf16),
            jax.ShapeDtypeStruct((crops, 256), bf16),
            jax.ShapeDtypeStruct((crops, channels), f32),
            jax.ShapeDtypeStruct((crops, channels), bf16),
        ],
        scratch_shapes=[
            pltpu.VMEM((crops, channels), f32),
            pltpu.VMEM((crops + parts * QUEUE_ROWS, parts * PROTO_ROWS), f32),
            pltpu.VMEM((parts * PROTO_ROWS, 256), bf16),
            pltpu.VMEM((parts * QUEUE_ROWS, 256), bf16),
            pltpu.VMEM((8, 256, 256), bf16),
        ]
        + fetch_scratch(HEAD_ROWS),
        compiler_params=params(),
        cost_estimate=BRIEF,
        name="head",
    )(index_scalar("dp"), summary, *bundle)


def plain_head(summary, project, protos, queue, pairs):
    crops = summary.shape[0]
    embedded = dot(summary, project)
    scale = lax.rsqrt(jnp.sum(embedded * embedded, 1, keepdims=True) + EPS_NORM)
    unit = (embedded * scale).astype(bf16)
    scores = dot(unit, protos)
    plan = jnp.exp(jnp.concatenate([scores, dot(queue, protos)], 0) / EPS_SINK)
    for sweep in range(SINK):
        plan = plan / jnp.sum(plan, 0, keepdims=True)
        plan = plan / jnp.sum(plan, 1, keepdims=True)
    plan = lax.dot_general(
        pairs, plan[:crops], NN, precision=lax.Precision.HIGHEST, preferred_element_type=f32
    )
    logits = scores / SOFTMAX_TEMPER
    loss = -jnp.sum(plan * jax.nn.log_softmax(logits, axis=1)) / crops
    score_grad = ((jax.nn.softmax(logits, axis=1) - plan) / (SOFTMAX_TEMPER * crops)).astype(bf16)
    unit_grad = dot(score_grad, protos, NT)
    inner = jnp.sum(embedded * unit_grad, 1, keepdims=True)
    embed_grad = (scale * unit_grad - embedded * (scale * scale * scale * inner)).astype(bf16)
    return loss.reshape(1, 1), unit, score_grad, embed_grad, dot(embed_grad, project, NT)


def picks(rows, columns, source):
    row = lax.broadcasted_iota(jnp.int32, (rows, columns), 0)
    column = lax.broadcasted_iota(jnp.int32, (rows, columns), 1)
    return jnp.where(row == source(column), 1.0, 0.0).astype(bf16)


def narrow_lanes(v):
    return jnp.concatenate([v[:, :HALF], v[:, HALF + GAP :]], 1)


def square_sum(v):
    return jnp.sum(jnp.sum(v * v, 1, keepdims=True), 0, keepdims=True)


def small_grads_kernel(
    m_ref, small_ref, summary_ref, embed_grad_ref, score_grad_ref, unit_ref,
    squeeze_ref, excite_ref, project_ref, protos_ref, squares_ref, hold_ref,
):
    m = m_ref[0]
    devices, each, _ = small_ref.shape
    for i in range(devices):
        hold_ref[pl.ds(each * i, each), :] = small_ref[i].astype(f32)
    wide, inner = QUADS * LANES, 8 * SE_LANES

    def rows_of(base, size):
        return hold_ref[:, pl.ds(pl.multiple_of(base, 128), size)]

    squeeze_grad = rows_of(wide + inner + 128 * m, 128).astype(bf16)
    squeeze_grad = dot(
        squeeze_grad, picks(128, 2 * SE_PART, lambda c: (c // SE_PART) * SE_LANES + c % SE_PART)
    ).astype(bf16)
    squares = []
    total_square = jnp.zeros((1, 1), f32)
    for q in range(QUADS):
        pooled = narrow_lanes(rows_of(q * LANES, LANES)).astype(bf16)
        part = dot(pooled, squeeze_grad, TN)
        squeeze_ref[pl.ds(QUAD * q, QUAD), :] = part
        total_square = total_square + square_sum(part)
    squares.append(total_square)
    act = rows_of(wide, inner).astype(bf16)
    act = dot(act, picks(inner, QUAD, lambda c: (c // SE_PART) * SE_LANES + c % SE_PART)).astype(bf16)
    excite_grad = narrow_lanes(rows_of(wide + 2 * inner + LANES * m, LANES)).astype(bf16)
    part = dot(act, excite_grad, TN)
    excite_ref[...] = part
    squares.append(square_sum(part))
    embed_grad = dot(embed_grad_ref[...], picks(256, 64, lambda c: 64 * m + c)).astype(bf16)
    summary = jnp.concatenate(
        [
            narrow_lanes(summary_ref[:, q * LANES : (q + 1) * LANES].astype(f32))
            for q in range(QUADS)
        ],
        1,
    ).astype(bf16)
    part = dot(embed_grad, summary, TN)
    project_ref[...] = part
    squares.append(square_sum(part))
    total_square = jnp.zeros((1, 1), f32)
    last = protos_ref.shape[0]
    for d in range(8):
        place = pl.ds(pl.multiple_of((QUADS * d + m) * PROTO_ROWS, PROTO_ROWS), PROTO_ROWS)
        part = dot(score_grad_ref[place, :], unit_ref[...])
        size = min(PROTO_ROWS, last - PROTO_ROWS * d)
        protos_ref[pl.ds(PROTO_ROWS * d, size), :] = part[:size]
        total_square = total_square + square_sum(part)
    squares.append(total_square)
    lane = lax.broadcasted_iota(jnp.int32, (1, 128), 1)
    squares_ref[...] = sum(jnp.where(lane == i, v, 0.0) for i, v in enumerate(squares))


def small_grads(small, summary, embed_grad, score_grad, unit, width):
    crops = summary.shape[0]
    return pl.pallas_call(
        small_grads_kernel,
        in_specs=[SCALAR] + [pl.BlockSpec(memory_space=pltpu.VMEM)] * 5,
        out_shape=[
            jax.ShapeDtypeStruct((QUADS * QUAD, 2 * SE_PART), f32),
            jax.ShapeDtypeStruct((QUAD, QUAD), f32),
            jax.ShapeDtypeStruct((64, QUADS * QUAD), f32),
            jax.ShapeDtypeStruct((width, 256), f32),
            jax.ShapeDtypeStruct((1, 128), f32),
        ],
        scratch_shapes=[pltpu.VMEM((crops, small.shape[2]), f32)],
        compiler_params=params(),
        cost_estimate=BRIEF,
        name="small_grads",
    )(index_scalar("mp"), small, summary, embed_grad, score_grad, unit)


def own_kernel_kernel(me_ref, v_ref, out_ref):
    value = v_ref[: 9 * GROUP].astype(f32)
    out_ref[...] = jnp.where(me_ref[0] % 2 == 1, value[:, 256 - HALF :], value[:, :HALF])


def own_kernel(v):
    return pl.pallas_call(
        own_kernel_kernel,
        in_specs=[SCALAR, pl.BlockSpec(memory_space=pltpu.VMEM)],
        out_shape=jax.ShapeDtypeStruct((9 * GROUP, HALF), f32),
        compiler_params=params(),
        cost_estimate=BRIEF,
        name="own_kernel",
    )(index_scalar("dp"), v)


def weight_sums_kernel(*refs):
    lane = lax.broadcasted_iota(jnp.int32, (1, 128), 1)
    refs[-1][...] = sum(
        jnp.where(lane == i, square_sum(ref[...]), 0.0) for i, ref in enumerate(refs[:-1])
    )


def weight_sums(weights):
    values = [w if w.shape[1] == 2 * SE_PART or w.shape[0] == w.shape[1] else w.T for w in weights]
    return pl.pallas_call(
        weight_sums_kernel,
        out_shape=jax.ShapeDtypeStruct((1, 128), f32),
        compiler_params=params(),
        cost_estimate=BRIEF,
        name="weight_sums",
    )(*values)


def squares_kernel(
    n_dp, n_mp, weights_ref, norms_ref, small_ref, expand_ref, g1_ref, g2_ref, g3_ref, out_ref,
):
    lane = lax.broadcasted_iota(jnp.int32, (1, 128), 1)

    def at(i, v):
        return jnp.where(lane == i, v, 0.0)

    portions = at(0, 1.0) + at(1, 1.0 / n_mp) + at(4, 1.0)
    for i in (2, 3, 5, 6):
        portions = portions + at(i, 1.0 / n_dp)
    weights = weights_ref[...] * portions
    small = small_ref[...]
    grads = at(4, expand_ref[...])
    for i, k in enumerate((2, 3, 5, 6)):
        grads = grads + at(k, small[:, i : i + 1] / n_dp)
    everywhere = 1.0 / (n_dp * n_mp)
    for k, ref in enumerate((g1_ref, g2_ref, g3_ref)):
        for row, first in ((1, 7), (0, 10)):
            grads = grads + at(first + k, square_sum(ref[row : row + 1, :]) * everywhere)
        weights = weights + at(7 + k, square_sum(norms_ref[k : k + 1, :]) * everywhere)
        weights = weights + at(10 + k, square_sum(norms_ref[3 + k : 4 + k, :]) * everywhere)
    out_ref[0:1, :] = weights
    out_ref[1:2, :] = grads


def squares(n_dp, n_mp, *values):
    return pl.pallas_call(
        functools.partial(squares_kernel, n_dp, n_mp),
        out_shape=jax.ShapeDtypeStruct((2, 128), f32),
        compiler_params=params(),
        cost_estimate=BRIEF,
        name="squares",
    )(*values)


def rate_of(norm_squares, i):
    norms = jnp.sqrt(norm_squares[:, i : i + 1] + EPS_NORM)
    return TRUST * norms[0:1] / (norms[1:2] + DECAY * norms[0:1])


def step(weight, gradient, momentum, norm_squares, i):
    return MOMENTUM * momentum + rate_of(norm_squares, i) * (gradient + DECAY * weight)


def lars_prepare_kernel(*refs):
    n = len(refs) // 5
    for i in range(n):
        weight, gradient, momentum = (refs[3 * i + j] for j in range(3))
        refs[3 * n + 2 * i][...] = gradient[...] + DECAY * weight[...]
        refs[3 * n + 2 * i + 1][...] = MOMENTUM * momentum[...]


def lars_prepare(items):
    return pl.pallas_call(
        lars_prepare_kernel,
        out_shape=[jax.ShapeDtypeStruct(w.shape, f32) for w, _, _ in items for _ in range(2)],
        compiler_params=params(),
        cost_estimate=BRIEF,
        name="lars_prepare",
    )(*[v for item in items for v in item])


def lars_kernel(
    first, m_ref, squares_ref, gains_ref, biases_ref, m_gains_ref, m_biases_ref, g1_ref, g2_ref, g3_ref, *refs
):
    norm_squares = squares_ref[...]
    n = (len(refs) - 4 * first - 2) // 3
    prepared, out = refs[3 * first : 3 * first + 2 * n], refs[3 * first + 2 * n :]
    for i in range(first):
        weight, gradient, momentum = (refs[3 * i + j] for j in range(3))
        out[i][...] = step(weight[...], gradient[...], momentum[...], norm_squares, i)
    for i in range(n):
        rate = rate_of(norm_squares, first + i)
        out[first + i][...] = prepared[2 * i + 1][...] + rate * prepared[2 * i][...]
    n = n + first - 1
    lanes = pl.ds(pl.multiple_of(m_ref[0] * LANES, LANES), LANES)
    for k, ref in enumerate((g1_ref, g2_ref, g3_ref)):
        own = narrow_lanes(ref[:, lanes])
        row = slice(k, k + 1)
        out[n + 1][row, :] = step(
            gains_ref[row, :], own[1:2], m_gains_ref[row, :], norm_squares, 7 + k
        )
        out[n + 2][row, :] = step(
            biases_ref[row, :], own[0:1], m_biases_ref[row, :], norm_squares, 10 + k
        )


def lars(norm_squares, items, norm_values, prepared):
    shapes = [w.shape for w, _, _ in items] + [v.shape for v in prepared[::2]]
    shapes += [norm_values[0].shape] * 2
    values = [norm_squares, *norm_values, *[v for item in items for v in item], *prepared]
    return pl.pallas_call(
        functools.partial(lars_kernel, len(items)),
        in_specs=[SCALAR] + [pl.BlockSpec(memory_space=pltpu.VMEM)] * len(values),
        out_shape=[jax.ShapeDtypeStruct(shape, f32) for shape in shapes],
        compiler_params=params(),
        cost_estimate=BRIEF,
        name="lars",
    )(index_scalar("mp"), *values)


def plain_finish(
    small, summary, unit, score_grad, embed_grad, grad_sums, channels_here, big_grads, weights, moments
):
    n_dp, n_mp, m_index = lax.axis_size("dp"), lax.axis_size("mp"), lax.axis_index("mp")
    w_reduce, w_group, w_squeeze, w_excite, w_expand, w_project, prototypes, bn_gains, bn_biases = weights
    small = small.reshape(-1, small.shape[-1])
    wide, inner = QUADS * LANES, 8 * SE_LANES
    pooled_all = pack_channels(small[:, :wide])
    act_all = pack_inner(small[:, wide : wide + inner])
    squeeze_all = pack_inner(small[:, wide + inner : wide + 2 * inner])
    excite_all = pack_channels(small[:, wide + 2 * inner :])

    def own(v, width):
        return lax.dynamic_slice_in_dim(v, m_index * width, width, 1)

    reduce_grad, kernel_grad, expand_grad = big_grads
    gain_part = own(pack_channels(jnp.stack([v[1] for v in grad_sums])), channels_here)
    bias_part = own(pack_channels(jnp.stack([v[0] for v in grad_sums])), channels_here)
    grads = [
        reduce_grad,
        kernel_grad,
        dot(pooled_all, own(squeeze_all, w_squeeze.shape[1]), TN),
        dot(act_all, own(excite_all, w_excite.shape[1]), TN),
        expand_grad,
        dot(pack_channels(summary), own(embed_grad, w_project.shape[1]), TN),
        dot(unit, own(score_grad, prototypes.shape[1]), TN),
    ]
    portions = [1.0, 1.0 / n_mp, 1.0 / n_dp, 1.0 / n_dp, 1.0, 1.0 / n_dp, 1.0 / n_dp]

    def shares(arrays, gain, bias):
        return jnp.concatenate(
            [
                jnp.stack([jnp.sum(a * a) * p for a, p in zip(arrays, portions)]),
                jnp.sum(gain * gain, 1) / n_dp,
                jnp.sum(bias * bias, 1) / n_dp,
            ]
        )

    norms = total(
        jnp.stack([shares(weights[:7], bn_gains, bn_biases), shares(grads, gain_part, bias_part)])
    )
    stepped = [
        step(w, g, m, norms, i) for i, (w, g, m) in enumerate(zip(weights[:7], grads, moments[:7]))
    ]
    for values, part, momentum, first in (
        (bn_gains, gain_part, moments[7], 7), (bn_biases, bias_part, moments[8], 10),
    ):
        stepped.append(
            jnp.concatenate(
                [
                    step(values[k : k + 1], part[k : k + 1], momentum[k : k + 1], norms, first + k)
                    for k in range(3)
                ]
            )
        )
    return stepped, norms


def body(
    block_input, output_grad, w_reduce, w_group, w_squeeze, w_excite, w_expand, w_project,
    prototypes, bn_gains, bn_biases, m_reduce, m_group, m_squeeze, m_excite, m_expand,
    m_project, m_protos, m_gains, m_biases, queue_store, queue_slots, crop_perm,
):
    n_dp = lax.axis_size("dp")
    n_mp = lax.axis_size("mp")
    m_index = lax.axis_index("mp")
    channels_here = block_input.shape[0]
    rows = block_input.shape[1] // n_mp
    crops = rows // PIXELS
    count = rows * n_dp * n_mp
    all_crops = crops * n_dp * n_mp
    quick = quick_mesh()
    weights = [
        w_reduce, w_group, w_squeeze, w_excite, w_expand, w_project, prototypes, bn_gains, bn_biases,
    ]
    moments = [
        m_reduce, m_group, m_squeeze, m_excite, m_expand, m_project, m_protos, m_gains, m_biases,
    ]

    slot_table = (
        queue_slots[0][:, None]
        == lax.broadcasted_iota(jnp.int32, (queue_slots.shape[1], queue_store.shape[0]), 1)
    ).astype(bf16)
    queue_rows = dot(slot_table, queue_store.astype(bf16)).astype(bf16)
    order = crop_perm[0]
    pairing = (order[None, :] == jnp.bitwise_xor(order, 1)[:, None]).astype(f32)
    kernel_low = gather_kernel(w_group)
    x_blocks = slab_blocks(block_input)
    y_grad_blocks = slab_blocks(output_grad)
    norms = spread(jnp.concatenate([bn_gains, bn_biases], 0), "mp")
    norms = spread_channels(norms.transpose(1, 0, 2).reshape(norms.shape[1], -1))
    if quick:
        low = gather_mp(shard_square(w_reduce)).reshape(-1, 256)
        expand_low = shard_square(w_expand)
        se_low = shard_excitation(w_squeeze, w_excite)
        low, x_blocks, norms, expand_low, se_low, *kernel_low = tie(
            low, x_blocks, norms, expand_low, se_low, *kernel_low
        )
        across, up = gather_sides(low)
        x_blocks = exchange(x_blocks)
        windows = dense_windows(kernel_low)
        across, up, windows = tie(across, up, windows)
        corner = gather_corner(across, up)
        x_blocks, se_low = tie(x_blocks, se_low)
        se_low = spread(se_low, "mp").reshape(-1, 256)
        reduce_pieces = gather_twins(low, across, up, corner)
        head_values = tie(w_project, prototypes, queue_rows, pairing, corner)
        bundle = shard_head(*head_values[:4])
    else:
        x_blocks = exchange(x_blocks)
        y_grad_parts = list(quad_blocks(exchange(y_grad_blocks)))
        reduce_pieces = gather_square(w_reduce)
        se_pieces = list(gather_excitation(w_squeeze, w_excite).reshape(8, -1, 256))
        expand_pieces = gather_square(w_expand)
        project_low, protos_low, queue_low, pairs = gather_head(
            w_project, prototypes, queue_rows, pairing
        )
        pairs = block_diagonal(pairs)
        windows = dense_windows(kernel_low)
    x = quad_blocks(x_blocks)

    reduced, sums1 = mix(x, reduce_pieces)
    if quick:
        sums1 = sum_axis(sums1, "dp")
        sums1, se_low = tie(sums1, se_low)
        se_across, se_up = gather_sides(se_low)
        sums1 = sum_axis(sums1, "mp")
        sums1, expand_low, se_across, se_up = tie(sums1, expand_low, se_across, se_up)
        expand_low = spread(expand_low, "mp").reshape(-1, 256)
        se_corner = gather_corner(se_across, se_up)
        y_grad_parts = [
            lax.dynamic_index_in_dim(y_grad_blocks, m_index ^ k, 0, keepdims=False) for k in range(QUADS)
        ]
    else:
        sums1 = total(sums1)
    grouped, sums2 = conv(reduced, sums1, norms, windows, count)
    if quick:
        sums2, se_corner = tie(sums2, se_corner)
        se_pieces = gather_twins(se_low, se_across, se_up, se_corner)
        sums2 = sum_axis(sums2, "dp")
        sums2, expand_low = tie(sums2, expand_low)
        across, up = gather_sides(expand_low)
        sums2 = sum_axis(sums2, "mp")
    else:
        sums2 = total(sums2)
    if quick:
        sums2, bundle, y_grad_parts[1], y_grad_parts[2] = tie(
            sums2, bundle, y_grad_parts[1], y_grad_parts[2]
        )
        bundle = spread(bundle, "mp").reshape(-1, 256)
        y_grad_parts[1] = lax.ppermute(y_grad_parts[1], "mp", flips("mp", 1))
        y_grad_parts[2] = lax.ppermute(y_grad_parts[2], "mp", flips("mp", 2))
    gated, pooled, squeezed, squeeze_act, gates = gate(grouped, sums2, norms, se_pieces, count)
    if quick:
        gated, across, up = tie(gated, across, up)
        corner = gather_corner(across, up)
        corner, bundle = tie(corner, bundle)
        expand_pieces = gather_twins(expand_low, across, up, corner)
    expanded, sums3 = mix(gated, expand_pieces)
    if quick:
        sums3, bundle = tie(sums3, bundle)
        sums3 = jnp.sum(spread(sums3, "dp"), 0)
        sums3, bundle, y_grad_parts[1], y_grad_parts[2] = tie(
            sums3, bundle, y_grad_parts[1], y_grad_parts[2]
        )
        across, up = gather_sides(bundle)
        sums3 = jnp.sum(spread(sums3, "mp"), 0)
        sums3, across, up = tie(sums3, across, up)
        corner = gather_corner(across, up)
    else:
        sums3 = total(sums3)
    *y_parts, summary = block_value(x, expanded, sums3, norms, count)
    if quick:
        summary, corner = tie(summary, corner)
        bundle = gather_twins(bundle, across, up, corner)
    summary = gather_all(summary)
    if quick:
        summary, y_grad_parts[3], y_parts[1] = tie(summary, y_grad_parts[3], y_parts[1])
        y_grad_parts[3] = lax.ppermute(y_grad_parts[3], "mp", flips("mp", 3))
        y_parts[1] = lax.ppermute(y_parts[1], "mp", flips("mp", 1))

    first_crop = ((lax.axis_index("dp") * n_mp + m_index) * crops).astype(jnp.int32)[None]
    if quick:
        loss, unit, score_grad, embed_grad, summary_grad, summary = head(
            summary, bundle, prototypes.shape[1]
        )
    else:
        summary = summary.reshape(all_crops, -1)
        loss, unit, score_grad, embed_grad, summary_grad = plain_head(
            summary, project_low, protos_low, queue_low, pairs
        )

    joined_grad, grad_sums3 = value_back(
        first_crop, x, expanded, sums3, norms, y_grad_parts, summary_grad, count
    )
    if quick:
        grad_sums3, y_parts[1] = tie(grad_sums3, y_parts[1])
    grad_sums3 = total(grad_sums3)
    if quick:
        grad_sums3, y_parts[2], y_parts[3] = tie(grad_sums3, y_parts[2], y_parts[3])
        y_parts[2] = lax.ppermute(y_parts[2], "mp", flips("mp", 2))
    expanded_grad, expand_all = all_grads(
        gated, joined_grad, expanded, sums3, norms, 2, grad_sums3, count
    )
    if quick:
        expand_part = lax.psum_scatter(expand_all, "dp", scatter_dimension=0, tiled=False)
    gated_grad = mix_back(expanded_grad, expand_pieces)
    act2_grad, grad_sums2, excite_grad, squeeze_grad = gate_back(
        gated_grad, grouped, sums2, norms, gates, squeezed, se_pieces, count
    )
    small = jnp.concatenate([pooled, squeeze_act, squeeze_grad, excite_grad], 1)
    if quick:
        grad_sums2, y_parts[2] = tie(grad_sums2, y_parts[2])
    grad_sums2 = total(grad_sums2)
    if quick:
        grad_sums2, small = tie(grad_sums2, small)
    small = gather_all(small)
    act1_grad, kernel_all, grad_sums1 = conv_back(
        act2_grad, grouped, sums2, grad_sums2, reduced, sums1, norms, windows, count
    )
    if quick:
        grad_sums1, kernel_all, small, expand_part = tie(
            grad_sums1, kernel_all, small, expand_part
        )
        expand_part = lax.psum_scatter(expand_part, "mp", scatter_dimension=0, tiled=False)
    grad_sums1 = total(grad_sums1)
    if quick:
        grad_sums1, y_parts[3] = tie(grad_sums1, y_parts[3])
        y_parts[3] = lax.ppermute(y_parts[3], "mp", flips("mp", 3))
    reduced_grad, reduce_sent = sent_grads(
        x, act1_grad, reduced, sums1, norms, 0, grad_sums1, count, True
    )
    if quick:
        reduced_grad, reduce_sent, expand_part, kernel_all = tie(
            reduced_grad, reduce_sent, expand_part, kernel_all
        )
        kernel_sum = lax.psum_scatter(kernel_all, "dp", scatter_dimension=0, tiled=False)
        reduce_got = from_twin(reduce_sent)
    reduce_kept = kept_grads(x, reduced_grad)
    if quick:
        reduced_grad, reduce_got, reduce_kept = tie(reduced_grad, reduce_got, reduce_kept)
        corner = scatter_corner(reduce_kept, reduce_got)
    x_grad = out_blocks(mix_back(reduced_grad, reduce_pieces, joined_grad))
    if quick:
        x_grad, corner, y_parts[3] = tie(x_grad, corner, y_parts[3])
        x_grad = exchange(x_grad)
        across, up = corner_sums(reduce_kept, reduce_got, corner)
        across, up, small = tie(across, up, small)
        across, up = scatter_sides(across, up)
        squeeze_part, excite_part, project_part, protos_part, small_squares = small_grads(
            small, summary, embed_grad, score_grad, unit, prototypes.shape[1]
        )
        expand_grad, expand_square = own_plain(expand_part)
        across, up, small_squares, expand_square, kernel_sum = tie(
            across, up, small_squares, expand_square, kernel_sum
        )
        kernel_sum = kernel_sum.reshape(QUADS, LANES // QUADS, 256)
        own, *parts = side_sums(reduce_kept, reduce_got, across, up, kernel_sum)
        parts = scatter_mp(own, parts)
        input_grad = out_channels(list(x_grad), channels_here, f32, jnp.zeros((1,), jnp.int32))
        block_output = out_channels(y_parts, channels_here, bf16, index_scalar("mp"))
        prepared = lars_prepare(
            [
                (w_squeeze, squeeze_part, m_squeeze),
                (w_excite, excite_part, m_excite),
                (w_expand.T, expand_grad, m_expand.T),
                (w_project.T, project_part, m_project.T),
                (prototypes.T, protos_part, m_protos.T),
            ]
        )
        weight_squares = weight_sums(weights[:7])
        shares = squares(
            n_dp, n_mp, weight_squares, norms, small_squares, expand_square,
            grad_sums1, grad_sums2, grad_sums3,
        )
        parts, input_grad, block_output, shares, *prepared = tie(
            parts, input_grad, block_output, shares, *prepared
        )
        reduce_grad, kernel_sum, big_squares = own_square(parts)
        kernel_sum = parts_mp(kernel_sum)
        norm_squares = jnp.sum(spread(shares + big_squares, "dp"), 0)
        norm_squares, *kernel_sum = tie(norm_squares, *kernel_sum)
        kernel_grad = own_kernel(in_order(kernel_sum, m_index).reshape(LANES, 256))
        norm_squares = jnp.sum(spread(norm_squares, "mp"), 0)
        (
            mom_reduce, mom_group, mom_squeeze, mom_excite, mom_expand, mom_project, mom_protos,
            mom_gains, mom_biases,
        ) = lars(
            norm_squares,
            [(w_reduce.T, reduce_grad, m_reduce.T), (w_group.T, kernel_grad, m_group.T)],
            [bn_gains, bn_biases, m_gains, m_biases, grad_sums1, grad_sums2, grad_sums3], prepared,
        )
        stepped = [
            mom_reduce.T, mom_group.T, mom_squeeze, mom_excite, mom_expand.T, mom_project.T,
            mom_protos.T, mom_gains, mom_biases,
        ]
    else:
        input_grad = natural_channels(exchange(x_grad), channels_here, f32)
        block_output = natural_channels(
            exchange(out_blocks(jnp.stack(y_parts))), channels_here, bf16
        )
        big_grads = (
            scatter_square(jnp.stack([reduce_kept, reduce_sent], 1).reshape(expand_all.shape)),
            scatter_kernel(kernel_all[:, : 9 * GROUP]),
            scatter_square(expand_all),
        )
        stepped, norm_squares = plain_finish(
            small, summary, unit, score_grad, embed_grad, (grad_sums1, grad_sums2, grad_sums3),
            channels_here, big_grads, weights, moments,
        )
    param_norms = jnp.sqrt(norm_squares[:, :13].T + EPS_NORM)
    return (block_output, loss[0, 0], input_grad, *stepped, param_norms)


def solution(mesh):
    split = P("dp", "mp")
    turned = P("mp", "dp")
    rows = P("dp", None)
    columns = P(None, "mp")
    return jax.shard_map(
        body,
        mesh=mesh,
        in_specs=(
            turned, turned, split, rows, columns, columns, split, columns, columns, columns, columns,
            split, rows, columns, columns, split, columns, columns, columns, columns, rows, rows, rows,
        ),
        out_specs=(
            turned, P(), turned, split, rows, columns, columns, split, columns, columns, columns,
            columns, P(),
        ),
        check_vma=False,
    )
```

```python
import functools

import jax
import jax.numpy as jnp
import numpy as np
from jax import lax
from jax.experimental import pallas as pl
from jax.experimental.pallas import tpu as pltpu
from jax.sharding import PartitionSpec as P

HW = 14
PIXELS = HW * HW
SINK = 3
EPS_BN = 1e-05
EPS_NORM = 1e-06
EPS_SINK = 0.05
SOFTMAX_TEMPER = 0.1
TRUST = 0.001
DECAY = 1e-06
MOMENTUM = 0.9

QUADS = 4
QUAD = 504
HALF = 252
LANES = 512
GAP = LANES - QUAD
GROUP = 56
SE_PART = 63
SE_LANES = 64
PITCH = 16
VMEM_BYTES = 60 * 1024 * 1024
f32 = jnp.float32
bf16 = jnp.bfloat16
NN = (((1,), (0,)), ((), ()))
NT = (((1,), (1,)), ((), ()))
TN = (((0,), (0,)), ((), ()))


def dot(a, b, dims=NN):
    return lax.dot_general(a, b, dims, preferred_element_type=f32)


def widen(v, axis):
    first = lax.slice_in_dim(v, 0, HALF, axis=axis)
    last = lax.slice_in_dim(v, HALF, QUAD, axis=axis)
    shape = list(v.shape)
    shape[axis] = GAP
    return jnp.concatenate([first, jnp.zeros(shape, v.dtype), last], axis)


def narrow(v, axis):
    first = lax.slice_in_dim(v, 0, HALF, axis=axis)
    last = lax.slice_in_dim(v, HALF + GAP, LANES, axis=axis)
    return jnp.concatenate([first, last], axis)


def spread_channels(v):
    lead = v.shape[:-1]
    return widen(v.reshape(lead + (QUADS, QUAD)), len(lead) + 1).reshape(lead + (QUADS * LANES,))


def pack_channels(v):
    lead = v.shape[:-1]
    return narrow(v.reshape(lead + (QUADS, LANES)), len(lead) + 1).reshape(lead + (QUADS * QUAD,))


def half_rows(v, position):
    pad = 256 - HALF
    padded = jnp.pad(v, ((pad, pad),) + ((0, 0),) * (v.ndim - 1))
    return lax.dynamic_slice_in_dim(padded, pad * (1 - position % 2), 256, 0)


def unhalf_rows(v, position):
    return lax.dynamic_slice_in_dim(v, (256 - HALF) * (position % 2), HALF, 0)


def spread_inner(v):
    lead = v.shape[:-1]
    parts = v.shape[-1] // SE_PART
    v = v.reshape(lead + (parts, SE_PART))
    v = jnp.pad(v, ((0, 0),) * (v.ndim - 1) + ((0, SE_LANES - SE_PART),))
    return v.reshape(lead + (parts * SE_LANES,))


def pack_inner(v):
    lead = v.shape[:-1]
    parts = v.shape[-1] // SE_LANES
    return v.reshape(lead + (parts, SE_LANES))[..., :SE_PART].reshape(lead + (parts * SE_PART,))


def flips(axis, bit):
    return [(i, i ^ bit) for i in range(lax.axis_size(axis))]


def spread(v, axis):
    n = lax.axis_size(axis)
    return lax.all_to_all(
        jnp.broadcast_to(v[None], (n,) + v.shape), axis, split_axis=0, concat_axis=0, tiled=True
    )


def sum_axis(v, axis):
    n = lax.axis_size(axis)
    bit = 1
    while bit < n:
        v = v + lax.ppermute(v, axis, flips(axis, bit))
        bit *= 2
    return v


def total(v):
    return jnp.sum(spread(jnp.sum(spread(v, "dp"), 0), "mp"), 0)


def tie(*values):
    return lax.optimization_barrier(values)


def gather_all(v):
    n = lax.axis_size("dp") * lax.axis_size("mp")
    out = lax.all_to_all(
        jnp.broadcast_to(v[None], (n,) + v.shape),
        ("dp", "mp"),
        split_axis=0,
        concat_axis=0,
        tiled=True,
    )
    return out


def in_order(parts, me):
    out = []
    for j in range(len(parts)):
        v = parts[0]
        for k in range(1, len(parts)):
            v = jnp.where((me ^ k) == j, parts[k], v)
        out.append(v)
    return jnp.stack(out)


def exchange(blocks):
    return lax.all_to_all(blocks, "mp", split_axis=0, concat_axis=0, tiled=True)


def parts_mp(v):
    return [v] + [lax.ppermute(v, "mp", flips("mp", k)) for k in range(1, lax.axis_size("mp"))]


def gather_mp(v):
    return in_order(parts_mp(v), lax.axis_index("mp"))


def diagonal(axis_size):
    return [(i, i ^ 4 if i % 2 == 0 else i ^ 2) for i in range(axis_size)]


def gather_sides(v):
    return lax.ppermute(v, "dp", flips("dp", 2)), lax.ppermute(v, "dp", flips("dp", 4))


def gather_corner(across, up):
    even = lax.axis_index("dp") % 2 == 0
    return lax.ppermute(jnp.where(even, across, up), "dp", diagonal(8))


def gather_twins(own, across, up, corner):
    pieces = []
    for got in (own, across, up, corner):
        pieces += [got, lax.ppermute(got, "dp", flips("dp", 1))]
    return pieces


def gather_dp(v):
    across, up = gather_sides(v)
    return gather_twins(v, across, up, gather_corner(across, up))


def scatter_corner(kept, got):
    return lax.ppermute(twin_sum(kept, got), "dp", diagonal(8))


def from_twin(sent):
    return lax.ppermute(sent, "dp", flips("dp", 1))


def scatter_sides(across, up):
    return lax.ppermute(across, "dp", flips("dp", 2)), lax.ppermute(up, "dp", flips("dp", 4))


def scatter_mp(own, parts):
    return [own] + [lax.ppermute(v, "mp", flips("mp", k + 1)) for k, v in enumerate(parts)]


def quick_mesh():
    return lax.axis_size("dp") == 2 * QUADS and lax.axis_size("mp") == QUADS


def slab_blocks(v):
    n = lax.axis_size("mp")
    blocks = v.T.reshape(n, v.shape[1] // n, v.shape[0])
    return widen(blocks, 2) if quick_mesh() else blocks


def quad_blocks(blocks):
    if quick_mesh():
        return blocks
    rows = blocks.shape[1]
    full = spread_channels(blocks.transpose(1, 0, 2).reshape(rows, -1))
    return full.reshape(rows, QUADS, LANES).transpose(1, 0, 2)


def out_blocks(blocks):
    if quick_mesh():
        return blocks
    n = lax.axis_size("mp")
    rows = blocks.shape[1]
    full = pack_channels(blocks.transpose(1, 0, 2).reshape(rows, -1))
    return full.reshape(rows, n, -1).transpose(1, 0, 2)


def natural_channels(blocks, channels, dtype):
    return blocks.astype(dtype).reshape(-1, channels).T


def out_channels(parts, channels, dtype, me):
    return natural_channels(join_rows(parts, dtype, me), channels, dtype)


def shard_square(w):
    return half_rows(widen(w.astype(bf16), 1), lax.axis_index("dp")).T


def gather_square(w):
    full = lax.all_gather(w.astype(bf16), "mp", axis=1, tiled=True)
    full = lax.all_gather(full, "dp", axis=0, tiled=True)
    full = spread_channels(spread_channels(full).T)
    return full.reshape(QUADS, LANES, 2 * QUADS, 256).transpose(2, 0, 1, 3)


def scatter_square(g):
    full = g.transpose(1, 2, 0, 3).reshape(QUADS * LANES, 2 * QUADS * 256)
    full = pack_channels(pack_channels(full).T)
    part = lax.psum_scatter(full, "dp", scatter_dimension=0, tiled=True)
    return lax.psum_scatter(part, "mp", scatter_dimension=1, tiled=True).astype(f32)


def gather_kernel(w):
    low = w.astype(bf16)
    if quick_mesh():
        return gather_dp(half_rows(low, lax.axis_index("dp")).T)
    full = lax.all_gather(low, "dp", axis=0, tiled=True)
    return spread_channels(full.T).reshape(-1, 2 * QUADS, 256).transpose(1, 0, 2)


def scatter_kernel(g):
    full = pack_channels(g.transpose(1, 0, 2).reshape(g.shape[1], -1)).T
    part = lax.psum_scatter(full, "dp", scatter_dimension=0, tiled=True).astype(f32)
    return lax.psum(part, "mp")


SE_ROWS = 256
HEAD_ROWS = 208
PROTO_ROWS = 96
QUEUE_ROWS = 32


def shard_excitation(w_squeeze, w_excite):
    d = lax.axis_index("dp")
    squeeze = lax.dynamic_slice_in_dim(w_squeeze, d * HALF, HALF, 0).astype(bf16)
    squeeze = spread_inner(half_rows(squeeze, d))
    excite = lax.dynamic_slice_in_dim(w_excite, d * SE_PART, SE_PART, 0).astype(bf16)
    excite = jnp.pad(widen(excite, 1), ((0, SE_LANES - SE_PART), (0, 0)))
    excite = jnp.concatenate([excite[:, 128 * i : 128 * (i + 1)] for i in range(4)], 0)
    return jnp.concatenate([squeeze, excite], 1)


def shard_head(w_project, prototypes, queue_rows, pairing):
    d = lax.axis_index("dp")
    m = lax.axis_index("mp")
    project = lax.dynamic_slice_in_dim(w_project, d * HALF, HALF, 0).astype(bf16)
    project = half_rows(project, d).T
    protos = jnp.pad(prototypes.T, ((0, 2 * QUADS * PROTO_ROWS - prototypes.shape[1]), (0, 0)))
    protos = lax.dynamic_slice_in_dim(protos, d * PROTO_ROWS, PROTO_ROWS, 0).astype(bf16)
    queue = lax.dynamic_slice_in_dim(queue_rows, m * QUEUE_ROWS, QUEUE_ROWS, 0)
    size = pairing.shape[0]
    lane = lax.broadcasted_iota(jnp.int32, (size, 256), 1)
    pairing = jnp.where(lane // size == d, jnp.tile(pairing, (1, 256 // size)), 0.0)
    pairing = jnp.pad(pairing.astype(bf16), ((0, 16 - size), (0, 0)))
    return jnp.concatenate([project, protos, queue, pairing], 0)


def gather_excitation(w_squeeze, w_excite):
    squeeze = lax.all_gather(w_squeeze.astype(bf16), "mp", axis=1, tiled=True)
    excite = lax.all_gather(w_excite.astype(bf16), "mp", axis=1, tiled=True)
    squeeze = spread_channels(spread_inner(squeeze).T).T
    excite = spread_inner(spread_channels(excite).T).T
    squeeze = squeeze.reshape(8, 256, 4, 128).transpose(0, 2, 1, 3)
    excite = excite.reshape(8, 64, 4, 4, 128).transpose(0, 2, 3, 1, 4).reshape(8, 4, 256, 128)
    return jnp.concatenate([squeeze, excite], 3)


def gather_head(w_project, prototypes, queue_rows, pairing):
    project = lax.all_gather(w_project.astype(bf16), "mp", axis=1, tiled=True)
    protos = lax.all_gather(prototypes.astype(bf16), "mp", axis=1, tiled=True)
    queue = lax.all_gather(queue_rows, "dp", axis=0, tiled=True)
    pairs = lax.all_gather(pairing, "dp")
    return spread_channels(project.T).T, protos, queue, pairs


def block_diagonal(pairs):
    images, size = pairs.shape[:2]
    return (
        jnp.eye(images, dtype=f32)[:, None, :, None] * pairs.astype(f32)[:, :, None, :]
    ).reshape(images * size, images * size)


BRIEF = pl.CostEstimate(flops=1, bytes_accessed=1, transcendentals=0)


def params(*semantics):
    return pltpu.CompilerParams(vmem_limit_bytes=VMEM_BYTES)


def column_sums(stats_ref, a, b):
    stats_ref[0:1, :] = jnp.sum(a, 0, keepdims=True)
    stats_ref[1:2, :] = jnp.sum(b, 0, keepdims=True)


def index_scalar(axis):
    quick = quick_mesh()
    return (lax.axis_index(axis) if quick else jnp.zeros((), jnp.int32)).astype(jnp.int32)[None]


SCALAR = pl.BlockSpec(memory_space=pltpu.SMEM)


def half_block(index):
    return pl.ds(pl.multiple_of(index * 256, 256), 256)


def join_rows_kernel(me_ref, *refs):
    out_ref = refs[-1]
    for k, part in enumerate(refs[:-1]):
        v = part[...].astype(f32)
        v = jnp.concatenate([v[:, :HALF], v[:, HALF + GAP :]], 1)
        out_ref[me_ref[0] ^ k] = v.astype(out_ref.dtype)


def join_rows(parts, dtype, me):
    rows = parts[0].shape[0]
    return pl.pallas_call(
        join_rows_kernel,
        in_specs=[SCALAR] + [pl.BlockSpec(memory_space=pltpu.VMEM)] * len(parts),
        out_shape=jax.ShapeDtypeStruct((len(parts), rows, QUAD), dtype),
        compiler_params=params(),
        cost_estimate=BRIEF,
        name="join_rows",
    )(me, *parts)


def piece_list(w):
    return w if isinstance(w, list) else [w[b].reshape(-1, 256) for b in range(8)]


def half_of(ref, index):
    return ref[index // 2, :, half_block(index % 2)]


def mix_kernel(me_ref, x_ref, *refs):
    out_ref, stats_ref = refs[8:]
    turned = jnp.concatenate([half_of(x_ref, me_ref[0] ^ b) for b in range(8)], 1)
    acc = dot(turned, jnp.concatenate([refs[b][...] for b in range(8)], 1), NT)
    out_ref[...] = acc
    column_sums(stats_ref, acc, acc * acc)


def mix(x, w):
    _, rows, _ = x.shape
    width = QUADS * LANES
    return pl.pallas_call(
        mix_kernel,
        grid=(QUADS,),
        in_specs=[SCALAR, pl.BlockSpec(x.shape, lambda m: (0, 0, 0))]
        + [pl.BlockSpec((LANES, 256), lambda m: (m, 0))] * 8,
        out_specs=[
            pl.BlockSpec((rows, LANES), lambda m: (0, m)),
            pl.BlockSpec((2, LANES), lambda m: (0, m)),
        ],
        out_shape=[
            jax.ShapeDtypeStruct((rows, width), f32),
            jax.ShapeDtypeStruct((2, width), f32),
        ],
        compiler_params=params(),
        cost_estimate=BRIEF,
        name="mix",
    )(index_scalar("dp"), x, *piece_list(w))


def mix_back_kernel(rest, me_ref, g_ref, *refs):
    out_ref, hold_ref, sems = refs[8 + rest :]

    def copy(b):
        source = refs[b].at[pl.ds(0, QUADS * LANES)]
        return pltpu.make_async_copy(source, hold_ref.at[b], sems.at[b])

    for b in range(8):
        copy(b).start()
    for b in range(0, 8, 2):
        copy(b).wait()
        copy(b + 1).wait()
        pair = dot(g_ref[...], jnp.concatenate([hold_ref[b], hold_ref[b + 1]], 1))
        for i in range(2):
            index = me_ref[0] ^ (b + i)
            acc = pair[:, 256 * i : 256 * (i + 1)]
            if rest:
                acc = acc + refs[8][:, half_block(index)]
                out_ref[index // 2, :, half_block(index % 2)] = acc.astype(bf16)
            else:
                out_ref[:, half_block(index)] = acc


def mix_back(g, w, rest=None):
    rows, width = g.shape
    if rest is None:
        more, out = [], jax.ShapeDtypeStruct((rows, width), f32)
    else:
        more, out = [rest], jax.ShapeDtypeStruct((QUADS, rows, LANES), bf16)
    return pl.pallas_call(
        functools.partial(mix_back_kernel, len(more)),
        in_specs=[SCALAR, pl.BlockSpec(memory_space=pltpu.VMEM)]
        + [pl.BlockSpec(memory_space=pl.ANY)] * 8
        + [pl.BlockSpec(memory_space=pltpu.VMEM)] * len(more),
        out_specs=pl.BlockSpec(memory_space=pltpu.VMEM),
        out_shape=out,
        scratch_shapes=[
            pltpu.VMEM((8, QUADS * LANES, 256), bf16),
            pltpu.SemaphoreType.DMA((8,)),
        ],
        compiler_params=params(),
        cost_estimate=BRIEF,
        name="mix_back",
    )(index_scalar("dp"), g, *piece_list(w), *more)


def piece_grads(me_ref, x_ref, g, odd, out_ref):
    wanted = jnp.concatenate([half_of(x_ref, me_ref[0] ^ (2 * i + odd)) for i in range(4)], 1)
    result = dot(g.T, wanted)
    for i in range(4):
        out_ref[i, 0] = result[:, 256 * i : 256 * (i + 1)].astype(bf16)


def sent_grads_kernel(
    k, sloped, count, me_ref, x_ref, g_ref, a_ref, sums_ref, norms_ref, grad_sums_ref, grad_ref, out_ref
):
    grad, values = g_ref[...].astype(f32), a_ref[...]
    if sloped:
        _, _, scale, shift = affine(sums_ref[...], norms_ref[...], k, count)
        grad = grad * swish_slope(values * scale + shift)
    grad = norm_back(
        grad, values, sums_ref[...], norms_ref[...], k, grad_sums_ref[...], count
    ).astype(bf16)
    grad_ref[...] = grad
    piece_grads(me_ref, x_ref, grad, 1, out_ref)


PIECES = jax.ShapeDtypeStruct((4, QUADS, LANES, 256), bf16)


def pieces_spec():
    return pl.BlockSpec((4, 1, LANES, 256), lambda m: (0, m, 0, 0))


def sent_grads(x, g, a, sums, norms, k, grad_sums, count, sloped):
    rows, width = a.shape
    return pl.pallas_call(
        functools.partial(sent_grads_kernel, k, sloped, count),
        grid=(QUADS,),
        in_specs=[
            SCALAR, pl.BlockSpec(x.shape, lambda m: (0, 0, 0)), quad_spec(rows), quad_spec(rows),
            quad_spec(2), quad_spec(6), quad_spec(2),
        ],
        out_specs=[quad_spec(rows), pieces_spec()],
        out_shape=[jax.ShapeDtypeStruct((rows, width), bf16), PIECES],
        compiler_params=params(),
        cost_estimate=BRIEF,
        name="sent_grads",
    )(index_scalar("dp"), x, g, a, sums, norms, grad_sums)


def all_grads_kernel(
    k, count, x_ref, g_ref, a_ref, sums_ref, norms_ref, grad_sums_ref, grad_ref, out_ref
):
    grad = norm_back(
        g_ref[...], a_ref[...], sums_ref[...], norms_ref[...], k, grad_sums_ref[...], count
    ).astype(bf16)
    grad_ref[...] = grad
    turned = grad.T
    for q in range(QUADS):
        result = dot(turned, x_ref[q])
        for i in range(2):
            out_ref[2 * q + i, 0] = result[:, 256 * i : 256 * (i + 1)].astype(bf16)


def all_grads(x, g, a, sums, norms, k, grad_sums, count):
    rows, width = a.shape
    return pl.pallas_call(
        functools.partial(all_grads_kernel, k, count),
        grid=(QUADS,),
        in_specs=[
            pl.BlockSpec(x.shape, lambda m: (0, 0, 0)), quad_spec(rows), quad_spec(rows),
            quad_spec(2), quad_spec(6), quad_spec(2),
        ],
        out_specs=[
            quad_spec(rows), pl.BlockSpec((8, 1, LANES, 256), lambda m: (0, m, 0, 0)),
        ],
        out_shape=[
            jax.ShapeDtypeStruct((rows, width), bf16),
            jax.ShapeDtypeStruct((8, QUADS, LANES, 256), bf16),
        ],
        compiler_params=params(),
        cost_estimate=BRIEF,
        name="all_grads",
    )(x, g, a, sums, norms, grad_sums)


def kept_grads_kernel(me_ref, x_ref, g_ref, out_ref):
    piece_grads(me_ref, x_ref, g_ref[...], 0, out_ref)


def kept_grads(x, g):
    rows, width = g.shape
    return pl.pallas_call(
        kept_grads_kernel,
        grid=(QUADS,),
        in_specs=[SCALAR, pl.BlockSpec(x.shape, lambda m: (0, 0, 0)), quad_spec(rows)],
        out_specs=pieces_spec(),
        out_shape=PIECES,
        compiler_params=params(),
        cost_estimate=BRIEF,
        name="kept_grads",
    )(index_scalar("dp"), x, g)


def entry_spec(shape, i, steps):
    return pl.BlockSpec((None, shape[1] // steps) + shape[2:], lambda m, i=i: (i, m, 0, 0))


def twin_sum_kernel(a_ref, b_ref, out_ref):
    out_ref[...] = (a_ref[...].astype(f32) + b_ref[...].astype(f32)).astype(bf16)


def twin_sum(kept, got):
    shape = kept.shape
    steps = min(2, shape[1])
    return pl.pallas_call(
        twin_sum_kernel,
        grid=(steps,),
        in_specs=[entry_spec(shape, 3, steps)] * 2,
        out_specs=pl.BlockSpec((shape[1] // steps,) + shape[2:], lambda m: (m, 0, 0)),
        out_shape=jax.ShapeDtypeStruct(shape[1:], bf16),
        compiler_params=params(),
        cost_estimate=BRIEF,
        name="twin_sum",
    )(kept, got)


def corner_sums_kernel(me_ref, a1_ref, b1_ref, a2_ref, b2_ref, corner_ref, across_ref, up_ref):
    even = me_ref[0] % 2 == 0
    corner = corner_ref[...].astype(f32)
    across = a1_ref[...].astype(f32) + b1_ref[...].astype(f32)
    across_ref[...] = (across + jnp.where(even, corner, 0.0)).astype(bf16)
    up = a2_ref[...].astype(f32) + b2_ref[...].astype(f32)
    up_ref[...] = (up + jnp.where(even, 0.0, corner)).astype(bf16)


def corner_sums(kept, got, corner):
    shape = kept.shape
    steps = min(2, shape[1])
    block = pl.BlockSpec((shape[1] // steps,) + shape[2:], lambda m: (m, 0, 0))
    return pl.pallas_call(
        corner_sums_kernel,
        grid=(steps,),
        in_specs=[SCALAR] + [entry_spec(shape, i, steps) for i in (1, 1, 2, 2)] + [block],
        out_specs=[block, block],
        out_shape=[jax.ShapeDtypeStruct(shape[1:], bf16)] * 2,
        compiler_params=params(),
        cost_estimate=BRIEF,
        name="corner_sums",
    )(index_scalar("dp"), kept, got, kept, got, corner)


def side_sums_kernel(me_ref, a_ref, b_ref, across_ref, up_ref, more_ref, out_ref, *parts):
    value = (
        a_ref[...].astype(f32)
        + b_ref[...].astype(f32)
        + across_ref[...].astype(f32)
        + up_ref[...].astype(f32)
    )
    rows = value.shape[0]

    @pl.when(pl.program_id(0) == 0)
    def _():
        out_ref[:rows, :] = value
        out_ref[rows:, :] = more_ref[...].astype(f32)

    for k, part in enumerate(parts):

        @pl.when(pl.program_id(0) == k + 1)
        def _(part=part):
            part[:rows, :] = value.astype(bf16)
            part[rows:, :] = more_ref[...]


def side_sums(kept, got, across, up, more):
    _, n, *shape = kept.shape
    rows = shape[0] + more.shape[1]
    entry = pl.BlockSpec((None, None, *shape), lambda k, me: (0, me[0] ^ k, 0, 0))
    block = pl.BlockSpec((None, *shape), lambda k, me: (me[0] ^ k, 0, 0))
    spec = pltpu.PrefetchScalarGridSpec(
        num_scalar_prefetch=1,
        grid=(n,),
        in_specs=[
            entry, entry, block, block,
            pl.BlockSpec((None,) + more.shape[1:], lambda k, me: (me[0] ^ k, 0, 0)),
        ],
        out_specs=[pl.BlockSpec((rows, 256), lambda k, me: (0, 0))] * n,
    )
    return pl.pallas_call(
        side_sums_kernel,
        grid_spec=spec,
        out_shape=[jax.ShapeDtypeStruct((rows, 256), f32)]
        + [jax.ShapeDtypeStruct((rows, 256), bf16)] * (n - 1),
        compiler_params=params(),
        cost_estimate=BRIEF,
        name="side_sums",
    )(index_scalar("mp"), kept, got, across, up, more)


def without_padding(value, odd):
    row = lax.broadcasted_iota(jnp.int32, (QUAD, 1), 0)
    value = jnp.where(row < HALF, value[:QUAD], value[GAP:])
    return jnp.where(odd, value[:, 256 - HALF :], value[:, :HALF])


def own_plain_kernel(me_ref, own_ref, out_ref, square_ref):
    value = without_padding(own_ref[...].astype(f32), me_ref[0] % 2 == 1)
    out_ref[...] = value
    square_ref[...] = square_sum(value)


def own_plain(v):
    return pl.pallas_call(
        own_plain_kernel,
        in_specs=[SCALAR, pl.BlockSpec(memory_space=pltpu.VMEM)],
        out_shape=[
            jax.ShapeDtypeStruct((QUAD, HALF), f32), jax.ShapeDtypeStruct((1, 1), f32),
        ],
        compiler_params=params(),
        cost_estimate=BRIEF,
        name="own_plain",
    )(index_scalar("dp"), v)


def gradient_lane(i):
    lane = lax.broadcasted_iota(jnp.int32, (2, 128), 1)
    row = lax.broadcasted_iota(jnp.int32, (2, 128), 0)
    return (lane == i) & (row == 1)


def own_square_kernel(me_ref, own_ref, *refs):
    out_ref, more_ref, squares_ref = refs[-3:]
    value = own_ref[...]
    for part in refs[:-3]:
        value = value + part[...].astype(f32)
    more = value[LANES:]
    value = without_padding(value[:LANES], me_ref[0] % 2 == 1)
    out_ref[...] = value
    more_ref[...] = more.astype(bf16)
    squares_ref[...] = jnp.where(gradient_lane(0), square_sum(value), 0.0) + jnp.where(
        gradient_lane(1), square_sum(more), 0.0
    )


def own_square(parts):
    return pl.pallas_call(
        own_square_kernel,
        in_specs=[SCALAR] + [pl.BlockSpec(memory_space=pltpu.VMEM)] * len(parts),
        out_shape=[
            jax.ShapeDtypeStruct((QUAD, HALF), f32),
            jax.ShapeDtypeStruct((parts[0].shape[0] - LANES, 256), bf16),
            jax.ShapeDtypeStruct((2, 128), f32),
        ],
        compiler_params=params(),
        cost_estimate=BRIEF,
        name="own_square",
    )(index_scalar("dp"), *parts)


def affine(sums, norms, k, count):
    mean = sums[0:1] / count
    inverse = lax.rsqrt(sums[1:2] / count - mean * mean + EPS_BN)
    scale = inverse * norms[k : k + 1]
    return mean, inverse, scale, norms[3 + k : 4 + k] - mean * scale


def quad_spec(rows):
    return pl.BlockSpec((rows, LANES), lambda q: (0, q))


def block_spec(rows):
    return pl.BlockSpec((None, rows, LANES), lambda q: (q, 0, 0))


def crop_totals(ref, crops):
    return jnp.concatenate(
        [jnp.sum(ref[pl.ds(PIXELS * c, PIXELS), :], 0, keepdims=True) for c in range(crops)], 0
    )


def turned_quad(rows):
    return pl.BlockSpec((rows, LANES), lambda k, me, *_: (0, me[0] ^ k))


def turned_block(rows):
    return pl.BlockSpec((None, rows, LANES), lambda k, me, *_: (me[0] ^ k, 0, 0))


def whole_part(rows):
    return pl.BlockSpec((rows, LANES), lambda k, *_: (0, 0))


def value_kernel(crops, count, me_ref, x_ref, a_ref, sums_ref, norms_ref, *refs):
    parts, summary_ref, work_ref = refs[:-2], refs[-2], refs[-1]
    _, _, scale, shift = affine(sums_ref[...], norms_ref[...], 2, count)
    work_ref[...] = swish(x_ref[...].astype(f32) + a_ref[...] * scale + shift)
    for k, part in enumerate(parts):

        @pl.when(pl.program_id(0) == k)
        def _(part=part):
            part[...] = work_ref[...].astype(bf16)

    summary_ref[...] = (crop_totals(work_ref, crops) / PIXELS).astype(bf16)


def block_value(x, a, sums, norms, count):
    rows, width = a.shape
    crops = rows // PIXELS
    spec = pltpu.PrefetchScalarGridSpec(
        num_scalar_prefetch=1,
        grid=(QUADS,),
        in_specs=[turned_block(rows), turned_quad(rows), turned_quad(2), turned_quad(6)],
        out_specs=[whole_part(rows)] * QUADS + [turned_quad(crops)],
        scratch_shapes=[pltpu.VMEM((rows, LANES), f32)],
    )
    return pl.pallas_call(
        functools.partial(value_kernel, crops, count),
        grid_spec=spec,
        out_shape=[jax.ShapeDtypeStruct((rows, LANES), bf16)] * QUADS
        + [jax.ShapeDtypeStruct((crops, width), bf16)],
        compiler_params=params(),
        cost_estimate=BRIEF,
        name="value",
    )(index_scalar("mp"), x, a, sums, norms)


def value_back_kernel(
    crops, count, me_ref, first_ref, x_ref, a_ref, sums_ref, norms_ref, do_ref, *refs
):
    parts, (out_ref, stats_ref, work_ref) = refs[:-3], refs[-3:]
    for k, part in enumerate(parts):

        @pl.when(pl.program_id(0) == k)
        def _(part=part):
            work_ref[...] = part[...].astype(f32)

    mean, inverse, scale, shift = affine(sums_ref[...], norms_ref[...], 2, count)
    values = a_ref[...]
    row = lax.broadcasted_iota(jnp.int32, (do_ref.shape[0], 1), 0)
    own = jnp.concatenate(
        [
            jnp.sum(jnp.where(row == first_ref[0] + c, do_ref[...], 0.0), 0, keepdims=True)
            for c in range(crops)
        ],
        0,
    )
    slope = swish_slope(x_ref[...].astype(f32) + values * scale + shift)
    grad = (work_ref[...] + rows_of_crops(own / PIXELS, values.shape[0])) * slope
    out_ref[...] = grad
    column_sums(stats_ref, grad, grad * ((values - mean) * inverse))


def value_back(first, x, a, sums, norms, dy_parts, do, count):
    rows, width = a.shape
    spec = pltpu.PrefetchScalarGridSpec(
        num_scalar_prefetch=2,
        grid=(QUADS,),
        in_specs=[
            turned_block(rows), turned_quad(rows), turned_quad(2), turned_quad(6),
            turned_quad(do.shape[0]),
        ]
        + [whole_part(rows)] * QUADS,
        out_specs=[turned_quad(rows), turned_quad(2)],
        scratch_shapes=[pltpu.VMEM((rows, LANES), f32)],
    )
    return pl.pallas_call(
        functools.partial(value_back_kernel, rows // PIXELS, count),
        grid_spec=spec,
        out_shape=[
            jax.ShapeDtypeStruct((rows, width), f32), jax.ShapeDtypeStruct((2, width), f32),
        ],
        compiler_params=params(),
        cost_estimate=BRIEF,
        name="value_back",
    )(index_scalar("mp"), first, x, a, sums, norms, do, *dy_parts)


def norm_back(grad, values, sums, norms, k, grad_sums, count):
    mean, inverse, scale, _ = affine(sums, norms, k, count)
    centred = (values - mean) * inverse
    return scale * (grad - (grad_sums[0:1] + centred * grad_sums[1:2]) / count)


def lane_mask(low, high, rows=GROUP):
    lane = lax.broadcasted_iota(jnp.int32, (rows, 256), 1)
    return (lane >= low) & (lane < high)


def dense_kernel(me_ref, *refs):
    out_ref, hold_ref = refs[8:]

    @pl.when(pl.program_id(0) == 0)
    def _():
        for b in range(8):
            hold_ref[me_ref[0] ^ b] = refs[b][...]

    even = hold_ref[2 * pl.program_id(0)].astype(f32)
    odd = hold_ref[2 * pl.program_id(0) + 1].astype(f32)
    row = lax.broadcasted_iota(jnp.int32, (256, 256), 0)
    edge = jnp.zeros((32, 256), f32)
    centre = lane_mask(96, 124) | lane_mask(132, 160)
    for tap in range(9):
        e = even[GROUP * tap : GROUP * (tap + 1)]
        o = odd[GROUP * tap : GROUP * (tap + 1)]
        first = [jnp.where(lane_mask(GROUP * g, GROUP * (g + 1)), e, 0.0) for g in range(4)]
        last = [
            jnp.where(lane_mask(32 + GROUP * g, 32 + GROUP * (g + 1)), o, 0.0) for g in range(4)
        ]
        out_ref[0, 0, tap] = jnp.concatenate(first + [edge], 0).astype(bf16)
        out_ref[0, 1, tap] = jnp.concatenate([edge] + last, 0).astype(bf16)
        across = jnp.where(centre, jnp.concatenate([e[:, 128:], o[:, :128]], 1), 0.0)
        upper = jnp.concatenate(
            [jnp.zeros((96, 256), f32), across, jnp.zeros((104, 256), f32)], 0
        )
        lower = jnp.concatenate(
            [jnp.zeros((104, 256), f32), across, jnp.zeros((96, 256), f32)], 0
        )
        out_ref[0, 2, tap] = (
            jnp.where(row < 124, upper, 0.0) + jnp.where(row >= 132, lower, 0.0)
        ).astype(bf16)


def dense_windows(kernel):
    pieces = [kernel[b] for b in range(8)]
    return pl.pallas_call(
        dense_kernel,
        grid=(QUADS,),
        in_specs=[SCALAR] + [pl.BlockSpec(memory_space=pltpu.VMEM)] * 8,
        out_specs=pl.BlockSpec((1, 3, 9, 256, 256), lambda q: (q, 0, 0, 0, 0)),
        out_shape=jax.ShapeDtypeStruct((QUADS, 3, 9, 256, 256), bf16),
        scratch_shapes=[pltpu.VMEM((8,) + pieces[0].shape, bf16)],
        compiler_params=params(),
        cost_estimate=BRIEF,
        name="dense_windows",
    )(index_scalar("dp"), *pieces)


WINDOWS = (0, 256, 128)


def place_pixels(pad_ref, moved_ref, source_ref, crops):
    for crop in range(crops):
        for row in range(HW):
            pad_ref[pl.ds(PITCH + 256 * crop + PITCH * (row + 1), HW), :] = source_ref[
                pl.ds(PIXELS * crop + HW * row, HW), :
            ]
    for shift in range(3):
        moved_ref[shift] = pad_ref[pl.ds(PITCH - 1 + shift, 256 * crops), :].astype(bf16)


def tap_rows(moved_ref, dy, dx, low, crops):
    return jnp.concatenate(
        [
            moved_ref[dx, pl.ds(256 * crop + PITCH * dy, PITCH * HW), pl.ds(low, 256)]
            for crop in range(crops)
        ],
        0,
    )


def take_pixels(target_ref, source_ref, crops):
    for crop in range(crops):
        for row in range(HW):
            target_ref[pl.ds(PIXELS * crop + HW * row, HW), :] = source_ref[
                pl.ds(PITCH * HW * crop + PITCH * row, HW), :
            ]


def swish(v):
    return v / (1.0 + jnp.exp(-v))


def swish_slope(v):
    sigma = 1.0 / (1.0 + jnp.exp(-v))
    return sigma * (1.0 + v * (1.0 - sigma))


def conv_kernel(crops, count, a_ref, sums_ref, norms_ref, w_ref, out_ref, stats_ref, pad_ref, moved_ref, wide_ref, act_ref):
    @pl.when(pl.program_id(0) == 0)
    def _():
        pad_ref[...] = jnp.zeros_like(pad_ref)

    _, _, scale, shift = affine(sums_ref[...], norms_ref[...], 0, count)
    act = swish(a_ref[...] * scale + shift)
    act_ref[...] = act.astype(bf16).astype(f32)
    place_pixels(pad_ref, moved_ref, act_ref, crops)
    for window, low in enumerate(WINDOWS):
        taps = [tap_rows(moved_ref, tap // 3, tap % 3, low, crops) for tap in range(9)]
        acc = dot(jnp.concatenate(taps, 1), w_ref[0, window].reshape(9 * 256, 256))
        if window < 2:
            wide_ref[:, pl.ds(low, 256)] = acc
        else:
            wide_ref[:, pl.ds(low, 256)] += acc
    take_pixels(act_ref, wide_ref, crops)
    result = act_ref[...].astype(bf16)
    out_ref[...] = result
    result = result.astype(f32)
    column_sums(stats_ref, result, result * result)


def conv(a, sums, norms, windows, count):
    rows, width = a.shape
    crops = rows // PIXELS
    return pl.pallas_call(
        functools.partial(conv_kernel, crops, count),
        grid=(QUADS,),
        in_specs=[
            quad_spec(rows), quad_spec(2), quad_spec(6),
            pl.BlockSpec((1, 3, 9, 256, 256), lambda q: (q, 0, 0, 0, 0)),
        ],
        out_specs=[
            pl.BlockSpec((rows, LANES), lambda q: (0, q)),
            pl.BlockSpec((2, LANES), lambda q: (0, q)),
        ],
        out_shape=[
            jax.ShapeDtypeStruct((rows, width), bf16),
            jax.ShapeDtypeStruct((2, width), f32),
        ],
        scratch_shapes=[
            pltpu.VMEM((2 * PITCH + 256 * crops, LANES), f32),
            pltpu.VMEM((3, 256 * crops, LANES), bf16),
            pltpu.VMEM((PITCH * HW * crops, LANES), f32),
            pltpu.VMEM((rows, LANES), f32),
        ],
        compiler_params=params(),
        cost_estimate=BRIEF,
        name="conv",
    )(a, sums, norms, windows)


def conv_back_kernel(
    crops, count, g_ref, a2_ref, sums2_ref, grad_sums_ref, a_ref, sums_ref, norms_ref, w_ref,
    out_ref, grads_ref, stats_ref,
    pad_ref, moved_ref, pad_x_ref, moved_x_ref, wide_ref, act_ref, hold_ref,
):
    @pl.when(pl.program_id(0) == 0)
    def _():
        pad_ref[...] = jnp.zeros_like(pad_ref)
        pad_x_ref[...] = jnp.zeros_like(pad_x_ref)

    norms = norms_ref[...]
    grad = norm_back(
        g_ref[...], a2_ref[...].astype(f32), sums2_ref[...], norms, 1, grad_sums_ref[...], count
    )
    act_ref[...] = grad.astype(bf16).astype(f32)
    place_pixels(pad_ref, moved_ref, act_ref, crops)
    values = a_ref[...]
    mean, inverse, scale, shift = affine(sums_ref[...], norms, 0, count)
    normed = values * scale + shift
    act_ref[...] = swish(normed).astype(bf16).astype(f32)
    place_pixels(pad_x_ref, moved_x_ref, act_ref, crops)
    for window, low in enumerate(WINDOWS):
        taps = [tap_rows(moved_ref, 2 - tap // 3, 2 - tap % 3, low, crops) for tap in range(9)]
        weight = jnp.concatenate([w_ref[0, window, tap] for tap in range(9)], 1)
        acc = dot(jnp.concatenate(taps, 1), weight, NT)
        if window < 2:
            wide_ref[:, pl.ds(low, 256)] = acc
        else:
            wide_ref[:, pl.ds(low, 256)] += acc
    take_pixels(act_ref, wide_ref, crops)
    result = act_ref[...].astype(bf16)
    out_ref[...] = result
    grad = result.astype(f32) * swish_slope(normed)
    column_sums(stats_ref, grad, grad * ((values - mean) * inverse))
    centre = lane_mask(96, 124) | lane_mask(132, 160)
    row = lax.broadcasted_iota(jnp.int32, (GROUP, 256), 0)
    mids = [
        tap_rows(moved_ref, 1, 1, low, crops) for low in WINDOWS
    ]
    for tap in range(9):
        pieces = []
        for window, low in enumerate(WINDOWS):
            pieces.append(
                dot(tap_rows(moved_x_ref, tap // 3, tap % 3, low, crops), mids[window], TN)
            )
        even = sum(
            jnp.where(lane_mask(GROUP * g, GROUP * (g + 1)), pieces[0][GROUP * g : GROUP * (g + 1)], 0.0)
            for g in range(4)
        )
        odd = sum(
            jnp.where(
                lane_mask(32 + GROUP * g, 32 + GROUP * (g + 1)),
                pieces[1][32 + GROUP * g : 32 + GROUP * (g + 1)],
                0.0,
            )
            for g in range(4)
        )
        across = jnp.where(
            centre, jnp.where(row < GROUP // 2, pieces[2][96:152], pieces[2][104:160]), 0.0
        )
        nothing = jnp.zeros((GROUP, 128), f32)
        even = even + jnp.concatenate([nothing, across[:, :128]], 1)
        odd = odd + jnp.concatenate([across[:, 128:], nothing], 1)
        hold_ref[0, pl.ds(GROUP * tap, GROUP), :] = even
        hold_ref[1, pl.ds(GROUP * tap, GROUP), :] = odd
    grads_ref[:, : 9 * GROUP, :] = hold_ref[...].astype(bf16)
    grads_ref[:, 9 * GROUP :, :] = jnp.zeros((2, LANES - 9 * GROUP, 256), bf16)


def conv_back(g, a2, sums2, grad_sums, a, sums, norms, windows, count):
    rows, width = a.shape
    crops = rows // PIXELS
    return pl.pallas_call(
        functools.partial(conv_back_kernel, crops, count),
        grid=(QUADS,),
        in_specs=[
            quad_spec(rows), quad_spec(rows), quad_spec(2), quad_spec(2), quad_spec(rows),
            quad_spec(2), quad_spec(6),
            pl.BlockSpec((1, 3, 9, 256, 256), lambda q: (q, 0, 0, 0, 0)),
        ],
        out_specs=[
            quad_spec(rows), pl.BlockSpec((2, LANES, 256), lambda q: (q, 0, 0)), quad_spec(2),
        ],
        scratch_shapes=[
            pltpu.VMEM((2 * PITCH + 256 * crops, LANES), f32),
            pltpu.VMEM((3, 256 * crops, LANES), bf16),
            pltpu.VMEM((2 * PITCH + 256 * crops, LANES), f32),
            pltpu.VMEM((3, 256 * crops, LANES), bf16),
            pltpu.VMEM((PITCH * HW * crops, LANES), f32),
            pltpu.VMEM((rows, LANES), f32),
            pltpu.VMEM((2, 9 * GROUP, 256), f32),
        ],
        out_shape=[
            jax.ShapeDtypeStruct((rows, width), bf16),
            jax.ShapeDtypeStruct((8, LANES, 256), bf16),
            jax.ShapeDtypeStruct((2, width), f32),
        ],
        compiler_params=params(),
        cost_estimate=BRIEF,
        name="conv_back",
    )(g, a2, sums2, grad_sums, a, sums, norms, windows)


def squeeze_weight(se_ref, d):
    return jnp.concatenate([se_ref[d, m, :, :128] for m in range(QUADS)], 1)


def excite_weight(se_ref, m):
    return jnp.concatenate(
        [
            jnp.concatenate(
                [se_ref[d, m, 64 * i : 64 * (i + 1), 128:] for i in range(4)], 1
            )
            for d in range(2 * QUADS)
        ],
        0,
    )


def rows_of_crops(values, rows):
    row = lax.broadcasted_iota(jnp.int32, (rows, 1), 0)
    out = values[0:1]
    for c in range(1, values.shape[0]):
        out = jnp.where(row >= PIXELS * c, values[c : c + 1], out)
    return out


def fetch_pieces(me_ref, pieces, hold_ref, sems, offset):
    size = hold_ref.shape[2]
    copies = [
        pltpu.make_async_copy(
            piece.at[pl.ds(offset + m * size, size)],
            hold_ref.at[me_ref[0] ^ b, m],
            sems.at[b * QUADS + m],
        )
        for b, piece in enumerate(pieces)
        for m in range(QUADS)
    ]
    for copy in copies:
        copy.start()
    return copies


def fetch_scratch(size):
    return [
        pltpu.VMEM((2 * QUADS, QUADS, size, 256), bf16),
        pltpu.SemaphoreType.DMA((8 * QUADS,)),
    ]


def gate_kernel(crops, count, me_ref, a_ref, sums_ref, norms_ref, *refs):
    h_ref, pooled_ref, squeezed_ref, act_ref, gate_ref, f2_ref, se_ref, sems = refs[8:]
    copies = fetch_pieces(me_ref, refs[:8], se_ref, sems, 0)
    rows = a_ref.shape[0]
    _, _, scale, shift = affine(sums_ref[...], norms_ref[...], 1, count)
    f2_ref[...] = swish(a_ref[...].astype(f32) * scale + shift)
    pooled = jnp.concatenate(
        [
            jnp.sum(f2_ref[pl.ds(PIXELS * c, PIXELS), :], 0, keepdims=True) / PIXELS
            for c in range(crops)
        ],
        0,
    ).astype(bf16)
    pooled_ref[...] = pooled
    for copy in copies:
        copy.wait()
    squeezed = sum(
        dot(pooled[:, 256 * d : 256 * (d + 1)], squeeze_weight(se_ref, d)) for d in range(8)
    )
    squeezed_ref[...] = squeezed
    act = swish(squeezed).astype(bf16)
    act_ref[...] = act
    for m in range(QUADS):
        lanes = pl.ds(m * LANES, LANES)
        gate = 1.0 / (1.0 + jnp.exp(-dot(act, excite_weight(se_ref, m))))
        gate_ref[:, lanes] = gate
        h_ref[m] = (f2_ref[:, lanes] * rows_of_crops(gate, rows)).astype(bf16)


def gate(a, sums, norms, se, count):
    rows, width = a.shape
    crops = rows // PIXELS
    return pl.pallas_call(
        functools.partial(gate_kernel, crops, count),
        in_specs=[SCALAR] + [pl.BlockSpec(memory_space=pltpu.VMEM)] * 3
        + [pl.BlockSpec(memory_space=pl.ANY)] * 8,
        out_shape=[
            jax.ShapeDtypeStruct((QUADS, rows, LANES), bf16),
            jax.ShapeDtypeStruct((crops, width), bf16),
            jax.ShapeDtypeStruct((crops, 512), f32),
            jax.ShapeDtypeStruct((crops, 512), bf16),
            jax.ShapeDtypeStruct((crops, width), f32),
        ],
        scratch_shapes=[pltpu.VMEM((rows, width), f32)] + fetch_scratch(SE_ROWS),
        compiler_params=params(),
        cost_estimate=BRIEF,
        name="gate",
    )(index_scalar("dp"), a, sums, norms, *se)


def gate_back_kernel(
    crops, count, me_ref, dh_ref, a_ref, sums_ref, norms_ref, gate_ref, squeezed_ref, *refs
):
    q_ref, stats_ref, excite_grad_ref, squeeze_grad_ref, work_ref, se_ref, sems = refs[8:]
    copies = fetch_pieces(me_ref, refs[:8], se_ref, sems, 0)
    rows = a_ref.shape[0]
    for m in range(QUADS):
        lanes = pl.ds(m * LANES, LANES)
        _, _, scale, shift = affine(sums_ref[:, lanes], norms_ref[:, lanes], 1, count)
        normed = a_ref[:, lanes].astype(f32) * scale + shift
        work_ref[:, lanes] = dh_ref[:, lanes] * swish(normed)
    sums = jnp.concatenate(
        [
            jnp.sum(work_ref[pl.ds(PIXELS * c, PIXELS), :], 0, keepdims=True)
            for c in range(crops)
        ],
        0,
    )
    gates = gate_ref[...]
    excite_grad = (sums * gates * (1.0 - gates)).astype(bf16)
    excite_grad_ref[...] = excite_grad
    for copy in copies:
        copy.wait()
    act_grad = sum(
        dot(excite_grad[:, m * LANES : (m + 1) * LANES], excite_weight(se_ref, m), NT)
        for m in range(QUADS)
    )
    squeeze_grad = (act_grad * swish_slope(squeezed_ref[...])).astype(bf16)
    squeeze_grad_ref[...] = squeeze_grad
    for d in range(8):
        lanes = pl.ds(d * 256, 256)
        pooled_grad = dot(squeeze_grad, squeeze_weight(se_ref, d), NT) / PIXELS
        values = a_ref[:, lanes].astype(f32)
        mean, inverse, scale, shift = affine(sums_ref[:, lanes], norms_ref[:, lanes], 1, count)
        normed = values * scale + shift
        q = (
            dh_ref[:, lanes] * rows_of_crops(gate_ref[:, lanes], rows)
            + rows_of_crops(pooled_grad, rows)
        ) * swish_slope(normed)
        q_ref[:, lanes] = q
        centred = (values - mean) * inverse
        stats_ref[0:1, lanes] = jnp.sum(q, 0, keepdims=True)
        stats_ref[1:2, lanes] = jnp.sum(q * centred, 0, keepdims=True)


def gate_back(dh, a, sums, norms, gates, squeezed, se, count):
    rows, width = a.shape
    crops = rows // PIXELS
    return pl.pallas_call(
        functools.partial(gate_back_kernel, crops, count),
        in_specs=[SCALAR] + [pl.BlockSpec(memory_space=pltpu.VMEM)] * 6
        + [pl.BlockSpec(memory_space=pl.ANY)] * 8,
        out_shape=[
            jax.ShapeDtypeStruct((rows, width), f32),
            jax.ShapeDtypeStruct((2, width), f32),
            jax.ShapeDtypeStruct((crops, width), bf16),
            jax.ShapeDtypeStruct((crops, 512), bf16),
        ],
        scratch_shapes=[pltpu.VMEM((rows, width), f32)] + fetch_scratch(SE_ROWS),
        compiler_params=params(),
        cost_estimate=BRIEF,
        name="gate_back",
    )(index_scalar("dp"), dh, a, sums, norms, gates, squeezed, *se)


def head_kernel(
    width, me_ref, summary_ref, *refs
):
    (
        loss_ref, unit_ref, score_grad_ref, embed_grad_ref, summary_grad_ref, all_ref,
        hold_ref, plan_ref, protos_ref, queue_ref, project_ref, bundle_ref, sems,
    ) = refs[8:]
    copies = fetch_pieces(me_ref, refs[:8], bundle_ref, sems, 0)
    crops = all_ref.shape[0]
    each = summary_ref.shape[1]
    for i in range(summary_ref.shape[0]):
        hold_ref[pl.ds(each * i, each), :] = summary_ref[i].astype(f32)
    all_ref[...] = hold_ref[...].astype(bf16)
    for copy in copies:
        copy.wait()
    parts = 2 * QUADS * QUADS
    for i in range(parts):
        d, m = i // QUADS, i % QUADS
        low = 64
        project_ref[d, pl.ds(64 * m, 64), :] = bundle_ref[d, m, 0:low, :]
        protos_ref[pl.ds(PROTO_ROWS * i, PROTO_ROWS), :] = bundle_ref[d, m, low : low + PROTO_ROWS, :]
        low = low + PROTO_ROWS
        queue_ref[pl.ds(QUEUE_ROWS * i, QUEUE_ROWS), :] = bundle_ref[d, m, low : low + QUEUE_ROWS, :]
    protos = protos_ref[...]
    embedded = sum(
        dot(all_ref[:, 256 * d : 256 * (d + 1)], project_ref[d], NT) for d in range(8)
    )
    scale = lax.rsqrt(jnp.sum(embedded * embedded, 1, keepdims=True) + EPS_NORM)
    unit = (embedded * scale).astype(bf16)
    unit_ref[...] = unit
    scores = dot(unit, protos, NT)
    lane = lax.broadcasted_iota(jnp.int32, (1, parts * PROTO_ROWS), 1)
    block = lane // PROTO_ROWS
    there = (block // QUADS) * PROTO_ROWS + (lane - block * PROTO_ROWS) < width
    first = jnp.where(there, jnp.exp(scores / EPS_SINK), 0.0)
    plan_ref[pl.ds(0, crops), :] = first

    size, large_size = 4 * crops, 8 * crops

    def partial_sums(value):
        return jnp.sum(value.reshape(-1, 8, value.shape[1]), 0)

    def rows_at(i):
        return pl.ds(pl.multiple_of(crops + i * size, crops), size)

    def fill(i, column):
        place = pl.multiple_of(i * large_size, large_size)
        value = jnp.exp(dot(queue_ref[pl.ds(place, large_size), :], protos, NT) / EPS_SINK)
        plan_ref[pl.ds(pl.multiple_of(place + crops, crops), large_size), :] = value
        return column + partial_sums(value)

    steps = parts * QUEUE_ROWS // size
    column = lax.fori_loop(
        0, parts * QUEUE_ROWS // large_size, fill, partial_sums(first)
    )
    column = jnp.sum(column, 0, keepdims=True)
    large = jnp.where(column > 1e37, 2.0**-8, 1.0)
    inverse = jnp.where(there, 1.0 / (column * large), 0.0)
    for sweep in range(SINK - 1):

        def balanced(place, inverse=inverse, sweep=sweep):
            value = plan_ref[place, :]
            if sweep == 0:
                value = value * large
            value = value * inverse
            value = value * (1.0 / jnp.sum(value, 1, keepdims=True))
            plan_ref[place, :] = value
            return partial_sums(value)

        column = lax.fori_loop(
            0, steps, lambda i, column: column + balanced(rows_at(i)), balanced(pl.ds(0, crops))
        )
        inverse = jnp.where(there, 1.0 / jnp.sum(column, 0, keepdims=True), 0.0)
    value = plan_ref[pl.ds(0, crops), :] * inverse
    value = value / jnp.sum(value, 1, keepdims=True)
    pairs = jnp.concatenate(
        [bundle_ref[d, 0, HEAD_ROWS - 16 : HEAD_ROWS, :].astype(f32)[:8, :crops] for d in range(8)], 0
    )
    plan = lax.dot_general(
        pairs, value, NN, precision=lax.Precision.HIGHEST, preferred_element_type=f32
    )
    logits = scores / SOFTMAX_TEMPER
    top = jnp.max(jnp.where(there, logits, -jnp.inf), 1, keepdims=True)
    power = jnp.where(there, jnp.exp(logits - top), 0.0)
    mass = jnp.sum(power, 1, keepdims=True)
    entropy = jnp.sum(plan * (logits - (top + jnp.log(mass))), 1, keepdims=True)
    loss_ref[...] = -jnp.sum(entropy, 0, keepdims=True) / crops
    score_grad = ((power / mass - plan) / (SOFTMAX_TEMPER * crops)).astype(bf16)
    score_grad_ref[...] = score_grad.T
    unit_grad = dot(score_grad, protos)
    inner = jnp.sum(embedded * unit_grad, 1, keepdims=True)
    embed_grad = (scale * unit_grad - embedded * (scale * scale * scale * inner)).astype(bf16)
    embed_grad_ref[...] = embed_grad
    for d in range(8):
        summary_grad_ref[:, 256 * d : 256 * (d + 1)] = dot(embed_grad, project_ref[d])


def head(summary, bundle, width):
    devices, each, channels = summary.shape
    crops = devices * each
    parts = 2 * QUADS * QUADS
    return pl.pallas_call(
        functools.partial(head_kernel, width),
        in_specs=[SCALAR, pl.BlockSpec(memory_space=pltpu.VMEM)]
        + [pl.BlockSpec(memory_space=pl.ANY)] * 8,
        out_shape=[
            jax.ShapeDtypeStruct((1, 1), f32),
            jax.ShapeDtypeStruct((crops, 256), bf16),
            jax.ShapeDtypeStruct((parts * PROTO_ROWS, crops), bf16),
            jax.ShapeDtypeStruct((crops, 256), bf16),
            jax.ShapeDtypeStruct((crops, channels), f32),
            jax.ShapeDtypeStruct((crops, channels), bf16),
        ],
        scratch_shapes=[
            pltpu.VMEM((crops, channels), f32),
            pltpu.VMEM((crops + parts * QUEUE_ROWS, parts * PROTO_ROWS), f32),
            pltpu.VMEM((parts * PROTO_ROWS, 256), bf16),
            pltpu.VMEM((parts * QUEUE_ROWS, 256), bf16),
            pltpu.VMEM((8, 256, 256), bf16),
        ]
        + fetch_scratch(HEAD_ROWS),
        compiler_params=params(),
        cost_estimate=BRIEF,
        name="head",
    )(index_scalar("dp"), summary, *bundle)


def plain_head(summary, project, protos, queue, pairs):
    crops = summary.shape[0]
    embedded = dot(summary, project)
    scale = lax.rsqrt(jnp.sum(embedded * embedded, 1, keepdims=True) + EPS_NORM)
    unit = (embedded * scale).astype(bf16)
    scores = dot(unit, protos)
    plan = jnp.exp(jnp.concatenate([scores, dot(queue, protos)], 0) / EPS_SINK)
    for sweep in range(SINK):
        plan = plan / jnp.sum(plan, 0, keepdims=True)
        plan = plan / jnp.sum(plan, 1, keepdims=True)
    plan = lax.dot_general(
        pairs, plan[:crops], NN, precision=lax.Precision.HIGHEST, preferred_element_type=f32
    )
    logits = scores / SOFTMAX_TEMPER
    loss = -jnp.sum(plan * jax.nn.log_softmax(logits, axis=1)) / crops
    score_grad = ((jax.nn.softmax(logits, axis=1) - plan) / (SOFTMAX_TEMPER * crops)).astype(bf16)
    unit_grad = dot(score_grad, protos, NT)
    inner = jnp.sum(embedded * unit_grad, 1, keepdims=True)
    embed_grad = (scale * unit_grad - embedded * (scale * scale * scale * inner)).astype(bf16)
    return loss.reshape(1, 1), unit, score_grad, embed_grad, dot(embed_grad, project, NT)


def picks(rows, columns, source):
    row = lax.broadcasted_iota(jnp.int32, (rows, columns), 0)
    column = lax.broadcasted_iota(jnp.int32, (rows, columns), 1)
    return jnp.where(row == source(column), 1.0, 0.0).astype(bf16)


def narrow_lanes(v):
    return jnp.concatenate([v[:, :HALF], v[:, HALF + GAP :]], 1)


def square_sum(v):
    return jnp.sum(jnp.sum(v * v, 1, keepdims=True), 0, keepdims=True)


def small_grads_kernel(
    m_ref, small_ref, summary_ref, embed_grad_ref, score_grad_ref, unit_ref,
    squeeze_ref, excite_ref, project_ref, protos_ref, squares_ref, hold_ref,
):
    m = m_ref[0]
    devices, each, _ = small_ref.shape
    for i in range(devices):
        hold_ref[pl.ds(each * i, each), :] = small_ref[i].astype(f32)
    wide, inner = QUADS * LANES, 8 * SE_LANES

    def rows_of(base, size):
        return hold_ref[:, pl.ds(pl.multiple_of(base, 128), size)]

    squeeze_grad = rows_of(wide + inner + 128 * m, 128).astype(bf16)
    squeeze_grad = dot(
        squeeze_grad, picks(128, 2 * SE_PART, lambda c: (c // SE_PART) * SE_LANES + c % SE_PART)
    ).astype(bf16)
    squares = []
    total_square = jnp.zeros((1, 1), f32)
    for q in range(QUADS):
        pooled = narrow_lanes(rows_of(q * LANES, LANES)).astype(bf16)
        part = dot(pooled, squeeze_grad, TN)
        squeeze_ref[pl.ds(QUAD * q, QUAD), :] = part
        total_square = total_square + square_sum(part)
    squares.append(total_square)
    act = rows_of(wide, inner).astype(bf16)
    act = dot(act, picks(inner, QUAD, lambda c: (c // SE_PART) * SE_LANES + c % SE_PART)).astype(bf16)
    excite_grad = narrow_lanes(rows_of(wide + 2 * inner + LANES * m, LANES)).astype(bf16)
    part = dot(act, excite_grad, TN)
    excite_ref[...] = part
    squares.append(square_sum(part))
    embed_grad = dot(embed_grad_ref[...], picks(256, 64, lambda c: 64 * m + c)).astype(bf16)
    summary = jnp.concatenate(
        [
            narrow_lanes(summary_ref[:, q * LANES : (q + 1) * LANES].astype(f32))
            for q in range(QUADS)
        ],
        1,
    ).astype(bf16)
    part = dot(embed_grad, summary, TN)
    project_ref[...] = part
    squares.append(square_sum(part))
    total_square = jnp.zeros((1, 1), f32)
    last = protos_ref.shape[0]
    for d in range(8):
        place = pl.ds(pl.multiple_of((QUADS * d + m) * PROTO_ROWS, PROTO_ROWS), PROTO_ROWS)
        part = dot(score_grad_ref[place, :], unit_ref[...])
        size = min(PROTO_ROWS, last - PROTO_ROWS * d)
        protos_ref[pl.ds(PROTO_ROWS * d, size), :] = part[:size]
        total_square = total_square + square_sum(part)
    squares.append(total_square)
    lane = lax.broadcasted_iota(jnp.int32, (1, 128), 1)
    squares_ref[...] = sum(jnp.where(lane == i, v, 0.0) for i, v in enumerate(squares))


def small_grads(small, summary, embed_grad, score_grad, unit, width):
    crops = summary.shape[0]
    return pl.pallas_call(
        small_grads_kernel,
        in_specs=[SCALAR] + [pl.BlockSpec(memory_space=pltpu.VMEM)] * 5,
        out_shape=[
            jax.ShapeDtypeStruct((QUADS * QUAD, 2 * SE_PART), f32),
            jax.ShapeDtypeStruct((QUAD, QUAD), f32),
            jax.ShapeDtypeStruct((64, QUADS * QUAD), f32),
            jax.ShapeDtypeStruct((width, 256), f32),
            jax.ShapeDtypeStruct((1, 128), f32),
        ],
        scratch_shapes=[pltpu.VMEM((crops, small.shape[2]), f32)],
        compiler_params=params(),
        cost_estimate=BRIEF,
        name="small_grads",
    )(index_scalar("mp"), small, summary, embed_grad, score_grad, unit)


def own_kernel_kernel(me_ref, v_ref, out_ref):
    value = v_ref[: 9 * GROUP].astype(f32)
    out_ref[...] = jnp.where(me_ref[0] % 2 == 1, value[:, 256 - HALF :], value[:, :HALF])


def own_kernel(v):
    return pl.pallas_call(
        own_kernel_kernel,
        in_specs=[SCALAR, pl.BlockSpec(memory_space=pltpu.VMEM)],
        out_shape=jax.ShapeDtypeStruct((9 * GROUP, HALF), f32),
        compiler_params=params(),
        cost_estimate=BRIEF,
        name="own_kernel",
    )(index_scalar("dp"), v)


def weight_sums_kernel(*refs):
    lane = lax.broadcasted_iota(jnp.int32, (1, 128), 1)
    refs[-1][...] = sum(
        jnp.where(lane == i, square_sum(ref[...]), 0.0) for i, ref in enumerate(refs[:-1])
    )


def weight_sums(weights):
    values = [w if w.shape[1] == 2 * SE_PART or w.shape[0] == w.shape[1] else w.T for w in weights]
    return pl.pallas_call(
        weight_sums_kernel,
        out_shape=jax.ShapeDtypeStruct((1, 128), f32),
        compiler_params=params(),
        cost_estimate=BRIEF,
        name="weight_sums",
    )(*values)


def squares_kernel(
    n_dp, n_mp, weights_ref, norms_ref, small_ref, expand_ref, g1_ref, g2_ref, g3_ref, out_ref,
):
    lane = lax.broadcasted_iota(jnp.int32, (1, 128), 1)

    def at(i, v):
        return jnp.where(lane == i, v, 0.0)

    portions = at(0, 1.0) + at(1, 1.0 / n_mp) + at(4, 1.0)
    for i in (2, 3, 5, 6):
        portions = portions + at(i, 1.0 / n_dp)
    weights = weights_ref[...] * portions
    small = small_ref[...]
    grads = at(4, expand_ref[...])
    for i, k in enumerate((2, 3, 5, 6)):
        grads = grads + at(k, small[:, i : i + 1] / n_dp)
    everywhere = 1.0 / (n_dp * n_mp)
    for k, ref in enumerate((g1_ref, g2_ref, g3_ref)):
        for row, first in ((1, 7), (0, 10)):
            grads = grads + at(first + k, square_sum(ref[row : row + 1, :]) * everywhere)
        weights = weights + at(7 + k, square_sum(norms_ref[k : k + 1, :]) * everywhere)
        weights = weights + at(10 + k, square_sum(norms_ref[3 + k : 4 + k, :]) * everywhere)
    out_ref[0:1, :] = weights
    out_ref[1:2, :] = grads


def squares(n_dp, n_mp, *values):
    return pl.pallas_call(
        functools.partial(squares_kernel, n_dp, n_mp),
        out_shape=jax.ShapeDtypeStruct((2, 128), f32),
        compiler_params=params(),
        cost_estimate=BRIEF,
        name="squares",
    )(*values)


def rate_of(norm_squares, i):
    norms = jnp.sqrt(norm_squares[:, i : i + 1] + EPS_NORM)
    return TRUST * norms[0:1] / (norms[1:2] + DECAY * norms[0:1])


def step(weight, gradient, momentum, norm_squares, i):
    return MOMENTUM * momentum + rate_of(norm_squares, i) * (gradient + DECAY * weight)


def lars_prepare_kernel(*refs):
    n = len(refs) // 5
    for i in range(n):
        weight, gradient, momentum = (refs[3 * i + j] for j in range(3))
        refs[3 * n + 2 * i][...] = gradient[...] + DECAY * weight[...]
        refs[3 * n + 2 * i + 1][...] = MOMENTUM * momentum[...]


def lars_prepare(items):
    return pl.pallas_call(
        lars_prepare_kernel,
        out_shape=[jax.ShapeDtypeStruct(w.shape, f32) for w, _, _ in items for _ in range(2)],
        compiler_params=params(),
        cost_estimate=BRIEF,
        name="lars_prepare",
    )(*[v for item in items for v in item])


def lars_kernel(
    first, m_ref, squares_ref, gains_ref, biases_ref, m_gains_ref, m_biases_ref, g1_ref, g2_ref, g3_ref, *refs
):
    norm_squares = squares_ref[...]
    n = (len(refs) - 4 * first - 2) // 3
    prepared, out = refs[3 * first : 3 * first + 2 * n], refs[3 * first + 2 * n :]
    for i in range(first):
        weight, gradient, momentum = (refs[3 * i + j] for j in range(3))
        out[i][...] = step(weight[...], gradient[...], momentum[...], norm_squares, i)
    for i in range(n):
        rate = rate_of(norm_squares, first + i)
        out[first + i][...] = prepared[2 * i + 1][...] + rate * prepared[2 * i][...]
    n = n + first - 1
    lanes = pl.ds(pl.multiple_of(m_ref[0] * LANES, LANES), LANES)
    for k, ref in enumerate((g1_ref, g2_ref, g3_ref)):
        own = narrow_lanes(ref[:, lanes])
        row = slice(k, k + 1)
        out[n + 1][row, :] = step(
            gains_ref[row, :], own[1:2], m_gains_ref[row, :], norm_squares, 7 + k
        )
        out[n + 2][row, :] = step(
            biases_ref[row, :], own[0:1], m_biases_ref[row, :], norm_squares, 10 + k
        )


def lars(norm_squares, items, norm_values, prepared):
    shapes = [w.shape for w, _, _ in items] + [v.shape for v in prepared[::2]]
    shapes += [norm_values[0].shape] * 2
    values = [norm_squares, *norm_values, *[v for item in items for v in item], *prepared]
    return pl.pallas_call(
        functools.partial(lars_kernel, len(items)),
        in_specs=[SCALAR] + [pl.BlockSpec(memory_space=pltpu.VMEM)] * len(values),
        out_shape=[jax.ShapeDtypeStruct(shape, f32) for shape in shapes],
        compiler_params=params(),
        cost_estimate=BRIEF,
        name="lars",
    )(index_scalar("mp"), *values)


def plain_finish(
    small, summary, unit, score_grad, embed_grad, grad_sums, channels_here, big_grads, weights, moments
):
    n_dp, n_mp, m_index = lax.axis_size("dp"), lax.axis_size("mp"), lax.axis_index("mp")
    w_reduce, w_group, w_squeeze, w_excite, w_expand, w_project, prototypes, bn_gains, bn_biases = weights
    small = small.reshape(-1, small.shape[-1])
    wide, inner = QUADS * LANES, 8 * SE_LANES
    pooled_all = pack_channels(small[:, :wide])
    act_all = pack_inner(small[:, wide : wide + inner])
    squeeze_all = pack_inner(small[:, wide + inner : wide + 2 * inner])
    excite_all = pack_channels(small[:, wide + 2 * inner :])

    def own(v, width):
        return lax.dynamic_slice_in_dim(v, m_index * width, width, 1)

    reduce_grad, kernel_grad, expand_grad = big_grads
    gain_part = own(pack_channels(jnp.stack([v[1] for v in grad_sums])), channels_here)
    bias_part = own(pack_channels(jnp.stack([v[0] for v in grad_sums])), channels_here)
    grads = [
        reduce_grad,
        kernel_grad,
        dot(pooled_all, own(squeeze_all, w_squeeze.shape[1]), TN),
        dot(act_all, own(excite_all, w_excite.shape[1]), TN),
        expand_grad,
        dot(pack_channels(summary), own(embed_grad, w_project.shape[1]), TN),
        dot(unit, own(score_grad, prototypes.shape[1]), TN),
    ]
    portions = [1.0, 1.0 / n_mp, 1.0 / n_dp, 1.0 / n_dp, 1.0, 1.0 / n_dp, 1.0 / n_dp]

    def shares(arrays, gain, bias):
        return jnp.concatenate(
            [
                jnp.stack([jnp.sum(a * a) * p for a, p in zip(arrays, portions)]),
                jnp.sum(gain * gain, 1) / n_dp,
                jnp.sum(bias * bias, 1) / n_dp,
            ]
        )

    norms = total(
        jnp.stack([shares(weights[:7], bn_gains, bn_biases), shares(grads, gain_part, bias_part)])
    )
    stepped = [
        step(w, g, m, norms, i) for i, (w, g, m) in enumerate(zip(weights[:7], grads, moments[:7]))
    ]
    for values, part, momentum, first in (
        (bn_gains, gain_part, moments[7], 7), (bn_biases, bias_part, moments[8], 10),
    ):
        stepped.append(
            jnp.concatenate(
                [
                    step(values[k : k + 1], part[k : k + 1], momentum[k : k + 1], norms, first + k)
                    for k in range(3)
                ]
            )
        )
    return stepped, norms


def body(
    block_input, output_grad, w_reduce, w_group, w_squeeze, w_excite, w_expand, w_project,
    prototypes, bn_gains, bn_biases, m_reduce, m_group, m_squeeze, m_excite, m_expand,
    m_project, m_protos, m_gains, m_biases, queue_store, queue_slots, crop_perm,
):
    n_dp = lax.axis_size("dp")
    n_mp = lax.axis_size("mp")
    m_index = lax.axis_index("mp")
    channels_here = block_input.shape[0]
    rows = block_input.shape[1] // n_mp
    crops = rows // PIXELS
    count = rows * n_dp * n_mp
    all_crops = crops * n_dp * n_mp
    quick = quick_mesh()
    weights = [
        w_reduce, w_group, w_squeeze, w_excite, w_expand, w_project, prototypes, bn_gains, bn_biases,
    ]
    moments = [
        m_reduce, m_group, m_squeeze, m_excite, m_expand, m_project, m_protos, m_gains, m_biases,
    ]

    slot_table = (
        queue_slots[0][:, None]
        == lax.broadcasted_iota(jnp.int32, (queue_slots.shape[1], queue_store.shape[0]), 1)
    ).astype(bf16)
    queue_rows = dot(slot_table, queue_store.astype(bf16)).astype(bf16)
    order = crop_perm[0]
    pairing = (order[None, :] == jnp.bitwise_xor(order, 1)[:, None]).astype(f32)
    kernel_low = gather_kernel(w_group)
    x_blocks = slab_blocks(block_input)
    y_grad_blocks = slab_blocks(output_grad)
    norms = spread(jnp.concatenate([bn_gains, bn_biases], 0), "mp")
    norms = spread_channels(norms.transpose(1, 0, 2).reshape(norms.shape[1], -1))
    if quick:
        low = gather_mp(shard_square(w_reduce)).reshape(-1, 256)
        expand_low = shard_square(w_expand)
        se_low = shard_excitation(w_squeeze, w_excite)
        low, x_blocks, norms, expand_low, se_low, *kernel_low = tie(
            low, x_blocks, norms, expand_low, se_low, *kernel_low
        )
        across, up = gather_sides(low)
        x_blocks = exchange(x_blocks)
        windows = dense_windows(kernel_low)
        across, up, windows = tie(across, up, windows)
        corner = gather_corner(across, up)
        x_blocks, se_low = tie(x_blocks, se_low)
        se_low = spread(se_low, "mp").reshape(-1, 256)
        reduce_pieces = gather_twins(low, across, up, corner)
        head_values = tie(w_project, prototypes, queue_rows, pairing, corner)
        bundle = shard_head(*head_values[:4])
    else:
        x_blocks = exchange(x_blocks)
        y_grad_parts = list(quad_blocks(exchange(y_grad_blocks)))
        reduce_pieces = gather_square(w_reduce)
        se_pieces = list(gather_excitation(w_squeeze, w_excite).reshape(8, -1, 256))
        expand_pieces = gather_square(w_expand)
        project_low, protos_low, queue_low, pairs = gather_head(
            w_project, prototypes, queue_rows, pairing
        )
        pairs = block_diagonal(pairs)
        windows = dense_windows(kernel_low)
    x = quad_blocks(x_blocks)

    reduced, sums1 = mix(x, reduce_pieces)
    if quick:
        sums1 = sum_axis(sums1, "dp")
        sums1, se_low = tie(sums1, se_low)
        se_across, se_up = gather_sides(se_low)
        sums1 = sum_axis(sums1, "mp")
        sums1, expand_low, se_across, se_up = tie(sums1, expand_low, se_across, se_up)
        expand_low = spread(expand_low, "mp").reshape(-1, 256)
        se_corner = gather_corner(se_across, se_up)
        y_grad_parts = [
            lax.dynamic_index_in_dim(y_grad_blocks, m_index ^ k, 0, keepdims=False) for k in range(QUADS)
        ]
    else:
        sums1 = total(sums1)
    grouped, sums2 = conv(reduced, sums1, norms, windows, count)
    if quick:
        sums2, se_corner = tie(sums2, se_corner)
        se_pieces = gather_twins(se_low, se_across, se_up, se_corner)
        sums2 = sum_axis(sums2, "dp")
        sums2, expand_low = tie(sums2, expand_low)
        across, up = gather_sides(expand_low)
        sums2 = sum_axis(sums2, "mp")
    else:
        sums2 = total(sums2)
    if quick:
        sums2, bundle, y_grad_parts[1], y_grad_parts[2] = tie(
            sums2, bundle, y_grad_parts[1], y_grad_parts[2]
        )
        bundle = spread(bundle, "mp").reshape(-1, 256)
        y_grad_parts[1] = lax.ppermute(y_grad_parts[1], "mp", flips("mp", 1))
        y_grad_parts[2] = lax.ppermute(y_grad_parts[2], "mp", flips("mp", 2))
    gated, pooled, squeezed, squeeze_act, gates = gate(grouped, sums2, norms, se_pieces, count)
    if quick:
        gated, across, up = tie(gated, across, up)
        corner = gather_corner(across, up)
        corner, bundle = tie(corner, bundle)
        head_sides = gather_sides(bundle)
        expand_pieces = gather_twins(expand_low, across, up, corner)
    expanded, sums3 = mix(gated, expand_pieces)
    if quick:
        sums3, *head_sides = tie(sums3, *head_sides)
        sums3 = jnp.sum(spread(sums3, "dp"), 0)
        sums3, y_grad_parts[1], y_grad_parts[2], *head_sides = tie(
            sums3, y_grad_parts[1], y_grad_parts[2], *head_sides
        )
        head_corner = gather_corner(*head_sides)
        sums3 = jnp.sum(spread(sums3, "mp"), 0)
        sums3, head_corner = tie(sums3, head_corner)
        bundle = gather_twins(bundle, *head_sides, head_corner)
    else:
        sums3 = total(sums3)
    *y_parts, summary = block_value(x, expanded, sums3, norms, count)
    if quick:
        summary, *bundle = tie(summary, *bundle)
    summary = gather_all(summary)
    if quick:
        summary, y_grad_parts[3], y_parts[1] = tie(summary, y_grad_parts[3], y_parts[1])
        y_grad_parts[3] = lax.ppermute(y_grad_parts[3], "mp", flips("mp", 3))
        y_parts[1] = lax.ppermute(y_parts[1], "mp", flips("mp", 1))

    first_crop = ((lax.axis_index("dp") * n_mp + m_index) * crops).astype(jnp.int32)[None]
    if quick:
        loss, unit, score_grad, embed_grad, summary_grad, summary = head(
            summary, bundle, prototypes.shape[1]
        )
    else:
        summary = summary.reshape(all_crops, -1)
        loss, unit, score_grad, embed_grad, summary_grad = plain_head(
            summary, project_low, protos_low, queue_low, pairs
        )

    joined_grad, grad_sums3 = value_back(
        first_crop, x, expanded, sums3, norms, y_grad_parts, summary_grad, count
    )
    if quick:
        grad_sums3, y_parts[1] = tie(grad_sums3, y_parts[1])
    grad_sums3 = total(grad_sums3)
    if quick:
        grad_sums3, y_parts[2], y_parts[3] = tie(grad_sums3, y_parts[2], y_parts[3])
        y_parts[2] = lax.ppermute(y_parts[2], "mp", flips("mp", 2))
    expanded_grad, expand_all = all_grads(
        gated, joined_grad, expanded, sums3, norms, 2, grad_sums3, count
    )
    if quick:
        expand_part = lax.psum_scatter(expand_all, "dp", scatter_dimension=0, tiled=False)
    gated_grad = mix_back(expanded_grad, expand_pieces)
    act2_grad, grad_sums2, excite_grad, squeeze_grad = gate_back(
        gated_grad, grouped, sums2, norms, gates, squeezed, se_pieces, count
    )
    small = jnp.concatenate([pooled, squeeze_act, squeeze_grad, excite_grad], 1)
    if quick:
        grad_sums2, y_parts[2] = tie(grad_sums2, y_parts[2])
    grad_sums2 = total(grad_sums2)
    if quick:
        grad_sums2, small = tie(grad_sums2, small)
    small = gather_all(small)
    act1_grad, kernel_all, grad_sums1 = conv_back(
        act2_grad, grouped, sums2, grad_sums2, reduced, sums1, norms, windows, count
    )
    if quick:
        grad_sums1, kernel_all, small, expand_part = tie(
            grad_sums1, kernel_all, small, expand_part
        )
        expand_part = lax.psum_scatter(expand_part, "mp", scatter_dimension=0, tiled=False)
    grad_sums1 = total(grad_sums1)
    if quick:
        grad_sums1, y_parts[3] = tie(grad_sums1, y_parts[3])
        y_parts[3] = lax.ppermute(y_parts[3], "mp", flips("mp", 3))
    reduced_grad, reduce_sent = sent_grads(
        x, act1_grad, reduced, sums1, norms, 0, grad_sums1, count, True
    )
    if quick:
        reduced_grad, reduce_sent, expand_part, kernel_all = tie(
            reduced_grad, reduce_sent, expand_part, kernel_all
        )
        kernel_sum = lax.psum_scatter(kernel_all, "dp", scatter_dimension=0, tiled=False)
        reduce_got = from_twin(reduce_sent)
    reduce_kept = kept_grads(x, reduced_grad)
    if quick:
        reduced_grad, reduce_got, reduce_kept = tie(reduced_grad, reduce_got, reduce_kept)
        corner = scatter_corner(reduce_kept, reduce_got)
    x_grad = out_blocks(mix_back(reduced_grad, reduce_pieces, joined_grad))
    if quick:
        x_grad, corner, y_parts[3] = tie(x_grad, corner, y_parts[3])
        x_grad = exchange(x_grad)
        across, up = corner_sums(reduce_kept, reduce_got, corner)
        across, up, small = tie(across, up, small)
        across, up = scatter_sides(across, up)
        squeeze_part, excite_part, project_part, protos_part, small_squares = small_grads(
            small, summary, embed_grad, score_grad, unit, prototypes.shape[1]
        )
        expand_grad, expand_square = own_plain(expand_part)
        across, up, small_squares, expand_square, kernel_sum = tie(
            across, up, small_squares, expand_square, kernel_sum
        )
        kernel_sum = kernel_sum.reshape(QUADS, LANES // QUADS, 256)
        own, *parts = side_sums(reduce_kept, reduce_got, across, up, kernel_sum)
        parts = scatter_mp(own, parts)
        input_grad = out_channels(list(x_grad), channels_here, f32, jnp.zeros((1,), jnp.int32))
        block_output = out_channels(y_parts, channels_here, bf16, index_scalar("mp"))
        prepared = lars_prepare(
            [
                (w_squeeze, squeeze_part, m_squeeze),
                (w_excite, excite_part, m_excite),
                (w_expand.T, expand_grad, m_expand.T),
                (w_project.T, project_part, m_project.T),
                (prototypes.T, protos_part, m_protos.T),
            ]
        )
        weight_squares = weight_sums(weights[:7])
        shares = squares(
            n_dp, n_mp, weight_squares, norms, small_squares, expand_square,
            grad_sums1, grad_sums2, grad_sums3,
        )
        parts, input_grad, block_output, shares, *prepared = tie(
            parts, input_grad, block_output, shares, *prepared
        )
        reduce_grad, kernel_sum, big_squares = own_square(parts)
        kernel_sum = parts_mp(kernel_sum)
        norm_squares = jnp.sum(spread(shares + big_squares, "dp"), 0)
        norm_squares, *kernel_sum = tie(norm_squares, *kernel_sum)
        kernel_grad = own_kernel(in_order(kernel_sum, m_index).reshape(LANES, 256))
        norm_squares = jnp.sum(spread(norm_squares, "mp"), 0)
        (
            mom_reduce, mom_group, mom_squeeze, mom_excite, mom_expand, mom_project, mom_protos,
            mom_gains, mom_biases,
        ) = lars(
            norm_squares,
            [(w_reduce.T, reduce_grad, m_reduce.T), (w_group.T, kernel_grad, m_group.T)],
            [bn_gains, bn_biases, m_gains, m_biases, grad_sums1, grad_sums2, grad_sums3], prepared,
        )
        stepped = [
            mom_reduce.T, mom_group.T, mom_squeeze, mom_excite, mom_expand.T, mom_project.T,
            mom_protos.T, mom_gains, mom_biases,
        ]
    else:
        input_grad = natural_channels(exchange(x_grad), channels_here, f32)
        block_output = natural_channels(
            exchange(out_blocks(jnp.stack(y_parts))), channels_here, bf16
        )
        big_grads = (
            scatter_square(jnp.stack([reduce_kept, reduce_sent], 1).reshape(expand_all.shape)),
            scatter_kernel(kernel_all[:, : 9 * GROUP]),
            scatter_square(expand_all),
        )
        stepped, norm_squares = plain_finish(
            small, summary, unit, score_grad, embed_grad, (grad_sums1, grad_sums2, grad_sums3),
            channels_here, big_grads, weights, moments,
        )
    param_norms = jnp.sqrt(norm_squares[:, :13].T + EPS_NORM)
    return (block_output, loss[0, 0], input_grad, *stepped, param_norms)


def solution(mesh):
    split = P("dp", "mp")
    turned = P("mp", "dp")
    rows = P("dp", None)
    columns = P(None, "mp")
    return jax.shard_map(
        body,
        mesh=mesh,
        in_specs=(
            turned, turned, split, rows, columns, columns, split, columns, columns, columns, columns,
            split, rows, columns, columns, split, columns, columns, columns, columns, rows, rows, rows,
        ),
        out_specs=(
            turned, P(), turned, split, rows, columns, columns, split, columns, columns, columns,
            columns, P(),
        ),
        check_vma=False,
    )
```

```python
import functools

import jax
import jax.numpy as jnp
import numpy as np
from jax import lax
from jax.experimental import pallas as pl
from jax.experimental.pallas import tpu as pltpu
from jax.sharding import PartitionSpec as P

HW = 14
PIXELS = HW * HW
SINK = 3
EPS_BN = 1e-05
EPS_NORM = 1e-06
EPS_SINK = 0.05
SOFTMAX_TEMPER = 0.1
TRUST = 0.001
DECAY = 1e-06
MOMENTUM = 0.9

QUADS = 4
QUAD = 504
HALF = 252
LANES = 512
GAP = LANES - QUAD
GROUP = 56
SE_PART = 63
SE_LANES = 64
PITCH = 16
VMEM_BYTES = 60 * 1024 * 1024
f32 = jnp.float32
bf16 = jnp.bfloat16
NN = (((1,), (0,)), ((), ()))
NT = (((1,), (1,)), ((), ()))
TN = (((0,), (0,)), ((), ()))


def dot(a, b, dims=NN):
    return lax.dot_general(a, b, dims, preferred_element_type=f32)


def widen(v, axis):
    first = lax.slice_in_dim(v, 0, HALF, axis=axis)
    last = lax.slice_in_dim(v, HALF, QUAD, axis=axis)
    shape = list(v.shape)
    shape[axis] = GAP
    return jnp.concatenate([first, jnp.zeros(shape, v.dtype), last], axis)


def narrow(v, axis):
    first = lax.slice_in_dim(v, 0, HALF, axis=axis)
    last = lax.slice_in_dim(v, HALF + GAP, LANES, axis=axis)
    return jnp.concatenate([first, last], axis)


def spread_channels(v):
    lead = v.shape[:-1]
    return widen(v.reshape(lead + (QUADS, QUAD)), len(lead) + 1).reshape(lead + (QUADS * LANES,))


def pack_channels(v):
    lead = v.shape[:-1]
    return narrow(v.reshape(lead + (QUADS, LANES)), len(lead) + 1).reshape(lead + (QUADS * QUAD,))


def half_rows(v, position):
    pad = 256 - HALF
    padded = jnp.pad(v, ((pad, pad),) + ((0, 0),) * (v.ndim - 1))
    return lax.dynamic_slice_in_dim(padded, pad * (1 - position % 2), 256, 0)


def unhalf_rows(v, position):
    return lax.dynamic_slice_in_dim(v, (256 - HALF) * (position % 2), HALF, 0)


def spread_inner(v):
    lead = v.shape[:-1]
    parts = v.shape[-1] // SE_PART
    v = v.reshape(lead + (parts, SE_PART))
    v = jnp.pad(v, ((0, 0),) * (v.ndim - 1) + ((0, SE_LANES - SE_PART),))
    return v.reshape(lead + (parts * SE_LANES,))


def pack_inner(v):
    lead = v.shape[:-1]
    parts = v.shape[-1] // SE_LANES
    return v.reshape(lead + (parts, SE_LANES))[..., :SE_PART].reshape(lead + (parts * SE_PART,))


def flips(axis, bit):
    return [(i, i ^ bit) for i in range(lax.axis_size(axis))]


def spread(v, axis):
    n = lax.axis_size(axis)
    return lax.all_to_all(
        jnp.broadcast_to(v[None], (n,) + v.shape), axis, split_axis=0, concat_axis=0, tiled=True
    )


def sum_axis(v, axis):
    n = lax.axis_size(axis)
    bit = 1
    while bit < n:
        v = v + lax.ppermute(v, axis, flips(axis, bit))
        bit *= 2
    return v


def total(v):
    return jnp.sum(spread(jnp.sum(spread(v, "dp"), 0), "mp"), 0)


def tie(*values):
    return lax.optimization_barrier(values)


def gather_all(v):
    n = lax.axis_size("dp") * lax.axis_size("mp")
    out = lax.all_to_all(
        jnp.broadcast_to(v[None], (n,) + v.shape),
        ("dp", "mp"),
        split_axis=0,
        concat_axis=0,
        tiled=True,
    )
    return out


def in_order(parts, me):
    out = []
    for j in range(len(parts)):
        v = parts[0]
        for k in range(1, len(parts)):
            v = jnp.where((me ^ k) == j, parts[k], v)
        out.append(v)
    return jnp.stack(out)


def exchange(blocks):
    return lax.all_to_all(blocks, "mp", split_axis=0, concat_axis=0, tiled=True)


def parts_mp(v):
    return [v] + [lax.ppermute(v, "mp", flips("mp", k)) for k in range(1, lax.axis_size("mp"))]


def gather_mp(v):
    return in_order(parts_mp(v), lax.axis_index("mp"))


def diagonal(axis_size):
    return [(i, i ^ 4 if i % 2 == 0 else i ^ 2) for i in range(axis_size)]


def gather_sides(v):
    return lax.ppermute(v, "dp", flips("dp", 2)), lax.ppermute(v, "dp", flips("dp", 4))


def gather_corner(across, up):
    even = lax.axis_index("dp") % 2 == 0
    return lax.ppermute(jnp.where(even, across, up), "dp", diagonal(8))


def gather_twins(own, across, up, corner):
    pieces = []
    for got in (own, across, up, corner):
        pieces += [got, lax.ppermute(got, "dp", flips("dp", 1))]
    return pieces


def gather_dp(v):
    across, up = gather_sides(v)
    return gather_twins(v, across, up, gather_corner(across, up))


def scatter_corner(kept, got):
    return lax.ppermute(twin_sum(kept, got), "dp", diagonal(8))


def from_twin(sent):
    return lax.ppermute(sent, "dp", flips("dp", 1))


def scatter_sides(across, up):
    return lax.ppermute(across, "dp", flips("dp", 2)), lax.ppermute(up, "dp", flips("dp", 4))


def scatter_mp(own, parts):
    return [own] + [lax.ppermute(v, "mp", flips("mp", k + 1)) for k, v in enumerate(parts)]


def quick_mesh():
    return lax.axis_size("dp") == 2 * QUADS and lax.axis_size("mp") == QUADS


def slab_blocks(v):
    n = lax.axis_size("mp")
    blocks = v.T.reshape(n, v.shape[1] // n, v.shape[0])
    return widen(blocks, 2) if quick_mesh() else blocks


def quad_blocks(blocks):
    if quick_mesh():
        return blocks
    rows = blocks.shape[1]
    full = spread_channels(blocks.transpose(1, 0, 2).reshape(rows, -1))
    return full.reshape(rows, QUADS, LANES).transpose(1, 0, 2)


def out_blocks(blocks):
    if quick_mesh():
        return blocks
    n = lax.axis_size("mp")
    rows = blocks.shape[1]
    full = pack_channels(blocks.transpose(1, 0, 2).reshape(rows, -1))
    return full.reshape(rows, n, -1).transpose(1, 0, 2)


def natural_channels(blocks, channels, dtype):
    return blocks.astype(dtype).reshape(-1, channels).T


def out_channels(parts, channels, dtype, me):
    return natural_channels(join_rows(parts, dtype, me), channels, dtype)


def shard_square(w):
    return half_rows(widen(w.astype(bf16), 1), lax.axis_index("dp")).T


def gather_square(w):
    full = lax.all_gather(w.astype(bf16), "mp", axis=1, tiled=True)
    full = lax.all_gather(full, "dp", axis=0, tiled=True)
    full = spread_channels(spread_channels(full).T)
    return full.reshape(QUADS, LANES, 2 * QUADS, 256).transpose(2, 0, 1, 3)


def scatter_square(g):
    full = g.transpose(1, 2, 0, 3).reshape(QUADS * LANES, 2 * QUADS * 256)
    full = pack_channels(pack_channels(full).T)
    part = lax.psum_scatter(full, "dp", scatter_dimension=0, tiled=True)
    return lax.psum_scatter(part, "mp", scatter_dimension=1, tiled=True).astype(f32)


def gather_kernel(w):
    low = w.astype(bf16)
    if quick_mesh():
        return gather_dp(half_rows(low, lax.axis_index("dp")).T)
    full = lax.all_gather(low, "dp", axis=0, tiled=True)
    return spread_channels(full.T).reshape(-1, 2 * QUADS, 256).transpose(1, 0, 2)


def scatter_kernel(g):
    full = pack_channels(g.transpose(1, 0, 2).reshape(g.shape[1], -1)).T
    part = lax.psum_scatter(full, "dp", scatter_dimension=0, tiled=True).astype(f32)
    return lax.psum(part, "mp")


SE_ROWS = 256
HEAD_ROWS = 208
PROTO_ROWS = 96
QUEUE_ROWS = 32


def shard_excitation(w_squeeze, w_excite):
    d = lax.axis_index("dp")
    squeeze = lax.dynamic_slice_in_dim(w_squeeze, d * HALF, HALF, 0).astype(bf16)
    squeeze = spread_inner(half_rows(squeeze, d))
    excite = lax.dynamic_slice_in_dim(w_excite, d * SE_PART, SE_PART, 0).astype(bf16)
    excite = jnp.pad(widen(excite, 1), ((0, SE_LANES - SE_PART), (0, 0)))
    excite = jnp.concatenate([excite[:, 128 * i : 128 * (i + 1)] for i in range(4)], 0)
    return jnp.concatenate([squeeze, excite], 1)


def shard_head(w_project, prototypes, queue_rows, pairing):
    d = lax.axis_index("dp")
    m = lax.axis_index("mp")
    project = lax.dynamic_slice_in_dim(w_project, d * HALF, HALF, 0).astype(bf16)
    project = half_rows(project, d).T
    protos = jnp.pad(prototypes.T, ((0, 2 * QUADS * PROTO_ROWS - prototypes.shape[1]), (0, 0)))
    protos = lax.dynamic_slice_in_dim(protos, d * PROTO_ROWS, PROTO_ROWS, 0).astype(bf16)
    queue = lax.dynamic_slice_in_dim(queue_rows, m * QUEUE_ROWS, QUEUE_ROWS, 0)
    size = pairing.shape[0]
    lane = lax.broadcasted_iota(jnp.int32, (size, 256), 1)
    pairing = jnp.where(lane // size == d, jnp.tile(pairing, (1, 256 // size)), 0.0)
    pairing = jnp.pad(pairing.astype(bf16), ((0, 16 - size), (0, 0)))
    return jnp.concatenate([project, protos, queue, pairing], 0)


def gather_excitation(w_squeeze, w_excite):
    squeeze = lax.all_gather(w_squeeze.astype(bf16), "mp", axis=1, tiled=True)
    excite = lax.all_gather(w_excite.astype(bf16), "mp", axis=1, tiled=True)
    squeeze = spread_channels(spread_inner(squeeze).T).T
    excite = spread_inner(spread_channels(excite).T).T
    squeeze = squeeze.reshape(8, 256, 4, 128).transpose(0, 2, 1, 3)
    excite = excite.reshape(8, 64, 4, 4, 128).transpose(0, 2, 3, 1, 4).reshape(8, 4, 256, 128)
    return jnp.concatenate([squeeze, excite], 3)


def gather_head(w_project, prototypes, queue_rows, pairing):
    project = lax.all_gather(w_project.astype(bf16), "mp", axis=1, tiled=True)
    protos = lax.all_gather(prototypes.astype(bf16), "mp", axis=1, tiled=True)
    queue = lax.all_gather(queue_rows, "dp", axis=0, tiled=True)
    pairs = lax.all_gather(pairing, "dp")
    return spread_channels(project.T).T, protos, queue, pairs


def block_diagonal(pairs):
    images, size = pairs.shape[:2]
    return (
        jnp.eye(images, dtype=f32)[:, None, :, None] * pairs.astype(f32)[:, :, None, :]
    ).reshape(images * size, images * size)


BRIEF = pl.CostEstimate(flops=1, bytes_accessed=1, transcendentals=0)


def params(*semantics):
    return pltpu.CompilerParams(vmem_limit_bytes=VMEM_BYTES)


def column_sums(stats_ref, a, b):
    stats_ref[0:1, :] = jnp.sum(a, 0, keepdims=True)
    stats_ref[1:2, :] = jnp.sum(b, 0, keepdims=True)


def index_scalar(axis):
    quick = quick_mesh()
    return (lax.axis_index(axis) if quick else jnp.zeros((), jnp.int32)).astype(jnp.int32)[None]


SCALAR = pl.BlockSpec(memory_space=pltpu.SMEM)


def half_block(index):
    return pl.ds(pl.multiple_of(index * 256, 256), 256)


def join_rows_kernel(me_ref, *refs):
    out_ref = refs[-1]
    for k, part in enumerate(refs[:-1]):
        v = part[...].astype(f32)
        v = jnp.concatenate([v[:, :HALF], v[:, HALF + GAP :]], 1)
        out_ref[me_ref[0] ^ k] = v.astype(out_ref.dtype)


def join_rows(parts, dtype, me):
    rows = parts[0].shape[0]
    return pl.pallas_call(
        join_rows_kernel,
        in_specs=[SCALAR] + [pl.BlockSpec(memory_space=pltpu.VMEM)] * len(parts),
        out_shape=jax.ShapeDtypeStruct((len(parts), rows, QUAD), dtype),
        compiler_params=params(),
        cost_estimate=BRIEF,
        name="join_rows",
    )(me, *parts)


def piece_list(w):
    return w if isinstance(w, list) else [w[b].reshape(-1, 256) for b in range(8)]


def half_of(ref, index):
    return ref[index // 2, :, half_block(index % 2)]


def mix_kernel(me_ref, x_ref, *refs):
    out_ref, stats_ref = refs[8:]
    turned = jnp.concatenate([half_of(x_ref, me_ref[0] ^ b) for b in range(8)], 1)
    acc = dot(turned, jnp.concatenate([refs[b][...] for b in range(8)], 1), NT)
    out_ref[...] = acc
    column_sums(stats_ref, acc, acc * acc)


def mix(x, w):
    _, rows, _ = x.shape
    width = QUADS * LANES
    return pl.pallas_call(
        mix_kernel,
        grid=(QUADS,),
        in_specs=[SCALAR, pl.BlockSpec(x.shape, lambda m: (0, 0, 0))]
        + [pl.BlockSpec((LANES, 256), lambda m: (m, 0))] * 8,
        out_specs=[
            pl.BlockSpec((rows, LANES), lambda m: (0, m)),
            pl.BlockSpec((2, LANES), lambda m: (0, m)),
        ],
        out_shape=[
            jax.ShapeDtypeStruct((rows, width), f32),
            jax.ShapeDtypeStruct((2, width), f32),
        ],
        compiler_params=params(),
        cost_estimate=BRIEF,
        name="mix",
    )(index_scalar("dp"), x, *piece_list(w))


def mix_back_kernel(rest, me_ref, g_ref, *refs):
    out_ref, hold_ref, sems = refs[8 + rest :]

    def copy(b):
        source = refs[b].at[pl.ds(0, QUADS * LANES)]
        return pltpu.make_async_copy(source, hold_ref.at[b], sems.at[b])

    for b in range(8):
        copy(b).start()
    for b in range(0, 8, 2):
        copy(b).wait()
        copy(b + 1).wait()
        pair = dot(g_ref[...], jnp.concatenate([hold_ref[b], hold_ref[b + 1]], 1))
        for i in range(2):
            index = me_ref[0] ^ (b + i)
            acc = pair[:, 256 * i : 256 * (i + 1)]
            if rest:
                acc = acc + refs[8][:, half_block(index)]
                out_ref[index // 2, :, half_block(index % 2)] = acc.astype(bf16)
            else:
                out_ref[:, half_block(index)] = acc


def mix_back(g, w, rest=None):
    rows, width = g.shape
    if rest is None:
        more, out = [], jax.ShapeDtypeStruct((rows, width), f32)
    else:
        more, out = [rest], jax.ShapeDtypeStruct((QUADS, rows, LANES), bf16)
    return pl.pallas_call(
        functools.partial(mix_back_kernel, len(more)),
        in_specs=[SCALAR, pl.BlockSpec(memory_space=pltpu.VMEM)]
        + [pl.BlockSpec(memory_space=pl.ANY)] * 8
        + [pl.BlockSpec(memory_space=pltpu.VMEM)] * len(more),
        out_specs=pl.BlockSpec(memory_space=pltpu.VMEM),
        out_shape=out,
        scratch_shapes=[
            pltpu.VMEM((8, QUADS * LANES, 256), bf16),
            pltpu.SemaphoreType.DMA((8,)),
        ],
        compiler_params=params(),
        cost_estimate=BRIEF,
        name="mix_back",
    )(index_scalar("dp"), g, *piece_list(w), *more)


def piece_grads(me_ref, x_ref, g, odd, out_ref):
    wanted = jnp.concatenate([half_of(x_ref, me_ref[0] ^ (2 * i + odd)) for i in range(4)], 1)
    result = dot(g.T, wanted)
    for i in range(4):
        out_ref[i, 0] = result[:, 256 * i : 256 * (i + 1)].astype(bf16)


def sent_grads_kernel(
    k, sloped, count, me_ref, x_ref, g_ref, a_ref, sums_ref, norms_ref, grad_sums_ref, grad_ref, out_ref
):
    grad, values = g_ref[...].astype(f32), a_ref[...]
    if sloped:
        _, _, scale, shift = affine(sums_ref[...], norms_ref[...], k, count)
        grad = grad * swish_slope(values * scale + shift)
    grad = norm_back(
        grad, values, sums_ref[...], norms_ref[...], k, grad_sums_ref[...], count
    ).astype(bf16)
    grad_ref[...] = grad
    piece_grads(me_ref, x_ref, grad, 1, out_ref)


PIECES = jax.ShapeDtypeStruct((4, QUADS, LANES, 256), bf16)


def pieces_spec():
    return pl.BlockSpec((4, 1, LANES, 256), lambda m: (0, m, 0, 0))


def sent_grads(x, g, a, sums, norms, k, grad_sums, count, sloped):
    rows, width = a.shape
    return pl.pallas_call(
        functools.partial(sent_grads_kernel, k, sloped, count),
        grid=(QUADS,),
        in_specs=[
            SCALAR, pl.BlockSpec(x.shape, lambda m: (0, 0, 0)), quad_spec(rows), quad_spec(rows),
            quad_spec(2), quad_spec(6), quad_spec(2),
        ],
        out_specs=[quad_spec(rows), pieces_spec()],
        out_shape=[jax.ShapeDtypeStruct((rows, width), bf16), PIECES],
        compiler_params=params(),
        cost_estimate=BRIEF,
        name="sent_grads",
    )(index_scalar("dp"), x, g, a, sums, norms, grad_sums)


def all_grads_kernel(
    k, count, x_ref, g_ref, a_ref, sums_ref, norms_ref, grad_sums_ref, grad_ref, out_ref
):
    grad = norm_back(
        g_ref[...], a_ref[...], sums_ref[...], norms_ref[...], k, grad_sums_ref[...], count
    ).astype(bf16)
    grad_ref[...] = grad
    turned = grad.T
    for q in range(QUADS):
        result = dot(turned, x_ref[q])
        for i in range(2):
            out_ref[2 * q + i, 0] = result[:, 256 * i : 256 * (i + 1)].astype(bf16)


def all_grads(x, g, a, sums, norms, k, grad_sums, count):
    rows, width = a.shape
    return pl.pallas_call(
        functools.partial(all_grads_kernel, k, count),
        grid=(QUADS,),
        in_specs=[
            pl.BlockSpec(x.shape, lambda m: (0, 0, 0)), quad_spec(rows), quad_spec(rows),
            quad_spec(2), quad_spec(6), quad_spec(2),
        ],
        out_specs=[
            quad_spec(rows), pl.BlockSpec((8, 1, LANES, 256), lambda m: (0, m, 0, 0)),
        ],
        out_shape=[
            jax.ShapeDtypeStruct((rows, width), bf16),
            jax.ShapeDtypeStruct((8, QUADS, LANES, 256), bf16),
        ],
        compiler_params=params(),
        cost_estimate=BRIEF,
        name="all_grads",
    )(x, g, a, sums, norms, grad_sums)


def kept_grads_kernel(me_ref, x_ref, g_ref, out_ref):
    piece_grads(me_ref, x_ref, g_ref[...], 0, out_ref)


def kept_grads(x, g):
    rows, width = g.shape
    return pl.pallas_call(
        kept_grads_kernel,
        grid=(QUADS,),
        in_specs=[SCALAR, pl.BlockSpec(x.shape, lambda m: (0, 0, 0)), quad_spec(rows)],
        out_specs=pieces_spec(),
        out_shape=PIECES,
        compiler_params=params(),
        cost_estimate=BRIEF,
        name="kept_grads",
    )(index_scalar("dp"), x, g)


def entry_spec(shape, i, steps):
    return pl.BlockSpec((None, shape[1] // steps) + shape[2:], lambda m, i=i: (i, m, 0, 0))


def twin_sum_kernel(a_ref, b_ref, out_ref):
    out_ref[...] = (a_ref[...].astype(f32) + b_ref[...].astype(f32)).astype(bf16)


def twin_sum(kept, got):
    shape = kept.shape
    steps = min(2, shape[1])
    return pl.pallas_call(
        twin_sum_kernel,
        grid=(steps,),
        in_specs=[entry_spec(shape, 3, steps)] * 2,
        out_specs=pl.BlockSpec((shape[1] // steps,) + shape[2:], lambda m: (m, 0, 0)),
        out_shape=jax.ShapeDtypeStruct(shape[1:], bf16),
        compiler_params=params(),
        cost_estimate=BRIEF,
        name="twin_sum",
    )(kept, got)


def corner_sums_kernel(me_ref, a1_ref, b1_ref, a2_ref, b2_ref, corner_ref, across_ref, up_ref):
    even = me_ref[0] % 2 == 0
    corner = corner_ref[...].astype(f32)
    across = a1_ref[...].astype(f32) + b1_ref[...].astype(f32)
    across_ref[...] = (across + jnp.where(even, corner, 0.0)).astype(bf16)
    up = a2_ref[...].astype(f32) + b2_ref[...].astype(f32)
    up_ref[...] = (up + jnp.where(even, 0.0, corner)).astype(bf16)


def corner_sums(kept, got, corner):
    shape = kept.shape
    steps = min(2, shape[1])
    block = pl.BlockSpec((shape[1] // steps,) + shape[2:], lambda m: (m, 0, 0))
    return pl.pallas_call(
        corner_sums_kernel,
        grid=(steps,),
        in_specs=[SCALAR] + [entry_spec(shape, i, steps) for i in (1, 1, 2, 2)] + [block],
        out_specs=[block, block],
        out_shape=[jax.ShapeDtypeStruct(shape[1:], bf16)] * 2,
        compiler_params=params(),
        cost_estimate=BRIEF,
        name="corner_sums",
    )(index_scalar("dp"), kept, got, kept, got, corner)


def side_sums_kernel(me_ref, a_ref, b_ref, across_ref, up_ref, more_ref, out_ref, *parts):
    value = (
        a_ref[...].astype(f32)
        + b_ref[...].astype(f32)
        + across_ref[...].astype(f32)
        + up_ref[...].astype(f32)
    )
    rows = value.shape[0]

    @pl.when(pl.program_id(0) == 0)
    def _():
        out_ref[:rows, :] = value
        out_ref[rows:, :] = more_ref[...].astype(f32)

    for k, part in enumerate(parts):

        @pl.when(pl.program_id(0) == k + 1)
        def _(part=part):
            part[:rows, :] = value.astype(bf16)
            part[rows:, :] = more_ref[...]


def side_sums(kept, got, across, up, more):
    _, n, *shape = kept.shape
    rows = shape[0] + more.shape[1]
    entry = pl.BlockSpec((None, None, *shape), lambda k, me: (0, me[0] ^ k, 0, 0))
    block = pl.BlockSpec((None, *shape), lambda k, me: (me[0] ^ k, 0, 0))
    spec = pltpu.PrefetchScalarGridSpec(
        num_scalar_prefetch=1,
        grid=(n,),
        in_specs=[
            entry, entry, block, block,
            pl.BlockSpec((None,) + more.shape[1:], lambda k, me: (me[0] ^ k, 0, 0)),
        ],
        out_specs=[pl.BlockSpec((rows, 256), lambda k, me: (0, 0))] * n,
    )
    return pl.pallas_call(
        side_sums_kernel,
        grid_spec=spec,
        out_shape=[jax.ShapeDtypeStruct((rows, 256), f32)]
        + [jax.ShapeDtypeStruct((rows, 256), bf16)] * (n - 1),
        compiler_params=params(),
        cost_estimate=BRIEF,
        name="side_sums",
    )(index_scalar("mp"), kept, got, across, up, more)


def without_padding(value, odd):
    row = lax.broadcasted_iota(jnp.int32, (QUAD, 1), 0)
    value = jnp.where(row < HALF, value[:QUAD], value[GAP:])
    return jnp.where(odd, value[:, 256 - HALF :], value[:, :HALF])


def own_plain_kernel(me_ref, own_ref, out_ref, square_ref):
    value = without_padding(own_ref[...].astype(f32), me_ref[0] % 2 == 1)
    out_ref[...] = value
    square_ref[...] = square_sum(value)


def own_plain(v):
    return pl.pallas_call(
        own_plain_kernel,
        in_specs=[SCALAR, pl.BlockSpec(memory_space=pltpu.VMEM)],
        out_shape=[
            jax.ShapeDtypeStruct((QUAD, HALF), f32), jax.ShapeDtypeStruct((1, 1), f32),
        ],
        compiler_params=params(),
        cost_estimate=BRIEF,
        name="own_plain",
    )(index_scalar("dp"), v)


def gradient_lane(i):
    lane = lax.broadcasted_iota(jnp.int32, (2, 128), 1)
    row = lax.broadcasted_iota(jnp.int32, (2, 128), 0)
    return (lane == i) & (row == 1)


def own_square_kernel(me_ref, own_ref, *refs):
    out_ref, more_ref, squares_ref = refs[-3:]
    value = own_ref[...]
    for part in refs[:-3]:
        value = value + part[...].astype(f32)
    more = value[LANES:]
    value = without_padding(value[:LANES], me_ref[0] % 2 == 1)
    out_ref[...] = value
    more_ref[...] = more.astype(bf16)
    squares_ref[...] = jnp.where(gradient_lane(0), square_sum(value), 0.0) + jnp.where(
        gradient_lane(1), square_sum(more), 0.0
    )


def own_square(parts):
    return pl.pallas_call(
        own_square_kernel,
        in_specs=[SCALAR] + [pl.BlockSpec(memory_space=pltpu.VMEM)] * len(parts),
        out_shape=[
            jax.ShapeDtypeStruct((QUAD, HALF), f32),
            jax.ShapeDtypeStruct((parts[0].shape[0] - LANES, 256), bf16),
            jax.ShapeDtypeStruct((2, 128), f32),
        ],
        compiler_params=params(),
        cost_estimate=BRIEF,
        name="own_square",
    )(index_scalar("dp"), *parts)


def affine(sums, norms, k, count):
    mean = sums[0:1] / count
    inverse = lax.rsqrt(sums[1:2] / count - mean * mean + EPS_BN)
    scale = inverse * norms[k : k + 1]
    return mean, inverse, scale, norms[3 + k : 4 + k] - mean * scale


def quad_spec(rows):
    return pl.BlockSpec((rows, LANES), lambda q: (0, q))


def block_spec(rows):
    return pl.BlockSpec((None, rows, LANES), lambda q: (q, 0, 0))


def crop_totals(ref, crops):
    return jnp.concatenate(
        [jnp.sum(ref[pl.ds(PIXELS * c, PIXELS), :], 0, keepdims=True) for c in range(crops)], 0
    )


def turned_quad(rows):
    return pl.BlockSpec((rows, LANES), lambda k, me, *_: (0, me[0] ^ k))


def turned_block(rows):
    return pl.BlockSpec((None, rows, LANES), lambda k, me, *_: (me[0] ^ k, 0, 0))


def whole_part(rows):
    return pl.BlockSpec((rows, LANES), lambda k, *_: (0, 0))


def value_kernel(crops, count, me_ref, x_ref, a_ref, sums_ref, norms_ref, *refs):
    parts, summary_ref, work_ref = refs[:-2], refs[-2], refs[-1]
    _, _, scale, shift = affine(sums_ref[...], norms_ref[...], 2, count)
    work_ref[...] = swish(x_ref[...].astype(f32) + a_ref[...] * scale + shift)
    for k, part in enumerate(parts):

        @pl.when(pl.program_id(0) == k)
        def _(part=part):
            part[...] = work_ref[...].astype(bf16)

    summary_ref[...] = (crop_totals(work_ref, crops) / PIXELS).astype(bf16)


def block_value(x, a, sums, norms, count):
    rows, width = a.shape
    crops = rows // PIXELS
    spec = pltpu.PrefetchScalarGridSpec(
        num_scalar_prefetch=1,
        grid=(QUADS,),
        in_specs=[turned_block(rows), turned_quad(rows), turned_quad(2), turned_quad(6)],
        out_specs=[whole_part(rows)] * QUADS + [turned_quad(crops)],
        scratch_shapes=[pltpu.VMEM((rows, LANES), f32)],
    )
    return pl.pallas_call(
        functools.partial(value_kernel, crops, count),
        grid_spec=spec,
        out_shape=[jax.ShapeDtypeStruct((rows, LANES), bf16)] * QUADS
        + [jax.ShapeDtypeStruct((crops, width), bf16)],
        compiler_params=params(),
        cost_estimate=BRIEF,
        name="value",
    )(index_scalar("mp"), x, a, sums, norms)


def value_back_kernel(
    crops, count, me_ref, first_ref, x_ref, a_ref, sums_ref, norms_ref, do_ref, *refs
):
    parts, (out_ref, stats_ref, work_ref) = refs[:-3], refs[-3:]
    for k, part in enumerate(parts):

        @pl.when(pl.program_id(0) == k)
        def _(part=part):
            work_ref[...] = part[...].astype(f32)

    mean, inverse, scale, shift = affine(sums_ref[...], norms_ref[...], 2, count)
    values = a_ref[...]
    row = lax.broadcasted_iota(jnp.int32, (do_ref.shape[0], 1), 0)
    own = jnp.concatenate(
        [
            jnp.sum(jnp.where(row == first_ref[0] + c, do_ref[...], 0.0), 0, keepdims=True)
            for c in range(crops)
        ],
        0,
    )
    slope = swish_slope(x_ref[...].astype(f32) + values * scale + shift)
    grad = (work_ref[...] + rows_of_crops(own / PIXELS, values.shape[0])) * slope
    out_ref[...] = grad
    column_sums(stats_ref, grad, grad * ((values - mean) * inverse))


def value_back(first, x, a, sums, norms, dy_parts, do, count):
    rows, width = a.shape
    spec = pltpu.PrefetchScalarGridSpec(
        num_scalar_prefetch=2,
        grid=(QUADS,),
        in_specs=[
            turned_block(rows), turned_quad(rows), turned_quad(2), turned_quad(6),
            turned_quad(do.shape[0]),
        ]
        + [whole_part(rows)] * QUADS,
        out_specs=[turned_quad(rows), turned_quad(2)],
        scratch_shapes=[pltpu.VMEM((rows, LANES), f32)],
    )
    return pl.pallas_call(
        functools.partial(value_back_kernel, rows // PIXELS, count),
        grid_spec=spec,
        out_shape=[
            jax.ShapeDtypeStruct((rows, width), f32), jax.ShapeDtypeStruct((2, width), f32),
        ],
        compiler_params=params(),
        cost_estimate=BRIEF,
        name="value_back",
    )(index_scalar("mp"), first, x, a, sums, norms, do, *dy_parts)


def norm_back(grad, values, sums, norms, k, grad_sums, count):
    mean, inverse, scale, _ = affine(sums, norms, k, count)
    centred = (values - mean) * inverse
    return scale * (grad - (grad_sums[0:1] + centred * grad_sums[1:2]) / count)


def lane_mask(low, high, rows=GROUP):
    lane = lax.broadcasted_iota(jnp.int32, (rows, 256), 1)
    return (lane >= low) & (lane < high)


def dense_kernel(me_ref, *refs):
    out_ref, hold_ref = refs[8:]

    @pl.when(pl.program_id(0) == 0)
    def _():
        for b in range(8):
            hold_ref[me_ref[0] ^ b] = refs[b][...]

    even = hold_ref[2 * pl.program_id(0)].astype(f32)
    odd = hold_ref[2 * pl.program_id(0) + 1].astype(f32)
    row = lax.broadcasted_iota(jnp.int32, (256, 256), 0)
    edge = jnp.zeros((32, 256), f32)
    centre = lane_mask(96, 124) | lane_mask(132, 160)
    for tap in range(9):
        e = even[GROUP * tap : GROUP * (tap + 1)]
        o = odd[GROUP * tap : GROUP * (tap + 1)]
        first = [jnp.where(lane_mask(GROUP * g, GROUP * (g + 1)), e, 0.0) for g in range(4)]
        last = [
            jnp.where(lane_mask(32 + GROUP * g, 32 + GROUP * (g + 1)), o, 0.0) for g in range(4)
        ]
        out_ref[0, 0, tap] = jnp.concatenate(first + [edge], 0).astype(bf16)
        out_ref[0, 1, tap] = jnp.concatenate([edge] + last, 0).astype(bf16)
        across = jnp.where(centre, jnp.concatenate([e[:, 128:], o[:, :128]], 1), 0.0)
        upper = jnp.concatenate(
            [jnp.zeros((96, 256), f32), across, jnp.zeros((104, 256), f32)], 0
        )
        lower = jnp.concatenate(
            [jnp.zeros((104, 256), f32), across, jnp.zeros((96, 256), f32)], 0
        )
        out_ref[0, 2, tap] = (
            jnp.where(row < 124, upper, 0.0) + jnp.where(row >= 132, lower, 0.0)
        ).astype(bf16)


def dense_windows(kernel):
    pieces = [kernel[b] for b in range(8)]
    return pl.pallas_call(
        dense_kernel,
        grid=(QUADS,),
        in_specs=[SCALAR] + [pl.BlockSpec(memory_space=pltpu.VMEM)] * 8,
        out_specs=pl.BlockSpec((1, 3, 9, 256, 256), lambda q: (q, 0, 0, 0, 0)),
        out_shape=jax.ShapeDtypeStruct((QUADS, 3, 9, 256, 256), bf16),
        scratch_shapes=[pltpu.VMEM((8,) + pieces[0].shape, bf16)],
        compiler_params=params(),
        cost_estimate=BRIEF,
        name="dense_windows",
    )(index_scalar("dp"), *pieces)


WINDOWS = (0, 256, 128)


def place_pixels(pad_ref, moved_ref, source_ref, crops):
    for crop in range(crops):
        for row in range(HW):
            pad_ref[pl.ds(PITCH + 256 * crop + PITCH * (row + 1), HW), :] = source_ref[
                pl.ds(PIXELS * crop + HW * row, HW), :
            ]
    for shift in range(3):
        moved_ref[shift] = pad_ref[pl.ds(PITCH - 1 + shift, 256 * crops), :].astype(bf16)


def tap_rows(moved_ref, dy, dx, low, crops):
    return jnp.concatenate(
        [
            moved_ref[dx, pl.ds(256 * crop + PITCH * dy, PITCH * HW), pl.ds(low, 256)]
            for crop in range(crops)
        ],
        0,
    )


def take_pixels(target_ref, source_ref, crops):
    for crop in range(crops):
        for row in range(HW):
            target_ref[pl.ds(PIXELS * crop + HW * row, HW), :] = source_ref[
                pl.ds(PITCH * HW * crop + PITCH * row, HW), :
            ]


def swish(v):
    return v / (1.0 + jnp.exp(-v))


def swish_slope(v):
    sigma = 1.0 / (1.0 + jnp.exp(-v))
    return sigma * (1.0 + v * (1.0 - sigma))


def conv_kernel(crops, count, a_ref, sums_ref, norms_ref, w_ref, out_ref, stats_ref, pad_ref, moved_ref, wide_ref, act_ref):
    @pl.when(pl.program_id(0) == 0)
    def _():
        pad_ref[...] = jnp.zeros_like(pad_ref)

    _, _, scale, shift = affine(sums_ref[...], norms_ref[...], 0, count)
    act = swish(a_ref[...] * scale + shift)
    act_ref[...] = act.astype(bf16).astype(f32)
    place_pixels(pad_ref, moved_ref, act_ref, crops)
    for window, low in enumerate(WINDOWS):
        taps = [tap_rows(moved_ref, tap // 3, tap % 3, low, crops) for tap in range(9)]
        acc = dot(jnp.concatenate(taps, 1), w_ref[0, window].reshape(9 * 256, 256))
        if window < 2:
            wide_ref[:, pl.ds(low, 256)] = acc
        else:
            wide_ref[:, pl.ds(low, 256)] += acc
    take_pixels(act_ref, wide_ref, crops)
    result = act_ref[...].astype(bf16)
    out_ref[...] = result
    result = result.astype(f32)
    column_sums(stats_ref, result, result * result)


def conv(a, sums, norms, windows, count):
    rows, width = a.shape
    crops = rows // PIXELS
    return pl.pallas_call(
        functools.partial(conv_kernel, crops, count),
        grid=(QUADS,),
        in_specs=[
            quad_spec(rows), quad_spec(2), quad_spec(6),
            pl.BlockSpec((1, 3, 9, 256, 256), lambda q: (q, 0, 0, 0, 0)),
        ],
        out_specs=[
            pl.BlockSpec((rows, LANES), lambda q: (0, q)),
            pl.BlockSpec((2, LANES), lambda q: (0, q)),
        ],
        out_shape=[
            jax.ShapeDtypeStruct((rows, width), bf16),
            jax.ShapeDtypeStruct((2, width), f32),
        ],
        scratch_shapes=[
            pltpu.VMEM((2 * PITCH + 256 * crops, LANES), f32),
            pltpu.VMEM((3, 256 * crops, LANES), bf16),
            pltpu.VMEM((PITCH * HW * crops, LANES), f32),
            pltpu.VMEM((rows, LANES), f32),
        ],
        compiler_params=params(),
        cost_estimate=BRIEF,
        name="conv",
    )(a, sums, norms, windows)


def conv_back_kernel(
    crops, count, g_ref, a2_ref, sums2_ref, grad_sums_ref, a_ref, sums_ref, norms_ref, w_ref,
    out_ref, grads_ref, stats_ref,
    pad_ref, moved_ref, pad_x_ref, moved_x_ref, wide_ref, act_ref, hold_ref,
):
    @pl.when(pl.program_id(0) == 0)
    def _():
        pad_ref[...] = jnp.zeros_like(pad_ref)
        pad_x_ref[...] = jnp.zeros_like(pad_x_ref)

    norms = norms_ref[...]
    grad = norm_back(
        g_ref[...], a2_ref[...].astype(f32), sums2_ref[...], norms, 1, grad_sums_ref[...], count
    )
    act_ref[...] = grad.astype(bf16).astype(f32)
    place_pixels(pad_ref, moved_ref, act_ref, crops)
    values = a_ref[...]
    mean, inverse, scale, shift = affine(sums_ref[...], norms, 0, count)
    normed = values * scale + shift
    act_ref[...] = swish(normed).astype(bf16).astype(f32)
    place_pixels(pad_x_ref, moved_x_ref, act_ref, crops)
    for window, low in enumerate(WINDOWS):
        taps = [tap_rows(moved_ref, 2 - tap // 3, 2 - tap % 3, low, crops) for tap in range(9)]
        weight = jnp.concatenate([w_ref[0, window, tap] for tap in range(9)], 1)
        acc = dot(jnp.concatenate(taps, 1), weight, NT)
        if window < 2:
            wide_ref[:, pl.ds(low, 256)] = acc
        else:
            wide_ref[:, pl.ds(low, 256)] += acc
    take_pixels(act_ref, wide_ref, crops)
    result = act_ref[...].astype(bf16)
    out_ref[...] = result
    grad = result.astype(f32) * swish_slope(normed)
    column_sums(stats_ref, grad, grad * ((values - mean) * inverse))
    centre = lane_mask(96, 124) | lane_mask(132, 160)
    row = lax.broadcasted_iota(jnp.int32, (GROUP, 256), 0)
    mids = [
        tap_rows(moved_ref, 1, 1, low, crops) for low in WINDOWS
    ]
    for tap in range(9):
        pieces = []
        for window, low in enumerate(WINDOWS):
            pieces.append(
                dot(tap_rows(moved_x_ref, tap // 3, tap % 3, low, crops), mids[window], TN)
            )
        even = sum(
            jnp.where(lane_mask(GROUP * g, GROUP * (g + 1)), pieces[0][GROUP * g : GROUP * (g + 1)], 0.0)
            for g in range(4)
        )
        odd = sum(
            jnp.where(
                lane_mask(32 + GROUP * g, 32 + GROUP * (g + 1)),
                pieces[1][32 + GROUP * g : 32 + GROUP * (g + 1)],
                0.0,
            )
            for g in range(4)
        )
        across = jnp.where(
            centre, jnp.where(row < GROUP // 2, pieces[2][96:152], pieces[2][104:160]), 0.0
        )
        nothing = jnp.zeros((GROUP, 128), f32)
        even = even + jnp.concatenate([nothing, across[:, :128]], 1)
        odd = odd + jnp.concatenate([across[:, 128:], nothing], 1)
        hold_ref[0, pl.ds(GROUP * tap, GROUP), :] = even
        hold_ref[1, pl.ds(GROUP * tap, GROUP), :] = odd
    grads_ref[:, : 9 * GROUP, :] = hold_ref[...].astype(bf16)
    grads_ref[:, 9 * GROUP :, :] = jnp.zeros((2, LANES - 9 * GROUP, 256), bf16)


def conv_back(g, a2, sums2, grad_sums, a, sums, norms, windows, count):
    rows, width = a.shape
    crops = rows // PIXELS
    return pl.pallas_call(
        functools.partial(conv_back_kernel, crops, count),
        grid=(QUADS,),
        in_specs=[
            quad_spec(rows), quad_spec(rows), quad_spec(2), quad_spec(2), quad_spec(rows),
            quad_spec(2), quad_spec(6),
            pl.BlockSpec((1, 3, 9, 256, 256), lambda q: (q, 0, 0, 0, 0)),
        ],
        out_specs=[
            quad_spec(rows), pl.BlockSpec((2, LANES, 256), lambda q: (q, 0, 0)), quad_spec(2),
        ],
        scratch_shapes=[
            pltpu.VMEM((2 * PITCH + 256 * crops, LANES), f32),
            pltpu.VMEM((3, 256 * crops, LANES), bf16),
            pltpu.VMEM((2 * PITCH + 256 * crops, LANES), f32),
            pltpu.VMEM((3, 256 * crops, LANES), bf16),
            pltpu.VMEM((PITCH * HW * crops, LANES), f32),
            pltpu.VMEM((rows, LANES), f32),
            pltpu.VMEM((2, 9 * GROUP, 256), f32),
        ],
        out_shape=[
            jax.ShapeDtypeStruct((rows, width), bf16),
            jax.ShapeDtypeStruct((8, LANES, 256), bf16),
            jax.ShapeDtypeStruct((2, width), f32),
        ],
        compiler_params=params(),
        cost_estimate=BRIEF,
        name="conv_back",
    )(g, a2, sums2, grad_sums, a, sums, norms, windows)


def squeeze_weight(se_ref, d):
    return jnp.concatenate([se_ref[d, m, :, :128] for m in range(QUADS)], 1)


def excite_weight(se_ref, m):
    return jnp.concatenate(
        [
            jnp.concatenate(
                [se_ref[d, m, 64 * i : 64 * (i + 1), 128:] for i in range(4)], 1
            )
            for d in range(2 * QUADS)
        ],
        0,
    )


def rows_of_crops(values, rows):
    row = lax.broadcasted_iota(jnp.int32, (rows, 1), 0)
    out = values[0:1]
    for c in range(1, values.shape[0]):
        out = jnp.where(row >= PIXELS * c, values[c : c + 1], out)
    return out


def fetch_pieces(me_ref, pieces, hold_ref, sems, offset):
    size = hold_ref.shape[2]
    copies = [
        pltpu.make_async_copy(
            piece.at[pl.ds(offset + m * size, size)],
            hold_ref.at[me_ref[0] ^ b, m],
            sems.at[b * QUADS + m],
        )
        for b, piece in enumerate(pieces)
        for m in range(QUADS)
    ]
    for copy in copies:
        copy.start()
    return copies


def fetch_scratch(size):
    return [
        pltpu.VMEM((2 * QUADS, QUADS, size, 256), bf16),
        pltpu.SemaphoreType.DMA((8 * QUADS,)),
    ]


def gate_kernel(crops, count, me_ref, a_ref, sums_ref, norms_ref, *refs):
    h_ref, pooled_ref, squeezed_ref, act_ref, gate_ref, f2_ref, se_ref, sems = refs[8:]
    copies = fetch_pieces(me_ref, refs[:8], se_ref, sems, 0)
    rows = a_ref.shape[0]
    _, _, scale, shift = affine(sums_ref[...], norms_ref[...], 1, count)
    f2_ref[...] = swish(a_ref[...].astype(f32) * scale + shift)
    pooled = jnp.concatenate(
        [
            jnp.sum(f2_ref[pl.ds(PIXELS * c, PIXELS), :], 0, keepdims=True) / PIXELS
            for c in range(crops)
        ],
        0,
    ).astype(bf16)
    pooled_ref[...] = pooled
    for copy in copies:
        copy.wait()
    squeezed = sum(
        dot(pooled[:, 256 * d : 256 * (d + 1)], squeeze_weight(se_ref, d)) for d in range(8)
    )
    squeezed_ref[...] = squeezed
    act = swish(squeezed).astype(bf16)
    act_ref[...] = act
    for m in range(QUADS):
        lanes = pl.ds(m * LANES, LANES)
        gate = 1.0 / (1.0 + jnp.exp(-dot(act, excite_weight(se_ref, m))))
        gate_ref[:, lanes] = gate
        h_ref[m] = (f2_ref[:, lanes] * rows_of_crops(gate, rows)).astype(bf16)


def gate(a, sums, norms, se, count):
    rows, width = a.shape
    crops = rows // PIXELS
    return pl.pallas_call(
        functools.partial(gate_kernel, crops, count),
        in_specs=[SCALAR] + [pl.BlockSpec(memory_space=pltpu.VMEM)] * 3
        + [pl.BlockSpec(memory_space=pl.ANY)] * 8,
        out_shape=[
            jax.ShapeDtypeStruct((QUADS, rows, LANES), bf16),
            jax.ShapeDtypeStruct((crops, width), bf16),
            jax.ShapeDtypeStruct((crops, 512), f32),
            jax.ShapeDtypeStruct((crops, 512), bf16),
            jax.ShapeDtypeStruct((crops, width), f32),
        ],
        scratch_shapes=[pltpu.VMEM((rows, width), f32)] + fetch_scratch(SE_ROWS),
        compiler_params=params(),
        cost_estimate=BRIEF,
        name="gate",
    )(index_scalar("dp"), a, sums, norms, *se)


def gate_back_kernel(
    crops, count, me_ref, dh_from, a_ref, sums_ref, norms_ref, gate_ref, squeezed_ref, *refs
):
    (
        q_to, stats_ref, excite_grad_ref, squeeze_grad_ref,
        work_ref, dh_ref, q_ref, in_sems, out_sems, se_ref, sems,
    ) = refs[8:]

    def into(m):
        lanes = pl.ds(m * LANES, LANES)
        return pltpu.make_async_copy(dh_from.at[:, lanes], dh_ref.at[:, lanes], in_sems.at[m])

    def out_of(m):
        lanes = pl.ds(m * LANES, LANES)
        return pltpu.make_async_copy(q_ref.at[:, lanes], q_to.at[:, lanes], out_sems.at[m])

    for m in range(QUADS):
        into(m).start()
    copies = fetch_pieces(me_ref, refs[:8], se_ref, sems, 0)
    rows = a_ref.shape[0]
    for m in range(QUADS):
        into(m).wait()
        lanes = pl.ds(m * LANES, LANES)
        _, _, scale, shift = affine(sums_ref[:, lanes], norms_ref[:, lanes], 1, count)
        normed = a_ref[:, lanes].astype(f32) * scale + shift
        work_ref[:, lanes] = dh_ref[:, lanes] * swish(normed)
    sums = jnp.concatenate(
        [
            jnp.sum(work_ref[pl.ds(PIXELS * c, PIXELS), :], 0, keepdims=True)
            for c in range(crops)
        ],
        0,
    )
    gates = gate_ref[...]
    excite_grad = (sums * gates * (1.0 - gates)).astype(bf16)
    excite_grad_ref[...] = excite_grad
    for copy in copies:
        copy.wait()
    act_grad = sum(
        dot(excite_grad[:, m * LANES : (m + 1) * LANES], excite_weight(se_ref, m), NT)
        for m in range(QUADS)
    )
    squeeze_grad = (act_grad * swish_slope(squeezed_ref[...])).astype(bf16)
    squeeze_grad_ref[...] = squeeze_grad
    for d in range(8):
        lanes = pl.ds(d * 256, 256)
        pooled_grad = dot(squeeze_grad, squeeze_weight(se_ref, d), NT) / PIXELS
        values = a_ref[:, lanes].astype(f32)
        mean, inverse, scale, shift = affine(sums_ref[:, lanes], norms_ref[:, lanes], 1, count)
        normed = values * scale + shift
        q = (
            dh_ref[:, lanes] * rows_of_crops(gate_ref[:, lanes], rows)
            + rows_of_crops(pooled_grad, rows)
        ) * swish_slope(normed)
        q_ref[:, lanes] = q
        centred = (values - mean) * inverse
        stats_ref[0:1, lanes] = jnp.sum(q, 0, keepdims=True)
        stats_ref[1:2, lanes] = jnp.sum(q * centred, 0, keepdims=True)
        if d % 2:
            out_of(d // 2).start()
    for m in range(QUADS):
        out_of(m).wait()


def gate_back(dh, a, sums, norms, gates, squeezed, se, count):
    rows, width = a.shape
    crops = rows // PIXELS
    return pl.pallas_call(
        functools.partial(gate_back_kernel, crops, count),
        in_specs=[SCALAR, pl.BlockSpec(memory_space=pl.ANY)]
        + [pl.BlockSpec(memory_space=pltpu.VMEM)] * 5
        + [pl.BlockSpec(memory_space=pl.ANY)] * 8,
        out_specs=[pl.BlockSpec(memory_space=pl.ANY)] + [pl.BlockSpec(memory_space=pltpu.VMEM)] * 3,
        out_shape=[
            jax.ShapeDtypeStruct((rows, width), f32),
            jax.ShapeDtypeStruct((2, width), f32),
            jax.ShapeDtypeStruct((crops, width), bf16),
            jax.ShapeDtypeStruct((crops, 512), bf16),
        ],
        scratch_shapes=[pltpu.VMEM((rows, width), f32)] * 3
        + [pltpu.SemaphoreType.DMA((QUADS,))] * 2
        + fetch_scratch(SE_ROWS),
        compiler_params=params(),
        cost_estimate=BRIEF,
        name="gate_back",
    )(index_scalar("dp"), dh, a, sums, norms, gates, squeezed, *se)


def head_kernel(
    width, me_ref, summary_ref, *refs
):
    (
        loss_ref, unit_ref, score_grad_ref, embed_grad_ref, summary_grad_ref, all_ref,
        hold_ref, plan_ref, protos_ref, queue_ref, project_ref, bundle_ref, sems,
    ) = refs[8:]
    copies = fetch_pieces(me_ref, refs[:8], bundle_ref, sems, 0)
    crops = all_ref.shape[0]
    each = summary_ref.shape[1]
    for i in range(summary_ref.shape[0]):
        hold_ref[pl.ds(each * i, each), :] = summary_ref[i].astype(f32)
    all_ref[...] = hold_ref[...].astype(bf16)
    for copy in copies:
        copy.wait()
    parts = 2 * QUADS * QUADS
    for i in range(parts):
        d, m = i // QUADS, i % QUADS
        low = 64
        project_ref[d, pl.ds(64 * m, 64), :] = bundle_ref[d, m, 0:low, :]
        protos_ref[pl.ds(PROTO_ROWS * i, PROTO_ROWS), :] = bundle_ref[d, m, low : low + PROTO_ROWS, :]
        low = low + PROTO_ROWS
        queue_ref[pl.ds(QUEUE_ROWS * i, QUEUE_ROWS), :] = bundle_ref[d, m, low : low + QUEUE_ROWS, :]
    protos = protos_ref[...]
    embedded = sum(
        dot(all_ref[:, 256 * d : 256 * (d + 1)], project_ref[d], NT) for d in range(8)
    )
    scale = lax.rsqrt(jnp.sum(embedded * embedded, 1, keepdims=True) + EPS_NORM)
    unit = (embedded * scale).astype(bf16)
    unit_ref[...] = unit
    scores = dot(unit, protos, NT)
    lane = lax.broadcasted_iota(jnp.int32, (1, parts * PROTO_ROWS), 1)
    block = lane // PROTO_ROWS
    there = (block // QUADS) * PROTO_ROWS + (lane - block * PROTO_ROWS) < width
    first = jnp.where(there, jnp.exp(scores / EPS_SINK), 0.0)
    plan_ref[pl.ds(0, crops), :] = first

    size, large_size = 4 * crops, 8 * crops

    def partial_sums(value):
        return jnp.sum(value.reshape(-1, 8, value.shape[1]), 0)

    def rows_at(i):
        return pl.ds(pl.multiple_of(crops + i * size, crops), size)

    def fill(i, column):
        place = pl.multiple_of(i * large_size, large_size)
        value = jnp.exp(dot(queue_ref[pl.ds(place, large_size), :], protos, NT) / EPS_SINK)
        plan_ref[pl.ds(pl.multiple_of(place + crops, crops), large_size), :] = value
        return column + partial_sums(value)

    steps = parts * QUEUE_ROWS // size
    column = lax.fori_loop(
        0, parts * QUEUE_ROWS // large_size, fill, partial_sums(first)
    )
    column = jnp.sum(column, 0, keepdims=True)
    large = jnp.where(column > 1e37, 2.0**-8, 1.0)
    inverse = jnp.where(there, 1.0 / (column * large), 0.0)
    for sweep in range(SINK - 1):

        def balanced(place, inverse=inverse, sweep=sweep):
            value = plan_ref[place, :]
            if sweep == 0:
                value = value * large
            value = value * inverse
            value = value * (1.0 / jnp.sum(value, 1, keepdims=True))
            plan_ref[place, :] = value
            return partial_sums(value)

        column = lax.fori_loop(
            0, steps, lambda i, column: column + balanced(rows_at(i)), balanced(pl.ds(0, crops))
        )
        inverse = jnp.where(there, 1.0 / jnp.sum(column, 0, keepdims=True), 0.0)
    value = plan_ref[pl.ds(0, crops), :] * inverse
    value = value / jnp.sum(value, 1, keepdims=True)
    pairs = jnp.concatenate(
        [bundle_ref[d, 0, HEAD_ROWS - 16 : HEAD_ROWS, :].astype(f32)[:8, :crops] for d in range(8)], 0
    )
    plan = lax.dot_general(
        pairs, value, NN, precision=lax.Precision.HIGHEST, preferred_element_type=f32
    )
    logits = scores / SOFTMAX_TEMPER
    top = jnp.max(jnp.where(there, logits, -jnp.inf), 1, keepdims=True)
    power = jnp.where(there, jnp.exp(logits - top), 0.0)
    mass = jnp.sum(power, 1, keepdims=True)
    entropy = jnp.sum(plan * (logits - (top + jnp.log(mass))), 1, keepdims=True)
    loss_ref[...] = -jnp.sum(entropy, 0, keepdims=True) / crops
    score_grad = ((power / mass - plan) / (SOFTMAX_TEMPER * crops)).astype(bf16)
    score_grad_ref[...] = score_grad.T
    unit_grad = dot(score_grad, protos)
    inner = jnp.sum(embedded * unit_grad, 1, keepdims=True)
    embed_grad = (scale * unit_grad - embedded * (scale * scale * scale * inner)).astype(bf16)
    embed_grad_ref[...] = embed_grad
    for d in range(8):
        summary_grad_ref[:, 256 * d : 256 * (d + 1)] = dot(embed_grad, project_ref[d])


def head(summary, bundle, width):
    devices, each, channels = summary.shape
    crops = devices * each
    parts = 2 * QUADS * QUADS
    return pl.pallas_call(
        functools.partial(head_kernel, width),
        in_specs=[SCALAR, pl.BlockSpec(memory_space=pltpu.VMEM)]
        + [pl.BlockSpec(memory_space=pl.ANY)] * 8,
        out_shape=[
            jax.ShapeDtypeStruct((1, 1), f32),
            jax.ShapeDtypeStruct((crops, 256), bf16),
            jax.ShapeDtypeStruct((parts * PROTO_ROWS, crops), bf16),
            jax.ShapeDtypeStruct((crops, 256), bf16),
            jax.ShapeDtypeStruct((crops, channels), f32),
            jax.ShapeDtypeStruct((crops, channels), bf16),
        ],
        scratch_shapes=[
            pltpu.VMEM((crops, channels), f32),
            pltpu.VMEM((crops + parts * QUEUE_ROWS, parts * PROTO_ROWS), f32),
            pltpu.VMEM((parts * PROTO_ROWS, 256), bf16),
            pltpu.VMEM((parts * QUEUE_ROWS, 256), bf16),
            pltpu.VMEM((8, 256, 256), bf16),
        ]
        + fetch_scratch(HEAD_ROWS),
        compiler_params=params(),
        cost_estimate=BRIEF,
        name="head",
    )(index_scalar("dp"), summary, *bundle)


def plain_head(summary, project, protos, queue, pairs):
    crops = summary.shape[0]
    embedded = dot(summary, project)
    scale = lax.rsqrt(jnp.sum(embedded * embedded, 1, keepdims=True) + EPS_NORM)
    unit = (embedded * scale).astype(bf16)
    scores = dot(unit, protos)
    plan = jnp.exp(jnp.concatenate([scores, dot(queue, protos)], 0) / EPS_SINK)
    for sweep in range(SINK):
        plan = plan / jnp.sum(plan, 0, keepdims=True)
        plan = plan / jnp.sum(plan, 1, keepdims=True)
    plan = lax.dot_general(
        pairs, plan[:crops], NN, precision=lax.Precision.HIGHEST, preferred_element_type=f32
    )
    logits = scores / SOFTMAX_TEMPER
    loss = -jnp.sum(plan * jax.nn.log_softmax(logits, axis=1)) / crops
    score_grad = ((jax.nn.softmax(logits, axis=1) - plan) / (SOFTMAX_TEMPER * crops)).astype(bf16)
    unit_grad = dot(score_grad, protos, NT)
    inner = jnp.sum(embedded * unit_grad, 1, keepdims=True)
    embed_grad = (scale * unit_grad - embedded * (scale * scale * scale * inner)).astype(bf16)
    return loss.reshape(1, 1), unit, score_grad, embed_grad, dot(embed_grad, project, NT)


def picks(rows, columns, source):
    row = lax.broadcasted_iota(jnp.int32, (rows, columns), 0)
    column = lax.broadcasted_iota(jnp.int32, (rows, columns), 1)
    return jnp.where(row == source(column), 1.0, 0.0).astype(bf16)


def narrow_lanes(v):
    return jnp.concatenate([v[:, :HALF], v[:, HALF + GAP :]], 1)


def square_sum(v):
    return jnp.sum(jnp.sum(v * v, 1, keepdims=True), 0, keepdims=True)


def small_grads_kernel(
    m_ref, small_ref, summary_ref, embed_grad_ref, score_grad_ref, unit_ref,
    squeeze_ref, excite_ref, project_ref, protos_ref, squares_ref, hold_ref,
):
    m = m_ref[0]
    devices, each, _ = small_ref.shape
    for i in range(devices):
        hold_ref[pl.ds(each * i, each), :] = small_ref[i].astype(f32)
    wide, inner = QUADS * LANES, 8 * SE_LANES

    def rows_of(base, size):
        return hold_ref[:, pl.ds(pl.multiple_of(base, 128), size)]

    squeeze_grad = rows_of(wide + inner + 128 * m, 128).astype(bf16)
    squeeze_grad = dot(
        squeeze_grad, picks(128, 2 * SE_PART, lambda c: (c // SE_PART) * SE_LANES + c % SE_PART)
    ).astype(bf16)
    squares = []
    total_square = jnp.zeros((1, 1), f32)
    for q in range(QUADS):
        pooled = narrow_lanes(rows_of(q * LANES, LANES)).astype(bf16)
        part = dot(pooled, squeeze_grad, TN)
        squeeze_ref[pl.ds(QUAD * q, QUAD), :] = part
        total_square = total_square + square_sum(part)
    squares.append(total_square)
    act = rows_of(wide, inner).astype(bf16)
    act = dot(act, picks(inner, QUAD, lambda c: (c // SE_PART) * SE_LANES + c % SE_PART)).astype(bf16)
    excite_grad = narrow_lanes(rows_of(wide + 2 * inner + LANES * m, LANES)).astype(bf16)
    part = dot(act, excite_grad, TN)
    excite_ref[...] = part
    squares.append(square_sum(part))
    embed_grad = dot(embed_grad_ref[...], picks(256, 64, lambda c: 64 * m + c)).astype(bf16)
    summary = jnp.concatenate(
        [
            narrow_lanes(summary_ref[:, q * LANES : (q + 1) * LANES].astype(f32))
            for q in range(QUADS)
        ],
        1,
    ).astype(bf16)
    part = dot(embed_grad, summary, TN)
    project_ref[...] = part
    squares.append(square_sum(part))
    total_square = jnp.zeros((1, 1), f32)
    last = protos_ref.shape[0]
    for d in range(8):
        place = pl.ds(pl.multiple_of((QUADS * d + m) * PROTO_ROWS, PROTO_ROWS), PROTO_ROWS)
        part = dot(score_grad_ref[place, :], unit_ref[...])
        size = min(PROTO_ROWS, last - PROTO_ROWS * d)
        protos_ref[pl.ds(PROTO_ROWS * d, size), :] = part[:size]
        total_square = total_square + square_sum(part)
    squares.append(total_square)
    lane = lax.broadcasted_iota(jnp.int32, (1, 128), 1)
    squares_ref[...] = sum(jnp.where(lane == i, v, 0.0) for i, v in enumerate(squares))


def small_grads(small, summary, embed_grad, score_grad, unit, width):
    crops = summary.shape[0]
    return pl.pallas_call(
        small_grads_kernel,
        in_specs=[SCALAR] + [pl.BlockSpec(memory_space=pltpu.VMEM)] * 5,
        out_shape=[
            jax.ShapeDtypeStruct((QUADS * QUAD, 2 * SE_PART), f32),
            jax.ShapeDtypeStruct((QUAD, QUAD), f32),
            jax.ShapeDtypeStruct((64, QUADS * QUAD), f32),
            jax.ShapeDtypeStruct((width, 256), f32),
            jax.ShapeDtypeStruct((1, 128), f32),
        ],
        scratch_shapes=[pltpu.VMEM((crops, small.shape[2]), f32)],
        compiler_params=params(),
        cost_estimate=BRIEF,
        name="small_grads",
    )(index_scalar("mp"), small, summary, embed_grad, score_grad, unit)


def own_kernel_kernel(me_ref, v_ref, out_ref):
    value = v_ref[: 9 * GROUP].astype(f32)
    out_ref[...] = jnp.where(me_ref[0] % 2 == 1, value[:, 256 - HALF :], value[:, :HALF])


def own_kernel(v):
    return pl.pallas_call(
        own_kernel_kernel,
        in_specs=[SCALAR, pl.BlockSpec(memory_space=pltpu.VMEM)],
        out_shape=jax.ShapeDtypeStruct((9 * GROUP, HALF), f32),
        compiler_params=params(),
        cost_estimate=BRIEF,
        name="own_kernel",
    )(index_scalar("dp"), v)


def weight_sums_kernel(*refs):
    lane = lax.broadcasted_iota(jnp.int32, (1, 128), 1)
    refs[-1][...] = sum(
        jnp.where(lane == i, square_sum(ref[...]), 0.0) for i, ref in enumerate(refs[:-1])
    )


def weight_sums(weights):
    values = [w if w.shape[1] == 2 * SE_PART or w.shape[0] == w.shape[1] else w.T for w in weights]
    return pl.pallas_call(
        weight_sums_kernel,
        out_shape=jax.ShapeDtypeStruct((1, 128), f32),
        compiler_params=params(),
        cost_estimate=BRIEF,
        name="weight_sums",
    )(*values)


def squares_kernel(
    n_dp, n_mp, weights_ref, norms_ref, small_ref, expand_ref, g1_ref, g2_ref, g3_ref, out_ref,
):
    lane = lax.broadcasted_iota(jnp.int32, (1, 128), 1)

    def at(i, v):
        return jnp.where(lane == i, v, 0.0)

    portions = at(0, 1.0) + at(1, 1.0 / n_mp) + at(4, 1.0)
    for i in (2, 3, 5, 6):
        portions = portions + at(i, 1.0 / n_dp)
    weights = weights_ref[...] * portions
    small = small_ref[...]
    grads = at(4, expand_ref[...])
    for i, k in enumerate((2, 3, 5, 6)):
        grads = grads + at(k, small[:, i : i + 1] / n_dp)
    everywhere = 1.0 / (n_dp * n_mp)
    for k, ref in enumerate((g1_ref, g2_ref, g3_ref)):
        for row, first in ((1, 7), (0, 10)):
            grads = grads + at(first + k, square_sum(ref[row : row + 1, :]) * everywhere)
        weights = weights + at(7 + k, square_sum(norms_ref[k : k + 1, :]) * everywhere)
        weights = weights + at(10 + k, square_sum(norms_ref[3 + k : 4 + k, :]) * everywhere)
    out_ref[0:1, :] = weights
    out_ref[1:2, :] = grads


def squares(n_dp, n_mp, *values):
    return pl.pallas_call(
        functools.partial(squares_kernel, n_dp, n_mp),
        out_shape=jax.ShapeDtypeStruct((2, 128), f32),
        compiler_params=params(),
        cost_estimate=BRIEF,
        name="squares",
    )(*values)


def rate_of(norm_squares, i):
    norms = jnp.sqrt(norm_squares[:, i : i + 1] + EPS_NORM)
    return TRUST * norms[0:1] / (norms[1:2] + DECAY * norms[0:1])


def step(weight, gradient, momentum, norm_squares, i):
    return MOMENTUM * momentum + rate_of(norm_squares, i) * (gradient + DECAY * weight)


def lars_prepare_kernel(*refs):
    n = len(refs) // 5
    for i in range(n):
        weight, gradient, momentum = (refs[3 * i + j] for j in range(3))
        refs[3 * n + 2 * i][...] = gradient[...] + DECAY * weight[...]
        refs[3 * n + 2 * i + 1][...] = MOMENTUM * momentum[...]


def lars_prepare(items):
    return pl.pallas_call(
        lars_prepare_kernel,
        out_shape=[jax.ShapeDtypeStruct(w.shape, f32) for w, _, _ in items for _ in range(2)],
        compiler_params=params(),
        cost_estimate=BRIEF,
        name="lars_prepare",
    )(*[v for item in items for v in item])


def lars_kernel(
    first, n, m_ref, squares_ref, gains_ref, biases_ref, m_gains_ref, m_biases_ref,
    g1_ref, g2_ref, g3_ref, *refs
):
    size = 3 * first + 2 * n
    sources, refs = refs[:size], refs[size:]
    targets, refs = refs[: first + n], refs[first + n :]
    gains_out, biases_out, refs = refs[0], refs[1], refs[2:]
    held, out, (in_sems, out_sems) = refs[:size], refs[size : size + first + n], refs[-2:]

    def into(i):
        return pltpu.make_async_copy(sources[i], held[i], in_sems.at[i])

    def out_of(i):
        return pltpu.make_async_copy(out[i], targets[i], out_sems.at[i])

    for i in range(size):
        into(i).start()
    norm_squares = squares_ref[...]
    lanes = pl.ds(pl.multiple_of(m_ref[0] * LANES, LANES), LANES)
    for k, ref in enumerate((g1_ref, g2_ref, g3_ref)):
        own = narrow_lanes(ref[:, lanes])
        row = slice(k, k + 1)
        gains_out[row, :] = step(
            gains_ref[row, :], own[1:2], m_gains_ref[row, :], norm_squares, 7 + k
        )
        biases_out[row, :] = step(
            biases_ref[row, :], own[0:1], m_biases_ref[row, :], norm_squares, 10 + k
        )
    for i in range(first):
        for j in range(3):
            into(3 * i + j).wait()
        weight, gradient, momentum = (held[3 * i + j][...] for j in range(3))
        out[i][...] = step(weight, gradient, momentum, norm_squares, i)
        out_of(i).start()
    for i in range(n):
        at = 3 * first + 2 * i
        into(at).wait()
        into(at + 1).wait()
        out[first + i][...] = held[at + 1][...] + rate_of(norm_squares, first + i) * held[at][...]
        out_of(first + i).start()
    for i in range(first + n):
        out_of(i).wait()


def lars(norm_squares, items, norm_values, prepared):
    shapes = [w.shape for w, _, _ in items] + [v.shape for v in prepared[::2]]
    moved = [v for item in items for v in item] + list(prepared)
    fixed = [norm_squares, *norm_values]
    anywhere, vmem = pl.BlockSpec(memory_space=pl.ANY), pl.BlockSpec(memory_space=pltpu.VMEM)
    return pl.pallas_call(
        functools.partial(lars_kernel, len(items), len(prepared) // 2),
        in_specs=[SCALAR] + [vmem] * len(fixed) + [anywhere] * len(moved),
        out_specs=[anywhere] * len(shapes) + [vmem] * 2,
        out_shape=[jax.ShapeDtypeStruct(shape, f32) for shape in shapes + [norm_values[0].shape] * 2],
        scratch_shapes=[pltpu.VMEM(v.shape, f32) for v in moved]
        + [pltpu.VMEM(shape, f32) for shape in shapes]
        + [pltpu.SemaphoreType.DMA((len(moved),)), pltpu.SemaphoreType.DMA((len(shapes),))],
        compiler_params=params(),
        cost_estimate=BRIEF,
        name="lars",
    )(index_scalar("mp"), *fixed, *moved)


def plain_finish(
    small, summary, unit, score_grad, embed_grad, grad_sums, channels_here, big_grads, weights, moments
):
    n_dp, n_mp, m_index = lax.axis_size("dp"), lax.axis_size("mp"), lax.axis_index("mp")
    w_reduce, w_group, w_squeeze, w_excite, w_expand, w_project, prototypes, bn_gains, bn_biases = weights
    small = small.reshape(-1, small.shape[-1])
    wide, inner = QUADS * LANES, 8 * SE_LANES
    pooled_all = pack_channels(small[:, :wide])
    act_all = pack_inner(small[:, wide : wide + inner])
    squeeze_all = pack_inner(small[:, wide + inner : wide + 2 * inner])
    excite_all = pack_channels(small[:, wide + 2 * inner :])

    def own(v, width):
        return lax.dynamic_slice_in_dim(v, m_index * width, width, 1)

    reduce_grad, kernel_grad, expand_grad = big_grads
    gain_part = own(pack_channels(jnp.stack([v[1] for v in grad_sums])), channels_here)
    bias_part = own(pack_channels(jnp.stack([v[0] for v in grad_sums])), channels_here)
    grads = [
        reduce_grad,
        kernel_grad,
        dot(pooled_all, own(squeeze_all, w_squeeze.shape[1]), TN),
        dot(act_all, own(excite_all, w_excite.shape[1]), TN),
        expand_grad,
        dot(pack_channels(summary), own(embed_grad, w_project.shape[1]), TN),
        dot(unit, own(score_grad, prototypes.shape[1]), TN),
    ]
    portions = [1.0, 1.0 / n_mp, 1.0 / n_dp, 1.0 / n_dp, 1.0, 1.0 / n_dp, 1.0 / n_dp]

    def shares(arrays, gain, bias):
        return jnp.concatenate(
            [
                jnp.stack([jnp.sum(a * a) * p for a, p in zip(arrays, portions)]),
                jnp.sum(gain * gain, 1) / n_dp,
                jnp.sum(bias * bias, 1) / n_dp,
            ]
        )

    norms = total(
        jnp.stack([shares(weights[:7], bn_gains, bn_biases), shares(grads, gain_part, bias_part)])
    )
    stepped = [
        step(w, g, m, norms, i) for i, (w, g, m) in enumerate(zip(weights[:7], grads, moments[:7]))
    ]
    for values, part, momentum, first in (
        (bn_gains, gain_part, moments[7], 7), (bn_biases, bias_part, moments[8], 10),
    ):
        stepped.append(
            jnp.concatenate(
                [
                    step(values[k : k + 1], part[k : k + 1], momentum[k : k + 1], norms, first + k)
                    for k in range(3)
                ]
            )
        )
    return stepped, norms


def body(
    block_input, output_grad, w_reduce, w_group, w_squeeze, w_excite, w_expand, w_project,
    prototypes, bn_gains, bn_biases, m_reduce, m_group, m_squeeze, m_excite, m_expand,
    m_project, m_protos, m_gains, m_biases, queue_store, queue_slots, crop_perm,
):
    n_dp = lax.axis_size("dp")
    n_mp = lax.axis_size("mp")
    m_index = lax.axis_index("mp")
    channels_here = block_input.shape[0]
    rows = block_input.shape[1] // n_mp
    crops = rows // PIXELS
    count = rows * n_dp * n_mp
    all_crops = crops * n_dp * n_mp
    quick = quick_mesh()
    weights = [
        w_reduce, w_group, w_squeeze, w_excite, w_expand, w_project, prototypes, bn_gains, bn_biases,
    ]
    moments = [
        m_reduce, m_group, m_squeeze, m_excite, m_expand, m_project, m_protos, m_gains, m_biases,
    ]

    slot_table = (
        queue_slots[0][:, None]
        == lax.broadcasted_iota(jnp.int32, (queue_slots.shape[1], queue_store.shape[0]), 1)
    ).astype(bf16)
    queue_rows = dot(slot_table, queue_store.astype(bf16)).astype(bf16)
    order = crop_perm[0]
    pairing = (order[None, :] == jnp.bitwise_xor(order, 1)[:, None]).astype(f32)
    kernel_low = gather_kernel(w_group)
    x_blocks = slab_blocks(block_input)
    y_grad_blocks = slab_blocks(output_grad)
    norms = spread(jnp.concatenate([bn_gains, bn_biases], 0), "mp")
    norms = spread_channels(norms.transpose(1, 0, 2).reshape(norms.shape[1], -1))
    if quick:
        low = gather_mp(shard_square(w_reduce)).reshape(-1, 256)
        expand_low = shard_square(w_expand)
        se_low = shard_excitation(w_squeeze, w_excite)
        low, x_blocks, norms, expand_low, se_low, *kernel_low = tie(
            low, x_blocks, norms, expand_low, se_low, *kernel_low
        )
        across, up = gather_sides(low)
        x_blocks = exchange(x_blocks)
        windows = dense_windows(kernel_low)
        across, up, windows = tie(across, up, windows)
        corner = gather_corner(across, up)
        x_blocks, se_low = tie(x_blocks, se_low)
        se_low = spread(se_low, "mp").reshape(-1, 256)
        reduce_pieces = gather_twins(low, across, up, corner)
        head_values = tie(w_project, prototypes, queue_rows, pairing, corner)
        bundle = shard_head(*head_values[:4])
    else:
        x_blocks = exchange(x_blocks)
        y_grad_parts = list(quad_blocks(exchange(y_grad_blocks)))
        reduce_pieces = gather_square(w_reduce)
        se_pieces = list(gather_excitation(w_squeeze, w_excite).reshape(8, -1, 256))
        expand_pieces = gather_square(w_expand)
        project_low, protos_low, queue_low, pairs = gather_head(
            w_project, prototypes, queue_rows, pairing
        )
        pairs = block_diagonal(pairs)
        windows = dense_windows(kernel_low)
    x = quad_blocks(x_blocks)

    reduced, sums1 = mix(x, reduce_pieces)
    if quick:
        sums1 = sum_axis(sums1, "dp")
        sums1, se_low = tie(sums1, se_low)
        se_across, se_up = gather_sides(se_low)
        sums1 = sum_axis(sums1, "mp")
        sums1, expand_low, se_across, se_up = tie(sums1, expand_low, se_across, se_up)
        expand_low = spread(expand_low, "mp").reshape(-1, 256)
        se_corner = gather_corner(se_across, se_up)
        y_grad_parts = [
            lax.dynamic_index_in_dim(y_grad_blocks, m_index ^ k, 0, keepdims=False) for k in range(QUADS)
        ]
    else:
        sums1 = total(sums1)
    grouped, sums2 = conv(reduced, sums1, norms, windows, count)
    if quick:
        sums2, se_corner = tie(sums2, se_corner)
        se_pieces = gather_twins(se_low, se_across, se_up, se_corner)
        sums2 = sum_axis(sums2, "dp")
        sums2, expand_low = tie(sums2, expand_low)
        across, up = gather_sides(expand_low)
        sums2 = sum_axis(sums2, "mp")
    else:
        sums2 = total(sums2)
    if quick:
        sums2, bundle, y_grad_parts[1], y_grad_parts[2] = tie(
            sums2, bundle, y_grad_parts[1], y_grad_parts[2]
        )
        bundle = spread(bundle, "mp").reshape(-1, 256)
        y_grad_parts[1] = lax.ppermute(y_grad_parts[1], "mp", flips("mp", 1))
        y_grad_parts[2] = lax.ppermute(y_grad_parts[2], "mp", flips("mp", 2))
    gated, pooled, squeezed, squeeze_act, gates = gate(grouped, sums2, norms, se_pieces, count)
    if quick:
        gated, across, up = tie(gated, across, up)
        corner = gather_corner(across, up)
        corner, bundle = tie(corner, bundle)
        head_sides = gather_sides(bundle)
        expand_pieces = gather_twins(expand_low, across, up, corner)
    expanded, sums3 = mix(gated, expand_pieces)
    if quick:
        sums3, *head_sides = tie(sums3, *head_sides)
        sums3 = jnp.sum(spread(sums3, "dp"), 0)
        sums3, y_grad_parts[1], y_grad_parts[2], *head_sides = tie(
            sums3, y_grad_parts[1], y_grad_parts[2], *head_sides
        )
        head_corner = gather_corner(*head_sides)
        sums3 = jnp.sum(spread(sums3, "mp"), 0)
        sums3, head_corner = tie(sums3, head_corner)
        bundle = gather_twins(bundle, *head_sides, head_corner)
    else:
        sums3 = total(sums3)
    *y_parts, summary = block_value(x, expanded, sums3, norms, count)
    if quick:
        summary, *bundle = tie(summary, *bundle)
    summary = gather_all(summary)
    if quick:
        summary, y_grad_parts[3], y_parts[1] = tie(summary, y_grad_parts[3], y_parts[1])
        y_grad_parts[3] = lax.ppermute(y_grad_parts[3], "mp", flips("mp", 3))
        y_parts[1] = lax.ppermute(y_parts[1], "mp", flips("mp", 1))

    first_crop = ((lax.axis_index("dp") * n_mp + m_index) * crops).astype(jnp.int32)[None]
    if quick:
        loss, unit, score_grad, embed_grad, summary_grad, summary = head(
            summary, bundle, prototypes.shape[1]
        )
    else:
        summary = summary.reshape(all_crops, -1)
        loss, unit, score_grad, embed_grad, summary_grad = plain_head(
            summary, project_low, protos_low, queue_low, pairs
        )

    joined_grad, grad_sums3 = value_back(
        first_crop, x, expanded, sums3, norms, y_grad_parts, summary_grad, count
    )
    if quick:
        grad_sums3, y_parts[1] = tie(grad_sums3, y_parts[1])
    grad_sums3 = total(grad_sums3)
    if quick:
        grad_sums3, y_parts[2], y_parts[3] = tie(grad_sums3, y_parts[2], y_parts[3])
        y_parts[2] = lax.ppermute(y_parts[2], "mp", flips("mp", 2))
    expanded_grad, expand_all = all_grads(
        gated, joined_grad, expanded, sums3, norms, 2, grad_sums3, count
    )
    if quick:
        expand_part = lax.psum_scatter(expand_all, "dp", scatter_dimension=0, tiled=False)
    gated_grad = mix_back(expanded_grad, expand_pieces)
    act2_grad, grad_sums2, excite_grad, squeeze_grad = gate_back(
        gated_grad, grouped, sums2, norms, gates, squeezed, se_pieces, count
    )
    small = jnp.concatenate([pooled, squeeze_act, squeeze_grad, excite_grad], 1)
    if quick:
        grad_sums2, y_parts[2] = tie(grad_sums2, y_parts[2])
    grad_sums2 = total(grad_sums2)
    if quick:
        grad_sums2, small = tie(grad_sums2, small)
    small = gather_all(small)
    act1_grad, kernel_all, grad_sums1 = conv_back(
        act2_grad, grouped, sums2, grad_sums2, reduced, sums1, norms, windows, count
    )
    if quick:
        grad_sums1, kernel_all, small, expand_part = tie(
            grad_sums1, kernel_all, small, expand_part
        )
        expand_part = lax.psum_scatter(expand_part, "mp", scatter_dimension=0, tiled=False)
    grad_sums1 = total(grad_sums1)
    if quick:
        grad_sums1, y_parts[3] = tie(grad_sums1, y_parts[3])
        y_parts[3] = lax.ppermute(y_parts[3], "mp", flips("mp", 3))
    reduced_grad, reduce_sent = sent_grads(
        x, act1_grad, reduced, sums1, norms, 0, grad_sums1, count, True
    )
    if quick:
        reduced_grad, reduce_sent, expand_part, kernel_all = tie(
            reduced_grad, reduce_sent, expand_part, kernel_all
        )
        kernel_sum = lax.psum_scatter(kernel_all, "dp", scatter_dimension=0, tiled=False)
        reduce_got = from_twin(reduce_sent)
    reduce_kept = kept_grads(x, reduced_grad)
    if quick:
        reduced_grad, reduce_got, reduce_kept = tie(reduced_grad, reduce_got, reduce_kept)
        corner = scatter_corner(reduce_kept, reduce_got)
    x_grad = out_blocks(mix_back(reduced_grad, reduce_pieces, joined_grad))
    if quick:
        x_grad, corner, y_parts[3] = tie(x_grad, corner, y_parts[3])
        x_grad = exchange(x_grad)
        across, up = corner_sums(reduce_kept, reduce_got, corner)
        across, up, small = tie(across, up, small)
        across, up = scatter_sides(across, up)
        squeeze_part, excite_part, project_part, protos_part, small_squares = small_grads(
            small, summary, embed_grad, score_grad, unit, prototypes.shape[1]
        )
        expand_grad, expand_square = own_plain(expand_part)
        across, up, small_squares, expand_square, kernel_sum = tie(
            across, up, small_squares, expand_square, kernel_sum
        )
        kernel_sum = kernel_sum.reshape(QUADS, LANES // QUADS, 256)
        own, *parts = side_sums(reduce_kept, reduce_got, across, up, kernel_sum)
        parts = scatter_mp(own, parts)
        input_grad = out_channels(list(x_grad), channels_here, f32, jnp.zeros((1,), jnp.int32))
        block_output = out_channels(y_parts, channels_here, bf16, index_scalar("mp"))
        prepared = lars_prepare(
            [
                (w_squeeze, squeeze_part, m_squeeze),
                (w_excite, excite_part, m_excite),
                (w_expand.T, expand_grad, m_expand.T),
                (w_project.T, project_part, m_project.T),
                (prototypes.T, protos_part, m_protos.T),
            ]
        )
        weight_squares = weight_sums(weights[:7])
        shares = squares(
            n_dp, n_mp, weight_squares, norms, small_squares, expand_square,
            grad_sums1, grad_sums2, grad_sums3,
        )
        parts, input_grad, block_output, shares, *prepared = tie(
            parts, input_grad, block_output, shares, *prepared
        )
        reduce_grad, kernel_sum, big_squares = own_square(parts)
        kernel_sum = parts_mp(kernel_sum)
        norm_squares = jnp.sum(spread(shares + big_squares, "dp"), 0)
        norm_squares, *kernel_sum = tie(norm_squares, *kernel_sum)
        kernel_grad = own_kernel(in_order(kernel_sum, m_index).reshape(LANES, 256))
        norm_squares = jnp.sum(spread(norm_squares, "mp"), 0)
        (
            mom_reduce, mom_group, mom_squeeze, mom_excite, mom_expand, mom_project, mom_protos,
            mom_gains, mom_biases,
        ) = lars(
            norm_squares,
            [(w_reduce.T, reduce_grad, m_reduce.T), (w_group.T, kernel_grad, m_group.T)],
            [bn_gains, bn_biases, m_gains, m_biases, grad_sums1, grad_sums2, grad_sums3], prepared,
        )
        stepped = [
            mom_reduce.T, mom_group.T, mom_squeeze, mom_excite, mom_expand.T, mom_project.T,
            mom_protos.T, mom_gains, mom_biases,
        ]
    else:
        input_grad = natural_channels(exchange(x_grad), channels_here, f32)
        block_output = natural_channels(
            exchange(out_blocks(jnp.stack(y_parts))), channels_here, bf16
        )
        big_grads = (
            scatter_square(jnp.stack([reduce_kept, reduce_sent], 1).reshape(expand_all.shape)),
            scatter_kernel(kernel_all[:, : 9 * GROUP]),
            scatter_square(expand_all),
        )
        stepped, norm_squares = plain_finish(
            small, summary, unit, score_grad, embed_grad, (grad_sums1, grad_sums2, grad_sums3),
            channels_here, big_grads, weights, moments,
        )
    param_norms = jnp.sqrt(norm_squares[:, :13].T + EPS_NORM)
    return (block_output, loss[0, 0], input_grad, *stepped, param_norms)


def solution(mesh):
    split = P("dp", "mp")
    turned = P("mp", "dp")
    rows = P("dp", None)
    columns = P(None, "mp")
    return jax.shard_map(
        body,
        mesh=mesh,
        in_specs=(
            turned, turned, split, rows, columns, columns, split, columns, columns, columns, columns,
            split, rows, columns, columns, split, columns, columns, columns, columns, rows, rows, rows,
        ),
        out_specs=(
            turned, P(), turned, split, rows, columns, columns, split, columns, columns, columns,
            columns, P(),
        ),
        check_vma=False,
    )
```
